32 devices in a mesh: seq: 16 (over z, y, x), ffn: 2 (over core).
Axes of the slice: x: 2, y: 2, z: 4, core: 2. Of those that a mesh axis runs over, the one named last changes fastest.
Arguments:
- x_long: bfloat16 [2, 4096, 768], P(None, ('seq', 'ffn')), may hold values from -6 to 6
- x_glob: bfloat16 [2, 64, 768], P(None, ('seq', 'ffn')), may hold values from -6 to 6
- sentence: int32 [2, 16, 256], P(None, 'seq'), may hold values from 0 to 3, never falling along the last dimension, each value on 1 to 96 neighbouring positions
- dy_long: bfloat16 [2, 4096, 768], P(None, ('seq', 'ffn')), may hold values from -6 to 6
- dy_glob: bfloat16 [2, 64, 768], P(None, ('seq', 'ffn')), may hold values from -6 to 6
- owner_list: int32 [224], replicated, may hold values from 0 to 223, as said below
- w_master: float32 [448, 128, 128], P(('seq', 'ffn')), may hold values from -0.57735027 to 0.57735027
- m_old: float32 [448, 128, 128], P(('seq', 'ffn')), may hold values from -20.249516 to 20.249516
- v_old: float32 [448, 128, 128], P(('seq', 'ffn')), may hold values from 4.37632 to 437.632, as said below
- left_basis: float32 [448, 128, 128], P(('seq', 'ffn')), may hold values from -1 to 1, as said below
- right_basis: float32 [448, 128, 128], P(('seq', 'ffn')), may hold values from -1 to 1, as said below
- left_stats: float32 [448, 128, 128], P(('seq', 'ffn')), may hold values from 0 to 1064960, as said below
- right_stats: float32 [448, 128, 128], P(('seq', 'ffn')), may hold values from 0 to 1064960, as said below
- rel_table: float32 [169, 768], P(None, 'ffn'), may hold values from -6 to 6
- rel_m: float32 [169, 768], P(None, 'ffn'), may hold values from -3 to 3
- rel_v: float32 [169, 768], P(None, 'ffn'), may hold values from 0.17472 to 0.69888
- norm_params: float32 [4, 768], replicated, may hold values from -0.8 to 1.3
- norm_m: float32 [4, 768], replicated, may hold values from -64 to 64
- norm_v: float32 [4, 768], replicated, may hold values from 437.632 to 1747.2
Outputs:
- y_long: bfloat16 [2, 4096, 768], P(None, ('seq', 'ffn'))
- y_glob: bfloat16 [2, 64, 768], P(None, ('seq', 'ffn'))
- dx_long: float32 [2, 4096, 768], P(None, ('seq', 'ffn'))
- dx_glob: float32 [2, 64, 768], P(None, ('seq', 'ffn'))
- w_new: float32 [448, 128, 128], P(('seq', 'ffn'))
- m_new: float32 [448, 128, 128], P(('seq', 'ffn'))
- v_new: float32 [448, 128, 128], P(('seq', 'ffn'))
- left_basis_new: float32 [448, 128, 128], P(('seq', 'ffn'))
- right_basis_new: float32 [448, 128, 128], P(('seq', 'ffn'))
- left_stats_new: float32 [448, 128, 128], P(('seq', 'ffn'))
- right_stats_new: float32 [448, 128, 128], P(('seq', 'ffn'))
- rel_new: float32 [169, 768], P(None, 'ffn')
- rel_m_new: float32 [169, 768], P(None, 'ffn')
- rel_v_new: float32 [169, 768], P(None, 'ffn')
- norm_new: float32 [4, 768], replicated
- norm_m_new: float32 [4, 768], replicated
- norm_v_new: float32 [4, 768], replicated
The draws below stay inside these ranges and needn't reach their ends.
Inputs may be any that keep to these rules, and one draw needn't show every extreme that they name: For each sequence s and block b, sentence[s, b, t] never falls along t, every value is used, and no value covers more than 96 tokens. `owner_list`: all entries differ. `v_old`: positive. `left_basis`: each slot's matrix is orthogonal. `right_basis`: each slot's matrix is orthogonal. `left_stats`: each slot's matrix is diagonal with a positive diagonal. `right_stats`: each slot's matrix is diagonal with a positive diagonal.
All inputs are finite; a program needn't handle non-finite values.
Results may differ from the reference program's by a relative error of at most 0.015.
The reference program's roundings to bfloat16 on the way count: a program that leaves them out, or rounds other values in their place, can miss the bound.
Values may be sent and summed in bfloat16 or wider, within the bound.
No kernel may reach another device: no remote copies, remote signals or barrier semaphores. Data moves between devices by JAX's collectives and lax.ppermute only.
A program may use at most 192 MiB of HBM per device.

```python
import math
import jax
import jax.numpy as jnp
import numpy as np
from jax import lax

D = 768
HEADS = 12
HEAD_DIM = 64
FF = 3072
RADIUS = 84
BLK = 128
STEP = 10
SEQS = 2
TOK_DEV = 128
G_DEV = 2
BLOCK_LEN = 256
GLOB_BLOCK = 4
LENGTH = 4096
GLOBALS = 64
LABELS = 169
TILES = 216
SLOTS = 14
SLOT_TOTAL = 448
ROWS_ALL = 8320
N_SEQ = 16
N_FFN = 2


GRAD_FACTORS = (0.3, 0.3, 0.5, 0.1, 0.25, 0.5, 0.3)


def slot_owner(key):
    return jax.random.permutation(key, SLOTS * N_SEQ).astype(jnp.int32)


def slot_kinds(key):
    owner_order = slot_owner(key)
    slot_count = SLOTS * N_SEQ
    tile_of_slot = jnp.zeros((slot_count,), jnp.int32).at[owner_order].set(jnp.arange(slot_count, dtype=jnp.int32))
    attn_tiles = D * (D // N_FFN) // (BLK * BLK)
    ffn_tiles = D * (FF // N_FFN) // (BLK * BLK)
    bounds = jnp.array([attn_tiles, 2 * attn_tiles, 3 * attn_tiles, 4 * attn_tiles, 4 * attn_tiles + ffn_tiles, 4 * attn_tiles + 2 * ffn_tiles], jnp.int32)
    kind_ids = jnp.sum((tile_of_slot[:, None] >= bounds[None, :]).astype(jnp.int32), axis=1)
    return jnp.broadcast_to(kind_ids.reshape(N_SEQ, 1, SLOTS), (N_SEQ, N_FFN, SLOTS)).reshape(SLOT_TOTAL)


def grad_sizes(key):
    return jnp.array(GRAD_FACTORS, jnp.float32)[slot_kinds(key)] * math.sqrt(ROWS_ALL)


def orthogonal_set(key):
    first_vec = jax.random.normal(jax.random.fold_in(key, 1), (SLOT_TOTAL, BLK), jnp.float32)
    second_vec = jax.random.normal(jax.random.fold_in(key, 2), (SLOT_TOTAL, BLK), jnp.float32)
    first_vec = first_vec / jnp.sqrt(jnp.sum(first_vec * first_vec, axis=-1, keepdims=True))
    second_vec = second_vec / jnp.sqrt(jnp.sum(second_vec * second_vec, axis=-1, keepdims=True))
    inner = jnp.sum(first_vec * second_vec, axis=-1)
    identity = jnp.eye(BLK, dtype=jnp.float32)[None]
    return identity - 2.0 * first_vec[:, :, None] * first_vec[:, None, :] - 2.0 * second_vec[:, :, None] * second_vec[:, None, :] + 4.0 * inner[:, None, None] * first_vec[:, :, None] * second_vec[:, None, :]


def diagonal_set(key, sizes):
    factor = jnp.exp(jax.random.uniform(key, (SLOT_TOTAL, BLK), jnp.float32, 0.0, math.log(4.0)))
    diag_vals = factor * BLK * (sizes * sizes)[:, None]
    return diag_vals[:, :, None] * jnp.eye(BLK, dtype=jnp.float32)[None]


def draw_owner_list(key, part):
    return slot_owner(key)


def draw_w_master(key, part):
    kind_ids = slot_kinds(key)
    key = jax.random.fold_in(key, 11)
    spreads = jnp.array([D ** (-0.5), D ** (-0.5), D ** (-0.5), (D // 16) ** (-0.5), D ** (-0.5), FF ** (-0.5), D ** (-0.5)], jnp.float32)[kind_ids]
    return jax.random.truncated_normal(key, -4.0, 4.0, (SLOT_TOTAL, BLK, BLK), jnp.float32) * spreads[:, None, None]


def draw_m_old(key, part):
    sizes = grad_sizes(key)
    key = jax.random.fold_in(key, 12)
    return jax.random.truncated_normal(key, -4.0, 4.0, (SLOT_TOTAL, BLK, BLK), jnp.float32) * (0.111 * sizes)[:, None, None]


def draw_v_old(key, part):
    sizes = grad_sizes(key)
    key = jax.random.fold_in(key, 13)
    factor = jnp.exp(jax.random.uniform(key, (SLOT_TOTAL, BLK, BLK), jnp.float32, 0.0, math.log(4.0)))
    return factor * (0.0526 * sizes * sizes)[:, None, None]


def draw_left_basis(key, part):
    key = jax.random.fold_in(key, 14)
    return orthogonal_set(key)


def draw_right_basis(key, part):
    key = jax.random.fold_in(key, 15)
    return orthogonal_set(key)


def draw_left_stats(key, part):
    sizes = grad_sizes(key)
    key = jax.random.fold_in(key, 16)
    return diagonal_set(key, sizes)


def draw_right_stats(key, part):
    sizes = grad_sizes(key)
    key = jax.random.fold_in(key, 17)
    return diagonal_set(key, sizes)


def draw_norm_params(key, part):
    key = jax.random.fold_in(key, 18)
    gains = jax.random.uniform(jax.random.fold_in(key, 1), (2, D), jnp.float32, 0.7, 1.3)
    biases = jax.random.truncated_normal(jax.random.fold_in(key, 2), -4.0, 4.0, (2, D), jnp.float32) * 0.2
    return jnp.stack([gains[0], biases[0], gains[1], biases[1]])


def levels(stream_key, dims, shards, smallest, largest):
    level, own = 1.0, jax.random.fold_in(stream_key, 6)
    for axis_at, blocks in shards:
        steps = jnp.exp(jax.random.uniform(jax.random.fold_in(own, axis_at), (blocks,), jnp.float32, smallest / len(shards), largest / len(shards)))
        level = level * jnp.repeat(steps, dims[axis_at] // blocks).reshape([-1 if axis == axis_at else 1 for axis in range(len(dims))])
    return level


def profile(amount, total, reach, skew):
    weights = [(1 << 20) // math.isqrt(rank ** skew) + 1 for rank in range(2, amount + 1)]
    spare, holding = total - reach - (amount - 1), [1] * (amount - 1)
    while spare > 0:
        free = [i for i in range(amount - 1) if holding[i] < reach]
        whole, budget = sum([weights[i] for i in free]), spare
        for i in free:
            extra = min(reach - holding[i], max(1, budget * weights[i] // whole), spare)
            holding[i] = holding[i] + extra
            spare = spare - extra
    return np.array([reach] + holding)


def ragged(stream_key, count, total, most, lean):
    if count == 2:
        one = jax.random.randint(stream_key, (), max(1, total - most), min(most, total - 1) + 1)
        return jnp.stack([one, total - one])
    tallies = jnp.asarray(profile(count, total, most, lean), jnp.int32)
    couples = (count - 1) // 2
    source_of, receiver = tallies[1:1 + 2 * couples:2], tallies[2:2 + 2 * couples:2]
    margin = jnp.minimum(source_of - 1, most - receiver)
    shifted = jax.random.randint(jax.random.fold_in(stream_key, 1), (couples,), 0, 1 << 20) % (margin + 1)
    tallies = tallies.at[1:1 + 2 * couples:2].set(source_of - shifted).at[2:2 + 2 * couples:2].set(receiver + shifted)
    return tallies[jax.random.permutation(jax.random.fold_in(stream_key, 2), count)]


def bell_draw(rng, dims, scale, most, shards=(), held_as=jnp.bfloat16):
    values = jax.random.normal(rng, dims, jnp.float32) * scale
    if len(shards) > 0:
        values = levels(rng, dims, shards, -0.22, 0.18) * values
    return jnp.clip(values, min=-most, max=most).astype(held_as)


def setup_inputs(seed: int = 0) -> dict:
    splits = jax.random.split(jax.random.key(seed), 20)
    return {
        "x_long": bell_draw(splits[0], (SEQS, LENGTH, D), 1.0, 6.0, ((1, 32),)),
        "x_glob": bell_draw(splits[1], (SEQS, GLOBALS, D), 1.0, 6.0, ((1, 32),)),
        "sentence": jax.vmap(lambda own: jnp.searchsorted(jnp.cumsum(ragged(own, GLOB_BLOCK, BLOCK_LEN, 3 * TOK_DEV // (2 * G_DEV), 2)), jnp.arange(BLOCK_LEN), side="right"))(jax.random.split(splits[2], SEQS * N_SEQ)).reshape((SEQS, N_SEQ, BLOCK_LEN)).astype(jnp.int32),
        "dy_long": bell_draw(splits[3], (SEQS, LENGTH, D), 1.0, 6.0, ((1, 32),)),
        "dy_glob": bell_draw(splits[4], (SEQS, GLOBALS, D), 1.0, 6.0, ((1, 32),)),
        "owner_list": draw_owner_list(jax.random.fold_in(splits[19], 71), 0),
        "w_master": draw_w_master(jax.random.fold_in(splits[19], 71), 0),
        "m_old": draw_m_old(jax.random.fold_in(splits[19], 71), 0),
        "v_old": draw_v_old(jax.random.fold_in(splits[19], 71), 0),
        "left_basis": draw_left_basis(jax.random.fold_in(splits[19], 71), 0),
        "right_basis": draw_right_basis(jax.random.fold_in(splits[19], 71), 0),
        "left_stats": draw_left_stats(jax.random.fold_in(splits[19], 71), 0),
        "right_stats": draw_right_stats(jax.random.fold_in(splits[19], 71), 0),
        "rel_table": bell_draw(splits[13], (LABELS, D), 1.0, 6.0, ((1, 2),), jnp.float32),
        "rel_m": bell_draw(splits[14], (LABELS, D), (0.0022 * ROWS_ALL ** 0.5), 3.0, ((1, 2),), jnp.float32),
        "rel_v": jnp.clip(jnp.exp(math.log(0.69888) - 1.3862944 * jax.random.uniform(splits[15], (LABELS, D), jnp.float32) ** levels(splits[15], (LABELS, D), ((1, 2),), -0.2, 0.2)), 0.17472, 0.69888),
        "norm_params": draw_norm_params(jax.random.fold_in(splits[19], 71), 0),
        "norm_m": bell_draw(splits[17], (4, D), (0.111 * ROWS_ALL ** 0.5), 64.0, (), jnp.float32),
        "norm_v": jnp.clip(jnp.exp(jax.random.uniform(splits[18], (4, D), jnp.float32, math.log(437.632), math.log(1747.2))), 437.632, 1747.2),
    }


@jax.custom_vjp
def low(v):
    return lax.optimization_barrier(v.astype(jnp.bfloat16)).astype(jnp.float32)

@jax.custom_vjp
def low_back(v):
    return v

def low_keep(v):
    return (low(v), None)

def low_pass(kept, grad):
    return (grad,)

def back_keep(v):
    return (v, None)

def back_low(kept, grad):
    return (low(grad),)
low.defvjp(low_keep, low_pass)
low_back.defvjp(back_keep, back_low)
BETA_ONE = 0.9
BETA_TWO = 0.95
LEARN_RATE = 0.02
ADAM_RATE = 0.6
WEIGHT_DECAY = 0.01
ADAM_EPS = 1e-08
NORM_EPS = 1e-12
NEG_FILL = -1e+30
TOP_PRECISION = lax.Precision.HIGHEST

def low_both(values):
    return low_back(low(values))

def matmul_high(left_mat, right_mat):
    return jnp.matmul(left_mat, right_mat, precision=TOP_PRECISION)

def einsum_high(formula, *operands):
    return jnp.einsum(formula, *operands, precision=TOP_PRECISION)

def assemble(tile_set, row_count, col_count):
    side_len = tile_set.shape[-1]
    tile_grid = tile_set.reshape(row_count // side_len, col_count // side_len, side_len, side_len)
    return tile_grid.transpose(0, 2, 1, 3).reshape(row_count, col_count)

def cut_tiles(matrix, side_len):
    row_count, col_count = matrix.shape
    tile_grid = matrix.reshape(row_count // side_len, side_len, col_count // side_len, side_len)
    return tile_grid.transpose(0, 2, 1, 3).reshape(-1, side_len, side_len)

def skew_rows(label_table, span_len):
    lead_dims = label_table.shape[:-2]
    row_count, labels = (label_table.shape[-2], label_table.shape[-1])
    padded = jnp.pad(label_table, [(0, 0)] * len(lead_dims) + [(0, 0), (0, span_len + 1 - labels)])
    flat_rows = padded.reshape(lead_dims + (row_count * (span_len + 1),))
    return flat_rows[..., :row_count * span_len].reshape(lead_dims + (row_count, span_len))

def layer_norm(values, gain_vec, offset):
    center = values - lax.optimization_barrier(jnp.mean(values, axis=-1, keepdims=True))
    spread = lax.optimization_barrier(jnp.mean(center * center, axis=-1, keepdims=True))
    return center * lax.rsqrt(spread + NORM_EPS) * gain_vec + offset

def two_softmax(first_part, second_part):
    top_val = jnp.maximum(lax.optimization_barrier(jnp.max(first_part, axis=-1)), lax.optimization_barrier(jnp.max(second_part, axis=-1)))[..., None]
    first_exp = jnp.exp(first_part - top_val)
    second_exp = jnp.exp(second_part - top_val)
    total_sum = lax.optimization_barrier(jnp.sum(first_exp, axis=-1, keepdims=True)) + lax.optimization_barrier(jnp.sum(second_exp, axis=-1, keepdims=True))
    return (first_exp / total_sum, second_exp / total_sum)

def attend_blocks(shared, pieces):
    k_all, v_all, rel_heads = shared
    q_long, k_ext, v_ext, q_glob, k_loc, v_loc, sent_grp, starts = pieces
    span_len = k_ext.shape[1]
    block_len = q_long.shape[1]
    glob_block = q_glob.shape[1]
    scale = HEAD_DIM ** (-0.5)
    key_pos = starts[:, None] - RADIUS + jnp.arange(span_len, dtype=jnp.int32)[None, :]
    offsets = jnp.arange(span_len, dtype=jnp.int32)[None, :] - jnp.arange(block_len, dtype=jnp.int32)[:, None]
    band_ok = (offsets >= 0) & (offsets <= 2 * RADIUS)
    key_ok = (key_pos >= 0) & (key_pos < LENGTH)
    window_mask = band_ok[None, None] & key_ok[:, None, None, :]
    near_scores = einsum_high('gihe,gkhe->ghik', q_long, k_ext)
    rel_part = einsum_high('gihe,lhe->ghil', q_long, rel_heads)
    near_scores = low_back(jnp.where(window_mask, (near_scores + skew_rows(rel_part, span_len)) * scale, NEG_FILL))
    far_scores = low_back(einsum_high('gihe,jhe->ghij', q_long, k_all) * scale)
    p_near, p_far = two_softmax(near_scores, far_scores)
    out_long = einsum_high('ghik,gkhe->gihe', low(p_near), v_ext) + einsum_high('ghij,jhe->gihe', low(p_far), v_all)
    sent_mask = (sent_grp[:, None, :] == jnp.arange(glob_block, dtype=jnp.int32)[None, :, None])[:, None]
    own_scores = low_back(jnp.where(sent_mask, einsum_high('grhe,gthe->ghrt', q_glob, k_loc) * scale, NEG_FILL))
    glob_far = low_back(einsum_high('grhe,jhe->ghrj', q_glob, k_all) * scale)
    p_own, p_gfar = two_softmax(own_scores, glob_far)
    out_glob = einsum_high('ghrt,gthe->grhe', low(p_own), v_loc) + einsum_high('ghrj,jhe->grhe', low(p_gfar), v_all)
    return (out_long, out_glob)

def with_rims(blocks, block_len):
    zero_blk = jnp.zeros_like(blocks[:1])
    prev_rim = jnp.concatenate([zero_blk, blocks[:-1]], axis=0)[:, block_len - RADIUS:]
    next_rim = jnp.concatenate([blocks[1:], zero_blk], axis=0)[:, :RADIUS]
    return jnp.concatenate([prev_rim, blocks, next_rim], axis=1)

def sequence_forward(lowered, long_in, glob_in, sent_blocks):
    w_query, w_key, w_value, w_out, w_up, w_down, rel_heads, norms = lowered
    block_len = TOK_DEV * N_FFN
    glob_block = G_DEV * N_FFN
    rows_in = jnp.concatenate([long_in, glob_in], axis=0)
    query = low_both(matmul_high(rows_in, w_query)).reshape(-1, HEADS, HEAD_DIM)
    key_rows = low_both(matmul_high(rows_in, w_key)).reshape(-1, HEADS, HEAD_DIM)
    value_rows = low_both(matmul_high(rows_in, w_value)).reshape(-1, HEADS, HEAD_DIM)
    q_long = query[:LENGTH].reshape(N_SEQ, block_len, HEADS, HEAD_DIM)
    k_blk = key_rows[:LENGTH].reshape(N_SEQ, block_len, HEADS, HEAD_DIM)
    v_blk = value_rows[:LENGTH].reshape(N_SEQ, block_len, HEADS, HEAD_DIM)
    q_glob = query[LENGTH:].reshape(N_SEQ, glob_block, HEADS, HEAD_DIM)
    k_all = key_rows[LENGTH:]
    v_all = value_rows[LENGTH:]
    k_ext = with_rims(k_blk, block_len)
    v_ext = with_rims(v_blk, block_len)
    starts = jnp.arange(N_SEQ, dtype=jnp.int32) * block_len
    group_len = math.gcd(N_SEQ, 4)

    def grouped(values):
        return values.reshape((N_SEQ // group_len, group_len) + values.shape[1:])
    step_attend = jax.checkpoint(attend_blocks)
    shared = (k_all, v_all, rel_heads)
    out_long, out_glob = lax.map(lambda pieces: step_attend(shared, pieces), tuple((grouped(member) for member in (q_long, k_ext, v_ext, q_glob, k_blk, v_blk, sent_blocks, starts))))
    out_rows = low_both(jnp.concatenate([out_long.reshape(LENGTH, D), out_glob.reshape(GLOBALS, D)], axis=0))
    attn_rows = low_back(matmul_high(out_rows, w_out))
    mid_rows = rows_in + attn_rows
    norm_one = layer_norm(mid_rows, norms[0], norms[1])
    up_pre = low_back(matmul_high(low(norm_one), w_up))
    act_rows = low(jax.nn.gelu(up_pre, approximate=True))
    down_rows = low_back(matmul_high(act_rows, w_down))
    layer_out = layer_norm(norm_one + down_rows, norms[2], norms[3])
    return (layer_out[:LENGTH], layer_out[LENGTH:])

def sandwich(left_q, middle, right_q):
    return einsum_high('nik,nkl->nil', einsum_high('nji,njk->nik', left_q, middle), right_q)

def chol_orth(matrix):
    gram_mat = einsum_high('nji,njk->nik', matrix, matrix)
    lower_f = jnp.linalg.cholesky(gram_mat)
    solved = lax.linalg.triangular_solve(lower_f, jnp.swapaxes(matrix, 1, 2), left_side=True, lower=True)
    return jnp.swapaxes(solved, 1, 2)

def soap_update(grad_tile, weight, first_mom, second_mom, left_q, right_q, left_s, right_s):
    rotated = sandwich(left_q, grad_tile, right_q)
    first_mom = BETA_ONE * first_mom + (1.0 - BETA_ONE) * rotated
    second_mom = BETA_TWO * second_mom + (1.0 - BETA_TWO) * rotated * rotated
    direction = first_mom / (1.0 - BETA_ONE ** STEP) / (jnp.sqrt(second_mom / (1.0 - BETA_TWO ** STEP)) + ADAM_EPS)
    back_rot = einsum_high('nik,nlk->nil', einsum_high('nij,njk->nik', left_q, direction), right_q)
    weight = weight - LEARN_RATE * (back_rot + WEIGHT_DECAY * weight)
    left_s = BETA_TWO * left_s + (1.0 - BETA_TWO) * einsum_high('nik,njk->nij', grad_tile, grad_tile)
    right_s = BETA_TWO * right_s + (1.0 - BETA_TWO) * einsum_high('nki,nkj->nij', grad_tile, grad_tile)
    left_q = chol_orth(einsum_high('nij,njk->nik', left_s, left_q))
    right_q = chol_orth(einsum_high('nij,njk->nik', right_s, right_q))
    return (weight, first_mom, second_mom, left_q, right_q, left_s, right_s)

def adam_update(grad_vals, param, first_mom, second_mom, decay_rate):
    first_mom = BETA_ONE * first_mom + (1.0 - BETA_ONE) * grad_vals
    second_mom = BETA_TWO * second_mom + (1.0 - BETA_TWO) * grad_vals * grad_vals
    direction = first_mom / (1.0 - BETA_ONE ** STEP) / (jnp.sqrt(second_mom / (1.0 - BETA_TWO ** STEP)) + ADAM_EPS)
    return (param - ADAM_RATE * (direction + decay_rate * param), first_mom, second_mom)

def reference(x_long, x_glob, sentence, dy_long, dy_glob, owner_list, w_master, m_old, v_old, left_basis, right_basis, left_stats, right_stats, rel_table, rel_m, rel_v, norm_params, norm_m, norm_v):
    head_local = D // N_FFN
    hidden_local = FF // N_FFN
    attn_tiles = D * head_local // (BLK * BLK)
    ffn_tiles = D * hidden_local // (BLK * BLK)
    slot_count = SLOTS * N_SEQ
    owner_used = owner_list[:TILES]

    def halves(state):
        return state.reshape(N_SEQ, N_FFN, SLOTS, BLK, BLK).transpose(1, 0, 2, 3, 4).reshape(N_FFN, slot_count, BLK, BLK)

    def whole(state_halves):
        return state_halves.reshape(N_FFN, N_SEQ, SLOTS, BLK, BLK).transpose(1, 0, 2, 3, 4).reshape(N_SEQ * N_FFN * SLOTS, BLK, BLK)
    master_halves = halves(w_master)
    tile_sets = [jnp.take(master_halves[half_idx], owner_used, axis=0) for half_idx in range(N_FFN)]

    def joined(first_tile, last_tile, row_count, col_count, axis_idx):
        return jnp.concatenate([assemble(tile_set[first_tile:last_tile], row_count, col_count) for tile_set in tile_sets], axis=axis_idx)
    w_query = joined(0, attn_tiles, D, head_local, 1)
    w_key = joined(attn_tiles, 2 * attn_tiles, D, head_local, 1)
    w_value = joined(2 * attn_tiles, 3 * attn_tiles, D, head_local, 1)
    w_out = joined(3 * attn_tiles, 4 * attn_tiles, head_local, D, 0)
    w_up = joined(4 * attn_tiles, 4 * attn_tiles + ffn_tiles, D, hidden_local, 1)
    w_down = joined(4 * attn_tiles + ffn_tiles, TILES, hidden_local, D, 0)
    params = (w_query, w_key, w_value, w_out, w_up, w_down, rel_table, norm_params)

    def layer_forward(weights, long_in, glob_in):
        lowered = tuple((low(member) for member in weights[:6])) + (low(weights[6]).reshape(LABELS, HEADS, HEAD_DIM), weights[7])
        step_fn = jax.checkpoint(sequence_forward)
        return lax.map(lambda pieces: step_fn(lowered, *pieces), (long_in, glob_in, sentence))
    (y_long, y_glob), pull_back = jax.vjp(layer_forward, params, x_long.astype(jnp.float32), x_glob.astype(jnp.float32))
    grads, dx_long, dx_glob = pull_back((dy_long.astype(jnp.float32), dy_glob.astype(jnp.float32)))
    g_query, g_key, g_value, g_out, g_up, g_down, g_rel, g_norm = grads
    slot_sets = []
    for half_idx in range(N_FFN):
        col_lo = half_idx * head_local
        hid_lo = half_idx * hidden_local
        tile_rows = jnp.concatenate([cut_tiles(g_query[:, col_lo:col_lo + head_local], BLK), cut_tiles(g_key[:, col_lo:col_lo + head_local], BLK), cut_tiles(g_value[:, col_lo:col_lo + head_local], BLK), cut_tiles(g_out[col_lo:col_lo + head_local, :], BLK), cut_tiles(g_up[:, hid_lo:hid_lo + hidden_local], BLK), cut_tiles(g_down[hid_lo:hid_lo + hidden_local, :], BLK)], axis=0)
        slot_sets.append(jnp.zeros((slot_count, BLK, BLK), jnp.float32).at[owner_used].set(tile_rows))
    grad_slots = whole(jnp.stack(slot_sets))
    w_new, m_new, v_new, left_q, right_q, left_s, right_s = soap_update(grad_slots, w_master, m_old, v_old, left_basis, right_basis, left_stats, right_stats)
    rel_new, rel_m_new, rel_v_new = adam_update(g_rel, rel_table, rel_m, rel_v, WEIGHT_DECAY)
    norm_new, norm_m_new, norm_v_new = adam_update(g_norm, norm_params, norm_m, norm_v, 0.0)
    return (y_long.astype(jnp.bfloat16), y_glob.astype(jnp.bfloat16), dx_long, dx_glob, w_new, m_new, v_new, left_q, right_q, left_s, right_s, rel_new, rel_m_new, rel_v_new, norm_new, norm_m_new, norm_v_new)
```

```python
import math

import jax
import jax.numpy as jnp
from jax import lax
from jax.experimental import pallas as pl
from jax.experimental.pallas import tpu as pltpu
from jax.sharding import PartitionSpec as P

HEADS = 12
FF = 3072
RADIUS = 84
STEP = 10


BETA_ONE = 0.9
BETA_TWO = 0.95
LEARN_RATE = 0.02
ADAM_RATE = 0.6
WEIGHT_DECAY = 0.01
ADAM_EPS = 1e-08
NORM_EPS = 1e-12
NEG_FILL = -1e30
TOP_PRECISION = lax.Precision.HIGHEST


def with_halo(cells, sides, width):
    for axis, dim in sides:
        count = lax.axis_size(axis)
        ends = count - 1
        head = lax.slice_in_dim(cells, 0, width, axis=dim)
        tail = lax.slice_in_dim(cells, cells.shape[dim] - width, cells.shape[dim], axis=dim)
        cells = jnp.concatenate(
            [
                lax.ppermute(tail, axis, [(i, (i + 1) % count) for i in range(ends)]),
                cells,
                lax.ppermute(head, axis, [((i + 1) % count, i) for i in range(ends)]),
            ],
            axis=dim,
        )
    return cells


def assemble(tile_set, row_count, col_count):
    side_len = tile_set.shape[-1]
    tile_grid = tile_set.reshape(row_count // side_len, col_count // side_len, side_len, side_len)
    return tile_grid.transpose(0, 2, 1, 3).reshape(row_count, col_count)


def cut_tiles(matrix, side_len):
    row_count, col_count = matrix.shape
    tile_grid = matrix.reshape(row_count // side_len, side_len, col_count // side_len, side_len)
    return tile_grid.transpose(0, 2, 1, 3).reshape(-1, side_len, side_len)


def skew_rows(label_table, span_len):
    lead_dims = label_table.shape[:-2]
    row_count, labels = (label_table.shape[-2], label_table.shape[-1])
    padded = jnp.pad(label_table, [(0, 0)] * len(lead_dims) + [(0, 0), (0, span_len + 1 - labels)])
    flat_rows = padded.reshape(lead_dims + (row_count * (span_len + 1),))
    return flat_rows[..., : row_count * span_len].reshape(lead_dims + (row_count, span_len))


def unskew_rows(score_grid, labels):
    lead_dims = score_grid.shape[:-2]
    row_count, span_len = (score_grid.shape[-2], score_grid.shape[-1])
    padded = jnp.pad(score_grid, [(0, 0)] * len(lead_dims) + [(0, 0), (0, 1)])
    flat_rows = padded.reshape(lead_dims + (row_count * (span_len + 1),))
    flat_rows = jnp.pad(flat_rows, [(0, 0)] * len(lead_dims) + [(0, row_count)])
    return flat_rows.reshape(lead_dims + (row_count, span_len + 2))[..., :labels]


def layer_norm(values, gain_vec, offset):
    center = values - jnp.mean(values, axis=-1, keepdims=True)
    spread = jnp.mean(center * center, axis=-1, keepdims=True)
    return center * lax.rsqrt(spread + NORM_EPS) * gain_vec + offset


def gelu_tanh(values):
    return jax.nn.gelu(values, approximate=True)


def log_total(first_part, second_part):
    top_val = jnp.maximum(jnp.max(first_part, axis=-1), jnp.max(second_part, axis=-1))
    total_sum = jnp.sum(jnp.exp(first_part - top_val[..., None]), axis=-1) + jnp.sum(
        jnp.exp(second_part - top_val[..., None]), axis=-1
    )
    return top_val + jnp.log(total_sum)


def scores_of(queries, keys_in):
    return jnp.einsum("gihe,gkhe->ghik", queries, keys_in, preferred_element_type=jnp.float32)


def weigh_values(weights, values):
    return jnp.einsum("ghik,gkhe->gihe", weights, values, preferred_element_type=jnp.float32)


def key_grad(score_grads, queries, scale):
    return (
        jnp.einsum("ghik,gihe->gkhe", score_grads, queries, preferred_element_type=jnp.float32)
        * scale
    )


def long_scores(q_long, k_ext, k_all, rel_heads, window_mask, scale):
    near_scores = scores_of(q_long, k_ext)
    rel_part = jnp.einsum("gihe,lhe->ghil", q_long, rel_heads, preferred_element_type=jnp.float32)
    near_scores = jnp.where(
        window_mask, (near_scores + skew_rows(rel_part, k_ext.shape[1])) * scale, NEG_FILL
    )
    return (near_scores, scores_of(q_long, k_all) * scale)


def glob_scores(q_glob, k_loc, k_all, sent_mask, scale):
    own_scores = jnp.where(sent_mask, scores_of(q_glob, k_loc) * scale, NEG_FILL)
    return (own_scores, scores_of(q_glob, k_all) * scale)


def part_back(first_part, second_part, lse_rows, grad_out, v_first, v_second):
    p_first = jnp.exp(first_part - lse_rows[..., None])
    p_second = jnp.exp(second_part - lse_rows[..., None])
    dp_first = scores_of(grad_out, v_first)
    dp_second = scores_of(grad_out, v_second)
    row_delta = jnp.sum(p_first * dp_first, axis=-1) + jnp.sum(p_second * dp_second, axis=-1)
    ds_first = (p_first * (dp_first - row_delta[..., None])).astype(jnp.bfloat16)
    ds_second = (p_second * (dp_second - row_delta[..., None])).astype(jnp.bfloat16)
    dv_first = jnp.einsum(
        "ghik,gihe->gkhe",
        p_first.astype(jnp.bfloat16),
        grad_out,
        preferred_element_type=jnp.float32,
    )
    dv_second = jnp.einsum(
        "ghik,gihe->gkhe",
        p_second.astype(jnp.bfloat16),
        grad_out,
        preferred_element_type=jnp.float32,
    )
    return (ds_first, ds_second, dv_first, dv_second)


def einsum_high(formula, *operands):
    return jnp.einsum(formula, *operands, precision=TOP_PRECISION)


def seq_bits(count):
    return [1 << at for at in range(count.bit_length() - 1)]


def swap_with(values, bit):
    count = lax.axis_size("seq")
    return lax.ppermute(values, "seq", [(i, i ^ bit) for i in range(count)])


def slot_parts(slots, count):
    bits = seq_bits(count)
    low, high = bits[:2], bits[2:]
    half = slots // 2
    return [(0, half, low + high), (half, slots, low[::-1] + high)]


def gather_slots(tiles):
    gathered = []
    for first, last, order in slot_parts(tiles.shape[0], lax.axis_size("seq")):
        cells = tiles[first:last]
        for bit in order[::-1]:
            cells = jnp.concatenate([cells, swap_with(cells, bit)], axis=0)
        gathered.append(cells)
    return gathered


def slot_places(owners, slots):
    count = lax.axis_size("seq")
    apart = (owners // slots) ^ lax.axis_index("seq")
    inner = owners % slots
    place = jnp.zeros_like(owners)
    for first, last, order in slot_parts(slots, count):
        index = jnp.zeros_like(owners)
        for at, bit in enumerate(order):
            index = index + jnp.where((apart & bit) != 0, count >> (at + 1), 0)
        here = (inner >= first) & (inner < last)
        place = jnp.where(here, first * count + index * (last - first) + inner - first, place)
    return place


def scatter_slots(cells_all, slots):
    sums = []
    count = lax.axis_size("seq")
    for first, last, order in slot_parts(slots, count):
        cells = cells_all[first * count : last * count]
        for bit in order:
            half = cells.shape[0] // 2
            got = swap_with(cells[half:], bit)
            cells = cells[:half].astype(jnp.float32) + got.astype(jnp.float32)
            if bit != order[-1]:
                cells = cells.astype(jnp.bfloat16)
        sums.append(cells)
    return jnp.concatenate(sums, axis=0)


BF = jnp.bfloat16
F32 = jnp.float32


def split_two(x):
    hi = x.astype(BF)
    return hi, (x - hi.astype(F32)).astype(BF)


def split_three(x):
    hi = x.astype(BF)
    rest = x - hi.astype(F32)
    mid = rest.astype(BF)
    return hi, mid, (rest - mid.astype(F32)).astype(BF)


def left_six(parts, axis):
    h, m, l = parts
    return jnp.concatenate([h, h, m, m, h, l], axis=axis)


def right_six(parts, axis):
    h, m, l = parts
    return jnp.concatenate([h, m, h, m, l, h], axis=axis)


def left_three(parts, axis):
    h, l = parts
    return jnp.concatenate([h, h, l], axis=axis)


def right_three(parts, axis):
    h, l = parts
    return jnp.concatenate([h, l, h], axis=axis)


def dot_on(a, b, ca, cb):
    return lax.dot_general(a, b, (((ca,), (cb,)), ((), ())), preferred_element_type=F32)


def dot_six(a, b, ca, cb):
    return dot_on(left_six(split_three(a), ca), right_six(split_three(b), cb), ca, cb)


def dot_three(a, b, ca, cb):
    return dot_on(left_three(split_two(a), ca), right_three(split_two(b), cb), ca, cb)


PANEL = 32


def panel_inverse(a_ref, t_ref, npad, side, at):
    groups = PANEL // 8
    iota = lax.broadcasted_iota(jnp.int32, (8, npad), 0)
    a = []
    for i in range(PANEL):
        rows = a_ref[pl.ds(at + i, npad, stride=side), :]
        cols = rows.T[at : at + PANEL]
        a.append([cols[8 * g : 8 * g + 8] for g in range(groups)])
    z = [[None] * groups for _ in range(PANEL)]
    for j in range(PANEL):
        gj, sj = divmod(j, 8)
        r = lax.rsqrt(a[j][gj][sj : sj + 1])
        u = [None if g < gj else a[j][g] * r for g in range(groups)]
        below = list(u)
        below[gj] = jnp.where(iota > sj, u[gj], 0.0)
        for k in range(j + 1, PANEL):
            gk, sk = divmod(k, 8)
            row = u[gk][sk : sk + 1]
            for g in range(gk, groups):
                a[k][g] = a[k][g] - u[g] * row
        for c in range(j):
            row = z[c][gj][sj : sj + 1] * r
            z[c][gj] = jnp.where(iota == sj, row, z[c][gj]) - below[gj] * row
            for g in range(gj + 1, groups):
                z[c][g] = z[c][g] - u[g] * row
        z[j] = [
            jnp.zeros((8, npad), F32)
            if g < gj
            else (jnp.where(iota == sj, r, 0.0) - below[g] * r if g == gj else -u[g] * r)
            for g in range(groups)
        ]
    fill = jnp.zeros((side - PANEL, npad), F32)
    for c in range(PANEL):
        t_ref[pl.ds(c, npad, stride=PANEL), :] = jnp.concatenate(z[c] + [fill], axis=0).T


def soap_kernel(
    n, npad, g_ref, w_ref, m_ref, v_ref, ql_ref, qr_ref, sl_ref, sr_ref,
    w_out, m_out, v_out, ql_out, qr_out, sl_out, sr_out, a_ref, y_ref, mat_ref, t_ref,
):
    side = g_ref.shape[-1]
    eye = (
        lax.broadcasted_iota(jnp.int32, (side, side), 0)
        == lax.broadcasted_iota(jnp.int32, (side, side), 1)
    ).astype(F32)

    def first(i, carry):
        grad = g_ref[i]
        left, right = ql_ref[i], qr_ref[i]
        rotated = dot_three(dot_three(left, grad, 0, 0), right, 1, 0)
        mom = BETA_ONE * m_ref[i] + (1.0 - BETA_ONE) * rotated
        sec = BETA_TWO * v_ref[i] + (1.0 - BETA_TWO) * rotated * rotated
        m_out[i] = mom
        v_out[i] = sec
        step = (
            mom / (1.0 - BETA_ONE**STEP) / (jnp.sqrt(sec / (1.0 - BETA_TWO**STEP)) + ADAM_EPS)
        )
        back = dot_three(dot_three(left, step, 1, 0), right, 1, 1)
        w = w_ref[i]
        w_out[i] = w - LEARN_RATE * (back + WEIGHT_DECAY * w)
        parts = split_two(grad)
        new_l = BETA_TWO * sl_ref[i] + (1.0 - BETA_TWO) * dot_on(
            left_three(parts, 1), right_three(parts, 1), 1, 1
        )
        new_r = BETA_TWO * sr_ref[i] + (1.0 - BETA_TWO) * dot_on(
            left_three(parts, 0), right_three(parts, 0), 0, 0
        )
        sl_out[i] = new_l
        sr_out[i] = new_r
        for at, stats, basis in ((0, new_l, left), (1, new_r, right)):
            mat = dot_six(stats, basis, 1, 0)
            mat_ref[2 * i + at] = mat
            parts = split_three(mat)
            gram = dot_on(left_six(parts, 0), right_six(parts, 0), 0, 0)
            rows = pl.ds(pl.multiple_of((2 * i + at) * side, side), side)
            a_ref[rows, :] = gram
            y_ref[rows, :] = eye
        return carry

    lax.fori_loop(0, n, first, 0)
    if npad > 2 * n:
        a_ref[2 * n * side :, :] = jnp.concatenate([eye] * (npad - 2 * n), axis=0)
    for at in range(0, side, PANEL):
        panel_inverse(a_ref, t_ref, npad, side, at)

        def update(b, carry):
            t = t_ref[pl.ds(pl.multiple_of(b * PANEL, PANEL), PANEL), :][:, :PANEL]
            base = pl.multiple_of(b * side, side)
            rows = pl.ds(base + at, PANEL)
            both = jnp.concatenate([a_ref[rows, :], y_ref[rows, :]], axis=1)
            fresh = dot_six(t, both, 0, 0)
            y_ref[rows, :] = fresh[:, side:]
            if at + PANEL < side:
                parts = split_three(fresh)
                cut = tuple(p[:, :side] for p in parts)
                change = dot_on(left_six(cut, 0), right_six(parts, 0), 0, 0)[at + PANEL :]
                rest = pl.ds(base + at + PANEL, side - at - PANEL)
                a_ref[rest, :] = a_ref[rest, :] - change[:, :side]
                y_ref[rest, :] = y_ref[rest, :] - change[:, side:]
            return carry

        lax.fori_loop(0, 2 * n, update, 0)

    def last(i, carry):
        for at, out in ((0, ql_out), (1, qr_out)):
            rows = pl.ds(pl.multiple_of((2 * i + at) * side, side), side)
            out[i] = dot_three(mat_ref[2 * i + at], y_ref[rows, :], 1, 1)
        return carry

    lax.fori_loop(0, n, last, 0)


def soap_update(grad, *state):
    n, side = grad.shape[0], grad.shape[1]
    npad = -(-2 * n // 8) * 8
    shape = jax.ShapeDtypeStruct((n, side, side), F32)
    return pl.pallas_call(
        lambda *refs: soap_kernel(n, npad, *refs),
        out_shape=(shape,) * 7,
        in_specs=[pl.BlockSpec(memory_space=pltpu.VMEM)] * 8,
        out_specs=(pl.BlockSpec(memory_space=pltpu.VMEM),) * 7,
        scratch_shapes=[
            pltpu.VMEM((npad * side, side), F32),
            pltpu.VMEM((npad * side, side), F32),
            pltpu.VMEM((2 * n, side, side), F32),
            pltpu.VMEM((npad * PANEL, side), F32),
        ],
        compiler_params=pltpu.CompilerParams(vmem_limit_bytes=48 * 2**20),
        name="soap",
    )(grad, *state)


def adam_update(grad_vals, param, first_mom, second_mom, decay_rate):
    first_mom = BETA_ONE * first_mom + (1.0 - BETA_ONE) * grad_vals
    second_mom = BETA_TWO * second_mom + (1.0 - BETA_TWO) * grad_vals * grad_vals
    direction = (
        first_mom
        / (1.0 - BETA_ONE**STEP)
        / (jnp.sqrt(second_mom / (1.0 - BETA_TWO**STEP)) + ADAM_EPS)
    )
    return (param - ADAM_RATE * (direction + decay_rate * param), first_mom, second_mom)


def on_device(
    x_long,
    x_glob,
    sentence,
    dy_long,
    dy_glob,
    owner_list,
    w_master,
    m_old,
    v_old,
    left_basis,
    right_basis,
    left_stats,
    right_stats,
    rel_table,
    rel_m,
    rel_v,
    norm_params,
    norm_m,
    norm_v,
):
    ffn_count = lax.axis_size("ffn")
    seq_count = lax.axis_size("seq")
    seq_total, tok_half, model_dim = x_long.shape
    glob_half = x_glob.shape[1]
    block_len = tok_half * ffn_count
    glob_block = glob_half * ffn_count
    head_local = model_dim // ffn_count
    hidden_local = FF // ffn_count
    heads_here = HEADS // ffn_count
    head_size = model_dim // HEADS
    score_scale = head_size ** (-0.5)
    side_len = w_master.shape[1]
    attn_tiles = model_dim * head_local // (side_len * side_len)
    ffn_tiles = model_dim * hidden_local // (side_len * side_len)
    tile_count = 4 * attn_tiles + 2 * ffn_tiles
    slot_count = owner_list.shape[0]
    owner_used = owner_list[:tile_count]
    labels = rel_table.shape[0]
    span_len = block_len + 2 * RADIUS
    group_len = math.gcd(seq_total, 4)
    half_index = lax.axis_index("ffn")
    places = slot_places(owner_list, w_master.shape[0])
    gathered = jnp.concatenate(gather_slots(w_master.astype(jnp.bfloat16)), axis=0)
    tile_set = jnp.take(gathered, places[:tile_count], axis=0)
    w_qkv = jnp.concatenate(
        [
            assemble(
                tile_set[part_idx * attn_tiles : (part_idx + 1) * attn_tiles], model_dim, head_local
            )
            for part_idx in range(3)
        ],
        axis=1,
    )
    w_out = assemble(tile_set[3 * attn_tiles : 4 * attn_tiles], head_local, model_dim)
    w_up = assemble(tile_set[4 * attn_tiles : 4 * attn_tiles + ffn_tiles], model_dim, hidden_local)
    w_down = assemble(tile_set[4 * attn_tiles + ffn_tiles : tile_count], hidden_local, model_dim)
    rel_heads = rel_table.astype(jnp.bfloat16).reshape(labels, heads_here, head_size)
    start_pos = lax.axis_index("seq") * block_len
    key_pos = start_pos - RADIUS + jnp.arange(span_len, dtype=jnp.int32)
    offsets = (
        jnp.arange(span_len, dtype=jnp.int32)[None, :]
        - jnp.arange(block_len, dtype=jnp.int32)[:, None]
    )
    window_mask = (
        (offsets >= 0)
        & (offsets <= 2 * RADIUS)
        & (key_pos >= 0)[None, :]
        & (key_pos < block_len * seq_count)[None, :]
    )[None, None]
    sent_mask = (
        sentence[:, 0][:, None, :] == jnp.arange(glob_block, dtype=jnp.int32)[None, :, None]
    )[:, None]

    def split_heads(values):
        return values.reshape(values.shape[:-1] + (heads_here, head_size))

    def merge_heads(values):
        return values.reshape(values.shape[:-2] + (head_local,))

    def grouped(values):
        return values.reshape((seq_total // group_len, group_len) + values.shape[1:])

    def ungrouped(values):
        return values.reshape((seq_total,) + values.shape[2:])

    def project_keys(rows_in):
        proj_rows = jnp.einsum(
            "snd,dc->snc", rows_in, w_qkv, preferred_element_type=jnp.float32
        ).astype(jnp.bfloat16)
        key_ext = with_halo(proj_rows[:, :block_len, head_local:], (("seq", 1),), RADIUS)
        glob_kv = lax.all_gather(proj_rows[:, block_len:, head_local:], "seq", axis=1, tiled=True)
        return (proj_rows, key_ext, glob_kv)

    def attention_inputs(proj_rows, key_ext, glob_kv):
        return (
            split_heads(proj_rows[:, :block_len, :head_local]),
            split_heads(proj_rows[:, block_len:, :head_local]),
            split_heads(key_ext[..., :head_local]),
            split_heads(key_ext[..., head_local:]),
            split_heads(glob_kv[..., :head_local]),
            split_heads(glob_kv[..., head_local:]),
        )

    def attend_group(pieces):
        q_long, q_glob, k_ext, v_ext, k_all, v_all, sent_grp = pieces
        k_loc = k_ext[:, RADIUS : RADIUS + block_len]
        v_loc = v_ext[:, RADIUS : RADIUS + block_len]
        near_scores, far_scores = long_scores(
            q_long, k_ext, k_all, rel_heads, window_mask, score_scale
        )
        lse_long = log_total(near_scores, far_scores)
        out_long = weigh_values(
            jnp.exp(near_scores - lse_long[..., None]).astype(jnp.bfloat16), v_ext
        ) + weigh_values(jnp.exp(far_scores - lse_long[..., None]).astype(jnp.bfloat16), v_all)
        own_scores, glob_far = glob_scores(q_glob, k_loc, k_all, sent_grp, score_scale)
        lse_glob = log_total(own_scores, glob_far)
        out_glob = weigh_values(
            jnp.exp(own_scores - lse_glob[..., None]).astype(jnp.bfloat16), v_loc
        ) + weigh_values(jnp.exp(glob_far - lse_glob[..., None]).astype(jnp.bfloat16), v_all)
        return (out_long.astype(jnp.bfloat16), out_glob.astype(jnp.bfloat16), lse_long, lse_glob)

    def attend_back(pieces):
        (
            q_long,
            q_glob,
            k_ext,
            v_ext,
            k_all,
            v_all,
            sent_grp,
            lse_long,
            lse_glob,
            do_long,
            do_glob,
        ) = pieces
        k_loc = k_ext[:, RADIUS : RADIUS + block_len]
        v_loc = v_ext[:, RADIUS : RADIUS + block_len]
        near_scores, far_scores = long_scores(
            q_long, k_ext, k_all, rel_heads, window_mask, score_scale
        )
        ds_near, ds_far, dv_ext, dv_all = part_back(
            near_scores, far_scores, lse_long, do_long, v_ext, v_all
        )
        rel_rows = unskew_rows(ds_near, labels)
        dq_long = (
            weigh_values(ds_near, k_ext)
            + weigh_values(ds_far, k_all)
            + jnp.einsum("ghil,lhe->gihe", rel_rows, rel_heads, preferred_element_type=jnp.float32)
        ) * score_scale
        d_rel = (
            jnp.einsum("ghil,gihe->lhe", rel_rows, q_long, preferred_element_type=jnp.float32)
            * score_scale
        )
        dk_ext = key_grad(ds_near, q_long, score_scale)
        dk_all = key_grad(ds_far, q_long, score_scale)
        own_scores, glob_far = glob_scores(q_glob, k_loc, k_all, sent_grp, score_scale)
        ds_own, ds_gfar, dv_loc, dv_gall = part_back(
            own_scores, glob_far, lse_glob, do_glob, v_loc, v_all
        )
        dq_glob = (weigh_values(ds_own, k_loc) + weigh_values(ds_gfar, k_all)) * score_scale
        dk_loc = key_grad(ds_own, q_glob, score_scale)
        dk_all = dk_all + key_grad(ds_gfar, q_glob, score_scale)
        dv_all = dv_all + dv_gall
        return (dq_long, dq_glob, dk_ext, dv_ext, dk_loc, dv_loc, dk_all, dv_all, d_rel)

    long_rows, glob_rows = (
        lax.all_gather(x_long, "ffn", axis=1, tiled=True),
        lax.all_gather(x_glob, "ffn", axis=1, tiled=True),
    )
    all_rows = jnp.concatenate([long_rows, glob_rows], axis=1)
    proj_rows, key_ext, glob_kv = project_keys(all_rows)
    att_in = attention_inputs(proj_rows, key_ext, glob_kv)
    fwd_out = lax.map(attend_group, tuple((grouped(member) for member in att_in + (sent_mask,))))
    out_long, out_glob, lse_long, lse_glob = tuple((ungrouped(member) for member in fwd_out))
    out_rows = jnp.concatenate([merge_heads(out_long), merge_heads(out_glob)], axis=1)
    attn_part = jnp.einsum("snc,cd->snd", out_rows, w_out, preferred_element_type=jnp.float32)
    attn_full = lax.psum(attn_part, "ffn")
    mid_rows = all_rows.astype(jnp.float32) + attn_full
    norm_one = layer_norm(mid_rows, norm_params[0], norm_params[1])
    norm_low = norm_one.astype(jnp.bfloat16)
    up_pre = jnp.einsum("snd,df->snf", norm_low, w_up, preferred_element_type=jnp.float32)
    act_low = gelu_tanh(up_pre).astype(jnp.bfloat16)
    down_part = jnp.einsum("snf,fd->snd", act_low, w_down, preferred_element_type=jnp.float32)
    gelu_val, gelu_back = jax.vjp(gelu_tanh, up_pre)
    down_full = lax.psum(down_part, "ffn")
    pre_out = norm_one + down_full
    layer_out = layer_norm(pre_out, norm_params[2], norm_params[3])
    y_long = lax.dynamic_slice_in_dim(
        layer_out[:, :block_len], half_index * tok_half, tok_half, 1
    ).astype(jnp.bfloat16)
    y_glob = lax.dynamic_slice_in_dim(
        layer_out[:, block_len:], half_index * glob_half, glob_half, 1
    ).astype(jnp.bfloat16)
    grad_long, grad_glob = (
        lax.all_gather(dy_long, "ffn", axis=1, tiled=True),
        lax.all_gather(dy_glob, "ffn", axis=1, tiled=True),
    )
    grad_rows = jnp.concatenate([grad_long, grad_glob], axis=1).astype(jnp.float32)
    norm_two_val, norm_two_back = jax.vjp(layer_norm, pre_out, norm_params[2], norm_params[3])
    d_pre, d_gain_two, d_bias_two = norm_two_back(grad_rows)
    d_pre_low = d_pre.astype(jnp.bfloat16)
    grad_down = jnp.einsum("snf,snd->fd", act_low, d_pre_low, preferred_element_type=jnp.float32)
    d_act = jnp.einsum("snd,fd->snf", d_pre_low, w_down, preferred_element_type=jnp.float32)
    d_up = gelu_back(d_act)[0].astype(jnp.bfloat16)
    grad_up = jnp.einsum("snd,snf->df", norm_low, d_up, preferred_element_type=jnp.float32)
    d_norm_part = jnp.einsum("snf,df->snd", d_up, w_up, preferred_element_type=jnp.float32)
    d_norm_one = lax.psum(d_norm_part, "ffn") + d_pre
    norm_one_val, norm_one_back = jax.vjp(layer_norm, mid_rows, norm_params[0], norm_params[1])
    d_mid, d_gain_one, d_bias_one = norm_one_back(d_norm_one)
    d_mid_low = d_mid.astype(jnp.bfloat16)
    norm_grad = jnp.stack([d_gain_one, d_bias_one, d_gain_two, d_bias_two])
    add_long = lax.dynamic_slice_in_dim(d_mid[:, :block_len], half_index * tok_half, tok_half, 1)
    add_glob = lax.dynamic_slice_in_dim(d_mid[:, block_len:], half_index * glob_half, glob_half, 1)
    grad_out = jnp.einsum("snc,snd->cd", out_rows, d_mid_low, preferred_element_type=jnp.float32)
    d_out_rows = jnp.einsum(
        "snd,cd->snc", d_mid_low, w_out, preferred_element_type=jnp.float32
    ).astype(jnp.bfloat16)
    back_in = attention_inputs(*project_keys(all_rows))
    back_pieces = back_in + (
        sent_mask,
        lse_long,
        lse_glob,
        split_heads(d_out_rows[:, :block_len]),
        split_heads(d_out_rows[:, block_len:]),
    )
    back_out = lax.map(attend_back, tuple((grouped(member) for member in back_pieces)))
    dq_long, dq_glob, dk_ext, dv_ext, dk_loc, dv_loc, dk_all, dv_all = tuple(
        (ungrouped(member) for member in back_out[:8])
    )
    rel_grad = jnp.sum(back_out[8], axis=0).reshape(labels, head_local)
    dkv_ext = jnp.concatenate([merge_heads(dk_ext), merge_heads(dv_ext)], axis=-1)
    dkv_all = jnp.concatenate([merge_heads(dk_all), merge_heads(dv_all)], axis=-1)
    dkv_glob = lax.psum_scatter(dkv_all, "seq", scatter_dimension=1, tiled=True)
    rim_rows = jnp.concatenate([dkv_ext[:, :RADIUS], dkv_ext[:, RADIUS + block_len :]], axis=1)
    rim_back = with_halo(rim_rows.astype(jnp.bfloat16), (("seq", 1),), RADIUS).astype(
        rim_rows.dtype
    )
    dkv_long = dkv_ext[:, RADIUS : RADIUS + block_len] + jnp.concatenate(
        [merge_heads(dk_loc), merge_heads(dv_loc)], axis=-1
    )
    dkv_long = dkv_long.at[:, :RADIUS].add(rim_back[:, :RADIUS])
    dkv_long = dkv_long.at[:, block_len - RADIUS :].add(rim_back[:, 3 * RADIUS :])
    d_proj = jnp.concatenate(
        [
            jnp.concatenate([merge_heads(dq_long), dkv_long], axis=-1),
            jnp.concatenate([merge_heads(dq_glob), dkv_glob], axis=-1),
        ],
        axis=1,
    ).astype(jnp.bfloat16)
    grad_qkv = jnp.einsum("snd,snc->dc", all_rows, d_proj, preferred_element_type=jnp.float32)
    d_in = jnp.einsum("snc,dc->snd", d_proj, w_qkv, preferred_element_type=jnp.float32)
    dx_long, dx_glob = (
        lax.psum_scatter(
            d_in[:, :block_len].astype(jnp.bfloat16), "ffn", scatter_dimension=1, tiled=True
        ).astype(jnp.float32),
        lax.psum_scatter(
            d_in[:, block_len:].astype(jnp.bfloat16), "ffn", scatter_dimension=1, tiled=True
        ).astype(jnp.float32),
    )
    dx_long = dx_long + add_long
    dx_glob = dx_glob + add_glob
    tile_rows = jnp.concatenate(
        [
            cut_tiles(grad_qkv[:, part_idx * head_local : (part_idx + 1) * head_local], side_len)
            for part_idx in range(3)
        ]
        + [
            cut_tiles(grad_out, side_len),
            cut_tiles(grad_up, side_len),
            cut_tiles(grad_down, side_len),
        ],
        axis=0,
    )
    held = jnp.zeros((slot_count,), jnp.int32).at[places].set(jnp.arange(slot_count, dtype=jnp.int32))
    tile_low = jnp.concatenate(
        [tile_rows.astype(jnp.bfloat16), jnp.zeros((slot_count - tile_count, side_len, side_len), jnp.bfloat16)]
    )
    owned_grads = scatter_slots(jnp.take(tile_low, held, axis=0), w_master.shape[0])
    rel_sum, norm_sum = lax.psum((rel_grad, norm_grad), "seq")
    w_new, m_new, v_new, left_q, right_q, left_s, right_s = soap_update(
        owned_grads, w_master, m_old, v_old, left_basis, right_basis, left_stats, right_stats
    )
    rel_new, rel_m_new, rel_v_new = adam_update(rel_sum, rel_table, rel_m, rel_v, WEIGHT_DECAY)
    norm_new, norm_m_new, norm_v_new = adam_update(norm_sum, norm_params, norm_m, norm_v, 0.0)
    return (
        y_long,
        y_glob,
        dx_long,
        dx_glob,
        w_new,
        m_new,
        v_new,
        left_q,
        right_q,
        left_s,
        right_s,
        rel_new,
        rel_m_new,
        rel_v_new,
        norm_new,
        norm_m_new,
        norm_v_new,
    )


def solution(mesh):
    in_specs = (
        P(None, ("seq", "ffn"), None),
        P(None, ("seq", "ffn"), None),
        P(None, "seq", None),
        P(None, ("seq", "ffn"), None),
        P(None, ("seq", "ffn"), None),
        P(),
        P(("seq", "ffn"), None, None),
        P(("seq", "ffn"), None, None),
        P(("seq", "ffn"), None, None),
        P(("seq", "ffn"), None, None),
        P(("seq", "ffn"), None, None),
        P(("seq", "ffn"), None, None),
        P(("seq", "ffn"), None, None),
        P(None, "ffn"),
        P(None, "ffn"),
        P(None, "ffn"),
        P(),
        P(),
        P(),
    )
    out_specs = (
        P(None, ("seq", "ffn"), None),
        P(None, ("seq", "ffn"), None),
        P(None, ("seq", "ffn"), None),
        P(None, ("seq", "ffn"), None),
        P(("seq", "ffn"), None, None),
        P(("seq", "ffn"), None, None),
        P(("seq", "ffn"), None, None),
        P(("seq", "ffn"), None, None),
        P(("seq", "ffn"), None, None),
        P(("seq", "ffn"), None, None),
        P(("seq", "ffn"), None, None),
        P(None, "ffn"),
        P(None, "ffn"),
        P(None, "ffn"),
        P(),
        P(),
        P(),
    )
    return jax.shard_map(
        on_device, mesh=mesh, in_specs=in_specs, out_specs=out_specs, check_vma=False
    )
```

```python
import functools
import math

import jax
import jax.numpy as jnp
from jax import lax
from jax.experimental import pallas as pl
from jax.experimental.pallas import tpu as pltpu
from jax.sharding import PartitionSpec as P

HEADS = 12
FF = 3072
RADIUS = 84
STEP = 10

BETA_ONE = 0.9
BETA_TWO = 0.95
LEARN_RATE = 0.02
ADAM_RATE = 0.6
WEIGHT_DECAY = 0.01
ADAM_EPS = 1e-08
NORM_EPS = 1e-12
NEG_FILL = -1e30
BF = jnp.bfloat16
F32 = jnp.float32


def seq_bits(count):
    return [1 << at for at in range(count.bit_length() - 1)]


def swap_with(values, bit):
    count = lax.axis_size("seq")
    return lax.ppermute(values, "seq", [(i, i ^ bit) for i in range(count)])


def slot_parts(slots, count):
    bits = seq_bits(count)
    low, high = bits[:2], bits[2:]
    orders = (low + high[::-1], [low[1], high[0], low[0]] + high[1:], [high[0]] + low + high[1:])
    cuts = [slots * at // 14 for at in (0, 5, 10, 14)]
    return [(a, b, order) for a, b, order in zip(cuts, cuts[1:], orders) if b > a]


def part_rows(parts, side, extra):
    rows = [(last - first) * side for first, last, _ in parts]
    return rows[:-1] + [rows[-1] + extra]


def slot_places(owners, slots, rows, side):
    count = lax.axis_size("seq")
    apart = (owners // slots) ^ lax.axis_index("seq")
    inner = owners % slots
    place, row, base = jnp.zeros_like(owners), jnp.zeros_like(owners), 0
    for (first, last, order), many in zip(slot_parts(slots, count), rows):
        index = jnp.zeros_like(owners)
        for at, bit in enumerate(order):
            index = index + jnp.where((apart & bit) != 0, count >> (at + 1), 0)
        here = (inner >= first) & (inner < last)
        place = jnp.where(here, first * count + index * (last - first) + inner - first, place)
        row = jnp.where(here, base + index * many + (inner - first) * side, row)
        base += many * count
    return place, row


def move_kernel(starts, adding, *refs):
    count = len(starts)
    ins, outs, rest = refs[: 2 * count], refs[2 * count : 3 * count], refs[3 * count :]
    held, sems = rest[:-1], rest[-1]
    copies = []
    for at, out in enumerate(outs):
        rows = out.shape[0] if adding else out.shape[0] // 2
        for side in range(2):
            target = held[2 * at + side] if adding else out.at[pl.ds(side * rows, rows)]
            source = ins[2 * at + side].at[pl.ds(starts[at][side], rows)]
            copies.append(pltpu.make_async_copy(source, target, sems.at[2 * at + side]))
            copies[-1].start()
    for at, out in enumerate(outs):
        copies[2 * at].wait()
        copies[2 * at + 1].wait()
        if adding:
            one, two = held[2 * at], held[2 * at + 1]
            step = next(s for s in (128, 64, 48, 32, 16) if out.shape[0] % s == 0)

            def add(i, carry):
                rows = pl.ds(pl.multiple_of(i * step, 16), step)
                out[rows, :] = (one[rows, :].astype(F32) + two[rows, :].astype(F32)).astype(out.dtype)
                return carry

            lax.fori_loop(0, out.shape[0] // step, add, 0)


def move_rows(entries, adding):
    starts = tuple((entry[1], entry[3]) for entry in entries)
    shapes = [((1 if adding else 2) * entry[4], entry[0].shape[1]) for entry in entries]
    return pl.pallas_call(
        functools.partial(move_kernel, starts, adding),
        grid=(1,),
        out_shape=tuple(jax.ShapeDtypeStruct(shape, BF) for shape in shapes),
        in_specs=[pl.BlockSpec(memory_space=pl.ANY)] * (2 * len(entries)),
        out_specs=tuple(pl.BlockSpec(shape, lambda i: (0, 0)) for shape in shapes),
        scratch_shapes=[pltpu.VMEM(shape, BF) for shape in shapes for _ in range(2) if adding]
        + [pltpu.SemaphoreType.DMA((2 * len(entries),))],
        cost_estimate=pl.CostEstimate(
            flops=0, bytes_accessed=sum(6 * math.prod(s) for s in shapes), transcendentals=0
        ),
        compiler_params=pltpu.CompilerParams(vmem_limit_bytes=56 * 2**20),
        name="add_rows" if adding else "join_rows",
    )(*[array for entry in entries for array in (entry[0], entry[2])])


def gather_rows(cells, orders):
    last = len(orders[0]) - 1
    known = cells
    fresh = [[swap_with(c, order[last]) for c, order in zip(cells, orders)]]
    for step in range(last - 1, -1, -1):
        sent = [[swap_with(c, order[step]) for c, order in zip(run, orders)] for run in [known] + fresh]
        if step == 0:
            return list(zip(*([known] + fresh + sent)))
        known = move_rows([(c, 0, f, 0, c.shape[0]) for c, f in zip(known, fresh[0])], False)
        fresh = sent
        if step > 1:
            fresh = [move_rows([(c, 0, f, 0, c.shape[0]) for c, f in zip(*sent)], False)]
    return None


def scatter_rows(cells, starts, rows, orders, everywhere, order_everywhere):
    last = len(order_everywhere) - 1
    ahead = [cells[a + 3 * r // 4 : a + r] for a, r in zip(starts, rows)]
    behind = [cells[a + r // 2 : a + 3 * r // 4] for a, r in zip(starts, rows)]
    kept = [(cells, a, r // 2) for a, r in zip(starts, rows)]
    for step in range(last + 1):
        got = [swap_with(send, order[step]) for send, order in zip(ahead, orders)]
        got_all = swap_with(everywhere, order_everywhere[step])
        if step == last:
            return [(array, g) for (array, _, _), g in zip(kept, got)], (everywhere, got_all)
        later = [swap_with(send, order[step]) for send, order in zip(behind, orders)]
        if step + 1 == last:
            on = [(array, a + r // 2, g, 0, r // 2) for (array, a, r), g in zip(kept, got)]
        else:
            on = [(array, a + 3 * r // 4, g, r // 4, r // 4) for (array, a, r), g in zip(kept, got)]
            on += [(array, a + r // 2, g, 0, r // 4) for (array, a, r), g in zip(kept, got)]
        sums = move_rows(on + [(everywhere, 0, got_all, 0, everywhere.shape[0])], True)
        ahead, behind, everywhere = sums[: len(orders)], sums[len(orders) : -1], sums[-1]
        keeps = move_rows([(array, a, g, 0, r // 2) for (array, a, r), g in zip(kept, later)], True)
        kept = [(keep, 0, keep.shape[0]) for keep in keeps]
    return None


def split_two(x):
    hi = x.astype(BF)
    return hi, (x - hi.astype(F32)).astype(BF)


def split_three(x):
    hi = x.astype(BF)
    rest = x - hi.astype(F32)
    mid = rest.astype(BF)
    return hi, mid, (rest - mid.astype(F32)).astype(BF)


def left_six(parts, axis):
    h, m, l = parts
    return jnp.concatenate([h, h, m, m, h, l], axis=axis)


def right_six(parts, axis):
    h, m, l = parts
    return jnp.concatenate([h, m, h, m, l, h], axis=axis)


def left_three(parts, axis):
    h, l = parts
    return jnp.concatenate([h, h, l], axis=axis)


def right_three(parts, axis):
    h, l = parts
    return jnp.concatenate([h, l, h], axis=axis)


def dot_on(a, b, ca, cb):
    return lax.dot_general(a, b, (((ca,), (cb,)), ((), ())), preferred_element_type=F32)


def dot_six(a, b, ca, cb):
    return dot_on(left_six(split_three(a), ca), right_six(split_three(b), cb), ca, cb)


def dot_three(a, b, ca, cb):
    return dot_on(left_three(split_two(a), ca), right_three(split_two(b), cb), ca, cb)


PANEL = 32
SLOTS_AT_ONCE = 2


def panel_inverse(a_ref, t_ref, npad, side, at):
    groups = PANEL // 8
    iota = lax.broadcasted_iota(jnp.int32, (8, npad), 0)
    a = []
    for i in range(PANEL):
        rows = a_ref[pl.ds(at + i, npad, stride=side), :]
        cols = rows.T[at : at + PANEL]
        a.append([cols[8 * g : 8 * g + 8] for g in range(groups)])
    z = [[None] * groups for _ in range(PANEL)]
    for j in range(PANEL):
        gj, sj = divmod(j, 8)
        r = lax.rsqrt(a[j][gj][sj : sj + 1])
        u = [None if g < gj else a[j][g] * r for g in range(groups)]
        below = list(u)
        below[gj] = jnp.where(iota > sj, u[gj], 0.0)
        for k in range(j + 1, PANEL):
            gk, sk = divmod(k, 8)
            row = u[gk][sk : sk + 1]
            for g in range(gk, groups):
                a[k][g] = a[k][g] - u[g] * row
        for c in range(j):
            row = z[c][gj][sj : sj + 1] * r
            z[c][gj] = jnp.where(iota == sj, row, z[c][gj]) - below[gj] * row
            for g in range(gj + 1, groups):
                z[c][g] = z[c][g] - u[g] * row
        z[j] = [
            jnp.zeros((8, npad), F32)
            if g < gj
            else (jnp.where(iota == sj, r, 0.0) - below[g] * r if g == gj else -u[g] * r)
            for g in range(groups)
        ]
    fill = jnp.zeros((side - PANEL, npad), F32)
    for c in range(PANEL):
        t_ref[pl.ds(c, npad, stride=PANEL), :] = jnp.concatenate(z[c] + [fill], axis=0).T


def soap_kernel(npad, grad_count, *refs):
    grad_refs = [(refs[2 * at], refs[2 * at + 1]) for at in range(grad_count)]
    refs = refs[2 * grad_count :]
    w_ref, m_ref, v_ref, ql_ref, qr_ref, sl_ref, sr_ref = refs[:7]
    w_out, m_out, v_out, ql_out, qr_out, sl_out, sr_out, a_ref, y_ref, mat_ref, t_ref = refs[7:]
    n = w_ref.shape[0]
    batch = next(b for b in (14, 7, 4, 2) if 2 * n % b == 0)
    side = w_ref.shape[-1]
    eye = (
        lax.broadcasted_iota(jnp.int32, (side, side), 0)
        == lax.broadcasted_iota(jnp.int32, (side, side), 1)
    ).astype(F32)

    def first(g_refs, base, at, carry, many):
        slots = [base + at * many + k for k in range(many)]
        tiles = [pl.ds(pl.multiple_of((at * many + k) * side, side), side) for k in range(many)]
        grads = [sum(g[rows, :].astype(F32) for g in g_refs) for rows in tiles]
        lefts = [ql_ref[i] for i in slots]
        rights = [qr_ref[i] for i in slots]
        halves = [split_two(x) for x in grads]
        new_l = [
            BETA_TWO * sl_ref[i] + (1.0 - BETA_TWO) * dot_on(left_three(p, 1), right_three(p, 1), 1, 1)
            for i, p in zip(slots, halves)
        ]
        new_r = [
            BETA_TWO * sr_ref[i] + (1.0 - BETA_TWO) * dot_on(left_three(p, 0), right_three(p, 0), 0, 0)
            for i, p in zip(slots, halves)
        ]
        mats = [dot_six(x, y, 1, 0) for x, y in zip(new_l + new_r, lefts + rights)]
        thirds = [split_three(x) for x in mats]
        grams = [dot_on(left_six(p, 0), right_six(p, 0), 0, 0) for p in thirds]
        turned = [dot_three(x, y, 0, 0) for x, y in zip(lefts, grads)]
        rotated = [dot_three(x, y, 1, 0) for x, y in zip(turned, rights)]
        moms = [BETA_ONE * m_ref[i] + (1.0 - BETA_ONE) * x for i, x in zip(slots, rotated)]
        secs = [BETA_TWO * v_ref[i] + (1.0 - BETA_TWO) * x * x for i, x in zip(slots, rotated)]
        steps = [
            x / (1.0 - BETA_ONE**STEP) / (jnp.sqrt(y / (1.0 - BETA_TWO**STEP)) + ADAM_EPS)
            for x, y in zip(moms, secs)
        ]
        turned = [dot_three(x, y, 1, 0) for x, y in zip(lefts, steps)]
        backs = [dot_three(x, y, 1, 1) for x, y in zip(turned, rights)]
        weights = [w_ref[i] for i in slots]
        for k, i in enumerate(slots):
            m_out[i] = moms[k]
            v_out[i] = secs[k]
            w_out[i] = weights[k] - LEARN_RATE * (backs[k] + WEIGHT_DECAY * weights[k])
            sl_out[i] = new_l[k]
            sr_out[i] = new_r[k]
            for kind in range(2):
                mat_ref[2 * i + kind] = mats[kind * many + k]
                rows = pl.ds(pl.multiple_of((2 * i + kind) * side, side), side)
                a_ref[rows, :] = grams[kind * many + k]
                y_ref[rows, :] = eye
        return carry

    base = 0
    for g_refs in grad_refs:
        here = g_refs[0].shape[0] // side
        pairs = here // SLOTS_AT_ONCE
        lax.fori_loop(0, pairs, functools.partial(first, g_refs, base, many=SLOTS_AT_ONCE), 0)
        for at in range(pairs * SLOTS_AT_ONCE, here):
            first(g_refs, base, at, 0, 1)
        base += here
    if npad > 2 * n:
        a_ref[2 * n * side :, :] = jnp.concatenate([eye] * (npad - 2 * n), axis=0)
    for at in range(0, side, PANEL):
        panel_inverse(a_ref, t_ref, npad, side, at)

        def update(i, carry):
            bases = [pl.multiple_of((i * batch + b) * side, side) for b in range(batch)]
            rows = [pl.ds(base + at, PANEL) for base in bases]
            both = [jnp.concatenate([a_ref[r, :], y_ref[r, :]], axis=1) for r in rows]
            turns = [
                t_ref[pl.ds(pl.multiple_of((i * batch + b) * PANEL, PANEL), PANEL), :][:, :PANEL]
                for b in range(batch)
            ]
            if at + PANEL < side:
                rest = [pl.ds(base + at + PANEL, side - at - PANEL) for base in bases]
                old = [(a_ref[r, :], y_ref[r, :]) for r in rest]
            fresh = [dot_six(t, x, 0, 0) for t, x in zip(turns, both)]
            if at + PANEL < side:
                changes = []
                for x in fresh:
                    parts = split_three(x)
                    cut = tuple(p[:, at + PANEL : side] for p in parts)
                    changes.append(dot_on(left_six(cut, 0), right_six(parts, 0), 0, 0))
                for r, (old_a, old_y), change in zip(rest, old, changes):
                    a_ref[r, :] = old_a - change[:, :side]
                    y_ref[r, :] = old_y - change[:, side:]
            for r, x in zip(rows, fresh):
                y_ref[r, :] = x[:, side:]
            return carry

        lax.fori_loop(0, 2 * n // batch, update, 0)

    def last(i, carry):
        mats = [mat_ref[2 * i], mat_ref[2 * i + 1]]
        rows = [pl.ds(pl.multiple_of((2 * i + k) * side, side), side) for k in range(2)]
        turns = [y_ref[r, :] for r in rows]
        left, right = [dot_three(x, y, 1, 1) for x, y in zip(mats, turns)]
        ql_out[i] = left
        qr_out[i] = right
        return carry

    lax.fori_loop(0, n, last, 0)


def soap_update(grads, state):
    n, side = state[0].shape[:2]
    npad = -(-2 * n // 8) * 8
    spec = pl.BlockSpec((n, side, side), lambda i: (0, 0, 0))
    return pl.pallas_call(
        functools.partial(soap_kernel, npad, len(grads)),
        grid=(1,),
        out_shape=tuple(jax.ShapeDtypeStruct(s.shape, F32) for s in state),
        in_specs=[pl.BlockSpec(g.shape, lambda i: (0, 0)) for pair in grads for g in pair] + [spec] * 7,
        out_specs=(spec,) * 7,
        scratch_shapes=[
            pltpu.VMEM((npad * side, side), F32),
            pltpu.VMEM((npad * side, side), F32),
            pltpu.VMEM((2 * n, side, side), F32),
            pltpu.VMEM((npad * PANEL, side), F32),
        ],
        cost_estimate=pl.CostEstimate(
            flops=n * 40 * side**3, bytes_accessed=n * 60 * side * side, transcendentals=0
        ),
        compiler_params=pltpu.CompilerParams(vmem_limit_bytes=56 * 2**20),
        name="soap",
    )(*[g for pair in grads for g in pair], *state)


LANES = 128
LABEL_PAD = 256
RIM = 96
PARALLEL_LIMIT = 56 * 2**20


def up_to(value, unit):
    return -(-value // unit) * unit


def whole(shape):
    return pl.BlockSpec(shape, lambda i: (0,) * len(shape))


def block_at(shape, *index):
    return pl.BlockSpec(shape, lambda i: index)


def any_space():
    return pl.BlockSpec(memory_space=pl.ANY)


def scalars():
    return pl.BlockSpec(memory_space=pltpu.SMEM)


def kernel_call(body, name, out_shape, in_specs, out_specs, scratch=(), aliases=None, flops=0, bytes_moved=0):
    return pl.pallas_call(
        body,
        name=name,
        grid=(1,),
        out_shape=out_shape,
        in_specs=in_specs,
        out_specs=out_specs,
        scratch_shapes=list(scratch),
        input_output_aliases=aliases or {},
        cost_estimate=pl.CostEstimate(flops=flops, bytes_accessed=bytes_moved, transcendentals=0),
        compiler_params=pltpu.CompilerParams(vmem_limit_bytes=PARALLEL_LIMIT),
    )


def start_tiles(row_ref, col_ref, kind_ref, sources, tiles, wall_ref, sems):
    base = 0
    for source, many in zip(sources, tiles):

        def start(i, carry):
            for k in range(many):
                place = base + i * many + k
                kind = kind_ref[place]

                @pl.when(kind < 2)
                def _():
                    row = pl.multiple_of(row_ref[place], LANES)
                    col = pl.multiple_of(col_ref[place], LANES)
                    pltpu.make_async_copy(
                        source.at[i, pl.ds(k * LANES, LANES)],
                        wall_ref.at[pl.ds(row, LANES), pl.ds(col, LANES)],
                        sems.at[kind],
                    ).start()

            return carry

        lax.fori_loop(0, source.shape[0], start, 0)
        base += source.shape[0] * many


def wait_rows(wall_ref, rows, sem):
    part = wall_ref.at[pl.ds(0, rows)]
    pltpu.make_async_copy(part, part, sem).wait()


def low_lanes(rows):
    return lax.broadcasted_iota(jnp.int32, (rows, LANES), 1) < LANES // 2


def stack_heads(pair):
    low = low_lanes(pair.shape[0])
    zero = jnp.zeros_like(pair)
    return jnp.concatenate([jnp.where(low, pair, zero), jnp.where(low, zero, pair)], axis=0)


def merge_stack(stacked):
    rows = stacked.shape[0] // 2
    return jnp.where(low_lanes(rows), stacked[:rows], stacked[rows:])


def skew(table, width):
    rows = table.shape[0] // 2
    padded = jnp.concatenate(
        [table, jnp.zeros((table.shape[0], width - table.shape[1]), F32)], axis=1
    )
    halves = [
        pltpu.roll(padded[at : at + rows], 0, 1, stride=1, stride_axis=0) for at in (0, rows)
    ]
    return jnp.concatenate(halves, axis=0)


def unskew(grid, width):
    rows = grid.shape[0] // 2
    lanes = grid.shape[1]
    parts = []
    for at in range(0, 2 * rows, 8):
        shift = (at % rows) % lanes
        part = grid[at : at + 8]
        parts.append(part if shift == 0 else pltpu.roll(part, lanes - shift, 1))
    moved = jnp.concatenate(parts, axis=0)
    index = lax.broadcasted_iota(jnp.int32, moved.shape, 0)
    for bit in (1, 2, 4):
        moved = jnp.where((index & bit) != 0, pltpu.roll(moved, lanes - bit, 1), moved)
    return moved[:, :width]


def softmax_rows(scores):
    top = jnp.max(scores, axis=-1, keepdims=True)
    raised = jnp.exp(scores - top)
    return raised * (1.0 / jnp.sum(raised, axis=-1, keepdims=True))


def window_keys(ref, base, at, width, ext, globs, cols):
    return jnp.concatenate(
        [ref[pl.ds(base + at, width), cols], ref[pl.ds(base + ext, globs), cols]], axis=0
    )


def glob_row_mask(shape, seq, glob_block):
    row = lax.broadcasted_iota(jnp.int32, shape, 0) % (shape[0] // 2)
    return (row >= seq * glob_block) & (row < (seq + 1) * glob_block)


def attend_kernel(dims, wall_at, row_ref, col_ref, kind_ref, xr_ref, left_ref, right_ref, far_ref, rel_ref, bias_ref, gbias_ref, *refs):
    q_ref, k_ref, v_ref, o_ref, part_ref, xe_ref, wall_out, wall_ref, sems = refs[-9:]
    sources = refs[:-9]
    seqs, block_len, glob_block, ext, width, globs, scale = dims
    feed_rows, attn_rows, qk_at, v_at, out_at, tiles = wall_at
    model_dim = xr_ref.shape[1]
    head_cols = q_ref.shape[1]
    start_tiles(row_ref, col_ref, kind_ref, sources, tiles, wall_ref, sems)
    span = ext + globs
    for seq in range(seqs):
        at = seq * span
        xe_ref[at : at + RIM] = left_ref[seq * RIM : (seq + 1) * RIM]
        at += RIM
        xe_ref[at : at + block_len] = xr_ref[seq * block_len : (seq + 1) * block_len]
        at += block_len
        xe_ref[at : at + RIM] = right_ref[seq * RIM : (seq + 1) * RIM]
        at += RIM
        if ext > block_len + 2 * RIM:
            xe_ref[at : seq * span + ext] = jnp.zeros((ext - block_len - 2 * RIM, model_dim), BF)
        xe_ref[seq * span + ext : (seq + 1) * span] = far_ref[seq * globs : (seq + 1) * globs]
    wait_rows(wall_ref, attn_rows, sems.at[0])
    wq_ref = wall_ref.at[pl.ds(qk_at, model_dim), pl.ds(0, head_cols)]
    wk_ref = wall_ref.at[pl.ds(qk_at, model_dim), pl.ds(head_cols, head_cols)]
    wv_ref = wall_ref.at[pl.ds(v_at, model_dim), pl.ds(0, head_cols)]
    wo_ref = wall_ref.at[pl.ds(out_at, head_cols)]
    pairs = head_cols // LANES
    glob_at = seqs * block_len
    glob_rows = q_ref.shape[0] - glob_at
    span = ext + globs
    chunks = block_len // LANES
    q_ref[...] = dot_on(xr_ref[...], wq_ref[...], 1, 0).astype(BF)

    def project(i, carry):
        rows = pl.ds(pl.multiple_of(i * 256, 256), 256)
        k_ref[rows, :] = dot_on(xe_ref[rows, :], wk_ref[...], 1, 0).astype(BF)
        v_ref[rows, :] = dot_on(xe_ref[rows, :], wv_ref[...], 1, 0).astype(BF)
        return carry

    lax.fori_loop(0, seqs * span // 256, project, 0)
    wait_rows(wall_ref, feed_rows, sems.at[1])
    keep = pltpu.make_async_copy(wall_ref, wall_out, sems.at[2])
    keep.start()

    def window(i, carry):
        seq, chunk = i // chunks, i % chunks
        rows = pl.ds(pl.multiple_of(i * LANES, LANES), LANES)
        base = pl.multiple_of(seq * span, LANES)
        at = pl.multiple_of(chunk * LANES, LANES)
        bias = bias_ref[chunk]
        bias = jnp.concatenate([bias, bias], axis=0)
        for pair in range(pairs):
            cols = slice(pair * LANES, (pair + 1) * LANES)
            query = stack_heads(q_ref[rows, cols] * scale)
            keys = window_keys(k_ref, base, at, width, ext, globs, cols)
            values = window_keys(v_ref, base, at, width, ext, globs, cols)
            scores = dot_on(query, keys, 1, 1)
            scores = scores + skew(dot_on(query, rel_ref[:, cols], 1, 1), width + globs) + bias
            weights = softmax_rows(scores).astype(BF)
            o_ref[rows, cols] = merge_stack(dot_on(weights, values, 1, 0)).astype(BF)
        return carry

    lax.fori_loop(0, seqs * chunks, window, 0)
    rows = slice(glob_at, glob_at + glob_rows)
    for pair in range(pairs):
        cols = slice(pair * LANES, (pair + 1) * LANES)
        query = stack_heads(q_ref[rows, cols] * scale)
        total = jnp.zeros((2 * glob_rows, LANES), F32)
        for seq in range(seqs):
            span_rows = slice(seq * span, (seq + 1) * span)
            bias = gbias_ref[seq]
            scores = dot_on(query, k_ref[span_rows, cols], 1, 1) + jnp.concatenate([bias, bias], axis=0)
            weights = softmax_rows(scores).astype(BF)
            out = dot_on(weights, v_ref[span_rows, cols], 1, 0)
            total = jnp.where(glob_row_mask(total.shape, seq, glob_block), out, total)
        o_ref[rows, cols] = merge_stack(total).astype(BF)
    part_ref[...] = dot_on(o_ref[...], wo_ref[...], 1, 0).astype(BF)
    keep.wait()


def norm_parts(values):
    center = values - jnp.mean(values, axis=-1, keepdims=True)
    spread = jnp.mean(center * center, axis=-1, keepdims=True)
    rate = lax.rsqrt(spread + NORM_EPS)
    return center * rate, rate


def norm_back(grad, normed, rate, gain):
    scaled = grad * gain
    return (
        scaled
        - jnp.mean(scaled, axis=-1, keepdims=True)
        - normed * jnp.mean(scaled * normed, axis=-1, keepdims=True)
    ) * rate


def row_loop(total, body):
    step = 176 if total % 176 == 0 else 16

    def run(i, carry):
        body(pl.ds(pl.multiple_of(i * step, 16), step))
        return carry

    lax.fori_loop(0, total // step, run, 0)


def col_loop(total, body, step=256):
    def run(i, carry):
        body(i)
        return carry

    lax.fori_loop(0, total // step, run, 0)


GELU_RATE = 0.7978845608028654
GELU_CUBE = 0.044715


def gelu_parts(u):
    square = u * u
    curve = jnp.tanh(GELU_RATE * u * (1.0 + GELU_CUBE * square))
    return square, curve


def feed_kernel(xr_ref, part_ref, got_ref, norm_ref, wu_ref, wd_ref, h_ref, hb_ref, u_ref, a_ref, down_ref):
    model_dim = xr_ref.shape[1]
    gain, offset = norm_ref[0:1], norm_ref[1:2]

    def norm(rows):
        mid = xr_ref[rows, :].astype(F32) + (part_ref[rows, :].astype(F32) + got_ref[rows, :].astype(F32))
        normed, _ = norm_parts(mid)
        out = normed * gain + offset
        h_ref[rows, :] = out
        hb_ref[rows, :] = out.astype(BF)

    row_loop(xr_ref.shape[0], norm)
    per_half = model_dim // 256

    def up(j):
        rows = pl.ds(pl.multiple_of((j // per_half) * model_dim, 256), model_dim)
        cols = pl.ds(pl.multiple_of((j % per_half) * 256, 256), 256)
        here = pl.ds(pl.multiple_of(j * 256, 256), 256)
        u = dot_on(hb_ref[...], wu_ref[rows, cols], 1, 0)
        u_ref[:, here] = u
        _, curve = gelu_parts(u)
        a_ref[:, here] = (0.5 * u * (1.0 + curve)).astype(BF)

    col_loop(u_ref.shape[1], up)

    def down(j):
        cols = pl.ds(pl.multiple_of(j * 256, 256), 256)
        down_ref[:, cols] = dot_on(a_ref[...], wd_ref[:, cols], 1, 0).astype(BF)

    col_loop(model_dim, down)


def feed_back_kernel(h_ref, down_ref, got_ref, u_ref, dy_ref, norm_ref, wu_ref, wd_ref,
                     y_ref, dx_ref, dxb_ref, du_ref, dh_ref, gn_ref):
    model_dim = h_ref.shape[1]
    gain, offset = norm_ref[2:3], norm_ref[3:4]
    gn_ref[...] = jnp.zeros_like(gn_ref)

    def norm(rows):
        out = h_ref[rows, :] + (down_ref[rows, :].astype(F32) + got_ref[rows, :].astype(F32))
        normed, rate = norm_parts(out)
        y_ref[rows, :] = (normed * gain + offset).astype(BF)
        grad = dy_ref[rows, :].astype(F32)
        gn_ref[0:1] += jnp.sum(grad * normed, axis=0, keepdims=True)
        gn_ref[1:2] += jnp.sum(grad, axis=0, keepdims=True)
        dx = norm_back(grad, normed, rate, gain)
        dx_ref[rows, :] = dx
        dxb_ref[rows, :] = dx.astype(BF)

    row_loop(h_ref.shape[0], norm)

    def act(j):
        here = pl.ds(pl.multiple_of(j * 256, 256), 256)
        da = dot_on(dxb_ref[...], wd_ref[here, :], 1, 1)
        u = u_ref[:, here]
        square, curve = gelu_parts(u)
        slope = 0.5 * (1.0 + curve) + 0.5 * u * (1.0 - curve * curve) * (
            GELU_RATE * (1.0 + 3.0 * GELU_CUBE * square)
        )
        du_ref[:, here] = (da * slope).astype(BF)

    col_loop(u_ref.shape[1], act)
    halves = u_ref.shape[1] // model_dim

    def lower(j):
        cols = pl.ds(pl.multiple_of(j * 256, 256), 256)
        total = 0.0
        for half in range(halves):
            rows = pl.ds(pl.multiple_of(half * model_dim + j * 256, 256), 256)
            total = total + dot_on(
                du_ref[:, half * model_dim : (half + 1) * model_dim], wu_ref[rows, :], 1, 1
            )
        dh_ref[:, cols] = total.astype(BF)

    col_loop(model_dim, lower)


def send_tiles(stage_ref, row, rows, first, place_ref, out_ref, sem):
    cols = stage_ref.shape[1] // LANES
    for r in range(rows):
        for c in range(cols):
            pltpu.make_async_copy(
                stage_ref.at[pl.ds(row + r * LANES, LANES), pl.ds(c * LANES, LANES)],
                out_ref.at[pl.ds(pl.multiple_of(place_ref[first + r * cols + c], 16), LANES)],
                sem,
            ).start()


def feed_grads_kernel(tiles_at, place_ref, a_ref, dxb_ref, hb_ref, du_ref, out_ref, down_stage, up_stage, sems):
    up_at, down_at = tiles_at
    model_dim = dxb_ref.shape[1]

    def down(j):
        row = pl.multiple_of(j * 256, 256)
        rows = pl.ds(row, 256)
        down_stage[rows, :] = dot_on(a_ref[:, rows], dxb_ref[...], 0, 0).astype(BF)
        send_tiles(down_stage, row, 2, down_at + j * 2 * (model_dim // LANES), place_ref, out_ref, sems.at[0])

    col_loop(a_ref.shape[1], down)

    def up(j):
        row = pl.multiple_of(j * 256, 256)
        rows = pl.ds(row, 256)
        up_stage[rows, :] = dot_on(hb_ref[:, rows], du_ref[...], 0, 0).astype(BF)
        send_tiles(
            up_stage, row, 2, up_at + j * 2 * (du_ref.shape[1] // LANES), place_ref, out_ref, sems.at[1]
        )

    col_loop(model_dim, up)
    pltpu.make_async_copy(down_stage, down_stage, sems.at[0]).wait()
    pltpu.make_async_copy(up_stage, up_stage, sems.at[1]).wait()


def attend_back_kernel(dims, attn_tiles, tile_counts, glob_at_rows, place_ref, norm_two_ref, xr_ref, part_ref, got_ref, dh_ref, dh_got_ref, dx_ref, o_ref,
                       q_ref, k_ref, v_ref, xe_ref, wo_ref, rel_ref, bias_ref, gbias_ref, norm_ref, grads_in,
                       grads_ref, dq_ref, dkv_ref, mid_ref, small_ref,
                       do_ref, midb_ref, dkv_acc, out_stage, q_stage, k_stage, v_stage, none_ref,
                       drel_ref, norms_ref, gn_ref, glob_stage, glob_low, sems):
    seqs, block_len, glob_block, ext, width, globs, scale = dims
    head_cols = q_ref.shape[1]
    pairs = head_cols // LANES
    glob_at = seqs * block_len
    glob_rows = q_ref.shape[0] - glob_at
    span = ext + globs
    chunks = block_len // LANES
    gain = norm_ref[0:1]
    gn_ref[...] = jnp.zeros_like(gn_ref)

    def norm(rows):
        mid = xr_ref[rows, :].astype(F32) + (part_ref[rows, :].astype(F32) + got_ref[rows, :].astype(F32))
        normed, rate = norm_parts(mid)
        grad = dh_ref[rows, :].astype(F32) + dh_got_ref[rows, :].astype(F32) + dx_ref[rows, :]
        gn_ref[0:1] += jnp.sum(grad * normed, axis=0, keepdims=True)
        gn_ref[1:2] += jnp.sum(grad, axis=0, keepdims=True)
        out = norm_back(grad, normed, rate, gain)
        mid_ref[rows, :] = out
        midb_ref[rows, :] = out.astype(BF)

    row_loop(xr_ref.shape[0], norm)
    do_ref[...] = dot_on(midb_ref[...], wo_ref[...], 1, 1).astype(BF)
    out_stage[...] = dot_on(o_ref[...], midb_ref[...], 0, 0).astype(BF)
    send_tiles(out_stage, 0, out_stage.shape[0] // LANES, 3 * attn_tiles, place_ref, grads_ref, sems.at[0])
    none_ref[...] = jnp.zeros_like(none_ref)
    spare = []
    for tile in range(*tile_counts):
        target = grads_ref.at[pl.ds(pl.multiple_of(place_ref[tile], 16), LANES)]
        spare.append(pltpu.make_async_copy(none_ref, target, sems.at[4]))
        spare[-1].start()
    dkv_acc[...] = jnp.zeros_like(dkv_acc)
    drel_ref[...] = jnp.zeros_like(drel_ref)

    def grads_of(scores, grad_out, values):
        weights = softmax_rows(scores)
        dp = dot_on(grad_out, values, 1, 1)
        delta = jnp.sum(weights * dp, axis=-1, keepdims=True)
        return weights.astype(BF), weights * (dp - delta)

    def window(i, carry):
        seq, chunk = i // chunks, i % chunks
        rows = pl.ds(pl.multiple_of(i * LANES, LANES), LANES)
        base = pl.multiple_of(seq * span, LANES)
        at = pl.multiple_of(chunk * LANES, LANES)
        near_rows = pl.ds(base + at, width)
        far_rows = pl.ds(base + ext, globs)
        bias = bias_ref[chunk]
        bias = jnp.concatenate([bias, bias], axis=0)
        near = lax.broadcasted_iota(jnp.int32, bias.shape, 1) < width
        for pair in range(pairs):
            cols = slice(pair * LANES, (pair + 1) * LANES)
            query = stack_heads(q_ref[rows, cols] * scale)
            grad_out = stack_heads(do_ref[rows, cols])
            keys = window_keys(k_ref, base, at, width, ext, globs, cols)
            values = window_keys(v_ref, base, at, width, ext, globs, cols)
            labels = rel_ref[:, cols]
            scores = dot_on(query, keys, 1, 1)
            scores = scores + skew(dot_on(query, labels, 1, 1), width + globs) + bias
            weights, ds = grads_of(scores, grad_out, values)
            dsb = ds.astype(BF)
            by_label = unskew(jnp.where(near, dsb.astype(F32), 0.0), LABEL_PAD).astype(BF)
            dv = dot_on(weights, grad_out, 0, 0)
            dk = dot_on(dsb, query, 0, 0)
            dq = dot_on(dsb, keys, 1, 0) + dot_on(by_label, labels, 1, 0)
            dq_ref[rows, cols] = (merge_stack(dq) * scale).astype(BF)
            drel_ref[:, cols] += dot_on(by_label, query, 0, 0)
            dkv_acc[pair, near_rows] += dk[:width]
            dkv_acc[pair, far_rows] += dk[width:]
            dkv_acc[pairs + pair, near_rows] += dv[:width]
            dkv_acc[pairs + pair, far_rows] += dv[width:]
        return carry

    lax.fori_loop(0, seqs * chunks, window, 0)
    rows = slice(glob_at, glob_at + glob_rows)
    for pair in range(pairs):
        cols = slice(pair * LANES, (pair + 1) * LANES)
        query = stack_heads(q_ref[rows, cols] * scale)
        grad_out = stack_heads(do_ref[rows, cols])
        total = jnp.zeros((2 * glob_rows, LANES), F32)
        for seq in range(seqs):
            span_rows = slice(seq * span, (seq + 1) * span)
            bias = gbias_ref[seq]
            keys = k_ref[span_rows, cols]
            scores = dot_on(query, keys, 1, 1) + jnp.concatenate([bias, bias], axis=0)
            weights, ds = grads_of(scores, grad_out, v_ref[span_rows, cols])
            own = glob_row_mask(ds.shape, seq, glob_block)
            weights = jnp.where(own, weights.astype(F32), 0.0).astype(BF)
            dsb = jnp.where(own, ds, 0.0).astype(BF)
            dkv_acc[pair, span_rows] += dot_on(dsb, query, 0, 0)
            dkv_acc[pairs + pair, span_rows] += dot_on(weights, grad_out, 0, 0)
            total = total + dot_on(dsb, keys, 1, 0)
        dq_ref[rows, cols] = (merge_stack(total) * scale).astype(BF)
    first_row, row_step, cells, per_block = glob_at_rows
    blocks = globs // per_block
    for seq in range(seqs):
        for r in range(per_block):
            source = pl.ds(seq * span + ext + r, blocks, stride=per_block)
            for c in range(2 * pairs):
                rows = pl.ds((seq * per_block + r) * 2 * pairs + c, blocks, stride=cells)
                glob_stage[rows, :] = dkv_acc[c, source, :]
    glob_low[...] = glob_stage[...].astype(BF)
    for i in range(blocks):
        pltpu.make_async_copy(
            glob_low.at[pl.ds(i * cells, cells)],
            grads_ref.at[pl.ds(first_row + (i + 1) * row_step - cells, cells)],
            sems.at[5],
        ).start()
    small_ref[:LABEL_PAD] = drel_ref[...].astype(BF)
    norms_ref[...] = jnp.zeros_like(norms_ref)
    for row, source in enumerate((gn_ref, gn_ref, norm_two_ref, norm_two_ref)):
        for half in range(source.shape[1] // head_cols):
            at = row * (source.shape[1] // head_cols) + half
            norms_ref[at : at + 1] = source[row % 2 : row % 2 + 1, half * head_cols : (half + 1) * head_cols]
    small_ref[LABEL_PAD:] = norms_ref[...].astype(BF)
    for c in range(2 * pairs):
        dkv_ref[:, c * LANES : (c + 1) * LANES] = dkv_acc[c].astype(BF)
    for at, stage in ((0, q_stage), (1, k_stage), (2, v_stage)):
        rows_ref = xr_ref if at == 0 else xe_ref
        grad = dq_ref[...] if at == 0 else dkv_ref[:, (at - 1) * head_cols : at * head_cols]

        def cut(j):
            row = pl.multiple_of(j * 256, 256)
            stage[pl.ds(row, 256), :] = dot_on(rows_ref[:, pl.ds(row, 256)], grad, 0, 0).astype(BF)
            send_tiles(
                stage, row, 2, at * attn_tiles + j * 2 * (head_cols // LANES), place_ref, grads_ref, sems.at[1 + at]
            )

        col_loop(stage.shape[0], cut)
    for at, stage in enumerate((out_stage, q_stage, k_stage, v_stage)):
        pltpu.make_async_copy(stage, stage, sems.at[at]).wait()
    for copy in spare:
        copy.wait()
    pltpu.make_async_copy(glob_low, glob_low, sems.at[5]).wait()


def swap_cores(values):
    count = lax.axis_size("ffn")
    return lax.ppermute(values, "ffn", [(i, i ^ 1) for i in range(count)])


def adam_update(grad_vals, param, first_mom, second_mom, decay_rate):
    first_mom = BETA_ONE * first_mom + (1.0 - BETA_ONE) * grad_vals
    second_mom = BETA_TWO * second_mom + (1.0 - BETA_TWO) * grad_vals * grad_vals
    direction = (
        first_mom
        / (1.0 - BETA_ONE**STEP)
        / (jnp.sqrt(second_mom / (1.0 - BETA_TWO**STEP)) + ADAM_EPS)
    )
    return (param - ADAM_RATE * (direction + decay_rate * param), first_mom, second_mom)


def on_device(
    x_long,
    x_glob,
    sentence,
    dy_long,
    dy_glob,
    owner_list,
    w_master,
    m_old,
    v_old,
    left_basis,
    right_basis,
    left_stats,
    right_stats,
    rel_table,
    rel_m,
    rel_v,
    norm_params,
    norm_m,
    norm_v,
):
    ffn_count = lax.axis_size("ffn")
    seq_count = lax.axis_size("seq")
    seqs, tok_half, model_dim = x_long.shape
    glob_half = x_glob.shape[1]
    block_len = tok_half * ffn_count
    glob_block = glob_half * ffn_count
    globs = glob_block * seq_count
    head_cols = model_dim // ffn_count
    hidden = FF // ffn_count
    scale = (model_dim // HEADS) ** (-0.5)
    slots, side = w_master.shape[:2]
    attn_tiles = model_dim * head_cols // (side * side)
    ffn_tiles = model_dim * hidden // (side * side)
    tile_count = 4 * attn_tiles + 2 * ffn_tiles
    slot_count = owner_list.shape[0]
    labels = rel_table.shape[0]
    half_index = lax.axis_index("ffn")
    first_half = half_index == 0
    parts = slot_parts(slots, seq_count)

    glob_cells = seqs * glob_block * model_dim // LANES
    rows_per = part_rows(parts, side, glob_cells)
    places, place_rows = slot_places(owner_list, slots, rows_per, side)
    held = jnp.sum(
        jnp.where(
            places[None, :] == jnp.arange(slot_count, dtype=jnp.int32)[:, None],
            jnp.arange(slot_count, dtype=jnp.int32)[None, :],
            0,
        ),
        axis=1,
    )
    per_row = model_dim // side
    up_rows = hidden // model_dim * model_dim
    qk_at = up_rows + hidden
    v_at = qk_at + model_dim
    out_at = v_at + model_dim
    head_tiles = head_cols // side
    up_tiles = hidden // side

    def tile_row_col(tile):
        kind_qkv = tile // attn_tiles
        inner = tile % attn_tiles
        qkv_row = jnp.where(kind_qkv == 2, v_at, qk_at) + inner // head_tiles * side
        qkv_col = jnp.where(kind_qkv == 1, head_cols, 0) + inner % head_tiles * side
        out_row = out_at + inner // per_row * side
        up = tile - 4 * attn_tiles
        up_col = up % up_tiles * side
        up_row = up_col // model_dim * model_dim + up // up_tiles * side
        down = up - ffn_tiles
        down_row = up_rows + down // per_row * side
        row = jnp.where(
            tile < 3 * attn_tiles,
            qkv_row,
            jnp.where(
                tile < 4 * attn_tiles,
                out_row,
                jnp.where(up < ffn_tiles, up_row, down_row),
            ),
        )
        col = jnp.where(
            tile < 3 * attn_tiles,
            qkv_col,
            jnp.where(
                tile < 4 * attn_tiles,
                inner % per_row * side,
                jnp.where(up < ffn_tiles, up_col % model_dim, down % per_row * side),
            ),
        )
        return row, col

    wall_row, wall_col = tile_row_col(held)
    wall_kind = jnp.where(held < 4 * attn_tiles, 0, jnp.where(held < tile_count, 1, 2))

    mine = jnp.concatenate([x_long, dy_long, x_glob, dy_glob], axis=1)
    other = swap_cores(mine)
    lower = jnp.where(first_half, mine, other)
    upper = jnp.where(first_half, other, mine)

    def block_rows(at, count):
        return jnp.concatenate([lower[:, at : at + count], upper[:, at : at + count]], axis=1)

    long_rows = block_rows(0, tok_half)
    dy_rows = block_rows(tok_half, tok_half)
    glob_rows = block_rows(2 * tok_half, glob_half)
    dy_globs = block_rows(2 * tok_half + glob_half, glob_half)
    used = seqs * (block_len + glob_block)
    row_count = seqs * block_len + up_to(seqs * glob_block, 16)
    pad_rows = jnp.zeros((row_count - used, model_dim), BF)

    def in_rows(long_part, glob_part):
        return jnp.concatenate(
            [long_part.reshape(-1, model_dim), glob_part.reshape(-1, model_dim), pad_rows]
        )

    x_rows = in_rows(long_rows, glob_rows)
    dy_all = in_rows(dy_rows, dy_globs)
    rim = jnp.where(first_half, x_long[:, :RIM], x_long[:, tok_half - RIM :])
    to_next = [(i * ffn_count + 1, (i + 1) * ffn_count + 1) for i in range(seq_count - 1)]
    to_last = [((i + 1) * ffn_count, i * ffn_count) for i in range(seq_count - 1)]
    rim = lax.ppermute(rim, ("seq", "ffn"), to_next + to_last)
    rim_other = swap_cores(rim)
    rim_left = jnp.where(first_half, rim_other, rim).reshape(-1, model_dim)
    rim_right = jnp.where(first_half, rim, rim_other).reshape(-1, model_dim)

    weights_low = w_master.astype(BF)
    glob_other = swap_cores(x_glob)
    glob_own = jnp.concatenate(
        [jnp.where(first_half, x_glob, glob_other), jnp.where(first_half, glob_other, x_glob)], axis=1
    )
    cells = [weights_low[a:b].reshape(-1, LANES) for a, b, _ in parts]
    cells[-1] = jnp.concatenate([cells[-1], glob_own.reshape(-1, LANES)])
    orders = [order for _, _, order in parts]
    gathered = [
        [piece.reshape(-1, rows, LANES) for piece in pieces]
        for pieces, rows in zip(gather_rows(cells, orders), rows_per)
    ]
    all_globs = jnp.concatenate([piece[:, -glob_cells:] for piece in gathered[-1]])
    tiles_per = tuple(last - first for (first, last, _), pieces in zip(parts, gathered) for _ in pieces)
    gathered = [piece for pieces in gathered for piece in pieces]
    all_globs = all_globs.reshape(seq_count, seqs, glob_block, model_dim)
    all_globs = all_globs.transpose(1, 0, 2, 3).reshape(seqs * globs, model_dim)
    reach = 2 * RADIUS
    width = up_to(LANES + 2 * RIM, LANES) if globs % LANES == 0 else up_to(LANES + 2 * RIM + globs, LANES) - globs
    ext = block_len - LANES + width
    span = ext + globs
    rel_low = jnp.pad(
        rel_table.astype(BF), ((RIM - RADIUS, LABEL_PAD - labels - RIM + RADIUS), (0, 0))
    )

    chunks = block_len // LANES
    chunk_at = jnp.arange(chunks, dtype=jnp.int32)[:, None, None] * LANES
    query_at = jnp.arange(LANES, dtype=jnp.int32)[None, :, None]
    key_at = jnp.arange(width + globs, dtype=jnp.int32)[None, None, :]
    token = lax.axis_index("seq") * block_len - RIM + chunk_at + key_at
    offset = key_at - query_at - (RIM - RADIUS)
    allowed = (
        (offset >= 0)
        & (offset <= reach)
        & (token >= 0)
        & (token < block_len * seq_count)
    ) | (key_at >= width)
    bias = jnp.where(allowed, 0.0, NEG_FILL).astype(F32)
    glob_bias_rows = row_count - seqs * block_len
    row_at = jnp.arange(glob_bias_rows, dtype=jnp.int32)[None, :, None]
    seq_at = jnp.arange(seqs, dtype=jnp.int32)[:, None, None]
    spread = jnp.pad(sentence[:, 0], ((0, 0), (RIM, span - RIM - block_len)), constant_values=-1)
    span_at = jnp.arange(span, dtype=jnp.int32)[None, None, :]
    own = (spread[:, None, :] == row_at - seq_at * glob_block) & (spread[:, None, :] >= 0)
    glob_bias = jnp.where(own | (span_at >= ext), 0.0, NEG_FILL).astype(F32)

    spec_up = block_at((up_rows, model_dim), 0, 0)
    spec_down = block_at((hidden, model_dim), 1, 0)
    spec_out = block_at((head_cols, model_dim), out_at // head_cols, 0)

    def rows_of(cols, dtype=BF, rows=row_count):
        return jax.ShapeDtypeStruct((rows, cols), dtype)

    def specs(arrays):
        return [whole(a.shape) for a in arrays]

    dims = (seqs, block_len, glob_block, ext, width, globs, scale)
    fwd_shapes = (
        rows_of(head_cols),
        rows_of(head_cols, rows=seqs * span),
        rows_of(head_cols, rows=seqs * span),
        rows_of(head_cols),
        rows_of(model_dim),
        rows_of(model_dim, rows=seqs * span),
    )
    wall_at = (
        2 * ffn_tiles // per_row * side,
        4 * attn_tiles // per_row * side,
        qk_at,
        v_at,
        out_at,
        tiles_per,
    )
    wall_shape = jax.ShapeDtypeStruct((out_at + head_cols, model_dim), BF)
    ins = [x_rows, rim_left, rim_right, all_globs, rel_low, bias, glob_bias]
    query, keys, values, heads_out, attn_part, x_ext, wall = kernel_call(
        functools.partial(attend_kernel, dims, wall_at),
        "attend",
        fwd_shapes + (wall_shape,),
        [scalars()] * 3 + specs(ins) + [any_space()] * len(gathered),
        tuple(specs(fwd_shapes)) + (any_space(),),
        [pltpu.VMEM(wall_shape.shape, BF), pltpu.SemaphoreType.DMA((3,))],
        flops=4 * 10**9,
        bytes_moved=10**7,
    )(wall_row, wall_col, wall_kind, *ins, *gathered)
    attn_got = swap_cores(attn_part)
    feed_shapes = (
        rows_of(model_dim, F32),
        rows_of(model_dim),
        rows_of(hidden, F32),
        rows_of(hidden),
        rows_of(model_dim),
    )
    norm_one, norm_low, up_pre, act_low, down_part = kernel_call(
        feed_kernel,
        "feed",
        feed_shapes,
        specs([x_rows, attn_part, attn_got, norm_params]) + [spec_up, spec_down],
        tuple(specs(feed_shapes)),
        flops=3 * 10**9,
        bytes_moved=10**7,
    )(x_rows, attn_part, attn_got, norm_params, wall, wall)
    down_got = swap_cores(down_part)
    norm_shape = jax.ShapeDtypeStruct((8, model_dim), F32)
    back_shapes = (
        rows_of(model_dim),
        rows_of(model_dim, F32),
        rows_of(model_dim),
        rows_of(hidden),
        rows_of(model_dim),
        norm_shape,
    )
    out_rows, d_pre, d_pre_low, d_up, d_norm_part, norm_two_grad = kernel_call(
        feed_back_kernel,
        "feed_back",
        back_shapes,
        specs([norm_one, down_part, down_got, up_pre, dy_all, norm_params]) + [spec_up, spec_down],
        tuple(specs(back_shapes)),
        flops=3 * 10**9,
        bytes_moved=10**7,
    )(norm_one, down_part, down_got, up_pre, dy_all, norm_params, wall, wall)
    d_norm_got = swap_cores(d_norm_part)
    grads_shape = jax.ShapeDtypeStruct((seq_count * sum(rows_per), LANES), BF)
    slot_grads = kernel_call(
        functools.partial(feed_grads_kernel, (4 * attn_tiles, 4 * attn_tiles + ffn_tiles)),
        "feed_grads",
        grads_shape,
        [scalars()] + specs([act_low, d_pre_low, norm_low, d_up]),
        any_space(),
        [
            pltpu.VMEM((hidden, model_dim), BF),
            pltpu.VMEM((model_dim, hidden), BF),
            pltpu.SemaphoreType.DMA((2,)),
        ],
        flops=3 * 10**9,
        bytes_moved=10**7,
    )(place_rows, act_low, d_pre_low, norm_low, d_up)
    ins = [
        x_rows,
        attn_part,
        attn_got,
        d_norm_part,
        d_norm_got,
        d_pre,
        heads_out,
        query,
        keys,
        values,
        x_ext,
    ]
    last_shapes = (
        grads_shape,
        rows_of(head_cols),
        rows_of(2 * head_cols, rows=seqs * span),
        rows_of(model_dim, F32),
        rows_of(head_cols, rows=LABEL_PAD + 16),
    )
    slot_grads, d_query, dkv, d_mid, small = kernel_call(
        functools.partial(
            attend_back_kernel,
            dims,
            attn_tiles,
            (tile_count, slot_count),
            (seq_count * sum(rows_per[:-1]), rows_per[-1], glob_cells, glob_block),
        ),
        "attend_back",
        last_shapes,
        [scalars(), whole(norm_shape.shape)]
        + specs(ins)
        + [spec_out]
        + specs([rel_low, bias, glob_bias, norm_params])
        + [any_space()],
        (any_space(),) + tuple(specs(last_shapes[1:])),
        [
            pltpu.VMEM((row_count, head_cols), BF),
            pltpu.VMEM((row_count, model_dim), BF),
            pltpu.VMEM((2 * head_cols // LANES, seqs * span, LANES), F32),
            pltpu.VMEM((head_cols, model_dim), BF),
            pltpu.VMEM((model_dim, head_cols), BF),
            pltpu.VMEM((model_dim, head_cols), BF),
            pltpu.VMEM((model_dim, head_cols), BF),
            pltpu.VMEM((side, side), BF),
            pltpu.VMEM((LABEL_PAD, head_cols), F32),
            pltpu.VMEM((16, head_cols), F32),
            pltpu.VMEM((8, model_dim), F32),
            pltpu.VMEM((seq_count * glob_cells, LANES), F32),
            pltpu.VMEM((seq_count * glob_cells, LANES), BF),
            pltpu.SemaphoreType.DMA((6,)),
        ],
        {2 + len(ins) + 5: 0},
        flops=8 * 10**9,
        bytes_moved=2 * 10**7,
    )(place_rows, norm_two_grad, *ins, wall, rel_low, bias, glob_bias, norm_params, slot_grads)

    dkv = dkv.reshape(seqs, span, 2 * head_cols)
    spans = [seq_count * rows for rows in rows_per]
    sums, small = scatter_rows(
        slot_grads,
        [sum(spans[:at]) for at in range(len(spans))],
        spans,
        orders,
        small,
        seq_bits(seq_count)[::-1],
    )
    dkv_glob = sum(term[-glob_cells:].astype(F32) for term in sums[-1])
    dkv_glob = dkv_glob.reshape(seqs, glob_block, 2 * head_cols)
    state = (w_master, m_old, v_old, left_basis, right_basis, left_stats, right_stats)
    w_new, m_new, v_new, left_q, right_q, left_s, right_s = soap_update(sums, state)

    small = small[0].astype(F32) + small[1].astype(F32)
    rel_sum = small[RIM - RADIUS : RIM - RADIUS + labels]
    norm_sum = small[LABEL_PAD : LABEL_PAD + 4 * ffn_count].reshape(norm_params.shape)
    rel_new, rel_m_new, rel_v_new = adam_update(rel_sum, rel_table, rel_m, rel_v, WEIGHT_DECAY)
    norm_new, norm_m_new, norm_v_new = adam_update(norm_sum, norm_params, norm_m, norm_v, 0.0)

    forward = [(i, i + 1) for i in range(seq_count - 1)]
    backward = [(i + 1, i) for i in range(seq_count - 1)]
    from_next = lax.ppermute(dkv[:, :RIM], "seq", backward)
    from_last = lax.ppermute(dkv[:, RIM + block_len : 2 * RIM + block_len], "seq", forward)
    gap = jnp.zeros((seqs, block_len - RIM, 2 * head_cols), F32)
    dkv_long = (
        dkv[:, RIM : RIM + block_len].astype(F32)
        + jnp.concatenate([from_last.astype(F32), gap], axis=1)
        + jnp.concatenate([gap, from_next.astype(F32)], axis=1)
    )
    d_proj = jnp.concatenate(
        [
            d_query,
            jnp.concatenate(
                [
                    dkv_long.reshape(-1, 2 * head_cols).astype(BF),
                    dkv_glob.reshape(-1, 2 * head_cols).astype(BF),
                    jnp.zeros((row_count - used, 2 * head_cols), BF),
                ]
            ),
        ],
        axis=1,
    )
    w_qkv = jnp.concatenate(
        [wall[qk_at : qk_at + model_dim], wall[v_at : v_at + model_dim, :head_cols]], axis=1
    )
    d_in = dot_on(d_proj, w_qkv, 1, 1)

    def own_half(values):
        long_part = values[: seqs * block_len].reshape(seqs, block_len, model_dim)
        glob_part = values[seqs * block_len : used].reshape(seqs, glob_block, model_dim)
        halves = [
            jnp.concatenate(
                [
                    long_part[:, i * tok_half : (i + 1) * tok_half],
                    glob_part[:, i * glob_half : (i + 1) * glob_half],
                ],
                axis=1,
            )
            for i in range(ffn_count)
        ]
        return (
            jnp.where(first_half, halves[0], halves[1]),
            jnp.where(first_half, halves[1], halves[0]),
        )

    kept, sent = own_half(d_in)
    dx = kept + swap_cores(sent.astype(BF)).astype(F32) + own_half(d_mid)[0]
    out_mine = own_half(out_rows)[0]
    return (
        out_mine[:, :tok_half],
        out_mine[:, tok_half:],
        dx[:, :tok_half],
        dx[:, tok_half:],
        w_new,
        m_new,
        v_new,
        left_q,
        right_q,
        left_s,
        right_s,
        rel_new,
        rel_m_new,
        rel_v_new,
        norm_new,
        norm_m_new,
        norm_v_new,
    )


def solution(mesh):
    in_specs = (
        P(None, ("seq", "ffn"), None),
        P(None, ("seq", "ffn"), None),
        P(None, "seq", None),
        P(None, ("seq", "ffn"), None),
        P(None, ("seq", "ffn"), None),
        P(),
        P(("seq", "ffn"), None, None),
        P(("seq", "ffn"), None, None),
        P(("seq", "ffn"), None, None),
        P(("seq", "ffn"), None, None),
        P(("seq", "ffn"), None, None),
        P(("seq", "ffn"), None, None),
        P(("seq", "ffn"), None, None),
        P(None, "ffn"),
        P(None, "ffn"),
        P(None, "ffn"),
        P(),
        P(),
        P(),
    )
    out_specs = (
        P(None, ("seq", "ffn"), None),
        P(None, ("seq", "ffn"), None),
        P(None, ("seq", "ffn"), None),
        P(None, ("seq", "ffn"), None),
        P(("seq", "ffn"), None, None),
        P(("seq", "ffn"), None, None),
        P(("seq", "ffn"), None, None),
        P(("seq", "ffn"), None, None),
        P(("seq", "ffn"), None, None),
        P(("seq", "ffn"), None, None),
        P(("seq", "ffn"), None, None),
        P(None, "ffn"),
        P(None, "ffn"),
        P(None, "ffn"),
        P(),
        P(),
        P(),
    )
    return jax.shard_map(
        on_device, mesh=mesh, in_specs=in_specs, out_specs=out_specs, check_vma=False
    )
```

```python
import functools
import math

import jax
import jax.numpy as jnp
from jax import lax
from jax.experimental import pallas as pl
from jax.experimental.pallas import tpu as pltpu
from jax.sharding import PartitionSpec as P

HEADS = 12
FF = 3072
RADIUS = 84
STEP = 10

BETA_ONE = 0.9
BETA_TWO = 0.95
LEARN_RATE = 0.02
ADAM_RATE = 0.6
WEIGHT_DECAY = 0.01
ADAM_EPS = 1e-08
NORM_EPS = 1e-12
NEG_FILL = -1e30
BF = jnp.bfloat16
F32 = jnp.float32


def seq_bits(count):
    return [1 << at for at in range(count.bit_length() - 1)]


def swap_with(values, bit):
    count = lax.axis_size("seq")
    return lax.ppermute(values, "seq", [(i, i ^ bit) for i in range(count)])


def slot_parts(slots, count):
    bits = seq_bits(count)
    low, high = bits[:3], bits[3:]
    cuts = [slots * at // 14 for at in (0, 5, 10, 14)]
    orders = [low[at:] + low[:at] + high for at in range(3)]
    return [(a, b, order) for a, b, order in zip(cuts, cuts[1:], orders) if b > a]


def part_rows(parts, side, extra):
    rows = [(last - first) * side for first, last, _ in parts]
    return rows[:-1] + [rows[-1] + extra]


def slot_places(owners, slots, rows, side):
    count = lax.axis_size("seq")
    apart = (owners // slots) ^ lax.axis_index("seq")
    inner = owners % slots
    place, row, base = jnp.zeros_like(owners), jnp.zeros_like(owners), 0
    for (first, last, order), many in zip(slot_parts(slots, count), rows):
        index = jnp.zeros_like(owners)
        for at, bit in enumerate(order):
            index = index + jnp.where((apart & bit) != 0, count >> (at + 1), 0)
        here = (inner >= first) & (inner < last)
        place = jnp.where(here, first * count + index * (last - first) + inner - first, place)
        row = jnp.where(here, base + index * many + (inner - first) * side, row)
        base += many * count
    return place, row


FAR_SIZE = 3 * 2**20


def move_kernel(plan, arrays, *refs):
    ins, outs, held, sems = refs[:arrays], refs[arrays : arrays + len(plan)], refs[arrays + len(plan) : -1], refs[-1]
    copies, sums, sem = [], [], 0
    for out, runs in zip(outs, plan):
        base = 0
        for rows, *terms in runs:
            here = out.at[pl.ds(base, rows)]
            targets = [here] if len(terms) == 1 else [held[len(sums) * 2 + k] for k in range(2)]
            waits = []
            for (at, start), target in zip(terms, targets):
                waits.append(pltpu.make_async_copy(ins[at].at[pl.ds(start, rows)], target, sems.at[sem]))
                waits[-1].start()
                sem += 1
            if len(terms) == 1:
                copies += waits
            else:
                sums.append((waits, targets, out, base, rows))
            base += rows
    for waits, (one, two), out, base, rows in sums:
        for wait in waits:
            wait.wait()
        step = next(s for s in (128, 64, 48, 32, 16) if rows % s == 0)

        def add(i, carry):
            at = pl.multiple_of(i * step, 16)
            total = one[pl.ds(at, step), :].astype(F32) + two[pl.ds(at, step), :].astype(F32)
            out[pl.ds(base + at, step), :] = total.astype(BF)
            return carry

        lax.fori_loop(0, rows // step, add, 0)
    for copy in copies:
        copy.wait()


def move_rows(outputs):
    arrays, plan, scratch, count = [], [], [], 0
    for runs in outputs:
        plan.append([])
        for rows, *terms in runs:
            places = []
            for array, start in terms:
                found = [i for i, other in enumerate(arrays) if other is array]
                if not found:
                    arrays.append(array)
                places.append((found[0] if found else len(arrays) - 1, start))
                count += 1
            plan[-1].append((rows, *places))
            if len(terms) == 2:
                scratch += [pltpu.VMEM((rows, terms[0][0].shape[1]), BF)] * 2
    shapes = [(sum(run[0] for run in runs), runs[0][1][0].shape[1]) for runs in outputs]
    return pl.pallas_call(
        functools.partial(move_kernel, plan, len(arrays)),
        grid=(1,),
        out_shape=tuple(jax.ShapeDtypeStruct(shape, BF) for shape in shapes),
        in_specs=[
            pl.BlockSpec(memory_space=pltpu.HBM if array.size > FAR_SIZE else pl.ANY) for array in arrays
        ],
        out_specs=tuple(whole(shape) for shape in shapes),
        scratch_shapes=scratch + [pltpu.SemaphoreType.DMA((count,))],
        cost_estimate=pl.CostEstimate(
            flops=0, bytes_accessed=sum(6 * math.prod(s) for s in shapes), transcendentals=0
        ),
        compiler_params=pltpu.CompilerParams(vmem_limit_bytes=16 * 2**20),
        name="add_rows" if scratch else "join_rows",
    )(*arrays)


def run_sum(rows, one, one_at, two, two_at):
    return (rows, (one, one_at), (two, two_at))


def gather_rows(cells, extra, rows, orders):
    own = sum(rows)
    shared = orders[0][3:][::-1]
    got = [swap_with(values, shared[0]) for values in (cells, extra)]
    devices = [[(cells, 0), (extra, -cells.shape[0])], [(got[0], 0), (got[1], -cells.shape[0])]]
    if len(shared) > 1:
        (cells,) = move_rows([[(array.shape[0], (array, 0)) for runs in devices for array, _ in runs]])
        for bit in shared[1:-1]:
            got = swap_with(cells, bit)
            (cells,) = move_rows([[(cells.shape[0], (cells, 0)), (cells.shape[0], (got, 0))]])
        got = swap_with(cells, shared[-1])
        devices = [[(run, i * own)] for run in (cells, got) for i in range(cells.shape[0] // own)]
    starts = [sum(rows[:at]) for at in range(len(rows))]

    def runs_of(start, many):
        runs = []
        for pieces in devices:
            left, at = many, start
            for array, shift in pieces:
                here = min(left, array.shape[0] - (at + shift))
                if here > 0:
                    runs.append((here, (array, at + shift)))
                    left, at = left - here, at + here
        return runs

    parts = move_rows([runs_of(start, many) for start, many in zip(starts, rows)])
    for step in (2, 1):
        got = [swap_with(part, order[step]) for part, order in zip(parts, orders)]
        parts = move_rows([[(p.shape[0], (p, 0)), (p.shape[0], (g, 0))] for p, g in zip(parts, got)])
    got = [swap_with(part, order[0]) for part, order in zip(parts, orders)]
    return list(zip(parts, got))


def scatter_rows(cells, rows, orders, everywhere, order_everywhere, carried):
    count = lax.axis_size("seq")
    spans = [count * many for many in rows]
    starts = [sum(spans[:at]) for at in range(len(spans))]
    sends = [cells[a + r // 2 : a + r] for a, r in zip(starts, spans)]
    kept = [(cells, a, r // 2) for a, r in zip(starts, spans)]

    def all_sum():
        return [run_sum(everywhere.shape[0], everywhere, 0, all_got, 0)]

    for step in range(3):
        got = [swap_with(send, order[step]) for send, order in zip(sends, orders)]
        all_got = swap_with(everywhere, order_everywhere[step])
        halves = [r // 2 for _, _, r in kept]
        if step < 2:
            *sends, everywhere = move_rows(
                [[run_sum(h, k, a + h, g, h)] for h, (k, a, _), g in zip(halves, kept, got)] + [all_sum()]
            )
            keeps = move_rows([[run_sum(h, k, a, g, 0)] for h, (k, a, _), g in zip(halves, kept, got)])
            kept = [(keep, 0, h) for keep, h in zip(keeps, halves)]
    devices = count // 8

    def merged(at, many):
        return [
            run_sum(r, k, i * r, g, i * r)
            for i in range(at, at + many)
            for r, (k, _, _), g in zip(rows, kept, got)
        ]

    half = devices // 2
    send, everywhere, *carried = move_rows([merged(half, half), all_sum()] + carried)
    (keep,) = move_rows([merged(0, half)])
    for step, bit in enumerate(orders[0][3:]):
        got_all = swap_with(send, bit)
        all_got = swap_with(everywhere, order_everywhere[3 + step])
        if bit == orders[0][-1]:
            return (keep, got_all), (everywhere, all_got), carried
        half = keep.shape[0] // 2
        send, everywhere = move_rows([[run_sum(half, keep, half, got_all, half)], all_sum()])
        (keep,) = move_rows([[run_sum(half, keep, 0, got_all, 0)]])
    return None


def split_two(x):
    hi = x.astype(BF)
    return hi, (x - hi.astype(F32)).astype(BF)


def split_three(x):
    hi = x.astype(BF)
    rest = x - hi.astype(F32)
    mid = rest.astype(BF)
    return hi, mid, (rest - mid.astype(F32)).astype(BF)


def left_six(parts, axis):
    h, m, l = parts
    return jnp.concatenate([h, h, m, m, h, l], axis=axis)


def right_six(parts, axis):
    h, m, l = parts
    return jnp.concatenate([h, m, h, m, l, h], axis=axis)


def left_three(parts, axis):
    h, l = parts
    return jnp.concatenate([h, h, l], axis=axis)


def right_three(parts, axis):
    h, l = parts
    return jnp.concatenate([h, l, h], axis=axis)


def dot_on(a, b, ca, cb):
    return lax.dot_general(a, b, (((ca,), (cb,)), ((), ())), preferred_element_type=F32)


def dot_six(a, b, ca, cb):
    return dot_on(left_six(split_three(a), ca), right_six(split_three(b), cb), ca, cb)


def dot_three(a, b, ca, cb):
    return dot_on(left_three(split_two(a), ca), right_three(split_two(b), cb), ca, cb)


PANEL = 32


def panel_inverse(a_ref, t_ref, npad, side, at):
    groups = PANEL // 8
    iota = lax.broadcasted_iota(jnp.int32, (8, npad), 0)
    a = []
    for i in range(PANEL):
        rows = a_ref[pl.ds(at + i, npad, stride=side), :]
        cols = rows.T[at : at + PANEL]
        a.append([cols[8 * g : 8 * g + 8] for g in range(groups)])
    z = [[None] * groups for _ in range(PANEL)]
    for j in range(PANEL):
        gj, sj = divmod(j, 8)
        r = lax.rsqrt(a[j][gj][sj : sj + 1])
        u = [None if g < gj else a[j][g] * r for g in range(groups)]
        below = list(u)
        below[gj] = jnp.where(iota > sj, u[gj], 0.0)
        for k in range(j + 1, PANEL):
            gk, sk = divmod(k, 8)
            row = u[gk][sk : sk + 1]
            for g in range(gk, groups):
                a[k][g] = a[k][g] - u[g] * row
        for c in range(j):
            row = z[c][gj][sj : sj + 1] * r
            z[c][gj] = jnp.where(iota == sj, row, z[c][gj]) - below[gj] * row
            for g in range(gj + 1, groups):
                z[c][g] = z[c][g] - u[g] * row
        z[j] = [
            jnp.zeros((8, npad), F32)
            if g < gj
            else (jnp.where(iota == sj, r, 0.0) - below[g] * r if g == gj else -u[g] * r)
            for g in range(groups)
        ]
    fill = jnp.zeros((side - PANEL, npad), F32)
    for c in range(PANEL):
        t_ref[pl.ds(c, npad, stride=PANEL), :] = jnp.concatenate(z[c] + [fill], axis=0).T


def adam_step(grad, refs, outs, where, decay_rate):
    param, first_mom, second_mom = [ref[where] for ref in refs]
    first_mom = BETA_ONE * first_mom + (1.0 - BETA_ONE) * grad
    second_mom = BETA_TWO * second_mom + (1.0 - BETA_TWO) * grad * grad
    direction = (
        first_mom
        / (1.0 - BETA_ONE**STEP)
        / (jnp.sqrt(second_mom / (1.0 - BETA_TWO**STEP)) + ADAM_EPS)
    )
    outs[0][where] = param - ADAM_RATE * (direction + decay_rate * param)
    outs[1][where] = first_mom
    outs[2][where] = second_mom


def small_updates(small_refs, refs, outs):
    total = small_refs[0][...].astype(F32) + small_refs[1][...].astype(F32)
    labels, cols = refs[0].shape
    rel = pltpu.roll(total, total.shape[0] - (RIM - RADIUS), 0)[:labels]
    adam_step(rel, refs[:3], outs[:3], (slice(None), slice(None)), WEIGHT_DECAY)
    halves = refs[3].shape[1] // cols
    for row in range(refs[3].shape[0]):
        for half in range(halves):
            at = SMALL_ROWS - 8 + row * halves + half
            where = (slice(row, row + 1), slice(half * cols, (half + 1) * cols))
            adam_step(total[at : at + 1], refs[3:], outs[3:], where, 0.0)


def soap_kernel(npad, kept_ref, got_ref, small_ref, small_got_ref, *refs):
    w_ref, m_ref, v_ref, ql_ref, qr_ref, sl_ref, sr_ref = refs[:7]
    w_out, m_out, v_out, ql_out, qr_out, sl_out, sr_out = refs[13:20]
    a_ref, y_ref, mat_ref, t_ref = refs[26:]
    small_updates((small_ref, small_got_ref), refs[7:13], refs[20:26])
    n = w_ref.shape[0]
    many = next(k for k in (2, 1) if n % k == 0)
    batch = next(b for b in (14, 7, 4, 2) if 2 * n % b == 0)
    side = w_ref.shape[-1]
    eye = (
        lax.broadcasted_iota(jnp.int32, (side, side), 0)
        == lax.broadcasted_iota(jnp.int32, (side, side), 1)
    ).astype(F32)

    def first(at, carry):
        slots = [at * many + k for k in range(many)]
        tiles = [pl.ds(pl.multiple_of(i * side, side), side) for i in slots]
        grads = [kept_ref[rows, :].astype(F32) + got_ref[rows, :].astype(F32) for rows in tiles]
        lefts = [ql_ref[i] for i in slots]
        rights = [qr_ref[i] for i in slots]
        halves = [split_two(x) for x in grads]
        new_l = [
            BETA_TWO * sl_ref[i] + (1.0 - BETA_TWO) * dot_on(left_three(p, 1), right_three(p, 1), 1, 1)
            for i, p in zip(slots, halves)
        ]
        new_r = [
            BETA_TWO * sr_ref[i] + (1.0 - BETA_TWO) * dot_on(left_three(p, 0), right_three(p, 0), 0, 0)
            for i, p in zip(slots, halves)
        ]
        mats = [dot_six(x, y, 1, 0) for x, y in zip(new_l + new_r, lefts + rights)]
        thirds = [split_three(x) for x in mats]
        grams = [dot_on(left_six(p, 0), right_six(p, 0), 0, 0) for p in thirds]
        turned = [dot_three(x, y, 0, 0) for x, y in zip(lefts, grads)]
        rotated = [dot_three(x, y, 1, 0) for x, y in zip(turned, rights)]
        moms = [BETA_ONE * m_ref[i] + (1.0 - BETA_ONE) * x for i, x in zip(slots, rotated)]
        secs = [BETA_TWO * v_ref[i] + (1.0 - BETA_TWO) * x * x for i, x in zip(slots, rotated)]
        steps = [
            x / (1.0 - BETA_ONE**STEP) / (jnp.sqrt(y / (1.0 - BETA_TWO**STEP)) + ADAM_EPS)
            for x, y in zip(moms, secs)
        ]
        turned = [dot_three(x, y, 1, 0) for x, y in zip(lefts, steps)]
        backs = [dot_three(x, y, 1, 1) for x, y in zip(turned, rights)]
        weights = [w_ref[i] for i in slots]
        for k, i in enumerate(slots):
            m_out[i] = moms[k]
            v_out[i] = secs[k]
            w_out[i] = weights[k] - LEARN_RATE * (backs[k] + WEIGHT_DECAY * weights[k])
            sl_out[i] = new_l[k]
            sr_out[i] = new_r[k]
            for kind in range(2):
                mat_ref[2 * i + kind] = mats[kind * many + k]
                rows = pl.ds(pl.multiple_of((2 * i + kind) * side, side), side)
                a_ref[rows, :] = grams[kind * many + k]
                y_ref[rows, :] = eye
        return carry

    lax.fori_loop(0, n // many, first, 0)
    if npad > 2 * n:
        a_ref[2 * n * side :, :] = jnp.concatenate([eye] * (npad - 2 * n), axis=0)
    for at in range(0, side, PANEL):
        panel_inverse(a_ref, t_ref, npad, side, at)

        def update(i, carry):
            bases = [pl.multiple_of((i * batch + b) * side, side) for b in range(batch)]
            rows = [pl.ds(base + at, PANEL) for base in bases]
            both = [jnp.concatenate([a_ref[r, :], y_ref[r, :]], axis=1) for r in rows]
            turns = [
                t_ref[pl.ds(pl.multiple_of((i * batch + b) * PANEL, PANEL), PANEL), :][:, :PANEL]
                for b in range(batch)
            ]
            if at + PANEL < side:
                rest = [pl.ds(base + at + PANEL, side - at - PANEL) for base in bases]
                old = [(a_ref[r, :], y_ref[r, :]) for r in rest]
            fresh = [dot_six(t, x, 0, 0) for t, x in zip(turns, both)]
            if at + PANEL < side:
                changes = []
                for x in fresh:
                    parts = split_three(x)
                    cut = tuple(p[:, at + PANEL : side] for p in parts)
                    changes.append(dot_on(left_six(cut, 0), right_six(parts, 0), 0, 0))
                for r, (old_a, old_y), change in zip(rest, old, changes):
                    a_ref[r, :] = old_a - change[:, :side]
                    y_ref[r, :] = old_y - change[:, side:]
            for r, x in zip(rows, fresh):
                y_ref[r, :] = x[:, side:]
            return carry

        lax.fori_loop(0, 2 * n // batch, update, 0)

    def last(i, carry):
        mats = [mat_ref[2 * i], mat_ref[2 * i + 1]]
        rows = [pl.ds(pl.multiple_of((2 * i + k) * side, side), side) for k in range(2)]
        turns = [y_ref[r, :] for r in rows]
        left, right = [dot_three(x, y, 1, 1) for x, y in zip(mats, turns)]
        ql_out[i] = left
        qr_out[i] = right
        return carry

    lax.fori_loop(0, n, last, 0)


def soap_update(grads, small, state, others):
    n, side = state[0].shape[:2]
    npad = -(-2 * n // 8) * 8
    ins = [*grads, *small, *state, *others]
    outs = [*state, *others]
    return pl.pallas_call(
        functools.partial(soap_kernel, npad),
        grid=(1,),
        out_shape=tuple(jax.ShapeDtypeStruct(s.shape, F32) for s in outs),
        in_specs=[whole(array.shape) for array in ins],
        out_specs=tuple(whole(array.shape) for array in outs),
        scratch_shapes=[
            pltpu.VMEM((npad * side, side), F32),
            pltpu.VMEM((npad * side, side), F32),
            pltpu.VMEM((2 * n, side, side), F32),
            pltpu.VMEM((npad * PANEL, side), F32),
        ],
        cost_estimate=pl.CostEstimate(
            flops=n * 40 * side**3, bytes_accessed=n * 60 * side * side, transcendentals=0
        ),
        compiler_params=pltpu.CompilerParams(vmem_limit_bytes=32 * 2**20),
        name="soap",
    )(*ins)


LANES = 128
LABEL_PAD = 256
RIM = 96
SMALL_ROWS = 192


def up_to(value, unit):
    return -(-value // unit) * unit


def block_at(shape, *index):
    return pl.BlockSpec(shape, lambda i: index, pipeline_mode=pl.Buffered(1))


def whole(shape):
    return block_at(shape, *[0] * len(shape))


def any_space():
    return pl.BlockSpec(memory_space=pl.ANY)


def far_space():
    return pl.BlockSpec(memory_space=pltpu.HBM)


def scalars():
    return pl.BlockSpec(memory_space=pltpu.SMEM)


def kernel_call(body, name, mib, out_shape, in_specs, out_specs, scratch=(), aliases=None, flops=0, bytes_moved=0):
    return pl.pallas_call(
        body,
        name=name,
        grid=(1,),
        out_shape=out_shape,
        in_specs=in_specs,
        out_specs=out_specs,
        scratch_shapes=list(scratch),
        input_output_aliases=aliases or {},
        cost_estimate=pl.CostEstimate(flops=flops, bytes_accessed=bytes_moved, transcendentals=0),
        compiler_params=pltpu.CompilerParams(vmem_limit_bytes=mib * 2**20),
    )


def start_tiles(row_ref, col_ref, kind_ref, sources, tiles, wall_ref, sems):
    base = 0
    for source, many in zip(sources, tiles):

        def start(i, carry):
            for k in range(many):
                place = base + i * many + k
                kind = kind_ref[place]

                @pl.when(kind < 2)
                def _():
                    row = pl.multiple_of(row_ref[place], LANES)
                    col = pl.multiple_of(col_ref[place], LANES)
                    pltpu.make_async_copy(
                        source.at[i, pl.ds(k * LANES, LANES)],
                        wall_ref.at[pl.ds(row, LANES), pl.ds(col, LANES)],
                        sems.at[kind],
                    ).start()

            return carry

        lax.fori_loop(0, source.shape[0], start, 0)
        base += source.shape[0] * many


def wait_rows(wall_ref, rows, sem):
    part = wall_ref.at[pl.ds(0, rows)]
    pltpu.make_async_copy(part, part, sem).wait()


def low_lanes(rows):
    return lax.broadcasted_iota(jnp.int32, (rows, LANES), 1) < LANES // 2


def stack_heads(pair):
    low = low_lanes(pair.shape[0])
    zero = jnp.zeros_like(pair)
    return jnp.concatenate([jnp.where(low, pair, zero), jnp.where(low, zero, pair)], axis=0)


def merge_stack(stacked):
    rows = stacked.shape[0] // 2
    return jnp.where(low_lanes(rows), stacked[:rows], stacked[rows:])


def skew(table, width):
    rows = table.shape[0] // 2
    padded = jnp.concatenate(
        [table, jnp.zeros((table.shape[0], width - table.shape[1]), F32)], axis=1
    )
    halves = [
        pltpu.roll(padded[at : at + rows], 0, 1, stride=1, stride_axis=0) for at in (0, rows)
    ]
    return jnp.concatenate(halves, axis=0)


def unskew(grid, width):
    rows = grid.shape[0] // 2
    lanes = grid.shape[1]
    parts = []
    for at in range(0, 2 * rows, 8):
        shift = (at % rows) % lanes
        part = grid[at : at + 8]
        parts.append(part if shift == 0 else pltpu.roll(part, lanes - shift, 1))
    moved = jnp.concatenate(parts, axis=0)
    index = lax.broadcasted_iota(jnp.int32, moved.shape, 0)
    for bit in (1, 2, 4):
        moved = jnp.where((index & bit) != 0, pltpu.roll(moved, lanes - bit, 1), moved)
    return moved[:, :width]


def softmax_rows(scores):
    top = jnp.max(scores, axis=-1, keepdims=True)
    raised = jnp.exp(scores - top)
    return raised * (1.0 / jnp.sum(raised, axis=-1, keepdims=True))


def window_keys(ref, base, at, width, ext, globs, cols):
    return jnp.concatenate(
        [ref[pl.ds(base + at, width), cols], ref[pl.ds(base + ext, globs), cols]], axis=0
    )


def glob_row_mask(shape, seq, glob_block):
    row = lax.broadcasted_iota(jnp.int32, shape, 0) % (shape[0] // 2)
    return (row >= seq * glob_block) & (row < (seq + 1) * glob_block)


def window_bias(block, blocks, chunk, dims):
    _, block_len, _, _, width, globs, _ = dims
    shape = (2 * LANES, width + globs)
    key = lax.broadcasted_iota(jnp.int32, shape, 1)
    query = lax.broadcasted_iota(jnp.int32, shape, 0) % LANES
    offset = key - query - (RIM - RADIUS)
    token = block * block_len - RIM + chunk * LANES + key
    near = (offset >= 0) & (offset <= 2 * RADIUS) & (token >= 0) & (token < blocks * block_len)
    return jnp.where(near | (key >= width), 0.0, NEG_FILL)


def attend_kernel(dims, wall_at, blocks, row_ref, col_ref, kind_ref, block_ref, xr_ref, rel_ref, gbias_ref,
                  left_ref, right_ref, *refs):
    q_ref, k_ref, v_ref, o_ref, part_ref, xe_ref, wall_out, wall_ref, glob_low, glob_cells, sems = refs[-11:]
    sources = refs[:-11]
    seqs, block_len, glob_block, ext, width, globs, scale = dims
    feed_rows, attn_rows, qk_at, v_at, out_at, tiles = wall_at
    model_dim = xr_ref.shape[1]
    head_cols = q_ref.shape[1]
    start_tiles(row_ref, col_ref, kind_ref, sources, tiles, wall_ref, sems)
    span = ext + globs
    cells = glob_low.shape[0] // blocks
    copies, base = [], 0
    for source in sources[-2:]:
        rows = source.shape[1] - cells
        for i in range(source.shape[0]):
            copies.append((source.at[i, pl.ds(rows, cells)], glob_low.at[pl.ds(base, cells)]))
            base += cells
    for source, target in copies:
        pltpu.make_async_copy(source, target, sems.at[3]).start()
    for seq in range(seqs):
        at = seq * span
        rim = pl.ds(seq * RIM, RIM)
        pltpu.make_async_copy(left_ref.at[rim], xe_ref.at[pl.ds(at, RIM)], sems.at[4]).start()
        pltpu.make_async_copy(
            right_ref.at[rim], xe_ref.at[pl.ds(at + RIM + block_len, RIM)], sems.at[4]
        ).start()
        at += RIM
        xe_ref[at : at + block_len] = xr_ref[seq * block_len : (seq + 1) * block_len]
        at += block_len + RIM
        if ext > block_len + 2 * RIM:
            xe_ref[at : seq * span + ext] = jnp.zeros((ext - block_len - 2 * RIM, model_dim), BF)
    pltpu.make_async_copy(glob_low, glob_low, sems.at[3]).wait()
    glob_cells[...] = glob_low[...].astype(F32)
    cols = model_dim // LANES
    for seq in range(seqs):
        for r in range(glob_block):
            at = seq * span + ext + r * blocks
            for c in range(cols):
                source = pl.ds((seq * glob_block + r) * cols + c, blocks, stride=cells)
                xe_ref[at : at + blocks, c * LANES : (c + 1) * LANES] = glob_cells[source, :].astype(BF)
    rims = xe_ref.at[pl.ds(0, 2 * seqs * RIM)]
    pltpu.make_async_copy(rims, rims, sems.at[4]).wait()
    wait_rows(wall_ref, attn_rows, sems.at[0])
    wq_ref = wall_ref.at[pl.ds(qk_at, model_dim), pl.ds(0, head_cols)]
    wk_ref = wall_ref.at[pl.ds(qk_at, model_dim), pl.ds(head_cols, head_cols)]
    wv_ref = wall_ref.at[pl.ds(v_at, model_dim), pl.ds(0, head_cols)]
    wo_ref = wall_ref.at[pl.ds(out_at, head_cols)]
    pairs = head_cols // LANES
    glob_at = seqs * block_len
    glob_rows = q_ref.shape[0] - glob_at
    span = ext + globs
    chunks = block_len // LANES
    q_ref[...] = dot_on(xr_ref[...], wq_ref[...], 1, 0).astype(BF)

    def project(i, carry):
        rows = pl.ds(pl.multiple_of(i * 256, 256), 256)
        k_ref[rows, :] = dot_on(xe_ref[rows, :], wk_ref[...], 1, 0).astype(BF)
        v_ref[rows, :] = dot_on(xe_ref[rows, :], wv_ref[...], 1, 0).astype(BF)
        return carry

    lax.fori_loop(0, seqs * span // 256, project, 0)
    wait_rows(wall_ref, feed_rows, sems.at[1])
    keep = pltpu.make_async_copy(wall_ref, wall_out, sems.at[2])
    keep.start()

    def window(i, carry):
        seq, chunk = i // chunks, i % chunks
        rows = pl.ds(pl.multiple_of(i * LANES, LANES), LANES)
        base = pl.multiple_of(seq * span, LANES)
        at = pl.multiple_of(chunk * LANES, LANES)
        bias = window_bias(block_ref[0], blocks, chunk, dims)
        for pair in range(pairs):
            cols = slice(pair * LANES, (pair + 1) * LANES)
            query = stack_heads(q_ref[rows, cols] * scale)
            keys = window_keys(k_ref, base, at, width, ext, globs, cols)
            values = window_keys(v_ref, base, at, width, ext, globs, cols)
            scores = dot_on(query, keys, 1, 1)
            scores = scores + skew(dot_on(query, rel_ref[:, cols], 1, 1), width + globs) + bias
            weights = softmax_rows(scores).astype(BF)
            o_ref[rows, cols] = merge_stack(dot_on(weights, values, 1, 0)).astype(BF)
        return carry

    lax.fori_loop(0, seqs * chunks, window, 0)
    rows = slice(glob_at, glob_at + glob_rows)
    for pair in range(pairs):
        cols = slice(pair * LANES, (pair + 1) * LANES)
        query = stack_heads(q_ref[rows, cols] * scale)
        total = jnp.zeros((2 * glob_rows, LANES), F32)
        for seq in range(seqs):
            span_rows = slice(seq * span, (seq + 1) * span)
            bias = gbias_ref[seq]
            scores = dot_on(query, k_ref[span_rows, cols], 1, 1) + jnp.concatenate([bias, bias], axis=0)
            weights = softmax_rows(scores).astype(BF)
            out = dot_on(weights, v_ref[span_rows, cols], 1, 0)
            total = jnp.where(glob_row_mask(total.shape, seq, glob_block), out, total)
        o_ref[rows, cols] = merge_stack(total).astype(BF)
    part_ref[...] = dot_on(o_ref[...], wo_ref[...], 1, 0).astype(BF)
    keep.wait()


def norm_parts(values):
    center = values - jnp.mean(values, axis=-1, keepdims=True)
    spread = jnp.mean(center * center, axis=-1, keepdims=True)
    rate = lax.rsqrt(spread + NORM_EPS)
    return center * rate, rate


def norm_back(grad, normed, rate, gain):
    scaled = grad * gain
    return (
        scaled
        - jnp.mean(scaled, axis=-1, keepdims=True)
        - normed * jnp.mean(scaled * normed, axis=-1, keepdims=True)
    ) * rate


def row_loop(total, body):
    step = 176 if total % 176 == 0 else 16

    def run(i, carry):
        body(pl.ds(pl.multiple_of(i * step, 16), step))
        return carry

    lax.fori_loop(0, total // step, run, 0)


def col_loop(total, body, step=256):
    def run(i, carry):
        body(i)
        return carry

    lax.fori_loop(0, total // step, run, 0)


GELU_RATE = 0.7978845608028654
GELU_CUBE = 0.044715


def gelu_parts(u):
    square = u * u
    curve = jnp.tanh(GELU_RATE * u * (1.0 + GELU_CUBE * square))
    return square, curve


def feed_kernel(xr_ref, part_ref, got_ref, norm_ref, wu_ref, wd_ref, h_ref, hb_ref, u_ref, a_ref, down_ref):
    model_dim = xr_ref.shape[1]
    gain, offset = norm_ref[0:1], norm_ref[1:2]

    def norm(rows):
        mid = xr_ref[rows, :].astype(F32) + (part_ref[rows, :].astype(F32) + got_ref[rows, :].astype(F32))
        normed, _ = norm_parts(mid)
        out = normed * gain + offset
        h_ref[rows, :] = out
        hb_ref[rows, :] = out.astype(BF)

    row_loop(xr_ref.shape[0], norm)
    per_half = model_dim // 256

    def up(j):
        rows = pl.ds(pl.multiple_of((j // per_half) * model_dim, 256), model_dim)
        cols = pl.ds(pl.multiple_of((j % per_half) * 256, 256), 256)
        here = pl.ds(pl.multiple_of(j * 256, 256), 256)
        u = dot_on(hb_ref[...], wu_ref[rows, cols], 1, 0)
        u_ref[:, here] = u
        _, curve = gelu_parts(u)
        a_ref[:, here] = (0.5 * u * (1.0 + curve)).astype(BF)

    col_loop(u_ref.shape[1], up)

    def down(j):
        cols = pl.ds(pl.multiple_of(j * 256, 256), 256)
        down_ref[:, cols] = dot_on(a_ref[...], wd_ref[:, cols], 1, 0).astype(BF)

    col_loop(model_dim, down)


def own_rows(ref, half, seqs, block_len, glob_block):
    per = block_len // 2
    long_part = [
        ref[pl.ds(pl.multiple_of(seq * block_len + half * per, per), per), :] for seq in range(seqs)
    ]
    base, few = seqs * block_len, glob_block // 2
    globs = ref[base:, :]
    glob_part = [
        jnp.where(
            half == 0,
            globs[seq * glob_block : seq * glob_block + few],
            globs[seq * glob_block + few : (seq + 1) * glob_block],
        )
        for seq in range(seqs)
    ]
    return long_part, glob_part


def feed_back_kernel(dims, half_ref, h_ref, down_ref, got_ref, u_ref, dy_ref, norm_ref, wu_ref, wd_ref,
                     y_long_ref, y_glob_ref, dx_ref, dxb_ref, du_ref, dh_ref, gn_ref, y_ref):
    model_dim = h_ref.shape[1]
    gain, offset = norm_ref[2:3], norm_ref[3:4]
    gn_ref[...] = jnp.zeros_like(gn_ref)

    def norm(rows):
        out = h_ref[rows, :] + (down_ref[rows, :].astype(F32) + got_ref[rows, :].astype(F32))
        normed, rate = norm_parts(out)
        y_ref[rows, :] = normed * gain + offset
        grad = dy_ref[rows, :].astype(F32)
        gn_ref[0:1] += jnp.sum(grad * normed, axis=0, keepdims=True)
        gn_ref[1:2] += jnp.sum(grad, axis=0, keepdims=True)
        dx = norm_back(grad, normed, rate, gain)
        dx_ref[rows, :] = dx
        dxb_ref[rows, :] = dx.astype(BF)

    row_loop(h_ref.shape[0], norm)
    long_part, glob_part = own_rows(y_ref, half_ref[0], *dims[:3])
    for seq in range(dims[0]):
        y_long_ref[seq] = long_part[seq].astype(BF)
        y_glob_ref[seq] = glob_part[seq].astype(BF)

    def act(j):
        here = pl.ds(pl.multiple_of(j * 256, 256), 256)
        da = dot_on(dxb_ref[...], wd_ref[here, :], 1, 1)
        u = u_ref[:, here]
        square, curve = gelu_parts(u)
        slope = 0.5 * (1.0 + curve) + 0.5 * u * (1.0 - curve * curve) * (
            GELU_RATE * (1.0 + 3.0 * GELU_CUBE * square)
        )
        du_ref[:, here] = (da * slope).astype(BF)

    col_loop(u_ref.shape[1], act)
    halves = u_ref.shape[1] // model_dim

    def lower(j):
        cols = pl.ds(pl.multiple_of(j * 256, 256), 256)
        total = 0.0
        for half in range(halves):
            rows = pl.ds(pl.multiple_of(half * model_dim + j * 256, 256), 256)
            total = total + dot_on(
                du_ref[:, half * model_dim : (half + 1) * model_dim], wu_ref[rows, :], 1, 1
            )
        dh_ref[:, cols] = total.astype(BF)

    col_loop(model_dim, lower)


def send_tiles(stage_ref, row, rows, first, place_ref, out_ref, sem):
    cols = stage_ref.shape[1] // LANES
    for r in range(rows):
        for c in range(cols):
            pltpu.make_async_copy(
                stage_ref.at[pl.ds(row + r * LANES, LANES), pl.ds(c * LANES, LANES)],
                out_ref.at[pl.ds(pl.multiple_of(place_ref[first + r * cols + c], 16), LANES)],
                sem,
            ).start()


def feed_grads_kernel(tiles_at, place_ref, a_ref, dxb_ref, hb_ref, du_ref, out_ref, down_stage, up_stage, sems):
    up_at, down_at = tiles_at
    model_dim = dxb_ref.shape[1]

    def down(j):
        row = pl.multiple_of(j * 256, 256)
        rows = pl.ds(row, 256)
        down_stage[rows, :] = dot_on(a_ref[:, rows], dxb_ref[...], 0, 0).astype(BF)
        send_tiles(down_stage, row, 2, down_at + j * 2 * (model_dim // LANES), place_ref, out_ref, sems.at[0])

    col_loop(a_ref.shape[1], down)

    def up(j):
        row = pl.multiple_of(j * 256, 256)
        rows = pl.ds(row, 256)
        up_stage[rows, :] = dot_on(hb_ref[:, rows], du_ref[...], 0, 0).astype(BF)
        send_tiles(
            up_stage, row, 2, up_at + j * 2 * (du_ref.shape[1] // LANES), place_ref, out_ref, sems.at[1]
        )

    col_loop(model_dim, up)
    pltpu.make_async_copy(down_stage, down_stage, sems.at[0]).wait()
    pltpu.make_async_copy(up_stage, up_stage, sems.at[1]).wait()


def attend_back_kernel(dims, blocks, attn_tiles, tile_counts, glob_at_rows, block_ref, place_ref, norm_two_ref, xr_ref, part_ref, got_ref, dh_ref, dh_got_ref, dx_ref, o_ref,
                       q_ref, k_ref, v_ref, xe_ref, wo_ref, rel_ref, gbias_ref, norm_ref, grads_in,
                       grads_ref, dq_ref, dkv_ref, mid_ref, small_ref,
                       do_ref, midb_ref, dkv_acc, out_stage, q_stage, k_stage, v_stage, none_ref,
                       drel_ref, norms_ref, gn_ref, glob_stage, glob_low, sems):
    seqs, block_len, glob_block, ext, width, globs, scale = dims
    head_cols = q_ref.shape[1]
    pairs = head_cols // LANES
    glob_at = seqs * block_len
    glob_rows = q_ref.shape[0] - glob_at
    span = ext + globs
    chunks = block_len // LANES
    gain = norm_ref[0:1]
    gn_ref[...] = jnp.zeros_like(gn_ref)

    def norm(rows):
        mid = xr_ref[rows, :].astype(F32) + (part_ref[rows, :].astype(F32) + got_ref[rows, :].astype(F32))
        normed, rate = norm_parts(mid)
        grad = dh_ref[rows, :].astype(F32) + dh_got_ref[rows, :].astype(F32) + dx_ref[rows, :]
        gn_ref[0:1] += jnp.sum(grad * normed, axis=0, keepdims=True)
        gn_ref[1:2] += jnp.sum(grad, axis=0, keepdims=True)
        out = norm_back(grad, normed, rate, gain)
        mid_ref[rows, :] = out
        midb_ref[rows, :] = out.astype(BF)

    row_loop(xr_ref.shape[0], norm)
    do_ref[...] = dot_on(midb_ref[...], wo_ref[...], 1, 1).astype(BF)
    out_stage[...] = dot_on(o_ref[...], midb_ref[...], 0, 0).astype(BF)
    send_tiles(out_stage, 0, out_stage.shape[0] // LANES, 3 * attn_tiles, place_ref, grads_ref, sems.at[0])
    none_ref[...] = jnp.zeros_like(none_ref)
    spare = []
    for tile in range(*tile_counts):
        target = grads_ref.at[pl.ds(pl.multiple_of(place_ref[tile], 16), LANES)]
        spare.append(pltpu.make_async_copy(none_ref, target, sems.at[4]))
        spare[-1].start()
    dkv_acc[...] = jnp.zeros_like(dkv_acc)
    drel_ref[...] = jnp.zeros_like(drel_ref)

    def grads_of(scores, grad_out, values):
        weights = softmax_rows(scores)
        dp = dot_on(grad_out, values, 1, 1)
        delta = jnp.sum(weights * dp, axis=-1, keepdims=True)
        return weights.astype(BF), weights * (dp - delta)

    def window(i, carry):
        seq, chunk = i // chunks, i % chunks
        rows = pl.ds(pl.multiple_of(i * LANES, LANES), LANES)
        base = pl.multiple_of(seq * span, LANES)
        at = pl.multiple_of(chunk * LANES, LANES)
        near_rows = pl.ds(base + at, width)
        far_rows = pl.ds(base + ext, globs)
        bias = window_bias(block_ref[0], blocks, chunk, dims)
        near = lax.broadcasted_iota(jnp.int32, bias.shape, 1) < width
        for pair in range(pairs):
            cols = slice(pair * LANES, (pair + 1) * LANES)
            query = stack_heads(q_ref[rows, cols] * scale)
            grad_out = stack_heads(do_ref[rows, cols])
            keys = window_keys(k_ref, base, at, width, ext, globs, cols)
            values = window_keys(v_ref, base, at, width, ext, globs, cols)
            labels = rel_ref[:, cols]
            scores = dot_on(query, keys, 1, 1)
            scores = scores + skew(dot_on(query, labels, 1, 1), width + globs) + bias
            weights, ds = grads_of(scores, grad_out, values)
            dsb = ds.astype(BF)
            by_label = unskew(jnp.where(near, dsb.astype(F32), 0.0), LABEL_PAD).astype(BF)
            dv = dot_on(weights, grad_out, 0, 0)
            dk = dot_on(dsb, query, 0, 0)
            dq = dot_on(dsb, keys, 1, 0) + dot_on(by_label, labels, 1, 0)
            dq_ref[rows, cols] = (merge_stack(dq) * scale).astype(BF)
            drel_ref[:, cols] += dot_on(by_label, query, 0, 0)
            dkv_acc[pair, near_rows] += dk[:width]
            dkv_acc[pair, far_rows] += dk[width:]
            dkv_acc[pairs + pair, near_rows] += dv[:width]
            dkv_acc[pairs + pair, far_rows] += dv[width:]
        return carry

    lax.fori_loop(0, seqs * chunks, window, 0)
    rows = slice(glob_at, glob_at + glob_rows)
    for pair in range(pairs):
        cols = slice(pair * LANES, (pair + 1) * LANES)
        query = stack_heads(q_ref[rows, cols] * scale)
        grad_out = stack_heads(do_ref[rows, cols])
        total = jnp.zeros((2 * glob_rows, LANES), F32)
        for seq in range(seqs):
            span_rows = slice(seq * span, (seq + 1) * span)
            bias = gbias_ref[seq]
            keys = k_ref[span_rows, cols]
            scores = dot_on(query, keys, 1, 1) + jnp.concatenate([bias, bias], axis=0)
            weights, ds = grads_of(scores, grad_out, v_ref[span_rows, cols])
            own = glob_row_mask(ds.shape, seq, glob_block)
            weights = jnp.where(own, weights.astype(F32), 0.0).astype(BF)
            dsb = jnp.where(own, ds, 0.0).astype(BF)
            dkv_acc[pair, span_rows] += dot_on(dsb, query, 0, 0)
            dkv_acc[pairs + pair, span_rows] += dot_on(weights, grad_out, 0, 0)
            total = total + dot_on(dsb, keys, 1, 0)
        dq_ref[rows, cols] = (merge_stack(total) * scale).astype(BF)
    first_row, row_step, cells, per_block = glob_at_rows
    for seq in range(seqs):
        for r in range(per_block):
            source = pl.ds(seq * span + ext + r * blocks, blocks)
            for c in range(2 * pairs):
                rows = pl.ds((seq * per_block + r) * 2 * pairs + c, blocks, stride=cells)
                glob_stage[rows, :] = dkv_acc[c, source, :]
    glob_low[...] = glob_stage[...].astype(BF)
    for i in range(blocks):
        pltpu.make_async_copy(
            glob_low.at[pl.ds(i * cells, cells)],
            grads_ref.at[pl.ds(first_row + (i + 1) * row_step - cells, cells)],
            sems.at[5],
        ).start()
    norms_ref[...] = jnp.zeros_like(norms_ref)
    for row, source in enumerate((gn_ref, gn_ref, norm_two_ref, norm_two_ref)):
        for half in range(source.shape[1] // head_cols):
            at = row * (source.shape[1] // head_cols) + half
            norms_ref[at : at + 1] = source[row % 2 : row % 2 + 1, half * head_cols : (half + 1) * head_cols]
    small_ref[...] = jnp.concatenate([drel_ref[: SMALL_ROWS - 8], norms_ref[...]], axis=0).astype(BF)
    for c in range(2 * pairs):
        dkv_ref[:, c * LANES : (c + 1) * LANES] = dkv_acc[c].astype(BF)
    for at, stage in ((0, q_stage), (1, k_stage), (2, v_stage)):
        rows_ref = xr_ref if at == 0 else xe_ref
        grad = dq_ref[...] if at == 0 else dkv_ref[:, (at - 1) * head_cols : at * head_cols]

        def cut(j):
            row = pl.multiple_of(j * 256, 256)
            stage[pl.ds(row, 256), :] = dot_on(rows_ref[:, pl.ds(row, 256)], grad, 0, 0).astype(BF)
            send_tiles(
                stage, row, 2, at * attn_tiles + j * 2 * (head_cols // LANES), place_ref, grads_ref, sems.at[1 + at]
            )

        col_loop(stage.shape[0], cut)
    for at, stage in enumerate((out_stage, q_stage, k_stage, v_stage)):
        pltpu.make_async_copy(stage, stage, sems.at[at]).wait()
    for copy in spare:
        copy.wait()
    pltpu.make_async_copy(glob_low, glob_low, sems.at[5]).wait()


def start_weights(wall_ref, at, head_cols, wqk_ref, wv_ref, sems):
    model_dim = wqk_ref.shape[0]
    copies = [
        pltpu.make_async_copy(wall_ref.at[pl.ds(at[0], model_dim)], wqk_ref, sems.at[0]),
        pltpu.make_async_copy(
            wall_ref.at[pl.ds(at[1], model_dim), pl.ds(0, head_cols)], wv_ref, sems.at[1]
        ),
    ]
    for copy in copies:
        copy.start()
    return copies


def back_rows(proj, wqk_ref, wv_ref):
    both = wqk_ref.shape[1]
    return dot_on(proj[:, :both], wqk_ref[...], 1, 1) + dot_on(proj[:, both:], wv_ref[...], 1, 1)


def dx_kernel(dims, at, half_ref, dq_ref, dkv_ref, next_ref, last_ref, mid_ref, wall_ref,
              keep_ref, send_ref, proj_ref, wqk_ref, wv_ref, sems):
    seqs, block_len, _, ext, _, globs, _ = dims
    head_cols = dq_ref.shape[1]
    copies = start_weights(wall_ref, at, head_cols, wqk_ref, wv_ref, sems)
    proj_ref[:, :head_cols] = dq_ref[: seqs * block_len]
    for seq in range(seqs):
        base, row = seq * (ext + globs) + RIM, seq * block_len
        middle = block_len - 2 * RIM
        own = dkv_ref[base : base + block_len].astype(F32)
        sums = [
            own[:RIM] + last_ref[seq * RIM : (seq + 1) * RIM].astype(F32),
            own[RIM : RIM + middle],
            own[RIM + middle :] + next_ref[seq * RIM : (seq + 1) * RIM].astype(F32),
        ]
        proj_ref[row : row + block_len, head_cols:] = jnp.concatenate(sums, axis=0).astype(BF)
    for copy in copies:
        copy.wait()
    per = block_len // 2
    for out_ref, half in ((keep_ref, half_ref[0]), (send_ref, 1 - half_ref[0])):
        for seq in range(seqs):
            rows = pl.ds(pl.multiple_of(seq * block_len + half * per, per), per)
            total = back_rows(proj_ref[rows, :], wqk_ref, wv_ref)
            if out_ref is keep_ref:
                total = total + mid_ref[rows, :]
            out_ref[seq] = total.astype(out_ref.dtype)


def dx_glob_kernel(dims, at, half_ref, dq_ref, kept_ref, got_ref, mid_ref, wall_ref,
                   keep_ref, send_ref, cells_ref, wqk_ref, wv_ref, sems):
    seqs, block_len, glob_block = dims[:3]
    head_cols = dq_ref.shape[1]
    base = seqs * block_len
    used, cols = seqs * glob_block, 2 * head_cols // LANES
    copies = start_weights(wall_ref, at, head_cols, wqk_ref, wv_ref, sems)
    first = kept_ref.shape[0] - used * cols
    cells_ref[...] = kept_ref[first:].astype(F32) + got_ref[first:].astype(F32)
    wide = [cells_ref[pl.ds(c, used, stride=cols), :] for c in range(cols)]
    dkv = jnp.concatenate(wide, axis=1)
    dkv = jnp.concatenate([dkv, jnp.zeros((dq_ref.shape[0] - base - used, 2 * head_cols), F32)], axis=0)
    proj = jnp.concatenate([dq_ref[base:], dkv.astype(BF)], axis=1)
    for copy in copies:
        copy.wait()
    total = back_rows(proj, wqk_ref, wv_ref)
    few = glob_block // 2
    here = half_ref[0] == 0
    for seq in range(seqs):
        start = seq * glob_block
        halves = [total[start : start + few], total[start + few : start + glob_block]]
        mids = [
            mid_ref[base + start : base + start + few, :],
            mid_ref[base + start + few : base + start + glob_block, :],
        ]
        keep_ref[seq] = jnp.where(here, halves[0] + mids[0], halves[1] + mids[1])
        send_ref[seq] = jnp.where(here, halves[1], halves[0]).astype(BF)


def swap_cores(values):
    count = lax.axis_size("ffn")
    return lax.ppermute(values, "ffn", [(i, i ^ 1) for i in range(count)])


def on_device(
    x_long,
    x_glob,
    sentence,
    dy_long,
    dy_glob,
    owner_list,
    w_master,
    m_old,
    v_old,
    left_basis,
    right_basis,
    left_stats,
    right_stats,
    rel_table,
    rel_m,
    rel_v,
    norm_params,
    norm_m,
    norm_v,
):
    ffn_count = lax.axis_size("ffn")
    seq_count = lax.axis_size("seq")
    seqs, tok_half, model_dim = x_long.shape
    glob_half = x_glob.shape[1]
    block_len = tok_half * ffn_count
    glob_block = glob_half * ffn_count
    globs = glob_block * seq_count
    head_cols = model_dim // ffn_count
    hidden = FF // ffn_count
    scale = (model_dim // HEADS) ** (-0.5)
    slots, side = w_master.shape[:2]
    attn_tiles = model_dim * head_cols // (side * side)
    ffn_tiles = model_dim * hidden // (side * side)
    tile_count = 4 * attn_tiles + 2 * ffn_tiles
    slot_count = owner_list.shape[0]
    labels = rel_table.shape[0]
    half_index = lax.axis_index("ffn")
    first_half = half_index == 0
    parts = slot_parts(slots, seq_count)

    glob_cells = seqs * glob_block * model_dim // LANES
    rows_per = part_rows(parts, side, glob_cells)
    places, place_rows = slot_places(owner_list, slots, rows_per, side)
    held = jnp.sum(
        jnp.where(
            places[None, :] == jnp.arange(slot_count, dtype=jnp.int32)[:, None],
            jnp.arange(slot_count, dtype=jnp.int32)[None, :],
            0,
        ),
        axis=1,
    )
    per_row = model_dim // side
    up_rows = hidden // model_dim * model_dim
    qk_at = up_rows + hidden
    v_at = qk_at + model_dim
    out_at = v_at + model_dim
    head_tiles = head_cols // side
    up_tiles = hidden // side

    def tile_row_col(tile):
        kind_qkv = tile // attn_tiles
        inner = tile % attn_tiles
        qkv_row = jnp.where(kind_qkv == 2, v_at, qk_at) + inner // head_tiles * side
        qkv_col = jnp.where(kind_qkv == 1, head_cols, 0) + inner % head_tiles * side
        out_row = out_at + inner // per_row * side
        up = tile - 4 * attn_tiles
        up_col = up % up_tiles * side
        up_row = up_col // model_dim * model_dim + up // up_tiles * side
        down = up - ffn_tiles
        down_row = up_rows + down // per_row * side
        row = jnp.where(
            tile < 3 * attn_tiles,
            qkv_row,
            jnp.where(
                tile < 4 * attn_tiles,
                out_row,
                jnp.where(up < ffn_tiles, up_row, down_row),
            ),
        )
        col = jnp.where(
            tile < 3 * attn_tiles,
            qkv_col,
            jnp.where(
                tile < 4 * attn_tiles,
                inner % per_row * side,
                jnp.where(up < ffn_tiles, up_col % model_dim, down % per_row * side),
            ),
        )
        return row, col

    wall_row, wall_col = tile_row_col(held)
    wall_kind = jnp.where(held < 4 * attn_tiles, 0, jnp.where(held < tile_count, 1, 2))

    mine = jnp.concatenate([x_long, dy_long, x_glob, dy_glob], axis=1)
    other = swap_cores(mine)
    lower = jnp.where(first_half, mine, other)
    upper = jnp.where(first_half, other, mine)

    def block_rows(at, count):
        return jnp.concatenate([lower[:, at : at + count], upper[:, at : at + count]], axis=1)

    long_rows = block_rows(0, tok_half)
    dy_rows = block_rows(tok_half, tok_half)
    glob_rows = block_rows(2 * tok_half, glob_half)
    dy_globs = block_rows(2 * tok_half + glob_half, glob_half)
    used = seqs * (block_len + glob_block)
    row_count = seqs * block_len + up_to(seqs * glob_block, 16)
    pad_rows = jnp.zeros((row_count - used, model_dim), BF)

    def in_rows(long_part, glob_part):
        return jnp.concatenate(
            [long_part.reshape(-1, model_dim), glob_part.reshape(-1, model_dim), pad_rows]
        )

    x_rows = in_rows(long_rows, glob_rows)
    dy_all = in_rows(dy_rows, dy_globs)
    rim = jnp.where(first_half, x_long[:, :RIM], x_long[:, tok_half - RIM :])
    to_next = [(i * ffn_count + 1, (i + 1) * ffn_count + 1) for i in range(seq_count - 1)]
    to_last = [((i + 1) * ffn_count, i * ffn_count) for i in range(seq_count - 1)]
    rim = lax.ppermute(rim, ("seq", "ffn"), to_next + to_last)
    rim_other = swap_cores(rim)
    rim_left = jnp.where(first_half, rim_other, rim).reshape(-1, model_dim)
    rim_right = jnp.where(first_half, rim, rim_other).reshape(-1, model_dim)

    weights_low = w_master.astype(BF)
    glob_other = swap_cores(x_glob)
    glob_own = jnp.concatenate(
        [jnp.where(first_half, x_glob, glob_other), jnp.where(first_half, glob_other, x_glob)], axis=1
    )
    orders = [order for _, _, order in parts]
    gathered = [
        [piece.reshape(-1, many, LANES) for piece in pieces]
        for pieces, many in zip(
            gather_rows(
                weights_low.reshape(-1, LANES), glob_own.reshape(-1, LANES), rows_per, orders
            ),
            rows_per,
        )
    ]
    tiles_per = tuple(last - first for (first, last, _), pieces in zip(parts, gathered) for _ in pieces)
    gathered = [piece for pieces in gathered for piece in pieces]
    reach = 2 * RADIUS
    width = up_to(LANES + 2 * RIM, LANES) if globs % LANES == 0 else up_to(LANES + 2 * RIM + globs, LANES) - globs
    ext = block_len - LANES + width
    span = ext + globs
    rel_low = jnp.pad(
        rel_table.astype(BF), ((RIM - RADIUS, LABEL_PAD - labels - RIM + RADIUS), (0, 0))
    )

    glob_bias_rows = row_count - seqs * block_len
    row_at = jnp.arange(glob_bias_rows, dtype=jnp.int32)[None, :, None]
    seq_at = jnp.arange(seqs, dtype=jnp.int32)[:, None, None]
    spread = jnp.pad(sentence[:, 0], ((0, 0), (RIM, span - RIM - block_len)), constant_values=-1)
    span_at = jnp.arange(span, dtype=jnp.int32)[None, None, :]
    own = (spread[:, None, :] == row_at - seq_at * glob_block) & (spread[:, None, :] >= 0)
    glob_bias = jnp.where(own | (span_at >= ext), 0.0, NEG_FILL).astype(F32)

    spec_up = block_at((up_rows, model_dim), 0, 0)
    spec_down = block_at((hidden, model_dim), 1, 0)
    spec_out = block_at((head_cols, model_dim), out_at // head_cols, 0)

    def rows_of(cols, dtype=BF, rows=row_count):
        return jax.ShapeDtypeStruct((rows, cols), dtype)

    def specs(arrays):
        return [whole(a.shape) for a in arrays]

    dims = (seqs, block_len, glob_block, ext, width, globs, scale)
    fwd_shapes = (
        rows_of(head_cols),
        rows_of(head_cols, rows=seqs * span),
        rows_of(head_cols, rows=seqs * span),
        rows_of(head_cols),
        rows_of(model_dim),
        rows_of(model_dim, rows=seqs * span),
    )
    wall_at = (
        2 * ffn_tiles // per_row * side,
        4 * attn_tiles // per_row * side,
        qk_at,
        v_at,
        out_at,
        tiles_per,
    )
    wall_shape = jax.ShapeDtypeStruct((out_at + head_cols, model_dim), BF)
    block_now = lax.axis_index("seq").astype(jnp.int32).reshape(1)
    ins = [x_rows, rel_low, glob_bias]
    query, keys, values, heads_out, attn_part, x_ext, wall = kernel_call(
        functools.partial(attend_kernel, dims, wall_at, seq_count),
        "attend",
        28,
        fwd_shapes + (wall_shape,),
        [scalars()] * 4 + specs(ins) + [any_space()] * (2 + len(gathered)),
        tuple(specs(fwd_shapes)) + (any_space(),),
        [
            pltpu.VMEM(wall_shape.shape, BF),
            pltpu.VMEM((seq_count * glob_cells, LANES), BF),
            pltpu.VMEM((seq_count * glob_cells, LANES), F32),
            pltpu.SemaphoreType.DMA((5,)),
        ],
        flops=4 * 10**9,
        bytes_moved=10**7,
    )(wall_row, wall_col, wall_kind, block_now, *ins, rim_left, rim_right, *gathered)
    attn_got = swap_cores(attn_part)
    feed_shapes = (
        rows_of(model_dim, F32),
        rows_of(model_dim),
        rows_of(hidden, F32),
        rows_of(hidden),
        rows_of(model_dim),
    )
    norm_one, norm_low, up_pre, act_low, down_part = kernel_call(
        feed_kernel,
        "feed",
        24,
        feed_shapes,
        specs([x_rows, attn_part, attn_got, norm_params]) + [spec_up, spec_down],
        tuple(specs(feed_shapes)),
        flops=3 * 10**9,
        bytes_moved=10**7,
    )(x_rows, attn_part, attn_got, norm_params, wall, wall)
    down_got = swap_cores(down_part)
    norm_shape = jax.ShapeDtypeStruct((8, model_dim), F32)
    half_now = half_index.astype(jnp.int32).reshape(1)
    back_shapes = (
        jax.ShapeDtypeStruct(x_long.shape, BF),
        jax.ShapeDtypeStruct(x_glob.shape, BF),
        rows_of(model_dim, F32),
        rows_of(model_dim),
        rows_of(hidden),
        rows_of(model_dim),
        norm_shape,
    )
    y_long, y_glob, d_pre, d_pre_low, d_up, d_norm_part, norm_two_grad = kernel_call(
        functools.partial(feed_back_kernel, dims),
        "feed_back",
        30,
        back_shapes,
        [scalars()]
        + specs([norm_one, down_part, down_got, up_pre, dy_all, norm_params])
        + [spec_up, spec_down],
        tuple(specs(back_shapes)),
        [pltpu.VMEM((row_count, model_dim), F32)],
        flops=3 * 10**9,
        bytes_moved=10**7,
    )(half_now, norm_one, down_part, down_got, up_pre, dy_all, norm_params, wall, wall)
    d_norm_got = swap_cores(d_norm_part)
    grads_shape = jax.ShapeDtypeStruct((seq_count * sum(rows_per), LANES), BF)
    slot_grads = kernel_call(
        functools.partial(feed_grads_kernel, (4 * attn_tiles, 4 * attn_tiles + ffn_tiles)),
        "feed_grads",
        16,
        grads_shape,
        [scalars()] + specs([act_low, d_pre_low, norm_low, d_up]),
        any_space(),
        [
            pltpu.VMEM((hidden, model_dim), BF),
            pltpu.VMEM((model_dim, hidden), BF),
            pltpu.SemaphoreType.DMA((2,)),
        ],
        flops=3 * 10**9,
        bytes_moved=10**7,
    )(place_rows, act_low, d_pre_low, norm_low, d_up)
    ins = [
        x_rows,
        attn_part,
        attn_got,
        d_norm_part,
        d_norm_got,
        d_pre,
        heads_out,
        query,
        keys,
        values,
        x_ext,
    ]
    last_shapes = (
        grads_shape,
        rows_of(head_cols),
        rows_of(2 * head_cols, rows=seqs * span),
        rows_of(model_dim, F32),
        rows_of(head_cols, rows=SMALL_ROWS),
    )
    slot_grads, d_query, dkv, d_mid, small = kernel_call(
        functools.partial(
            attend_back_kernel,
            dims,
            seq_count,
            attn_tiles,
            (tile_count, slot_count),
            (seq_count * sum(rows_per[:-1]), rows_per[-1], glob_cells, glob_block),
        ),
        "attend_back",
        32,
        last_shapes,
        [scalars(), scalars(), whole(norm_shape.shape)]
        + specs(ins)
        + [spec_out]
        + specs([rel_low, glob_bias, norm_params])
        + [any_space()],
        (any_space(),) + tuple(specs(last_shapes[1:])),
        [
            pltpu.VMEM((row_count, head_cols), BF),
            pltpu.VMEM((row_count, model_dim), BF),
            pltpu.VMEM((2 * head_cols // LANES, seqs * span, LANES), F32),
            pltpu.VMEM((head_cols, model_dim), BF),
            pltpu.VMEM((model_dim, head_cols), BF),
            pltpu.VMEM((model_dim, head_cols), BF),
            pltpu.VMEM((model_dim, head_cols), BF),
            pltpu.VMEM((side, side), BF),
            pltpu.VMEM((LABEL_PAD, head_cols), F32),
            pltpu.VMEM((8, head_cols), F32),
            pltpu.VMEM((8, model_dim), F32),
            pltpu.VMEM((seq_count * glob_cells, LANES), F32),
            pltpu.VMEM((seq_count * glob_cells, LANES), BF),
            pltpu.SemaphoreType.DMA((6,)),
        ],
        {3 + len(ins) + 4: 0},
        flops=8 * 10**9,
        bytes_moved=2 * 10**7,
    )(block_now, place_rows, norm_two_grad, *ins, wall, rel_low, glob_bias, norm_params, slot_grads)

    bits = seq_bits(seq_count)
    carried = [
        [(RIM, (dkv, seq * span + at)) for seq in range(seqs)] for at in (0, RIM + block_len)
    ]
    sums, small, (to_last, to_next) = scatter_rows(
        slot_grads, rows_per, orders, small, bits[3:] + bits[:3], carried
    )
    from_next = lax.ppermute(to_last, "seq", [(i + 1, i) for i in range(seq_count - 1)])
    from_last = lax.ppermute(to_next, "seq", [(i, i + 1) for i in range(seq_count - 1)])

    weights_at = (qk_at, v_at)
    weights_held = [
        pltpu.VMEM((model_dim, model_dim), BF),
        pltpu.VMEM((model_dim, head_cols), BF),
        pltpu.SemaphoreType.DMA((2,)),
    ]
    dx_shapes = (
        jax.ShapeDtypeStruct(x_long.shape, F32),
        jax.ShapeDtypeStruct(x_long.shape, BF),
    )
    ins = [d_query, dkv, from_next, from_last, d_mid]
    dx_kept, dx_sent = kernel_call(
        functools.partial(dx_kernel, dims, weights_at),
        "dx_long",
        20,
        dx_shapes,
        [scalars()] + specs(ins) + [any_space()],
        tuple(specs(dx_shapes)),
        [pltpu.VMEM((seqs * block_len, 3 * head_cols), BF)] + weights_held,
        flops=10**9,
        bytes_moved=10**7,
    )(half_now, *ins, wall)
    dx_long = dx_kept + swap_cores(dx_sent).astype(F32)
    glob_shapes = (
        jax.ShapeDtypeStruct(x_glob.shape, F32),
        jax.ShapeDtypeStruct(x_glob.shape, BF),
    )
    ins = [d_query, sums[0], sums[1], d_mid]
    dx_kept, dx_sent = kernel_call(
        functools.partial(dx_glob_kernel, dims, weights_at),
        "dx_glob",
        12,
        glob_shapes,
        [scalars()] + specs(ins) + [any_space()],
        tuple(specs(glob_shapes)),
        [pltpu.VMEM((glob_cells, LANES), F32)] + weights_held,
        flops=10**8,
        bytes_moved=10**6,
    )(half_now, *ins, wall)
    dx_glob = dx_kept + swap_cores(dx_sent).astype(F32)

    state = (w_master, m_old, v_old, left_basis, right_basis, left_stats, right_stats)
    others = (rel_table, rel_m, rel_v, norm_params, norm_m, norm_v)
    new_state = soap_update(sums, small, state, others)
    w_new, m_new, v_new, left_q, right_q, left_s, right_s = new_state[:7]
    rel_new, rel_m_new, rel_v_new, norm_new, norm_m_new, norm_v_new = new_state[7:]
    return (
        y_long,
        y_glob,
        dx_long,
        dx_glob,
        w_new,
        m_new,
        v_new,
        left_q,
        right_q,
        left_s,
        right_s,
        rel_new,
        rel_m_new,
        rel_v_new,
        norm_new,
        norm_m_new,
        norm_v_new,
    )


def solution(mesh):
    in_specs = (
        P(None, ("seq", "ffn"), None),
        P(None, ("seq", "ffn"), None),
        P(None, "seq", None),
        P(None, ("seq", "ffn"), None),
        P(None, ("seq", "ffn"), None),
        P(),
        P(("seq", "ffn"), None, None),
        P(("seq", "ffn"), None, None),
        P(("seq", "ffn"), None, None),
        P(("seq", "ffn"), None, None),
        P(("seq", "ffn"), None, None),
        P(("seq", "ffn"), None, None),
        P(("seq", "ffn"), None, None),
        P(None, "ffn"),
        P(None, "ffn"),
        P(None, "ffn"),
        P(),
        P(),
        P(),
    )
    out_specs = (
        P(None, ("seq", "ffn"), None),
        P(None, ("seq", "ffn"), None),
        P(None, ("seq", "ffn"), None),
        P(None, ("seq", "ffn"), None),
        P(("seq", "ffn"), None, None),
        P(("seq", "ffn"), None, None),
        P(("seq", "ffn"), None, None),
        P(("seq", "ffn"), None, None),
        P(("seq", "ffn"), None, None),
        P(("seq", "ffn"), None, None),
        P(("seq", "ffn"), None, None),
        P(None, "ffn"),
        P(None, "ffn"),
        P(None, "ffn"),
        P(),
        P(),
        P(),
    )
    return jax.shard_map(
        on_device, mesh=mesh, in_specs=in_specs, out_specs=out_specs, check_vma=False
    )
```

```python
import functools
import math

import jax
import jax.numpy as jnp
from jax import lax
from jax.experimental import pallas as pl
from jax.experimental.pallas import tpu as pltpu
from jax.sharding import PartitionSpec as P

HEADS = 12
FF = 3072
RADIUS = 84
STEP = 10

BETA_ONE = 0.9
BETA_TWO = 0.95
LEARN_RATE = 0.02
ADAM_RATE = 0.6
WEIGHT_DECAY = 0.01
ADAM_EPS = 1e-08
NORM_EPS = 1e-12
NEG_FILL = -1e30
BF = jnp.bfloat16
F32 = jnp.float32


def seq_bits(count):
    return [1 << at for at in range(count.bit_length() - 1)]


def swap_with(values, bit):
    count = lax.axis_size("seq")
    return lax.ppermute(values, "seq", [(i, i ^ bit) for i in range(count)])


def slot_parts(slots, count):
    bits = seq_bits(count)
    low, high = bits[:3], bits[3:]
    cuts = [slots * at // 14 for at in (0, 5, 10, 14)]
    orders = [low[at:] + low[:at] + high for at in range(3)]
    return [(a, b, order) for a, b, order in zip(cuts, cuts[1:], orders) if b > a]


def part_rows(parts, side, extra):
    rows = [(last - first) * side for first, last, _ in parts]
    return rows[:-1] + [rows[-1] + extra]


def slot_places(owners, slots, rows, side):
    count = lax.axis_size("seq")
    apart = (owners // slots) ^ lax.axis_index("seq")
    inner = owners % slots
    place, row, base = jnp.zeros_like(owners), jnp.zeros_like(owners), 0
    for (first, last, order), many in zip(slot_parts(slots, count), rows):
        index = jnp.zeros_like(owners)
        for at, bit in enumerate(order):
            index = index + jnp.where((apart & bit) != 0, count >> (at + 1), 0)
        here = (inner >= first) & (inner < last)
        place = jnp.where(here, first * count + index * (last - first) + inner - first, place)
        row = jnp.where(here, base + index * many + (inner - first) * side, row)
        base += many * count
    return place, row


FAR_SIZE = 3 * 2**20


def move_kernel(plan, arrays, *refs):
    ins, outs, held, sems = refs[:arrays], refs[arrays : arrays + len(plan)], refs[arrays + len(plan) : -1], refs[-1]
    copies, sums, sem = [], [], 0
    for out, runs in zip(outs, plan):
        base = 0
        for rows, *terms in runs:
            here = out.at[pl.ds(base, rows)]
            targets = [here] if len(terms) == 1 else [held[len(sums) * 2 + k] for k in range(2)]
            waits = []
            for (at, start), target in zip(terms, targets):
                waits.append(pltpu.make_async_copy(ins[at].at[pl.ds(start, rows)], target, sems.at[sem]))
                waits[-1].start()
                sem += 1
            if len(terms) == 1:
                copies += waits
            else:
                sums.append((waits, targets, out, base, rows))
            base += rows
    for waits, (one, two), out, base, rows in sums:
        for wait in waits:
            wait.wait()
        step = next(s for s in (128, 64, 48, 32, 16) if rows % s == 0)

        def add(i, carry):
            at = pl.multiple_of(i * step, 16)
            total = one[pl.ds(at, step), :].astype(F32) + two[pl.ds(at, step), :].astype(F32)
            out[pl.ds(base + at, step), :] = total.astype(BF)
            return carry

        lax.fori_loop(0, rows // step, add, 0)
    for copy in copies:
        copy.wait()


def move_rows(outputs):
    arrays, plan, scratch, count = [], [], [], 0
    for runs in outputs:
        plan.append([])
        for rows, *terms in runs:
            places = []
            for array, start in terms:
                found = [i for i, other in enumerate(arrays) if other is array]
                if not found:
                    arrays.append(array)
                places.append((found[0] if found else len(arrays) - 1, start))
                count += 1
            plan[-1].append((rows, *places))
            if len(terms) == 2:
                scratch += [pltpu.VMEM((rows, terms[0][0].shape[1]), BF)] * 2
    shapes = [(sum(run[0] for run in runs), runs[0][1][0].shape[1]) for runs in outputs]
    return pl.pallas_call(
        functools.partial(move_kernel, plan, len(arrays)),
        grid=(1,),
        out_shape=tuple(jax.ShapeDtypeStruct(shape, BF) for shape in shapes),
        in_specs=[
            pl.BlockSpec(memory_space=pltpu.HBM if array.size > FAR_SIZE else pl.ANY) for array in arrays
        ],
        out_specs=tuple(whole(shape) for shape in shapes),
        scratch_shapes=scratch + [pltpu.SemaphoreType.DMA((count,))],
        cost_estimate=pl.CostEstimate(
            flops=0, bytes_accessed=sum(6 * math.prod(s) for s in shapes), transcendentals=0
        ),
        compiler_params=pltpu.CompilerParams(vmem_limit_bytes=16 * 2**20),
        name="add_rows" if scratch else "join_rows",
    )(*arrays)


def run_sum(rows, one, one_at, two, two_at):
    return (rows, (one, one_at), (two, two_at))


def gather_rows(cells, extra, rows, orders):
    own = sum(rows)
    shared = orders[0][3:][::-1]
    got = [swap_with(values, shared[0]) for values in (cells, extra)]
    devices = [[(cells, 0), (extra, -cells.shape[0])], [(got[0], 0), (got[1], -cells.shape[0])]]
    if len(shared) > 1:
        (cells,) = move_rows([[(array.shape[0], (array, 0)) for runs in devices for array, _ in runs]])
        for bit in shared[1:-1]:
            got = swap_with(cells, bit)
            (cells,) = move_rows([[(cells.shape[0], (cells, 0)), (cells.shape[0], (got, 0))]])
        got = swap_with(cells, shared[-1])
        devices = [[(run, i * own)] for run in (cells, got) for i in range(cells.shape[0] // own)]
    starts = [sum(rows[:at]) for at in range(len(rows))]

    def runs_of(start, many):
        runs = []
        for pieces in devices:
            left, at = many, start
            for array, shift in pieces:
                here = min(left, array.shape[0] - (at + shift))
                if here > 0:
                    runs.append((here, (array, at + shift)))
                    left, at = left - here, at + here
        return runs

    parts = move_rows([runs_of(start, many) for start, many in zip(starts, rows)])
    for step in (2, 1):
        got = [swap_with(part, order[step]) for part, order in zip(parts, orders)]
        parts = move_rows([[(p.shape[0], (p, 0)), (p.shape[0], (g, 0))] for p, g in zip(parts, got)])
    got = [swap_with(part, order[0]) for part, order in zip(parts, orders)]
    return list(zip(parts, got))


def scatter_rows(cells, rows, orders, everywhere, order_everywhere, carried):
    count = lax.axis_size("seq")
    spans = [count * many for many in rows]
    starts = [sum(spans[:at]) for at in range(len(spans))]
    sends = [cells[a + r // 2 : a + r] for a, r in zip(starts, spans)]
    kept = move_rows([[(r // 2, (cells, a))] for a, r in zip(starts, spans)])
    kept = [(keep, 0, keep.shape[0]) for keep in kept]

    def all_sum():
        return [run_sum(everywhere.shape[0], everywhere, 0, all_got, 0)]

    for step in range(3):
        got = [swap_with(send, order[step]) for send, order in zip(sends, orders)]
        all_got = swap_with(everywhere, order_everywhere[step])
        halves = [r // 2 for _, _, r in kept]
        if step < 2:
            *sends, everywhere = move_rows(
                [[run_sum(h, k, a + h, g, h)] for h, (k, a, _), g in zip(halves, kept, got)] + [all_sum()]
            )
            keeps = move_rows([[run_sum(h, k, a, g, 0)] for h, (k, a, _), g in zip(halves, kept, got)])
            kept = [(keep, 0, h) for keep, h in zip(keeps, halves)]
    devices = count // 8

    def merged(at, many):
        return [
            run_sum(r, k, i * r, g, i * r)
            for i in range(at, at + many)
            for r, (k, _, _), g in zip(rows, kept, got)
        ]

    half = devices // 2
    send, everywhere, *carried = move_rows([merged(half, half), all_sum()] + carried)
    (keep,) = move_rows([merged(0, half)])
    for step, bit in enumerate(orders[0][3:]):
        got_all = swap_with(send, bit)
        all_got = swap_with(everywhere, order_everywhere[3 + step])
        if bit == orders[0][-1]:
            return (keep, got_all), (everywhere, all_got), carried
        half = keep.shape[0] // 2
        send, everywhere = move_rows([[run_sum(half, keep, half, got_all, half)], all_sum()])
        (keep,) = move_rows([[run_sum(half, keep, 0, got_all, 0)]])
    return None


def split_two(x):
    hi = x.astype(BF)
    return hi, (x - hi.astype(F32)).astype(BF)


def split_three(x):
    hi = x.astype(BF)
    rest = x - hi.astype(F32)
    mid = rest.astype(BF)
    return hi, mid, (rest - mid.astype(F32)).astype(BF)


def left_six(parts, axis):
    h, m, l = parts
    return jnp.concatenate([h, h, m, m, h, l], axis=axis)


def right_six(parts, axis):
    h, m, l = parts
    return jnp.concatenate([h, m, h, m, l, h], axis=axis)


def left_three(parts, axis):
    h, l = parts
    return jnp.concatenate([h, h, l], axis=axis)


def right_three(parts, axis):
    h, l = parts
    return jnp.concatenate([h, l, h], axis=axis)


def dot_on(a, b, ca, cb):
    return lax.dot_general(a, b, (((ca,), (cb,)), ((), ())), preferred_element_type=F32)


def dot_six(a, b, ca, cb):
    return dot_on(left_six(split_three(a), ca), right_six(split_three(b), cb), ca, cb)


def dot_one(a, b, ca, cb):
    return dot_on(a.astype(BF), b.astype(BF), ca, cb)


def dot_three(a, b, ca, cb):
    return dot_on(left_three(split_two(a), ca), right_three(split_two(b), cb), ca, cb)


PANEL = 32


def panel_inverse(a_ref, t_ref, npad, side, at):
    groups = PANEL // 8
    iota = lax.broadcasted_iota(jnp.int32, (8, npad), 0)
    a = []
    for i in range(PANEL):
        rows = a_ref[pl.ds(at + i, npad, stride=side), :]
        cols = rows.T[at : at + PANEL]
        a.append([cols[8 * g : 8 * g + 8] for g in range(groups)])
    z = [[None] * groups for _ in range(PANEL)]
    for j in range(PANEL):
        gj, sj = divmod(j, 8)
        r = lax.rsqrt(a[j][gj][sj : sj + 1])
        u = [None if g < gj else a[j][g] * r for g in range(groups)]
        below = list(u)
        below[gj] = jnp.where(iota > sj, u[gj], 0.0)
        for k in range(j + 1, PANEL):
            gk, sk = divmod(k, 8)
            row = u[gk][sk : sk + 1]
            for g in range(gk, groups):
                a[k][g] = a[k][g] - u[g] * row
        for c in range(j):
            row = z[c][gj][sj : sj + 1] * r
            z[c][gj] = jnp.where(iota == sj, row, z[c][gj]) - below[gj] * row
            for g in range(gj + 1, groups):
                z[c][g] = z[c][g] - u[g] * row
        z[j] = [
            jnp.zeros((8, npad), F32)
            if g < gj
            else (jnp.where(iota == sj, r, 0.0) - below[g] * r if g == gj else -u[g] * r)
            for g in range(groups)
        ]
    fill = jnp.zeros((side - PANEL, npad), F32)
    for c in range(PANEL):
        t_ref[pl.ds(c, npad, stride=PANEL), :] = jnp.concatenate(z[c] + [fill], axis=0).T


def adam_step(grad, refs, outs, where, decay_rate):
    param, first_mom, second_mom = [ref[where] for ref in refs]
    first_mom = BETA_ONE * first_mom + (1.0 - BETA_ONE) * grad
    second_mom = BETA_TWO * second_mom + (1.0 - BETA_TWO) * grad * grad
    direction = (
        first_mom
        / (1.0 - BETA_ONE**STEP)
        / (jnp.sqrt(second_mom / (1.0 - BETA_TWO**STEP)) + ADAM_EPS)
    )
    outs[0][where] = param - ADAM_RATE * (direction + decay_rate * param)
    outs[1][where] = first_mom
    outs[2][where] = second_mom


def small_updates(small_refs, refs, outs):
    total = small_refs[0][...].astype(F32) + small_refs[1][...].astype(F32)
    labels, cols = refs[0].shape
    rel = pltpu.roll(total, total.shape[0] - (RIM - RADIUS), 0)[:labels]
    adam_step(rel, refs[:3], outs[:3], (slice(None), slice(None)), WEIGHT_DECAY)
    halves = refs[3].shape[1] // cols
    for row in range(refs[3].shape[0]):
        for half in range(halves):
            at = SMALL_ROWS - 8 + row * halves + half
            where = (slice(row, row + 1), slice(half * cols, (half + 1) * cols))
            adam_step(total[at : at + 1], refs[3:], outs[3:], where, 0.0)


def soap_kernel(npad, kept_ref, got_ref, small_ref, small_got_ref, *refs):
    state, done = refs[:7], refs[13:20]
    given, a_ref, y_ref, mat_ref, t_ref, out_sems = refs[26:]
    n, side = state[0].shape[:2]
    many = next(k for k in (7, 2, 1) if n % k == 0)
    batch = next(b for b in (14, 7, 4, 2) if 2 * n % b == 0)
    small_updates((small_ref, small_got_ref), refs[7:13], refs[20:26])
    eye = (
        lax.broadcasted_iota(jnp.int32, (side, side), 0)
        == lax.broadcasted_iota(jnp.int32, (side, side), 1)
    ).astype(F32)

    def first(at, carry):
        slots = [at * many + k for k in range(many)]

        def old(kind):
            return [state[kind][i] for i in slots]

        lefts, rights = old(3), old(4)
        tiles = [pl.ds(pl.multiple_of(i * side, side), side) for i in slots]
        grads = [kept_ref[rows, :].astype(F32) + got_ref[rows, :].astype(F32) for rows in tiles]
        halves = [split_two(x) for x in grads]
        new_l = [
            BETA_TWO * x + (1.0 - BETA_TWO) * dot_on(left_three(p, 1), right_three(p, 1), 1, 1)
            for x, p in zip(old(5), halves)
        ]
        new_r = [
            BETA_TWO * x + (1.0 - BETA_TWO) * dot_on(left_three(p, 0), right_three(p, 0), 0, 0)
            for x, p in zip(old(6), halves)
        ]
        mats = [dot_six(x, y, 1, 0) for x, y in zip(new_l + new_r, lefts + rights)]
        thirds = [split_three(x) for x in mats]
        grams = [dot_on(left_six(p, 0), right_six(p, 0), 0, 0) for p in thirds]
        turned = [dot_one(x, y, 0, 0) for x, y in zip(lefts, grads)]
        rotated = [dot_one(x, y, 1, 0) for x, y in zip(turned, rights)]
        moms = [BETA_ONE * old_m + (1.0 - BETA_ONE) * x for old_m, x in zip(old(1), rotated)]
        secs = [BETA_TWO * old_v + (1.0 - BETA_TWO) * x * x for old_v, x in zip(old(2), rotated)]
        steps = [
            x / (1.0 - BETA_ONE**STEP) / (jnp.sqrt(y / (1.0 - BETA_TWO**STEP)) + ADAM_EPS)
            for x, y in zip(moms, secs)
        ]
        turned = [dot_one(x, y, 1, 0) for x, y in zip(lefts, steps)]
        backs = [dot_one(x, y, 1, 1) for x, y in zip(turned, rights)]
        weights = old(0)
        for k, i in enumerate(slots):
            given[0, i] = weights[k] - LEARN_RATE * (backs[k] + WEIGHT_DECAY * weights[k])
            given[1, i] = moms[k]
            given[2, i] = secs[k]
            given[5, i] = new_l[k]
            given[6, i] = new_r[k]
            for kind in range(2):
                mat_ref[2 * i + kind] = mats[kind * many + k]
                rows = pl.ds(pl.multiple_of((2 * i + kind) * side, side), side)
                a_ref[rows, :] = grams[kind * many + k]
                y_ref[rows, :] = eye
        return carry

    def send(kinds):
        copies = [pltpu.make_async_copy(given.at[k], done[k], out_sems.at[k]) for k in kinds]
        for copy in copies:
            copy.start()
        return copies

    lax.fori_loop(0, n // many, first, 0)
    copies = send((0, 1, 2, 5, 6))
    if npad > 2 * n:
        a_ref[2 * n * side :, :] = jnp.concatenate([eye] * (npad - 2 * n), axis=0)
    for at in range(0, side, PANEL):
        panel_inverse(a_ref, t_ref, npad, side, at)

        def update(i, carry):
            bases = [pl.multiple_of((i * batch + b) * side, side) for b in range(batch)]
            rows = [pl.ds(base + at, PANEL) for base in bases]
            both = [jnp.concatenate([a_ref[r, :], y_ref[r, :]], axis=1) for r in rows]
            turns = [
                t_ref[pl.ds(pl.multiple_of((i * batch + b) * PANEL, PANEL), PANEL), :][:, :PANEL]
                for b in range(batch)
            ]
            if at + PANEL < side:
                rest = [pl.ds(base + at + PANEL, side - at - PANEL) for base in bases]
                old = [(a_ref[r, :], y_ref[r, :]) for r in rest]
            fresh = [dot_six(t, x, 0, 0) for t, x in zip(turns, both)]
            if at + PANEL < side:
                changes = []
                for x in fresh:
                    parts = split_three(x)
                    cut = tuple(p[:, at + PANEL : side] for p in parts)
                    changes.append(dot_on(left_six(cut, 0), right_six(parts, 0), 0, 0))
                for r, (old_a, old_y), change in zip(rest, old, changes):
                    a_ref[r, :] = old_a - change[:, :side]
                    y_ref[r, :] = old_y - change[:, side:]
            for r, x in zip(rows, fresh):
                y_ref[r, :] = x[:, side:]
            return carry

        lax.fori_loop(0, 2 * n // batch, update, 0)

    def last(i, carry):
        mats = [mat_ref[2 * i], mat_ref[2 * i + 1]]
        rows = [pl.ds(pl.multiple_of((2 * i + k) * side, side), side) for k in range(2)]
        turns = [y_ref[r, :] for r in rows]
        left, right = [dot_three(x, y, 1, 1) for x, y in zip(mats, turns)]
        given[3, i] = left
        given[4, i] = right
        return carry

    lax.fori_loop(0, n, last, 0)
    for copy in copies + send((3, 4)):
        copy.wait()


def soap_update(grads, small, state, others):
    n, side = state[0].shape[:2]
    npad = -(-2 * n // 8) * 8
    ins = [*grads, *small, *state, *others]
    outs = [*state, *others]
    return pl.pallas_call(
        functools.partial(soap_kernel, npad),
        grid=(1,),
        out_shape=tuple(jax.ShapeDtypeStruct(s.shape, F32) for s in outs),
        in_specs=[whole(array.shape) for array in ins],
        out_specs=(far_space(),) * len(state) + tuple(whole(array.shape) for array in others),
        scratch_shapes=[
            pltpu.VMEM((7, n, side, side), F32),
            pltpu.VMEM((npad * side, side), F32),
            pltpu.VMEM((npad * side, side), F32),
            pltpu.VMEM((2 * n, side, side), F32),
            pltpu.VMEM((npad * PANEL, side), F32),
            pltpu.SemaphoreType.DMA((7,)),
        ],
        cost_estimate=pl.CostEstimate(
            flops=n * 40 * side**3, bytes_accessed=n * 60 * side * side, transcendentals=0
        ),
        compiler_params=pltpu.CompilerParams(vmem_limit_bytes=32 * 2**20),
        name="soap",
    )(*ins)


LANES = 128
LABEL_PAD = 256
RIM = 96
SMALL_ROWS = 192


def up_to(value, unit):
    return -(-value // unit) * unit


def block_at(shape, *index):
    return pl.BlockSpec(shape, lambda i: index, pipeline_mode=pl.Buffered(1))


def whole(shape):
    return block_at(shape, *[0] * len(shape))


def any_space():
    return pl.BlockSpec(memory_space=pl.ANY)


def far_space():
    return pl.BlockSpec(memory_space=pltpu.HBM)


def scalars():
    return pl.BlockSpec(memory_space=pltpu.SMEM)


def kernel_call(body, name, mib, out_shape, in_specs, out_specs, scratch=(), aliases=None, flops=0, bytes_moved=0):
    return pl.pallas_call(
        body,
        name=name,
        grid=(1,),
        out_shape=out_shape,
        in_specs=in_specs,
        out_specs=out_specs,
        scratch_shapes=list(scratch),
        input_output_aliases=aliases or {},
        cost_estimate=pl.CostEstimate(flops=flops, bytes_accessed=bytes_moved, transcendentals=0),
        compiler_params=pltpu.CompilerParams(vmem_limit_bytes=mib * 2**20),
    )


def start_tiles(row_ref, col_ref, kind_ref, sources, tiles, wall_ref, sems):
    base = 0
    for source, many in zip(sources, tiles):

        def start(i, carry):
            for k in range(many):
                place = base + i * many + k
                kind = kind_ref[place]

                @pl.when(kind < 2)
                def _():
                    row = pl.multiple_of(row_ref[place], LANES)
                    col = pl.multiple_of(col_ref[place], LANES)
                    pltpu.make_async_copy(
                        source.at[i, pl.ds(k * LANES, LANES)],
                        wall_ref.at[pl.ds(row, LANES), pl.ds(col, LANES)],
                        sems.at[kind],
                    ).start()

            return carry

        lax.fori_loop(0, source.shape[0], start, 0)
        base += source.shape[0] * many


def wait_rows(wall_ref, rows, sem):
    part = wall_ref.at[pl.ds(0, rows)]
    pltpu.make_async_copy(part, part, sem).wait()


def low_lanes(rows):
    return lax.broadcasted_iota(jnp.int32, (rows, LANES), 1) < LANES // 2


def stack_heads(pair):
    low = low_lanes(pair.shape[0])
    zero = jnp.zeros_like(pair)
    return jnp.concatenate([jnp.where(low, pair, zero), jnp.where(low, zero, pair)], axis=0)


def merge_stack(stacked):
    rows = stacked.shape[0] // 2
    return jnp.where(low_lanes(rows), stacked[:rows], stacked[rows:])


def skew(table, width):
    rows = table.shape[0] // 2
    padded = jnp.concatenate(
        [table, jnp.zeros((table.shape[0], width - table.shape[1]), F32)], axis=1
    )
    halves = [
        pltpu.roll(padded[at : at + rows], 0, 1, stride=1, stride_axis=0) for at in (0, rows)
    ]
    return jnp.concatenate(halves, axis=0)


def unskew(grid, width):
    rows = grid.shape[0] // 2
    lanes = grid.shape[1]
    parts = []
    for at in range(0, 2 * rows, 8):
        shift = (at % rows) % lanes
        part = grid[at : at + 8]
        parts.append(part if shift == 0 else pltpu.roll(part, lanes - shift, 1))
    moved = jnp.concatenate(parts, axis=0)
    index = lax.broadcasted_iota(jnp.int32, moved.shape, 0)
    for bit in (1, 2, 4):
        moved = jnp.where((index & bit) != 0, pltpu.roll(moved, lanes - bit, 1), moved)
    return moved[:, :width]


def softmax_rows(scores):
    top = jnp.max(scores, axis=-1, keepdims=True)
    raised = jnp.exp(scores - top)
    return raised * (1.0 / jnp.sum(raised, axis=-1, keepdims=True))


def window_keys(ref, base, at, width, ext, globs, cols):
    return jnp.concatenate(
        [ref[pl.ds(base + at, width), cols], ref[pl.ds(base + ext, globs), cols]], axis=0
    )


def glob_row_mask(shape, seq, glob_block):
    row = lax.broadcasted_iota(jnp.int32, shape, 0) % (shape[0] // 2)
    return (row >= seq * glob_block) & (row < (seq + 1) * glob_block)


def window_bias(block, blocks, chunk, dims):
    _, block_len, _, _, width, globs, _ = dims
    shape = (2 * LANES, width + globs)
    key = lax.broadcasted_iota(jnp.int32, shape, 1)
    query = lax.broadcasted_iota(jnp.int32, shape, 0) % LANES
    offset = key - query - (RIM - RADIUS)
    token = block * block_len - RIM + chunk * LANES + key
    near = (offset >= 0) & (offset <= 2 * RADIUS) & (token >= 0) & (token < blocks * block_len)
    return jnp.where(near | (key >= width), 0.0, NEG_FILL)


def attend_kernel(dims, wall_at, blocks, row_ref, col_ref, kind_ref, block_ref, xr_ref, rel_ref, gbias_ref,
                  left_ref, right_ref, *refs):
    q_ref, k_ref, v_ref, o_ref, part_ref, xe_ref, wall_out, wall_ref, glob_low, glob_cells, sems = refs[-11:]
    sources = refs[:-11]
    seqs, block_len, glob_block, ext, width, globs, scale = dims
    feed_rows, attn_rows, kv_at, q_at, out_at, tiles = wall_at
    model_dim = xr_ref.shape[1]
    head_cols = q_ref.shape[1]
    start_tiles(row_ref, col_ref, kind_ref, sources, tiles, wall_ref, sems)
    span = ext + globs
    cells = glob_low.shape[0] // blocks
    copies, base = [], 0
    for source in sources[-2:]:
        rows = source.shape[1] - cells
        for i in range(source.shape[0]):
            copies.append((source.at[i, pl.ds(rows, cells)], glob_low.at[pl.ds(base, cells)]))
            base += cells
    for source, target in copies:
        pltpu.make_async_copy(source, target, sems.at[3]).start()
    for seq in range(seqs):
        at = seq * span
        rim = pl.ds(seq * RIM, RIM)
        pltpu.make_async_copy(left_ref.at[rim], xe_ref.at[pl.ds(at, RIM)], sems.at[4]).start()
        pltpu.make_async_copy(
            right_ref.at[rim], xe_ref.at[pl.ds(at + RIM + block_len, RIM)], sems.at[4]
        ).start()
        at += RIM
        xe_ref[at : at + block_len] = xr_ref[seq * block_len : (seq + 1) * block_len]
        at += block_len + RIM
        if ext > block_len + 2 * RIM:
            xe_ref[at : seq * span + ext] = jnp.zeros((ext - block_len - 2 * RIM, model_dim), BF)
    pltpu.make_async_copy(glob_low, glob_low, sems.at[3]).wait()
    glob_cells[...] = glob_low[...].astype(F32)
    cols = model_dim // LANES
    for seq in range(seqs):
        for r in range(glob_block):
            at = seq * span + ext + r * blocks
            for c in range(cols):
                source = pl.ds((seq * glob_block + r) * cols + c, blocks, stride=cells)
                xe_ref[at : at + blocks, c * LANES : (c + 1) * LANES] = glob_cells[source, :].astype(BF)
    rims = xe_ref.at[pl.ds(0, 2 * seqs * RIM)]
    pltpu.make_async_copy(rims, rims, sems.at[4]).wait()
    wait_rows(wall_ref, attn_rows, sems.at[0])
    wq_ref = wall_ref.at[pl.ds(q_at, model_dim), pl.ds(0, head_cols)]
    wkv_ref = wall_ref.at[pl.ds(kv_at, model_dim)]
    wo_ref = wall_ref.at[pl.ds(out_at, head_cols)]
    pairs = head_cols // LANES
    glob_at = seqs * block_len
    glob_rows = q_ref.shape[0] - glob_at
    span = ext + globs
    chunks = block_len // LANES
    q_ref[...] = dot_on(xr_ref[...], wq_ref[...], 1, 0).astype(BF)

    def project(i, carry):
        rows = pl.ds(pl.multiple_of(i * 256, 256), 256)
        both = dot_on(xe_ref[rows, :], wkv_ref[...], 1, 0).astype(BF)
        k_ref[rows, :] = both[:, :head_cols]
        v_ref[rows, :] = both[:, head_cols:]
        return carry

    lax.fori_loop(0, seqs * span // 256, project, 0)
    wait_rows(wall_ref, feed_rows, sems.at[1])
    keep = pltpu.make_async_copy(wall_ref, wall_out, sems.at[2])
    keep.start()

    def window(i, carry):
        seq, chunk = i // chunks, i % chunks
        rows = pl.ds(pl.multiple_of(i * LANES, LANES), LANES)
        base = pl.multiple_of(seq * span, LANES)
        at = pl.multiple_of(chunk * LANES, LANES)
        bias = window_bias(block_ref[0], blocks, chunk, dims)
        cols = [slice(pair * LANES, (pair + 1) * LANES) for pair in range(pairs)]
        query = [stack_heads(q_ref[rows, c] * scale) for c in cols]
        keys = [window_keys(k_ref, base, at, width, ext, globs, c) for c in cols]
        values = [window_keys(v_ref, base, at, width, ext, globs, c) for c in cols]
        near = [dot_on(q, rel_ref[:, c], 1, 1) for q, c in zip(query, cols)]
        scores = [dot_on(q, k, 1, 1) for q, k in zip(query, keys)]
        scores = [x + skew(y, width + globs) + bias for x, y in zip(scores, near)]
        weights = [softmax_rows(x).astype(BF) for x in scores]
        outs = [merge_stack(dot_on(w, v, 1, 0)).astype(BF) for w, v in zip(weights, values)]
        for c, out in zip(cols, outs):
            o_ref[rows, c] = out
        return carry

    lax.fori_loop(0, seqs * chunks, window, 0)
    rows = slice(glob_at, glob_at + glob_rows)
    both = [(pair, seq) for pair in range(pairs) for seq in range(seqs)]
    cols = [slice(pair * LANES, (pair + 1) * LANES) for pair in range(pairs)]
    spans = [slice(seq * span, (seq + 1) * span) for seq in range(seqs)]
    query = [stack_heads(q_ref[rows, c] * scale) for c in cols]
    bias = [jnp.concatenate([gbias_ref[seq]] * 2, axis=0) for seq in range(seqs)]
    scores = [dot_on(query[pair], k_ref[spans[seq], cols[pair]], 1, 1) + bias[seq] for pair, seq in both]
    weights = [softmax_rows(x).astype(BF) for x in scores]
    outs = [dot_on(w, v_ref[spans[seq], cols[pair]], 1, 0) for w, (pair, seq) in zip(weights, both)]
    for pair in range(pairs):
        total = outs[pair * seqs]
        for seq in range(1, seqs):
            total = jnp.where(glob_row_mask(total.shape, seq, glob_block), outs[pair * seqs + seq], total)
        used = lax.broadcasted_iota(jnp.int32, total.shape, 0) % glob_rows < seqs * glob_block
        o_ref[rows, cols[pair]] = merge_stack(jnp.where(used, total, 0.0)).astype(BF)
    part_ref[...] = dot_on(o_ref[...], wo_ref[...], 1, 0).astype(BF)
    keep.wait()


def norm_parts(values):
    center = values - jnp.mean(values, axis=-1, keepdims=True)
    spread = jnp.mean(center * center, axis=-1, keepdims=True)
    rate = lax.rsqrt(spread + NORM_EPS)
    return center * rate, rate


def norm_back(grad, normed, rate, gain):
    scaled = grad * gain
    return (
        scaled
        - jnp.mean(scaled, axis=-1, keepdims=True)
        - normed * jnp.mean(scaled * normed, axis=-1, keepdims=True)
    ) * rate


def row_loop(total, body):
    step = 176 if total % 176 == 0 else 16

    def run(i, carry):
        body(pl.ds(pl.multiple_of(i * step, 16), step))
        return carry

    lax.fori_loop(0, total // step, run, 0)


def col_loop(total, body, step=256):
    def run(i, carry):
        body(i)
        return carry

    lax.fori_loop(0, total // step, run, 0)


GELU_RATE = 0.7978845608028654
GELU_CUBE = 0.044715


def gelu_parts(u):
    square = u * u
    curve = jnp.tanh(GELU_RATE * u * (1.0 + GELU_CUBE * square))
    return square, curve


def feed_kernel(xr_ref, part_ref, got_ref, norm_ref, wu_ref, wd_ref, h_ref, hb_ref, u_ref, a_ref, down_ref):
    model_dim = xr_ref.shape[1]
    gain, offset = norm_ref[0:1], norm_ref[1:2]

    def norm(rows):
        mid = xr_ref[rows, :].astype(F32) + (part_ref[rows, :].astype(F32) + got_ref[rows, :].astype(F32))
        normed, _ = norm_parts(mid)
        out = normed * gain + offset
        h_ref[rows, :] = out
        hb_ref[rows, :] = out.astype(BF)

    row_loop(xr_ref.shape[0], norm)
    per_half = model_dim // 256

    def up(j):
        rows = pl.ds(pl.multiple_of((j // per_half) * model_dim, 256), model_dim)
        cols = pl.ds(pl.multiple_of((j % per_half) * 256, 256), 256)
        here = pl.ds(pl.multiple_of(j * 256, 256), 256)
        u = dot_on(hb_ref[...], wu_ref[rows, cols], 1, 0)
        u_ref[:, here] = u
        _, curve = gelu_parts(u)
        a_ref[:, here] = (0.5 * u * (1.0 + curve)).astype(BF)

    col_loop(u_ref.shape[1], up)

    def down(j):
        cols = pl.ds(pl.multiple_of(j * 256, 256), 256)
        down_ref[:, cols] = dot_on(a_ref[...], wd_ref[:, cols], 1, 0).astype(BF)

    col_loop(model_dim, down)


def own_rows(ref, half, seqs, block_len, glob_block):
    per = block_len // 2
    long_part = [
        ref[pl.ds(pl.multiple_of(seq * block_len + half * per, per), per), :] for seq in range(seqs)
    ]
    base, few = seqs * block_len, glob_block // 2
    globs = ref[base:, :]
    glob_part = [
        jnp.where(
            half == 0,
            globs[seq * glob_block : seq * glob_block + few],
            globs[seq * glob_block + few : (seq + 1) * glob_block],
        )
        for seq in range(seqs)
    ]
    return long_part, glob_part


def feed_back_kernel(dims, half_ref, h_ref, down_ref, got_ref, u_ref, dy_ref, norm_ref, wu_ref, wd_ref,
                     y_long_ref, y_glob_ref, dx_ref, dxb_ref, du_ref, dh_ref, gn_ref, y_ref):
    model_dim = h_ref.shape[1]
    gain, offset = norm_ref[2:3], norm_ref[3:4]
    gn_ref[...] = jnp.zeros_like(gn_ref)

    def norm(rows):
        out = h_ref[rows, :] + (down_ref[rows, :].astype(F32) + got_ref[rows, :].astype(F32))
        normed, rate = norm_parts(out)
        y_ref[rows, :] = normed * gain + offset
        grad = dy_ref[rows, :].astype(F32)
        gn_ref[0:1] += jnp.sum(grad * normed, axis=0, keepdims=True)
        gn_ref[1:2] += jnp.sum(grad, axis=0, keepdims=True)
        dx = norm_back(grad, normed, rate, gain)
        dx_ref[rows, :] = dx
        dxb_ref[rows, :] = dx.astype(BF)

    row_loop(h_ref.shape[0], norm)
    long_part, glob_part = own_rows(y_ref, half_ref[0], *dims[:3])
    for seq in range(dims[0]):
        y_long_ref[seq] = long_part[seq].astype(BF)
        y_glob_ref[seq] = glob_part[seq].astype(BF)

    def act(j):
        here = pl.ds(pl.multiple_of(j * 256, 256), 256)
        da = dot_on(dxb_ref[...], wd_ref[here, :], 1, 1)
        u = u_ref[:, here]
        square, curve = gelu_parts(u)
        slope = 0.5 * (1.0 + curve) + 0.5 * u * (1.0 - curve * curve) * (
            GELU_RATE * (1.0 + 3.0 * GELU_CUBE * square)
        )
        du_ref[:, here] = (da * slope).astype(BF)

    col_loop(u_ref.shape[1], act)
    halves = u_ref.shape[1] // model_dim

    def lower(j):
        cols = pl.ds(pl.multiple_of(j * 256, 256), 256)
        total = 0.0
        for half in range(halves):
            rows = pl.ds(pl.multiple_of(half * model_dim + j * 256, 256), 256)
            total = total + dot_on(
                du_ref[:, half * model_dim : (half + 1) * model_dim], wu_ref[rows, :], 1, 1
            )
        dh_ref[:, cols] = total.astype(BF)

    col_loop(model_dim, lower)


def send_tiles(stage_ref, row, rows, first, place_ref, out_ref, sem):
    cols = stage_ref.shape[1] // LANES
    for r in range(rows):
        for c in range(cols):
            pltpu.make_async_copy(
                stage_ref.at[pl.ds(row + r * LANES, LANES), pl.ds(c * LANES, LANES)],
                out_ref.at[pl.ds(pl.multiple_of(place_ref[first + r * cols + c], 16), LANES)],
                sem,
            ).start()


def feed_grads_kernel(tiles_at, place_ref, a_ref, dxb_ref, hb_ref, du_ref, out_ref, down_stage, up_stage, sems):
    up_at, down_at = tiles_at
    model_dim = dxb_ref.shape[1]

    def down(j):
        row = pl.multiple_of(j * 256, 256)
        rows = pl.ds(row, 256)
        down_stage[rows, :] = dot_on(a_ref[:, rows], dxb_ref[...], 0, 0).astype(BF)
        send_tiles(down_stage, row, 2, down_at + j * 2 * (model_dim // LANES), place_ref, out_ref, sems.at[0])

    col_loop(a_ref.shape[1], down)

    def up(j):
        row = pl.multiple_of(j * 256, 256)
        rows = pl.ds(row, 256)
        up_stage[rows, :] = dot_on(hb_ref[:, rows], du_ref[...], 0, 0).astype(BF)
        send_tiles(
            up_stage, row, 2, up_at + j * 2 * (du_ref.shape[1] // LANES), place_ref, out_ref, sems.at[1]
        )

    col_loop(model_dim, up)
    pltpu.make_async_copy(down_stage, down_stage, sems.at[0]).wait()
    pltpu.make_async_copy(up_stage, up_stage, sems.at[1]).wait()


def attend_back_kernel(dims, blocks, attn_tiles, tile_counts, glob_at_rows, block_ref, place_ref, norm_two_ref, xr_ref, part_ref, got_ref, dh_ref, dh_got_ref, dx_ref, o_ref,
                       q_ref, k_ref, v_ref, xe_ref, wo_ref, rel_ref, gbias_ref, norm_ref, grads_in,
                       grads_ref, dq_ref, dkv_ref, mid_ref, small_ref,
                       do_ref, midb_ref, dkv_acc, out_stage, q_stage, k_stage, v_stage, none_ref,
                       drel_ref, norms_ref, gn_ref, glob_stage, glob_low, sems):
    seqs, block_len, glob_block, ext, width, globs, scale = dims
    head_cols = q_ref.shape[1]
    pairs = head_cols // LANES
    glob_at = seqs * block_len
    glob_rows = q_ref.shape[0] - glob_at
    span = ext + globs
    chunks = block_len // LANES
    gain = norm_ref[0:1]
    gn_ref[...] = jnp.zeros_like(gn_ref)

    def norm(rows):
        mid = xr_ref[rows, :].astype(F32) + (part_ref[rows, :].astype(F32) + got_ref[rows, :].astype(F32))
        normed, rate = norm_parts(mid)
        grad = dh_ref[rows, :].astype(F32) + dh_got_ref[rows, :].astype(F32) + dx_ref[rows, :]
        gn_ref[0:1] += jnp.sum(grad * normed, axis=0, keepdims=True)
        gn_ref[1:2] += jnp.sum(grad, axis=0, keepdims=True)
        out = norm_back(grad, normed, rate, gain)
        mid_ref[rows, :] = out
        midb_ref[rows, :] = out.astype(BF)

    row_loop(xr_ref.shape[0], norm)
    do_ref[...] = dot_on(midb_ref[...], wo_ref[...], 1, 1).astype(BF)
    out_stage[...] = dot_on(o_ref[...], midb_ref[...], 0, 0).astype(BF)
    send_tiles(out_stage, 0, out_stage.shape[0] // LANES, 3 * attn_tiles, place_ref, grads_ref, sems.at[0])
    none_ref[...] = jnp.zeros_like(none_ref)
    spare = []
    for tile in range(*tile_counts):
        target = grads_ref.at[pl.ds(pl.multiple_of(place_ref[tile], 16), LANES)]
        spare.append(pltpu.make_async_copy(none_ref, target, sems.at[4]))
        spare[-1].start()
    dkv_acc[...] = jnp.zeros_like(dkv_acc)
    drel_ref[...] = jnp.zeros_like(drel_ref)

    def grads_of(scores, grad_out, values):
        weights = softmax_rows(scores)
        dp = dot_on(grad_out, values, 1, 1)
        delta = jnp.sum(weights * dp, axis=-1, keepdims=True)
        return weights.astype(BF), weights * (dp - delta)

    def window(i, carry):
        seq, chunk = i // chunks, i % chunks
        rows = pl.ds(pl.multiple_of(i * LANES, LANES), LANES)
        base = pl.multiple_of(seq * span, LANES)
        at = pl.multiple_of(chunk * LANES, LANES)
        near_rows = pl.ds(base + at, width)
        far_rows = pl.ds(base + ext, globs)
        bias = window_bias(block_ref[0], blocks, chunk, dims)
        near = lax.broadcasted_iota(jnp.int32, bias.shape, 1) < width
        cols = [slice(pair * LANES, (pair + 1) * LANES) for pair in range(pairs)]
        query = [stack_heads(q_ref[rows, c] * scale) for c in cols]
        grad_out = [stack_heads(do_ref[rows, c]) for c in cols]
        keys = [window_keys(k_ref, base, at, width, ext, globs, c) for c in cols]
        values = [window_keys(v_ref, base, at, width, ext, globs, c) for c in cols]
        labels = [rel_ref[:, c] for c in cols]
        shifted = [dot_on(q, x, 1, 1) for q, x in zip(query, labels)]
        scores = [dot_on(q, k, 1, 1) for q, k in zip(query, keys)]
        scores = [x + skew(y, width + globs) + bias for x, y in zip(scores, shifted)]
        pairs_of = [grads_of(x, g, v) for x, g, v in zip(scores, grad_out, values)]
        dsb = [ds.astype(BF) for _, ds in pairs_of]
        by_label = [unskew(jnp.where(near, x.astype(F32), 0.0), LABEL_PAD).astype(BF) for x in dsb]
        dv = [dot_on(w, g, 0, 0) for (w, _), g in zip(pairs_of, grad_out)]
        dk = [dot_on(x, q, 0, 0) for x, q in zip(dsb, query)]
        dq = [
            dot_on(x, k, 1, 0) + dot_on(y, l, 1, 0) for x, k, y, l in zip(dsb, keys, by_label, labels)
        ]
        drel = [dot_on(y, q, 0, 0) for y, q in zip(by_label, query)]
        for pair, c in enumerate(cols):
            dq_ref[rows, c] = (merge_stack(dq[pair]) * scale).astype(BF)
            drel_ref[:, c] += drel[pair]
            for at_acc, grad in ((pair, dk[pair]), (pairs + pair, dv[pair])):
                dkv_acc[at_acc, near_rows] += grad[:width]
                dkv_acc[at_acc, far_rows] += grad[width:]
        return carry

    lax.fori_loop(0, seqs * chunks, window, 0)
    rows = slice(glob_at, glob_at + glob_rows)
    both = [(pair, seq) for pair in range(pairs) for seq in range(seqs)]
    cols = [slice(pair * LANES, (pair + 1) * LANES) for pair in range(pairs)]
    spans = [slice(seq * span, (seq + 1) * span) for seq in range(seqs)]
    query = [stack_heads(q_ref[rows, c] * scale) for c in cols]
    grad_out = [stack_heads(do_ref[rows, c]) for c in cols]
    bias = [jnp.concatenate([gbias_ref[seq]] * 2, axis=0) for seq in range(seqs)]
    keys = [k_ref[spans[seq], cols[pair]] for pair, seq in both]
    scores = [dot_on(query[pair], k, 1, 1) + bias[seq] for k, (pair, seq) in zip(keys, both)]
    grads = [
        grads_of(x, grad_out[pair], v_ref[spans[seq], cols[pair]]) for x, (pair, seq) in zip(scores, both)
    ]
    own = [glob_row_mask(scores[0].shape, seq, glob_block) for seq in range(seqs)]
    weights = [jnp.where(own[seq], w.astype(F32), 0.0).astype(BF) for (w, _), (_, seq) in zip(grads, both)]
    dsb = [jnp.where(own[seq], ds, 0.0).astype(BF) for (_, ds), (_, seq) in zip(grads, both)]
    dk = [dot_on(x, query[pair], 0, 0) for x, (pair, _) in zip(dsb, both)]
    dv = [dot_on(w, grad_out[pair], 0, 0) for w, (pair, _) in zip(weights, both)]
    dq = [dot_on(x, k, 1, 0) for x, k in zip(dsb, keys)]
    for pair in range(pairs):
        dq_ref[rows, cols[pair]] = (merge_stack(sum(dq[pair * seqs : (pair + 1) * seqs])) * scale).astype(BF)
        for seq in range(seqs):
            dkv_acc[pair, spans[seq]] += dk[pair * seqs + seq]
            dkv_acc[pairs + pair, spans[seq]] += dv[pair * seqs + seq]
    first_row, row_step, cells, per_block = glob_at_rows
    for seq in range(seqs):
        for r in range(per_block):
            source = pl.ds(seq * span + ext + r * blocks, blocks)
            for c in range(2 * pairs):
                rows = pl.ds((seq * per_block + r) * 2 * pairs + c, blocks, stride=cells)
                glob_stage[rows, :] = dkv_acc[c, source, :]
    glob_low[...] = glob_stage[...].astype(BF)
    for i in range(blocks):
        pltpu.make_async_copy(
            glob_low.at[pl.ds(i * cells, cells)],
            grads_ref.at[pl.ds(first_row + (i + 1) * row_step - cells, cells)],
            sems.at[5],
        ).start()
    norms_ref[...] = jnp.zeros_like(norms_ref)
    for row, source in enumerate((gn_ref, gn_ref, norm_two_ref, norm_two_ref)):
        for half in range(source.shape[1] // head_cols):
            at = row * (source.shape[1] // head_cols) + half
            norms_ref[at : at + 1] = source[row % 2 : row % 2 + 1, half * head_cols : (half + 1) * head_cols]
    small_ref[...] = jnp.concatenate([drel_ref[: SMALL_ROWS - 8], norms_ref[...]], axis=0).astype(BF)
    for c in range(2 * pairs):
        dkv_ref[:, c * LANES : (c + 1) * LANES] = dkv_acc[c].astype(BF)
    per = head_cols // LANES

    def cut(j):
        row = pl.multiple_of(j * 256, 256)
        rows = pl.ds(row, 256)
        first = 2 * per * j
        q_stage[rows, :] = dot_on(xr_ref[:, rows], dq_ref[...], 0, 0).astype(BF)
        send_tiles(q_stage, row, 2, first, place_ref, grads_ref, sems.at[1])
        both = dot_on(xe_ref[:, rows], dkv_ref[...], 0, 0).astype(BF)
        k_stage[rows, :] = both[:, :head_cols]
        v_stage[rows, :] = both[:, head_cols:]
        send_tiles(k_stage, row, 2, attn_tiles + first, place_ref, grads_ref, sems.at[2])
        send_tiles(v_stage, row, 2, 2 * attn_tiles + first, place_ref, grads_ref, sems.at[3])

    col_loop(q_stage.shape[0], cut)
    for at, stage in enumerate((out_stage, q_stage, k_stage, v_stage)):
        pltpu.make_async_copy(stage, stage, sems.at[at]).wait()
    for copy in spare:
        copy.wait()
    pltpu.make_async_copy(glob_low, glob_low, sems.at[5]).wait()


def start_weights(wall_ref, at, head_cols, wkv_ref, wq_ref, sems):
    model_dim = wkv_ref.shape[0]
    copies = [
        pltpu.make_async_copy(wall_ref.at[pl.ds(at[0], model_dim)], wkv_ref, sems.at[0]),
        pltpu.make_async_copy(
            wall_ref.at[pl.ds(at[1], model_dim), pl.ds(0, head_cols)], wq_ref, sems.at[1]
        ),
    ]
    for copy in copies:
        copy.start()
    return copies


def back_rows(proj, wkv_ref, wq_ref):
    cols = wq_ref.shape[1]
    return dot_on(proj[:, :cols], wq_ref[...], 1, 1) + dot_on(proj[:, cols:], wkv_ref[...], 1, 1)


def dx_kernel(dims, at, half_ref, dq_ref, dkv_ref, next_ref, last_ref, mid_ref, wall_ref,
              keep_ref, send_ref, proj_ref, wkv_ref, wq_ref, sems):
    seqs, block_len, _, ext, _, globs, _ = dims
    head_cols = dq_ref.shape[1]
    copies = start_weights(wall_ref, at, head_cols, wkv_ref, wq_ref, sems)
    proj_ref[:, :head_cols] = dq_ref[: seqs * block_len]
    for seq in range(seqs):
        base, row = seq * (ext + globs) + RIM, seq * block_len
        middle = block_len - 2 * RIM
        own = dkv_ref[base : base + block_len].astype(F32)
        sums = [
            own[:RIM] + last_ref[seq * RIM : (seq + 1) * RIM].astype(F32),
            own[RIM : RIM + middle],
            own[RIM + middle :] + next_ref[seq * RIM : (seq + 1) * RIM].astype(F32),
        ]
        proj_ref[row : row + block_len, head_cols:] = jnp.concatenate(sums, axis=0).astype(BF)
    for copy in copies:
        copy.wait()
    per = block_len // 2
    for out_ref, half in ((keep_ref, half_ref[0]), (send_ref, 1 - half_ref[0])):
        for seq in range(seqs):
            rows = pl.ds(pl.multiple_of(seq * block_len + half * per, per), per)
            total = back_rows(proj_ref[rows, :], wkv_ref, wq_ref)
            if out_ref is keep_ref:
                total = total + mid_ref[rows, :]
            out_ref[seq] = total.astype(out_ref.dtype)


def dx_glob_kernel(dims, at, half_ref, dq_ref, kept_ref, got_ref, mid_ref, wall_ref,
                   keep_ref, send_ref, cells_ref, wkv_ref, wq_ref, sems):
    seqs, block_len, glob_block = dims[:3]
    head_cols = dq_ref.shape[1]
    base = seqs * block_len
    used, cols = seqs * glob_block, 2 * head_cols // LANES
    copies = start_weights(wall_ref, at, head_cols, wkv_ref, wq_ref, sems)
    first = kept_ref.shape[0] - used * cols
    cells_ref[...] = kept_ref[first:].astype(F32) + got_ref[first:].astype(F32)
    wide = [cells_ref[pl.ds(c, used, stride=cols), :] for c in range(cols)]
    dkv = jnp.concatenate(wide, axis=1)
    dkv = jnp.concatenate([dkv, jnp.zeros((dq_ref.shape[0] - base - used, 2 * head_cols), F32)], axis=0)
    proj = jnp.concatenate([dq_ref[base:], dkv.astype(BF)], axis=1)
    for copy in copies:
        copy.wait()
    total = back_rows(proj, wkv_ref, wq_ref)
    few = glob_block // 2
    here = half_ref[0] == 0
    for seq in range(seqs):
        start = seq * glob_block
        halves = [total[start : start + few], total[start + few : start + glob_block]]
        mids = [
            mid_ref[base + start : base + start + few, :],
            mid_ref[base + start + few : base + start + glob_block, :],
        ]
        keep_ref[seq] = jnp.where(here, halves[0] + mids[0], halves[1] + mids[1])
        send_ref[seq] = jnp.where(here, halves[1], halves[0]).astype(BF)


def swap_cores(values):
    count = lax.axis_size("ffn")
    return lax.ppermute(values, "ffn", [(i, i ^ 1) for i in range(count)])


def on_device(
    x_long,
    x_glob,
    sentence,
    dy_long,
    dy_glob,
    owner_list,
    w_master,
    m_old,
    v_old,
    left_basis,
    right_basis,
    left_stats,
    right_stats,
    rel_table,
    rel_m,
    rel_v,
    norm_params,
    norm_m,
    norm_v,
):
    ffn_count = lax.axis_size("ffn")
    seq_count = lax.axis_size("seq")
    seqs, tok_half, model_dim = x_long.shape
    glob_half = x_glob.shape[1]
    block_len = tok_half * ffn_count
    glob_block = glob_half * ffn_count
    globs = glob_block * seq_count
    head_cols = model_dim // ffn_count
    hidden = FF // ffn_count
    scale = (model_dim // HEADS) ** (-0.5)
    slots, side = w_master.shape[:2]
    attn_tiles = model_dim * head_cols // (side * side)
    ffn_tiles = model_dim * hidden // (side * side)
    tile_count = 4 * attn_tiles + 2 * ffn_tiles
    slot_count = owner_list.shape[0]
    labels = rel_table.shape[0]
    half_index = lax.axis_index("ffn")
    first_half = half_index == 0
    parts = slot_parts(slots, seq_count)

    glob_cells = seqs * glob_block * model_dim // LANES
    rows_per = part_rows(parts, side, glob_cells)
    places, place_rows = slot_places(owner_list, slots, rows_per, side)
    held = jnp.sum(
        jnp.where(
            places[None, :] == jnp.arange(slot_count, dtype=jnp.int32)[:, None],
            jnp.arange(slot_count, dtype=jnp.int32)[None, :],
            0,
        ),
        axis=1,
    )
    per_row = model_dim // side
    up_rows = hidden // model_dim * model_dim
    kv_at = up_rows + hidden
    q_at = kv_at + model_dim
    out_at = q_at + model_dim
    head_tiles = head_cols // side
    up_tiles = hidden // side

    def tile_row_col(tile):
        kind_qkv = tile // attn_tiles
        inner = tile % attn_tiles
        qkv_row = jnp.where(kind_qkv == 0, q_at, kv_at) + inner // head_tiles * side
        qkv_col = jnp.where(kind_qkv == 2, head_cols, 0) + inner % head_tiles * side
        out_row = out_at + inner // per_row * side
        up = tile - 4 * attn_tiles
        up_col = up % up_tiles * side
        up_row = up_col // model_dim * model_dim + up // up_tiles * side
        down = up - ffn_tiles
        down_row = up_rows + down // per_row * side
        row = jnp.where(
            tile < 3 * attn_tiles,
            qkv_row,
            jnp.where(
                tile < 4 * attn_tiles,
                out_row,
                jnp.where(up < ffn_tiles, up_row, down_row),
            ),
        )
        col = jnp.where(
            tile < 3 * attn_tiles,
            qkv_col,
            jnp.where(
                tile < 4 * attn_tiles,
                inner % per_row * side,
                jnp.where(up < ffn_tiles, up_col % model_dim, down % per_row * side),
            ),
        )
        return row, col

    wall_row, wall_col = tile_row_col(held)
    wall_kind = jnp.where(held < 4 * attn_tiles, 0, jnp.where(held < tile_count, 1, 2))

    weights_low = w_master.astype(BF).reshape(-1, LANES)
    glob_other = swap_cores(x_glob)
    glob_own = jnp.concatenate(
        [jnp.where(first_half, x_glob, glob_other), jnp.where(first_half, glob_other, x_glob)], axis=1
    )
    orders = [order for _, _, order in parts]
    gathered = gather_rows(
        weights_low, glob_own.reshape(-1, LANES), rows_per, orders
    )
    gathered = [
        [piece.reshape(-1, many, LANES) for piece in pieces] for pieces, many in zip(gathered, rows_per)
    ]
    tiles_per = tuple(last - first for (first, last, _), pieces in zip(parts, gathered) for _ in pieces)
    gathered = [piece for pieces in gathered for piece in pieces]

    rim = jnp.where(first_half, x_long[:, :RIM], x_long[:, tok_half - RIM :])
    mine = jnp.concatenate([x_long, dy_long, x_glob, dy_glob], axis=1)
    spare = -mine.shape[1] % 8
    mine = jnp.concatenate([mine, jnp.zeros((seqs, spare, model_dim), BF)], axis=1)
    first, second = mine.reshape(-1, model_dim), rim.reshape(-1, model_dim)
    first, second, _ = move_rows(
        [[(first.shape[0], (first, 0))], [(second.shape[0], (second, 0))], [(16, (weights_low, 0))]]
    )
    mine, rim = first.reshape(mine.shape), second
    other = swap_cores(mine)
    lower = jnp.where(first_half, mine, other)
    upper = jnp.where(first_half, other, mine)

    def block_rows(at, count):
        return jnp.concatenate([lower[:, at : at + count], upper[:, at : at + count]], axis=1)

    long_rows = block_rows(0, tok_half)
    dy_rows = block_rows(tok_half, tok_half)
    glob_rows = block_rows(2 * tok_half, glob_half)
    dy_globs = block_rows(2 * tok_half + glob_half, glob_half)
    used = seqs * (block_len + glob_block)
    row_count = seqs * block_len + up_to(seqs * glob_block, 16)
    pad_rows = jnp.zeros((row_count - used, model_dim), BF)

    def in_rows(long_part, glob_part):
        return jnp.concatenate(
            [long_part.reshape(-1, model_dim), glob_part.reshape(-1, model_dim), pad_rows]
        )

    x_rows = in_rows(long_rows, glob_rows)
    dy_all = in_rows(dy_rows, dy_globs)
    to_next = [(i * ffn_count + 1, (i + 1) * ffn_count + 1) for i in range(seq_count - 1)]
    to_last = [((i + 1) * ffn_count, i * ffn_count) for i in range(seq_count - 1)]
    rim = lax.ppermute(rim, ("seq", "ffn"), to_next + to_last)
    rim_other = swap_cores(rim)
    rim_left = jnp.where(first_half, rim_other, rim)
    rim_right = jnp.where(first_half, rim, rim_other)

    reach = 2 * RADIUS
    width = up_to(LANES + 2 * RIM, LANES) if globs % LANES == 0 else up_to(LANES + 2 * RIM + globs, LANES) - globs
    ext = block_len - LANES + width
    span = ext + globs
    rel_low = jnp.pad(
        rel_table.astype(BF), ((RIM - RADIUS, LABEL_PAD - labels - RIM + RADIUS), (0, 0))
    )

    glob_bias_rows = row_count - seqs * block_len
    row_at = jnp.arange(glob_bias_rows, dtype=jnp.int32)[None, :, None]
    seq_at = jnp.arange(seqs, dtype=jnp.int32)[:, None, None]
    spread = jnp.pad(sentence[:, 0], ((0, 0), (RIM, span - RIM - block_len)), constant_values=-1)
    span_at = jnp.arange(span, dtype=jnp.int32)[None, None, :]
    own = (spread[:, None, :] == row_at - seq_at * glob_block) & (spread[:, None, :] >= 0)
    glob_bias = jnp.where(own | (span_at >= ext), 0.0, NEG_FILL).astype(F32)

    spec_up = block_at((up_rows, model_dim), 0, 0)
    spec_down = block_at((hidden, model_dim), 1, 0)
    spec_out = block_at((head_cols, model_dim), out_at // head_cols, 0)

    def rows_of(cols, dtype=BF, rows=row_count):
        return jax.ShapeDtypeStruct((rows, cols), dtype)

    def specs(arrays):
        return [whole(a.shape) for a in arrays]

    dims = (seqs, block_len, glob_block, ext, width, globs, scale)
    fwd_shapes = (
        rows_of(head_cols),
        rows_of(head_cols, rows=seqs * span),
        rows_of(head_cols, rows=seqs * span),
        rows_of(head_cols),
        rows_of(model_dim),
        rows_of(model_dim, rows=seqs * span),
    )
    wall_at = (
        2 * ffn_tiles // per_row * side,
        4 * attn_tiles // per_row * side,
        kv_at,
        q_at,
        out_at,
        tiles_per,
    )
    wall_shape = jax.ShapeDtypeStruct((out_at + head_cols, model_dim), BF)
    block_now = lax.axis_index("seq").astype(jnp.int32).reshape(1)
    ins = [x_rows, rel_low, glob_bias]
    query, keys, values, heads_out, attn_part, x_ext, wall = kernel_call(
        functools.partial(attend_kernel, dims, wall_at, seq_count),
        "attend",
        28,
        fwd_shapes + (wall_shape,),
        [scalars()] * 4 + specs(ins) + [any_space()] * (2 + len(gathered)),
        tuple(specs(fwd_shapes)) + (any_space(),),
        [
            pltpu.VMEM(wall_shape.shape, BF),
            pltpu.VMEM((seq_count * glob_cells, LANES), BF),
            pltpu.VMEM((seq_count * glob_cells, LANES), F32),
            pltpu.SemaphoreType.DMA((5,)),
        ],
        flops=4 * 10**9,
        bytes_moved=10**7,
    )(wall_row, wall_col, wall_kind, block_now, *ins, rim_left, rim_right, *gathered)
    attn_got = swap_cores(attn_part)
    feed_shapes = (
        rows_of(model_dim, F32),
        rows_of(model_dim),
        rows_of(hidden, F32),
        rows_of(hidden),
        rows_of(model_dim),
    )
    norm_one, norm_low, up_pre, act_low, down_part = kernel_call(
        feed_kernel,
        "feed",
        24,
        feed_shapes,
        specs([x_rows, attn_part, attn_got, norm_params]) + [spec_up, spec_down],
        tuple(specs(feed_shapes)),
        flops=3 * 10**9,
        bytes_moved=10**7,
    )(x_rows, attn_part, attn_got, norm_params, wall, wall)
    down_got = swap_cores(down_part)
    norm_shape = jax.ShapeDtypeStruct((8, model_dim), F32)
    half_now = half_index.astype(jnp.int32).reshape(1)
    back_shapes = (
        jax.ShapeDtypeStruct(x_long.shape, BF),
        jax.ShapeDtypeStruct(x_glob.shape, BF),
        rows_of(model_dim, F32),
        rows_of(model_dim),
        rows_of(hidden),
        rows_of(model_dim),
        norm_shape,
    )
    y_long, y_glob, d_pre, d_pre_low, d_up, d_norm_part, norm_two_grad = kernel_call(
        functools.partial(feed_back_kernel, dims),
        "feed_back",
        30,
        back_shapes,
        [scalars()]
        + specs([norm_one, down_part, down_got, up_pre, dy_all, norm_params])
        + [spec_up, spec_down],
        tuple(specs(back_shapes)),
        [pltpu.VMEM((row_count, model_dim), F32)],
        flops=3 * 10**9,
        bytes_moved=10**7,
    )(half_now, norm_one, down_part, down_got, up_pre, dy_all, norm_params, wall, wall)
    d_norm_got = swap_cores(d_norm_part)
    grads_shape = jax.ShapeDtypeStruct((seq_count * sum(rows_per), LANES), BF)
    slot_grads = kernel_call(
        functools.partial(feed_grads_kernel, (4 * attn_tiles, 4 * attn_tiles + ffn_tiles)),
        "feed_grads",
        16,
        grads_shape,
        [scalars()] + specs([act_low, d_pre_low, norm_low, d_up]),
        any_space(),
        [
            pltpu.VMEM((hidden, model_dim), BF),
            pltpu.VMEM((model_dim, hidden), BF),
            pltpu.SemaphoreType.DMA((2,)),
        ],
        flops=3 * 10**9,
        bytes_moved=10**7,
    )(place_rows, act_low, d_pre_low, norm_low, d_up)
    ins = [
        x_rows,
        attn_part,
        attn_got,
        d_norm_part,
        d_norm_got,
        d_pre,
        heads_out,
        query,
        keys,
        values,
        x_ext,
    ]
    last_shapes = (
        grads_shape,
        rows_of(head_cols),
        rows_of(2 * head_cols, rows=seqs * span),
        rows_of(model_dim, F32),
        rows_of(head_cols, rows=SMALL_ROWS),
    )
    slot_grads, d_query, dkv, d_mid, small = kernel_call(
        functools.partial(
            attend_back_kernel,
            dims,
            seq_count,
            attn_tiles,
            (tile_count, slot_count),
            (seq_count * sum(rows_per[:-1]), rows_per[-1], glob_cells, glob_block),
        ),
        "attend_back",
        32,
        last_shapes,
        [scalars(), scalars(), whole(norm_shape.shape)]
        + specs(ins)
        + [spec_out]
        + specs([rel_low, glob_bias, norm_params])
        + [any_space()],
        (any_space(),) + tuple(specs(last_shapes[1:])),
        [
            pltpu.VMEM((row_count, head_cols), BF),
            pltpu.VMEM((row_count, model_dim), BF),
            pltpu.VMEM((2 * head_cols // LANES, seqs * span, LANES), F32),
            pltpu.VMEM((head_cols, model_dim), BF),
            pltpu.VMEM((model_dim, head_cols), BF),
            pltpu.VMEM((model_dim, head_cols), BF),
            pltpu.VMEM((model_dim, head_cols), BF),
            pltpu.VMEM((side, side), BF),
            pltpu.VMEM((LABEL_PAD, head_cols), F32),
            pltpu.VMEM((8, head_cols), F32),
            pltpu.VMEM((8, model_dim), F32),
            pltpu.VMEM((seq_count * glob_cells, LANES), F32),
            pltpu.VMEM((seq_count * glob_cells, LANES), BF),
            pltpu.SemaphoreType.DMA((6,)),
        ],
        {3 + len(ins) + 4: 0},
        flops=8 * 10**9,
        bytes_moved=2 * 10**7,
    )(block_now, place_rows, norm_two_grad, *ins, wall, rel_low, glob_bias, norm_params, slot_grads)

    bits = seq_bits(seq_count)
    carried = [
        [(RIM, (dkv, seq * span + at)) for seq in range(seqs)] for at in (0, RIM + block_len)
    ]
    sums, small, (to_last, to_next) = scatter_rows(
        slot_grads, rows_per, orders, small, bits[3:] + bits[:3], carried
    )
    from_next = lax.ppermute(to_last, "seq", [(i + 1, i) for i in range(seq_count - 1)])
    from_last = lax.ppermute(to_next, "seq", [(i, i + 1) for i in range(seq_count - 1)])

    weights_at = (kv_at, q_at)
    weights_held = [
        pltpu.VMEM((model_dim, model_dim), BF),
        pltpu.VMEM((model_dim, head_cols), BF),
        pltpu.SemaphoreType.DMA((2,)),
    ]
    dx_shapes = (
        jax.ShapeDtypeStruct(x_long.shape, F32),
        jax.ShapeDtypeStruct(x_long.shape, BF),
    )
    ins = [d_query, dkv, from_next, from_last, d_mid]
    dx_kept, dx_sent = kernel_call(
        functools.partial(dx_kernel, dims, weights_at),
        "dx_long",
        20,
        dx_shapes,
        [scalars()] + specs(ins) + [any_space()],
        tuple(specs(dx_shapes)),
        [pltpu.VMEM((seqs * block_len, 3 * head_cols), BF)] + weights_held,
        flops=10**9,
        bytes_moved=10**7,
    )(half_now, *ins, wall)
    dx_long = dx_kept + swap_cores(dx_sent).astype(F32)
    glob_shapes = (
        jax.ShapeDtypeStruct(x_glob.shape, F32),
        jax.ShapeDtypeStruct(x_glob.shape, BF),
    )
    ins = [d_query, sums[0], sums[1], d_mid]
    dx_kept, dx_sent = kernel_call(
        functools.partial(dx_glob_kernel, dims, weights_at),
        "dx_glob",
        12,
        glob_shapes,
        [scalars()] + specs(ins) + [any_space()],
        tuple(specs(glob_shapes)),
        [pltpu.VMEM((glob_cells, LANES), F32)] + weights_held,
        flops=10**8,
        bytes_moved=10**6,
    )(half_now, *ins, wall)
    dx_glob = dx_kept + swap_cores(dx_sent).astype(F32)

    state = (w_master, m_old, v_old, left_basis, right_basis, left_stats, right_stats)
    others = (rel_table, rel_m, rel_v, norm_params, norm_m, norm_v)
    new_state = soap_update(sums, small, state, others)
    w_new, m_new, v_new, left_q, right_q, left_s, right_s = new_state[:7]
    rel_new, rel_m_new, rel_v_new, norm_new, norm_m_new, norm_v_new = new_state[7:]
    return (
        y_long,
        y_glob,
        dx_long,
        dx_glob,
        w_new,
        m_new,
        v_new,
        left_q,
        right_q,
        left_s,
        right_s,
        rel_new,
        rel_m_new,
        rel_v_new,
        norm_new,
        norm_m_new,
        norm_v_new,
    )


def solution(mesh):
    in_specs = (
        P(None, ("seq", "ffn"), None),
        P(None, ("seq", "ffn"), None),
        P(None, "seq", None),
        P(None, ("seq", "ffn"), None),
        P(None, ("seq", "ffn"), None),
        P(),
        P(("seq", "ffn"), None, None),
        P(("seq", "ffn"), None, None),
        P(("seq", "ffn"), None, None),
        P(("seq", "ffn"), None, None),
        P(("seq", "ffn"), None, None),
        P(("seq", "ffn"), None, None),
        P(("seq", "ffn"), None, None),
        P(None, "ffn"),
        P(None, "ffn"),
        P(None, "ffn"),
        P(),
        P(),
        P(),
    )
    out_specs = (
        P(None, ("seq", "ffn"), None),
        P(None, ("seq", "ffn"), None),
        P(None, ("seq", "ffn"), None),
        P(None, ("seq", "ffn"), None),
        P(("seq", "ffn"), None, None),
        P(("seq", "ffn"), None, None),
        P(("seq", "ffn"), None, None),
        P(("seq", "ffn"), None, None),
        P(("seq", "ffn"), None, None),
        P(("seq", "ffn"), None, None),
        P(("seq", "ffn"), None, None),
        P(None, "ffn"),
        P(None, "ffn"),
        P(None, "ffn"),
        P(),
        P(),
        P(),
    )
    return jax.shard_map(
        on_device, mesh=mesh, in_specs=in_specs, out_specs=out_specs, check_vma=False
    )
```

```python
import functools
import math

import jax
import jax.numpy as jnp
from jax import lax
from jax.experimental import pallas as pl
from jax.experimental.pallas import tpu as pltpu
from jax.sharding import PartitionSpec as P

HEADS = 12
FF = 3072
RADIUS = 84
STEP = 10

BETA_ONE = 0.9
BETA_TWO = 0.95
LEARN_RATE = 0.02
ADAM_RATE = 0.6
WEIGHT_DECAY = 0.01
ADAM_EPS = 1e-08
NORM_EPS = 1e-12
NEG_FILL = -1e30
BF = jnp.bfloat16
F32 = jnp.float32


def seq_bits(count):
    return [1 << at for at in range(count.bit_length() - 1)]


def swap_with(values, bit):
    count = lax.axis_size("seq")
    return lax.ppermute(values, "seq", [(i, i ^ bit) for i in range(count)])


def slot_parts(slots, count):
    bits = seq_bits(count)
    low, high = bits[:3], bits[3:]
    cuts = [slots * at // 14 for at in (0, 5, 10, 14)]
    orders = [low[at:] + low[:at] + high for at in range(3)]
    return [(a, b, order) for a, b, order in zip(cuts, cuts[1:], orders) if b > a]


def part_rows(parts, side, extra):
    rows = [(last - first) * side for first, last, _ in parts]
    return rows[:-1] + [rows[-1] + extra]


def slot_places(owners, slots, rows, side):
    count = lax.axis_size("seq")
    apart = (owners // slots) ^ lax.axis_index("seq")
    inner = owners % slots
    place, row, base = jnp.zeros_like(owners), jnp.zeros_like(owners), 0
    for (first, last, order), many in zip(slot_parts(slots, count), rows):
        index = jnp.zeros_like(owners)
        for at, bit in enumerate(order):
            index = index + jnp.where((apart & bit) != 0, count >> (at + 1), 0)
        here = (inner >= first) & (inner < last)
        place = jnp.where(here, first * count + index * (last - first) + inner - first, place)
        row = jnp.where(here, base + index * many + (inner - first) * side, row)
        base += many * count
    return place, row


FAR_SIZE = 3 * 2**20


def move_kernel(plan, arrays, *refs):
    ins, outs, held, sems = refs[:arrays], refs[arrays : arrays + len(plan)], refs[arrays + len(plan) : -1], refs[-1]
    copies, sums, sem = [], [], 0
    for out, runs in zip(outs, plan):
        base = 0
        for rows, *terms in runs:
            here = out.at[pl.ds(base, rows)]
            targets = [here] if len(terms) == 1 else [held[len(sums) * 2 + k] for k in range(2)]
            waits = []
            for (at, start), target in zip(terms, targets):
                waits.append(pltpu.make_async_copy(ins[at].at[pl.ds(start, rows)], target, sems.at[sem]))
                waits[-1].start()
                sem += 1
            if len(terms) == 1:
                copies += waits
            else:
                sums.append((waits, targets, out, base, rows))
            base += rows
    for waits, (one, two), out, base, rows in sums:
        for wait in waits:
            wait.wait()
        step = next(s for s in (128, 112, 64, 48, 32, 16) if rows % s == 0)

        def add(i, carry):
            at = pl.multiple_of(i * step, 16)
            total = one[pl.ds(at, step), :].astype(F32) + two[pl.ds(at, step), :].astype(F32)
            out[pl.ds(base + at, step), :] = total.astype(BF)
            return carry

        lax.fori_loop(0, rows // step, add, 0)
    for copy in copies:
        copy.wait()


def move_rows(outputs):
    arrays, plan, scratch, count = [], [], [], 0
    for runs in outputs:
        plan.append([])
        for rows, *terms in runs:
            places = []
            for array, start in terms:
                found = [i for i, other in enumerate(arrays) if other is array]
                if not found:
                    arrays.append(array)
                places.append((found[0] if found else len(arrays) - 1, start))
                count += 1
            plan[-1].append((rows, *places))
            if len(terms) == 2:
                scratch += [pltpu.VMEM((rows, terms[0][0].shape[1]), BF)] * 2
    shapes = [(sum(run[0] for run in runs), runs[0][1][0].shape[1]) for runs in outputs]
    return pl.pallas_call(
        functools.partial(move_kernel, plan, len(arrays)),
        grid=(1,),
        out_shape=tuple(jax.ShapeDtypeStruct(shape, BF) for shape in shapes),
        in_specs=[
            pl.BlockSpec(memory_space=pltpu.HBM if array.size > FAR_SIZE else pl.ANY) for array in arrays
        ],
        out_specs=tuple(whole(shape) for shape in shapes),
        scratch_shapes=scratch + [pltpu.SemaphoreType.DMA((count,))],
        cost_estimate=pl.CostEstimate(
            flops=0, bytes_accessed=sum(6 * math.prod(s) for s in shapes), transcendentals=0
        ),
        compiler_params=pltpu.CompilerParams(vmem_limit_bytes=16 * 2**20),
        name="add_rows" if scratch else "join_rows",
    )(*arrays)


def run_sum(rows, one, one_at, two, two_at):
    return (rows, (one, one_at), (two, two_at))


def gather_rows(cells, extra, rows, orders):
    own = sum(rows)
    shared = orders[0][3:][::-1]
    got = [swap_with(values, shared[0]) for values in (cells, extra)]
    devices = [[(cells, 0), (extra, -cells.shape[0])], [(got[0], 0), (got[1], -cells.shape[0])]]
    if len(shared) > 1:
        (cells,) = move_rows([[(array.shape[0], (array, 0)) for runs in devices for array, _ in runs]])
        for bit in shared[1:-1]:
            got = swap_with(cells, bit)
            (cells,) = move_rows([[(cells.shape[0], (cells, 0)), (cells.shape[0], (got, 0))]])
        got = swap_with(cells, shared[-1])
        devices = [[(run, i * own)] for run in (cells, got) for i in range(cells.shape[0] // own)]
    starts = [sum(rows[:at]) for at in range(len(rows))]

    def runs_of(start, many):
        runs = []
        for pieces in devices:
            left, at = many, start
            for array, shift in pieces:
                here = min(left, array.shape[0] - (at + shift))
                if here > 0:
                    runs.append((here, (array, at + shift)))
                    left, at = left - here, at + here
        return runs

    parts = move_rows([runs_of(start, many) for start, many in zip(starts, rows)])
    for step in (2, 1):
        got = [swap_with(part, order[step]) for part, order in zip(parts, orders)]
        parts = move_rows([[(p.shape[0], (p, 0)), (p.shape[0], (g, 0))] for p, g in zip(parts, got)])
    got = [swap_with(part, order[0]) for part, order in zip(parts, orders)]
    return list(zip(parts, got))


def scatter_rows(cells, rows, orders, everywhere, order_everywhere, carried):
    count = lax.axis_size("seq")
    spans = [count * many for many in rows]
    starts = [sum(spans[:at]) for at in range(len(spans))]
    sends = [cells[a + r // 2 : a + r] for a, r in zip(starts, spans)]
    kept = move_rows([[(r // 2, (cells, a))] for a, r in zip(starts, spans)])
    kept = [(keep, 0, keep.shape[0]) for keep in kept]

    def all_sum():
        return [run_sum(everywhere.shape[0], everywhere, 0, all_got, 0)]

    for step in range(3):
        got = [swap_with(send, order[step]) for send, order in zip(sends, orders)]
        all_got = swap_with(everywhere, order_everywhere[step])
        halves = [r // 2 for _, _, r in kept]
        if step < 2:
            *sends, everywhere = move_rows(
                [[run_sum(h, k, a + h, g, h)] for h, (k, a, _), g in zip(halves, kept, got)] + [all_sum()]
            )
            keeps = move_rows([[run_sum(h, k, a, g, 0)] for h, (k, a, _), g in zip(halves, kept, got)])
            kept = [(keep, 0, h) for keep, h in zip(keeps, halves)]
    devices = count // 8

    def merged(at, many):
        return [
            run_sum(r, k, i * r, g, i * r)
            for i in range(at, at + many)
            for r, (k, _, _), g in zip(rows, kept, got)
        ]

    half = devices // 2
    send, everywhere, *carried = move_rows([merged(half, half), all_sum()] + carried)
    (keep,) = move_rows([merged(0, half)])
    for step, bit in enumerate(orders[0][3:]):
        got_all = swap_with(send, bit)
        all_got = swap_with(everywhere, order_everywhere[3 + step])
        if bit == orders[0][-1]:
            return (keep, got_all), (everywhere, all_got), carried
        half = keep.shape[0] // 2
        send, everywhere = move_rows([[run_sum(half, keep, half, got_all, half)], all_sum()])
        (keep,) = move_rows([[run_sum(half, keep, 0, got_all, 0)]])
    return None


def split_two(x):
    hi = x.astype(BF)
    return hi, (x - hi.astype(F32)).astype(BF)


def split_three(x):
    hi = x.astype(BF)
    rest = x - hi.astype(F32)
    mid = rest.astype(BF)
    return hi, mid, (rest - mid.astype(F32)).astype(BF)


def left_six(parts, axis):
    h, m, l = parts
    return jnp.concatenate([h, h, m, m, h, l], axis=axis)


def right_six(parts, axis):
    h, m, l = parts
    return jnp.concatenate([h, m, h, m, l, h], axis=axis)


def left_three(parts, axis):
    h, l = parts
    return jnp.concatenate([h, h, l], axis=axis)


def right_three(parts, axis):
    h, l = parts
    return jnp.concatenate([h, l, h], axis=axis)


def dot_on(a, b, ca, cb):
    return lax.dot_general(a, b, (((ca,), (cb,)), ((), ())), preferred_element_type=F32)


def dot_six(a, b, ca, cb):
    return dot_on(left_six(split_three(a), ca), right_six(split_three(b), cb), ca, cb)


def dot_one(a, b, ca, cb):
    return dot_on(a.astype(BF), b.astype(BF), ca, cb)


def dot_three(a, b, ca, cb):
    return dot_on(left_three(split_two(a), ca), right_three(split_two(b), cb), ca, cb)


PANEL = 32


def panel_inverse(a_ref, t_ref, npad, side, at):
    groups = PANEL // 8
    iota = lax.broadcasted_iota(jnp.int32, (8, npad), 0)
    a = []
    for i in range(PANEL):
        rows = a_ref[pl.ds(at + i, npad, stride=side), :]
        cols = rows.T[at : at + PANEL]
        a.append([cols[8 * g : 8 * g + 8] for g in range(groups)])
    z = [[None] * groups for _ in range(PANEL)]
    for j in range(PANEL):
        gj, sj = divmod(j, 8)
        r = lax.rsqrt(a[j][gj][sj : sj + 1])
        u = [None if g < gj else a[j][g] * r for g in range(groups)]
        below = list(u)
        below[gj] = jnp.where(iota > sj, u[gj], 0.0)
        for k in range(j + 1, PANEL):
            gk, sk = divmod(k, 8)
            row = u[gk][sk : sk + 1]
            for g in range(gk, groups):
                a[k][g] = a[k][g] - u[g] * row
        for c in range(j):
            row = z[c][gj][sj : sj + 1] * r
            z[c][gj] = jnp.where(iota == sj, row, z[c][gj]) - below[gj] * row
            for g in range(gj + 1, groups):
                z[c][g] = z[c][g] - u[g] * row
        z[j] = [
            jnp.zeros((8, npad), F32)
            if g < gj
            else (jnp.where(iota == sj, r, 0.0) - below[g] * r if g == gj else -u[g] * r)
            for g in range(groups)
        ]
    fill = jnp.zeros((side - PANEL, npad), F32)
    for c in range(PANEL):
        t_ref[pl.ds(c, npad, stride=PANEL), :] = jnp.concatenate(z[c] + [fill], axis=0).T


def adam_step(grad, refs, outs, where, decay_rate):
    param, first_mom, second_mom = [ref[where] for ref in refs]
    first_mom = BETA_ONE * first_mom + (1.0 - BETA_ONE) * grad
    second_mom = BETA_TWO * second_mom + (1.0 - BETA_TWO) * grad * grad
    direction = (
        first_mom
        / (1.0 - BETA_ONE**STEP)
        / (jnp.sqrt(second_mom / (1.0 - BETA_TWO**STEP)) + ADAM_EPS)
    )
    outs[0][where] = param - ADAM_RATE * (direction + decay_rate * param)
    outs[1][where] = first_mom
    outs[2][where] = second_mom


def small_updates(small_refs, refs, outs):
    total = small_refs[0][...].astype(F32) + small_refs[1][...].astype(F32)
    labels, cols = refs[0].shape
    rel = pltpu.roll(total, total.shape[0] - (RIM - RADIUS), 0)[:labels]
    adam_step(rel, refs[:3], outs[:3], (slice(None), slice(None)), WEIGHT_DECAY)
    halves = refs[3].shape[1] // cols
    for row in range(refs[3].shape[0]):
        for half in range(halves):
            at = SMALL_ROWS - 8 + row * halves + half
            where = (slice(row, row + 1), slice(half * cols, (half + 1) * cols))
            adam_step(total[at : at + 1], refs[3:], outs[3:], where, 0.0)


def soap_kernel(npad, kept_ref, got_ref, small_ref, small_got_ref, *refs):
    state, done = refs[:7], refs[13:20]
    given, a_ref, y_ref, mat_ref, t_ref, out_sems = refs[26:]
    n, side = state[0].shape[:2]
    many = next(k for k in (7, 2, 1) if n % k == 0)
    batch = next(b for b in (14, 7, 4, 2) if 2 * n % b == 0)
    small_updates((small_ref, small_got_ref), refs[7:13], refs[20:26])
    eye = (
        lax.broadcasted_iota(jnp.int32, (side, side), 0)
        == lax.broadcasted_iota(jnp.int32, (side, side), 1)
    ).astype(F32)

    def first(at, carry):
        slots = [at * many + k for k in range(many)]

        def old(kind):
            return [state[kind][i] for i in slots]

        lefts, rights = old(3), old(4)
        tiles = [pl.ds(pl.multiple_of(i * side, side), side) for i in slots]
        grads = [kept_ref[rows, :].astype(F32) + got_ref[rows, :].astype(F32) for rows in tiles]
        halves = [split_two(x) for x in grads]
        new_l = [
            BETA_TWO * x + (1.0 - BETA_TWO) * dot_on(left_three(p, 1), right_three(p, 1), 1, 1)
            for x, p in zip(old(5), halves)
        ]
        new_r = [
            BETA_TWO * x + (1.0 - BETA_TWO) * dot_on(left_three(p, 0), right_three(p, 0), 0, 0)
            for x, p in zip(old(6), halves)
        ]
        mats = [dot_six(x, y, 1, 0) for x, y in zip(new_l + new_r, lefts + rights)]
        thirds = [split_three(x) for x in mats]
        grams = [dot_on(left_six(p, 0), right_six(p, 0), 0, 0) for p in thirds]
        for k, i in enumerate(slots):
            given[5, i] = new_l[k]
            given[6, i] = new_r[k]
            for kind in range(2):
                mat_ref[2 * i + kind] = mats[kind * many + k]
                rows = pl.ds(pl.multiple_of((2 * i + kind) * side, side), side)
                a_ref[rows, :] = grams[kind * many + k]
                y_ref[rows, :] = eye
        return carry

    def rotate(slots):
        def old(kind):
            return [state[kind][i] for i in slots]

        lefts, rights = old(3), old(4)
        tiles = [slice(i * side, (i + 1) * side) for i in slots]
        grads = [kept_ref[rows, :].astype(F32) + got_ref[rows, :].astype(F32) for rows in tiles]
        turned = [dot_one(x, y, 0, 0) for x, y in zip(lefts, grads)]
        rotated = [dot_one(x, y, 1, 0) for x, y in zip(turned, rights)]
        moms = [BETA_ONE * old_m + (1.0 - BETA_ONE) * x for old_m, x in zip(old(1), rotated)]
        secs = [BETA_TWO * old_v + (1.0 - BETA_TWO) * x * x for old_v, x in zip(old(2), rotated)]
        steps = [
            x / (1.0 - BETA_ONE**STEP) / (jnp.sqrt(y / (1.0 - BETA_TWO**STEP)) + ADAM_EPS)
            for x, y in zip(moms, secs)
        ]
        turned = [dot_one(x, y, 1, 0) for x, y in zip(lefts, steps)]
        backs = [dot_one(x, y, 1, 1) for x, y in zip(turned, rights)]
        for k, (i, weight) in enumerate(zip(slots, old(0))):
            given[0, i] = weight - LEARN_RATE * (backs[k] + WEIGHT_DECAY * weight)
            given[1, i] = moms[k]
            given[2, i] = secs[k]

    def send(kinds):
        copies = [pltpu.make_async_copy(given.at[k], done[k], out_sems.at[k]) for k in kinds]
        for copy in copies:
            copy.start()
        return copies

    lax.fori_loop(0, n // many, first, 0)
    copies = send((5, 6))
    if npad > 2 * n:
        a_ref[2 * n * side :, :] = jnp.concatenate([eye] * (npad - 2 * n), axis=0)
    for at in range(0, side, PANEL):
        beside = range(at * n // side, (at + PANEL) * n // side)
        rotate(list(beside))
        panel_inverse(a_ref, t_ref, npad, side, at)

        def update(i, carry):
            bases = [pl.multiple_of((i * batch + b) * side, side) for b in range(batch)]
            rows = [pl.ds(base + at, PANEL) for base in bases]
            both = [jnp.concatenate([a_ref[r, :], y_ref[r, :]], axis=1) for r in rows]
            turns = [
                t_ref[pl.ds(pl.multiple_of((i * batch + b) * PANEL, PANEL), PANEL), :][:, :PANEL]
                for b in range(batch)
            ]
            if at + PANEL < side:
                rest = [pl.ds(base + at + PANEL, side - at - PANEL) for base in bases]
                old = [(a_ref[r, :], y_ref[r, :]) for r in rest]
            fresh = [dot_six(t, x, 0, 0) for t, x in zip(turns, both)]
            if at + PANEL < side:
                changes = []
                for x in fresh:
                    parts = split_three(x)
                    cut = tuple(p[:, at + PANEL : side] for p in parts)
                    changes.append(dot_on(left_six(cut, 0), right_six(parts, 0), 0, 0))
                for r, (old_a, old_y), change in zip(rest, old, changes):
                    a_ref[r, :] = old_a - change[:, :side]
                    y_ref[r, :] = old_y - change[:, side:]
            for r, x in zip(rows, fresh):
                y_ref[r, :] = x[:, side:]
            return carry

        lax.fori_loop(0, 2 * n // batch, update, 0)

    copies += send((0, 1, 2))

    def last(at, carry):
        slots = [at * many + k for k in range(many)]
        both = [2 * i + k for i in slots for k in range(2)]
        mats = [mat_ref[j] for j in both]
        turns = [y_ref[pl.ds(pl.multiple_of(j * side, side), side), :] for j in both]
        bases = [dot_three(x, y, 1, 1) for x, y in zip(mats, turns)]
        for k, i in enumerate(slots):
            for kind in range(2):
                given[3 + kind, i] = bases[2 * k + kind]
                target = done[3 + kind].at[i]
                pltpu.make_async_copy(given.at[3 + kind, i], target, out_sems.at[3 + kind]).start()
        return carry

    lax.fori_loop(0, n // many, last, 0)
    for copy in copies:
        copy.wait()
    for kind in (3, 4):
        pltpu.make_async_copy(given.at[kind], done[kind], out_sems.at[kind]).wait()


def soap_update(grads, small, state, others):
    n, side = state[0].shape[:2]
    npad = -(-2 * n // 8) * 8
    ins = [*grads, *small, *state, *others]
    outs = [*state, *others]
    return pl.pallas_call(
        functools.partial(soap_kernel, npad),
        grid=(1,),
        out_shape=tuple(jax.ShapeDtypeStruct(s.shape, F32) for s in outs),
        in_specs=[whole(array.shape) for array in ins],
        out_specs=(far_space(),) * len(state) + tuple(whole(array.shape) for array in others),
        scratch_shapes=[
            pltpu.VMEM((7, n, side, side), F32),
            pltpu.VMEM((npad * side, side), F32),
            pltpu.VMEM((npad * side, side), F32),
            pltpu.VMEM((2 * n, side, side), F32),
            pltpu.VMEM((npad * PANEL, side), F32),
            pltpu.SemaphoreType.DMA((7,)),
        ],
        cost_estimate=pl.CostEstimate(
            flops=n * 40 * side**3, bytes_accessed=n * 60 * side * side, transcendentals=0
        ),
        compiler_params=pltpu.CompilerParams(vmem_limit_bytes=32 * 2**20),
        name="soap",
    )(*ins)


LANES = 128
LABEL_PAD = 256
RIM = 96
SMALL_ROWS = 192


def up_to(value, unit):
    return -(-value // unit) * unit


def block_at(shape, *index):
    return pl.BlockSpec(shape, lambda i: index, pipeline_mode=pl.Buffered(1))


def whole(shape):
    return block_at(shape, *[0] * len(shape))


def any_space():
    return pl.BlockSpec(memory_space=pl.ANY)


def far_space():
    return pl.BlockSpec(memory_space=pltpu.HBM)


def scalars():
    return pl.BlockSpec(memory_space=pltpu.SMEM)


def kernel_call(body, name, mib, out_shape, in_specs, out_specs, scratch=(), aliases=None, flops=0, bytes_moved=0):
    return pl.pallas_call(
        body,
        name=name,
        grid=(1,),
        out_shape=out_shape,
        in_specs=in_specs,
        out_specs=out_specs,
        scratch_shapes=list(scratch),
        input_output_aliases=aliases or {},
        cost_estimate=pl.CostEstimate(flops=flops, bytes_accessed=bytes_moved, transcendentals=0),
        compiler_params=pltpu.CompilerParams(vmem_limit_bytes=mib * 2**20),
    )


def start_tiles(row_ref, col_ref, kind_ref, sources, tiles, wall_ref, sems):
    base = 0
    for source, many in zip(sources, tiles):

        def start(i, carry):
            for k in range(many):
                place = base + i * many + k
                kind = kind_ref[place]

                @pl.when(kind < 2)
                def _():
                    row = pl.multiple_of(row_ref[place], LANES)
                    col = pl.multiple_of(col_ref[place], LANES)
                    pltpu.make_async_copy(
                        source.at[i, pl.ds(k * LANES, LANES)],
                        wall_ref.at[pl.ds(row, LANES), pl.ds(col, LANES)],
                        sems.at[kind],
                    ).start()

            return carry

        lax.fori_loop(0, source.shape[0], start, 0)
        base += source.shape[0] * many


def wait_rows(wall_ref, rows, sem):
    part = wall_ref.at[pl.ds(0, rows)]
    pltpu.make_async_copy(part, part, sem).wait()


def low_lanes(rows):
    return lax.broadcasted_iota(jnp.int32, (rows, LANES), 1) < LANES // 2


def stack_heads(pair):
    low = low_lanes(pair.shape[0])
    zero = jnp.zeros_like(pair)
    return jnp.concatenate([jnp.where(low, pair, zero), jnp.where(low, zero, pair)], axis=0)


def merge_stack(stacked):
    rows = stacked.shape[0] // 2
    return jnp.where(low_lanes(rows), stacked[:rows], stacked[rows:])


def skew(table, width):
    rows = table.shape[0] // 2
    padded = jnp.concatenate(
        [table, jnp.zeros((table.shape[0], width - table.shape[1]), F32)], axis=1
    )
    halves = [
        pltpu.roll(padded[at : at + rows], 0, 1, stride=1, stride_axis=0) for at in (0, rows)
    ]
    return jnp.concatenate(halves, axis=0)


def unskew(grid, width):
    rows = grid.shape[0] // 2
    lanes = grid.shape[1]
    parts = []
    for at in range(0, 2 * rows, 8):
        shift = (at % rows) % lanes
        part = grid[at : at + 8]
        parts.append(part if shift == 0 else pltpu.roll(part, lanes - shift, 1))
    moved = jnp.concatenate([part[:, :width] for part in parts], axis=0)
    lanes = width
    index = lax.broadcasted_iota(jnp.int32, moved.shape, 0)
    for bit in (1, 2, 4):
        moved = jnp.where((index & bit) != 0, pltpu.roll(moved, lanes - bit, 1), moved)
    return moved


def softmax_rows(scores):
    top = jnp.max(scores, axis=-1, keepdims=True)
    raised = jnp.exp(scores - top)
    return raised * (1.0 / jnp.sum(raised, axis=-1, keepdims=True))


def window_keys(ref, base, at, width, ext, globs, cols):
    return jnp.concatenate(
        [ref[pl.ds(base + at, width), cols], ref[pl.ds(base + ext, globs), cols]], axis=0
    )


def glob_row_mask(shape, seq, glob_block):
    row = lax.broadcasted_iota(jnp.int32, shape, 0) % (shape[0] // 2)
    return (row >= seq * glob_block) & (row < (seq + 1) * glob_block)


def window_bias(block, blocks, chunk, dims):
    _, block_len, _, _, width, globs, _ = dims
    shape = (2 * LANES, width + globs)
    key = lax.broadcasted_iota(jnp.int32, shape, 1)
    query = lax.broadcasted_iota(jnp.int32, shape, 0) % LANES
    offset = key - query - (RIM - RADIUS)
    token = block * block_len - RIM + chunk * LANES + key
    near = (offset >= 0) & (offset <= 2 * RADIUS) & (token >= 0) & (token < blocks * block_len)
    return jnp.where(near | (key >= width), 0.0, NEG_FILL)


def attend_kernel(dims, wall_at, blocks, row_ref, col_ref, kind_ref, block_ref, xr_ref, rel_ref, gbias_ref,
                  left_ref, right_ref, *refs):
    q_ref, k_ref, v_ref, o_ref, part_ref, xe_ref, wall_out, wall_ref, glob_low, glob_cells, sems = refs[-11:]
    sources = refs[:-11]
    seqs, block_len, glob_block, ext, width, globs, scale = dims
    feed_rows, attn_rows, kv_at, q_at, out_at, tiles = wall_at
    model_dim = xr_ref.shape[1]
    head_cols = q_ref.shape[1]
    start_tiles(row_ref, col_ref, kind_ref, sources, tiles, wall_ref, sems)
    span = ext + globs
    cells = glob_low.shape[0] // blocks
    copies, base = [], 0
    for source in sources[-2:]:
        rows = source.shape[1] - cells
        for i in range(source.shape[0]):
            copies.append((source.at[i, pl.ds(rows, cells)], glob_low.at[pl.ds(base, cells)]))
            base += cells
    for source, target in copies:
        pltpu.make_async_copy(source, target, sems.at[3]).start()
    for seq in range(seqs):
        at = seq * span
        rim = pl.ds(seq * RIM, RIM)
        pltpu.make_async_copy(left_ref.at[rim], xe_ref.at[pl.ds(at, RIM)], sems.at[4]).start()
        pltpu.make_async_copy(
            right_ref.at[rim], xe_ref.at[pl.ds(at + RIM + block_len, RIM)], sems.at[4]
        ).start()
        at += RIM
        xe_ref[at : at + block_len] = xr_ref[seq * block_len : (seq + 1) * block_len]
        at += block_len + RIM
        if ext > block_len + 2 * RIM:
            xe_ref[at : seq * span + ext] = jnp.zeros((ext - block_len - 2 * RIM, model_dim), BF)
    pltpu.make_async_copy(glob_low, glob_low, sems.at[3]).wait()
    glob_cells[...] = glob_low[...].astype(F32)
    cols = model_dim // LANES
    for seq in range(seqs):
        for r in range(glob_block):
            at = seq * span + ext + r * blocks
            for c in range(cols):
                source = pl.ds((seq * glob_block + r) * cols + c, blocks, stride=cells)
                xe_ref[at : at + blocks, c * LANES : (c + 1) * LANES] = glob_cells[source, :].astype(BF)
    rims = xe_ref.at[pl.ds(0, 2 * seqs * RIM)]
    pltpu.make_async_copy(rims, rims, sems.at[4]).wait()
    wait_rows(wall_ref, attn_rows, sems.at[0])
    wq_ref = wall_ref.at[pl.ds(q_at, model_dim), pl.ds(0, head_cols)]
    wkv_ref = wall_ref.at[pl.ds(kv_at, model_dim)]
    wo_ref = wall_ref.at[pl.ds(out_at, head_cols)]
    pairs = head_cols // LANES
    glob_at = seqs * block_len
    glob_rows = q_ref.shape[0] - glob_at
    span = ext + globs
    chunks = block_len // LANES
    q_ref[...] = dot_on(xr_ref[...], wq_ref[...], 1, 0).astype(BF)

    def project(i, carry):
        rows = pl.ds(pl.multiple_of(i * 256, 256), 256)
        both = dot_on(xe_ref[rows, :], wkv_ref[...], 1, 0).astype(BF)
        k_ref[rows, :] = both[:, :head_cols]
        v_ref[rows, :] = both[:, head_cols:]
        return carry

    lax.fori_loop(0, seqs * span // 256, project, 0)
    wait_rows(wall_ref, feed_rows, sems.at[1])
    keep = pltpu.make_async_copy(wall_ref, wall_out, sems.at[2])
    keep.start()

    def window(i, carry):
        seq, chunk = i // chunks, i % chunks
        rows = pl.ds(pl.multiple_of(i * LANES, LANES), LANES)
        base = pl.multiple_of(seq * span, LANES)
        at = pl.multiple_of(chunk * LANES, LANES)
        bias = window_bias(block_ref[0], blocks, chunk, dims)
        cols = [slice(pair * LANES, (pair + 1) * LANES) for pair in range(pairs)]
        query = [stack_heads(q_ref[rows, c] * scale) for c in cols]
        keys = [window_keys(k_ref, base, at, width, ext, globs, c) for c in cols]
        values = [window_keys(v_ref, base, at, width, ext, globs, c) for c in cols]
        near = [dot_on(q, rel_ref[:, c], 1, 1) for q, c in zip(query, cols)]
        scores = [dot_on(q, k, 1, 1) for q, k in zip(query, keys)]
        scores = [x + skew(y, width + globs) + bias for x, y in zip(scores, near)]
        weights = [softmax_rows(x).astype(BF) for x in scores]
        outs = [merge_stack(dot_on(w, v, 1, 0)).astype(BF) for w, v in zip(weights, values)]
        for c, out in zip(cols, outs):
            o_ref[rows, c] = out
        return carry

    lax.fori_loop(0, seqs * chunks, window, 0)
    rows = slice(glob_at, glob_at + glob_rows)
    both = [(pair, seq) for pair in range(pairs) for seq in range(seqs)]
    cols = [slice(pair * LANES, (pair + 1) * LANES) for pair in range(pairs)]
    spans = [slice(seq * span, (seq + 1) * span) for seq in range(seqs)]
    query = [stack_heads(q_ref[rows, c] * scale) for c in cols]
    bias = [jnp.concatenate([gbias_ref[seq]] * 2, axis=0) for seq in range(seqs)]
    scores = [dot_on(query[pair], k_ref[spans[seq], cols[pair]], 1, 1) + bias[seq] for pair, seq in both]
    weights = [softmax_rows(x).astype(BF) for x in scores]
    outs = [dot_on(w, v_ref[spans[seq], cols[pair]], 1, 0) for w, (pair, seq) in zip(weights, both)]
    for pair in range(pairs):
        total = outs[pair * seqs]
        for seq in range(1, seqs):
            total = jnp.where(glob_row_mask(total.shape, seq, glob_block), outs[pair * seqs + seq], total)
        used = lax.broadcasted_iota(jnp.int32, total.shape, 0) % glob_rows < seqs * glob_block
        o_ref[rows, cols[pair]] = merge_stack(jnp.where(used, total, 0.0)).astype(BF)
    part_ref[...] = dot_on(o_ref[...], wo_ref[...], 1, 0).astype(BF)
    keep.wait()


def norm_parts(values):
    center = values - jnp.mean(values, axis=-1, keepdims=True)
    spread = jnp.mean(center * center, axis=-1, keepdims=True)
    rate = lax.rsqrt(spread + NORM_EPS)
    return center * rate, rate


def norm_back(grad, normed, rate, gain):
    scaled = grad * gain
    return (
        scaled
        - jnp.mean(scaled, axis=-1, keepdims=True)
        - normed * jnp.mean(scaled * normed, axis=-1, keepdims=True)
    ) * rate


def row_loop(total, body):
    step = 176 if total % 176 == 0 else 16

    def run(i, carry):
        body(pl.ds(pl.multiple_of(i * step, 16), step))
        return carry

    lax.fori_loop(0, total // step, run, 0)


def col_loop(total, body, step=256):
    def run(i, carry):
        body(i)
        return carry

    lax.fori_loop(0, total // step, run, 0)


GELU_RATE = 0.7978845608028654
GELU_CUBE = 0.044715


def gelu_parts(u):
    square = u * u
    curve = jnp.tanh(GELU_RATE * u * (1.0 + GELU_CUBE * square))
    return square, curve


def feed_kernel(xr_ref, part_ref, got_ref, norm_ref, wu_ref, wd_ref, h_ref, hb_ref, u_ref, a_ref, down_ref):
    model_dim = xr_ref.shape[1]
    gain, offset = norm_ref[0:1], norm_ref[1:2]

    def norm(rows):
        mid = xr_ref[rows, :].astype(F32) + (part_ref[rows, :].astype(F32) + got_ref[rows, :].astype(F32))
        normed, _ = norm_parts(mid)
        out = normed * gain + offset
        h_ref[rows, :] = out
        hb_ref[rows, :] = out.astype(BF)

    row_loop(xr_ref.shape[0], norm)
    per_half = model_dim // 256

    def up(j):
        rows = pl.ds(pl.multiple_of((j // per_half) * model_dim, 256), model_dim)
        cols = pl.ds(pl.multiple_of((j % per_half) * 256, 256), 256)
        here = pl.ds(pl.multiple_of(j * 256, 256), 256)
        u = dot_on(hb_ref[...], wu_ref[rows, cols], 1, 0)
        u_ref[:, here] = u
        _, curve = gelu_parts(u)
        a_ref[:, here] = (0.5 * u * (1.0 + curve)).astype(BF)

    col_loop(u_ref.shape[1], up)

    def down(j):
        cols = pl.ds(pl.multiple_of(j * 256, 256), 256)
        down_ref[:, cols] = dot_on(a_ref[...], wd_ref[:, cols], 1, 0).astype(BF)

    col_loop(model_dim, down)


def own_rows(ref, half, seqs, block_len, glob_block):
    per = block_len // 2
    long_part = [
        ref[pl.ds(pl.multiple_of(seq * block_len + half * per, per), per), :] for seq in range(seqs)
    ]
    base, few = seqs * block_len, glob_block // 2
    globs = ref[base:, :]
    glob_part = [
        jnp.where(
            half == 0,
            globs[seq * glob_block : seq * glob_block + few],
            globs[seq * glob_block + few : (seq + 1) * glob_block],
        )
        for seq in range(seqs)
    ]
    return long_part, glob_part


def feed_back_kernel(dims, half_ref, h_ref, down_ref, got_ref, u_ref, dy_ref, norm_ref, wu_ref, wd_ref,
                     y_long_ref, y_glob_ref, dx_ref, dxb_ref, du_ref, dh_ref, gn_ref, y_ref):
    model_dim = h_ref.shape[1]
    gain, offset = norm_ref[2:3], norm_ref[3:4]
    gn_ref[...] = jnp.zeros_like(gn_ref)

    def norm(rows):
        out = h_ref[rows, :] + (down_ref[rows, :].astype(F32) + got_ref[rows, :].astype(F32))
        normed, rate = norm_parts(out)
        y_ref[rows, :] = normed * gain + offset
        grad = dy_ref[rows, :].astype(F32)
        gn_ref[0:1] += jnp.sum(grad * normed, axis=0, keepdims=True)
        gn_ref[1:2] += jnp.sum(grad, axis=0, keepdims=True)
        dx = norm_back(grad, normed, rate, gain)
        dx_ref[rows, :] = dx
        dxb_ref[rows, :] = dx.astype(BF)

    row_loop(h_ref.shape[0], norm)
    long_part, glob_part = own_rows(y_ref, half_ref[0], *dims[:3])
    for seq in range(dims[0]):
        y_long_ref[seq] = long_part[seq].astype(BF)
        y_glob_ref[seq] = glob_part[seq].astype(BF)

    def act(j):
        here = pl.ds(pl.multiple_of(j * 256, 256), 256)
        da = dot_on(dxb_ref[...], wd_ref[here, :], 1, 1)
        u = u_ref[:, here]
        square, curve = gelu_parts(u)
        slope = 0.5 * (1.0 + curve) + 0.5 * u * (1.0 - curve * curve) * (
            GELU_RATE * (1.0 + 3.0 * GELU_CUBE * square)
        )
        du_ref[:, here] = (da * slope).astype(BF)

    col_loop(u_ref.shape[1], act)
    halves = u_ref.shape[1] // model_dim

    def lower(j):
        cols = pl.ds(pl.multiple_of(j * 256, 256), 256)
        total = 0.0
        for half in range(halves):
            rows = pl.ds(pl.multiple_of(half * model_dim + j * 256, 256), 256)
            total = total + dot_on(
                du_ref[:, half * model_dim : (half + 1) * model_dim], wu_ref[rows, :], 1, 1
            )
        dh_ref[:, cols] = total.astype(BF)

    col_loop(model_dim, lower)


def send_tiles(stage_ref, row, rows, first, place_ref, out_ref, sem):
    cols = stage_ref.shape[1] // LANES
    for r in range(rows):
        for c in range(cols):
            pltpu.make_async_copy(
                stage_ref.at[pl.ds(row + r * LANES, LANES), pl.ds(c * LANES, LANES)],
                out_ref.at[pl.ds(pl.multiple_of(place_ref[first + r * cols + c], 16), LANES)],
                sem,
            ).start()


def feed_grads_kernel(tiles_at, place_ref, a_ref, dxb_ref, hb_ref, du_ref, out_ref, down_stage, up_stage, sems):
    up_at, down_at = tiles_at
    model_dim = dxb_ref.shape[1]

    def down(j):
        row = pl.multiple_of(j * 256, 256)
        rows = pl.ds(row, 256)
        down_stage[rows, :] = dot_on(a_ref[:, rows], dxb_ref[...], 0, 0).astype(BF)
        send_tiles(down_stage, row, 2, down_at + j * 2 * (model_dim // LANES), place_ref, out_ref, sems.at[0])

    col_loop(a_ref.shape[1], down)

    def up(j):
        row = pl.multiple_of(j * 256, 256)
        rows = pl.ds(row, 256)
        up_stage[rows, :] = dot_on(hb_ref[:, rows], du_ref[...], 0, 0).astype(BF)
        send_tiles(
            up_stage, row, 2, up_at + j * 2 * (du_ref.shape[1] // LANES), place_ref, out_ref, sems.at[1]
        )

    col_loop(model_dim, up)
    pltpu.make_async_copy(down_stage, down_stage, sems.at[0]).wait()
    pltpu.make_async_copy(up_stage, up_stage, sems.at[1]).wait()


def attend_back_kernel(dims, blocks, attn_tiles, tile_counts, glob_at_rows, block_ref, place_ref, norm_two_ref, xr_ref, part_ref, got_ref, dh_ref, dh_got_ref, dx_ref, o_ref,
                       q_ref, k_ref, v_ref, xe_ref, wo_ref, rel_ref, gbias_ref, norm_ref, grads_in,
                       grads_ref, dq_ref, dkv_ref, mid_ref, small_ref,
                       do_ref, midb_ref, dkv_acc, out_stage, q_stage, k_stage, v_stage, none_ref,
                       drel_ref, norms_ref, gn_ref, glob_stage, glob_low, sems):
    seqs, block_len, glob_block, ext, width, globs, scale = dims
    head_cols = q_ref.shape[1]
    pairs = head_cols // LANES
    glob_at = seqs * block_len
    glob_rows = q_ref.shape[0] - glob_at
    span = ext + globs
    chunks = block_len // LANES
    gain = norm_ref[0:1]
    gn_ref[...] = jnp.zeros_like(gn_ref)

    def norm(rows):
        mid = xr_ref[rows, :].astype(F32) + (part_ref[rows, :].astype(F32) + got_ref[rows, :].astype(F32))
        normed, rate = norm_parts(mid)
        grad = dh_ref[rows, :].astype(F32) + dh_got_ref[rows, :].astype(F32) + dx_ref[rows, :]
        gn_ref[0:1] += jnp.sum(grad * normed, axis=0, keepdims=True)
        gn_ref[1:2] += jnp.sum(grad, axis=0, keepdims=True)
        out = norm_back(grad, normed, rate, gain)
        mid_ref[rows, :] = out
        midb_ref[rows, :] = out.astype(BF)

    row_loop(xr_ref.shape[0], norm)
    do_ref[...] = dot_on(midb_ref[...], wo_ref[...], 1, 1).astype(BF)
    out_stage[...] = dot_on(o_ref[...], midb_ref[...], 0, 0).astype(BF)
    send_tiles(out_stage, 0, out_stage.shape[0] // LANES, 3 * attn_tiles, place_ref, grads_ref, sems.at[0])
    none_ref[...] = jnp.zeros_like(none_ref)
    spare = []
    for tile in range(*tile_counts):
        target = grads_ref.at[pl.ds(pl.multiple_of(place_ref[tile], 16), LANES)]
        spare.append(pltpu.make_async_copy(none_ref, target, sems.at[4]))
        spare[-1].start()
    dkv_acc[...] = jnp.zeros_like(dkv_acc)
    drel_ref[...] = jnp.zeros_like(drel_ref)

    def grads_of(scores, grad_out, values):
        weights = softmax_rows(scores)
        dp = dot_on(grad_out, values, 1, 1)
        delta = jnp.sum(weights * dp, axis=-1, keepdims=True)
        return weights.astype(BF), weights * (dp - delta)

    def window(i, carry):
        seq, chunk = i // chunks, i % chunks
        rows = pl.ds(pl.multiple_of(i * LANES, LANES), LANES)
        base = pl.multiple_of(seq * span, LANES)
        at = pl.multiple_of(chunk * LANES, LANES)
        near_rows = pl.ds(base + at, width)
        far_rows = pl.ds(base + ext, globs)
        bias = window_bias(block_ref[0], blocks, chunk, dims)
        near = lax.broadcasted_iota(jnp.int32, bias.shape, 1) < width
        cols = [slice(pair * LANES, (pair + 1) * LANES) for pair in range(pairs)]
        query = [stack_heads(q_ref[rows, c] * scale) for c in cols]
        grad_out = [stack_heads(do_ref[rows, c]) for c in cols]
        keys = [window_keys(k_ref, base, at, width, ext, globs, c) for c in cols]
        values = [window_keys(v_ref, base, at, width, ext, globs, c) for c in cols]
        labels = [rel_ref[:, c] for c in cols]
        shifted = [dot_on(q, x, 1, 1) for q, x in zip(query, labels)]
        scores = [dot_on(q, k, 1, 1) for q, k in zip(query, keys)]
        scores = [x + skew(y, width + globs) + bias for x, y in zip(scores, shifted)]
        pairs_of = [grads_of(x, g, v) for x, g, v in zip(scores, grad_out, values)]
        dsb = [ds.astype(BF) for _, ds in pairs_of]
        by_label = [unskew(jnp.where(near, x.astype(F32), 0.0), LABEL_PAD).astype(BF) for x in dsb]
        dv = [dot_on(w, g, 0, 0) for (w, _), g in zip(pairs_of, grad_out)]
        dk = [dot_on(x, q, 0, 0) for x, q in zip(dsb, query)]
        dq = [
            dot_on(x, k, 1, 0) + dot_on(y, l, 1, 0) for x, k, y, l in zip(dsb, keys, by_label, labels)
        ]
        drel = [dot_on(y, q, 0, 0) for y, q in zip(by_label, query)]
        for pair, c in enumerate(cols):
            dq_ref[rows, c] = (merge_stack(dq[pair]) * scale).astype(BF)
            drel_ref[:, c] += drel[pair]
            for at_acc, grad in ((pair, dk[pair]), (pairs + pair, dv[pair])):
                dkv_acc[at_acc, near_rows] += grad[:width]
                dkv_acc[at_acc, far_rows] += grad[width:]
        return carry

    lax.fori_loop(0, seqs * chunks, window, 0)
    rows = slice(glob_at, glob_at + glob_rows)
    both = [(pair, seq) for pair in range(pairs) for seq in range(seqs)]
    cols = [slice(pair * LANES, (pair + 1) * LANES) for pair in range(pairs)]
    spans = [slice(seq * span, (seq + 1) * span) for seq in range(seqs)]
    query = [stack_heads(q_ref[rows, c] * scale) for c in cols]
    grad_out = [stack_heads(do_ref[rows, c]) for c in cols]
    bias = [jnp.concatenate([gbias_ref[seq]] * 2, axis=0) for seq in range(seqs)]
    keys = [k_ref[spans[seq], cols[pair]] for pair, seq in both]
    scores = [dot_on(query[pair], k, 1, 1) + bias[seq] for k, (pair, seq) in zip(keys, both)]
    grads = [
        grads_of(x, grad_out[pair], v_ref[spans[seq], cols[pair]]) for x, (pair, seq) in zip(scores, both)
    ]
    own = [glob_row_mask(scores[0].shape, seq, glob_block) for seq in range(seqs)]
    weights = [jnp.where(own[seq], w.astype(F32), 0.0).astype(BF) for (w, _), (_, seq) in zip(grads, both)]
    dsb = [jnp.where(own[seq], ds, 0.0).astype(BF) for (_, ds), (_, seq) in zip(grads, both)]
    dk = [dot_on(x, query[pair], 0, 0) for x, (pair, _) in zip(dsb, both)]
    dv = [dot_on(w, grad_out[pair], 0, 0) for w, (pair, _) in zip(weights, both)]
    dq = [dot_on(x, k, 1, 0) for x, k in zip(dsb, keys)]
    for pair in range(pairs):
        dq_ref[rows, cols[pair]] = (merge_stack(sum(dq[pair * seqs : (pair + 1) * seqs])) * scale).astype(BF)
        for seq in range(seqs):
            dkv_acc[pair, spans[seq]] += dk[pair * seqs + seq]
            dkv_acc[pairs + pair, spans[seq]] += dv[pair * seqs + seq]
    first_row, row_step, cells, per_block = glob_at_rows
    for seq in range(seqs):
        for r in range(per_block):
            source = pl.ds(seq * span + ext + r * blocks, blocks)
            for c in range(2 * pairs):
                rows = pl.ds((seq * per_block + r) * 2 * pairs + c, blocks, stride=cells)
                glob_stage[rows, :] = dkv_acc[c, source, :]
    glob_low[...] = glob_stage[...].astype(BF)
    for i in range(blocks):
        pltpu.make_async_copy(
            glob_low.at[pl.ds(i * cells, cells)],
            grads_ref.at[pl.ds(first_row + (i + 1) * row_step - cells, cells)],
            sems.at[5],
        ).start()
    norms_ref[...] = jnp.zeros_like(norms_ref)
    for row, source in enumerate((gn_ref, gn_ref, norm_two_ref, norm_two_ref)):
        for half in range(source.shape[1] // head_cols):
            at = row * (source.shape[1] // head_cols) + half
            norms_ref[at : at + 1] = source[row % 2 : row % 2 + 1, half * head_cols : (half + 1) * head_cols]
    small_ref[...] = jnp.concatenate([drel_ref[: SMALL_ROWS - 8], norms_ref[...]], axis=0).astype(BF)
    for c in range(2 * pairs):
        dkv_ref[:, c * LANES : (c + 1) * LANES] = dkv_acc[c].astype(BF)
    per = head_cols // LANES

    def cut(j):
        row = pl.multiple_of(j * 256, 256)
        rows = pl.ds(row, 256)
        first = 2 * per * j
        q_stage[rows, :] = dot_on(xr_ref[:, rows], dq_ref[...], 0, 0).astype(BF)
        send_tiles(q_stage, row, 2, first, place_ref, grads_ref, sems.at[1])
        both = dot_on(xe_ref[:, rows], dkv_ref[...], 0, 0).astype(BF)
        k_stage[rows, :] = both[:, :head_cols]
        v_stage[rows, :] = both[:, head_cols:]
        send_tiles(k_stage, row, 2, attn_tiles + first, place_ref, grads_ref, sems.at[2])
        send_tiles(v_stage, row, 2, 2 * attn_tiles + first, place_ref, grads_ref, sems.at[3])

    col_loop(q_stage.shape[0], cut)
    for at, stage in enumerate((out_stage, q_stage, k_stage, v_stage)):
        pltpu.make_async_copy(stage, stage, sems.at[at]).wait()
    for copy in spare:
        copy.wait()
    pltpu.make_async_copy(glob_low, glob_low, sems.at[5]).wait()


def start_weights(wall_ref, at, head_cols, wkv_ref, wq_ref, sems):
    model_dim = wkv_ref.shape[0]
    copies = [
        pltpu.make_async_copy(wall_ref.at[pl.ds(at[0], model_dim)], wkv_ref, sems.at[0]),
        pltpu.make_async_copy(
            wall_ref.at[pl.ds(at[1], model_dim), pl.ds(0, head_cols)], wq_ref, sems.at[1]
        ),
    ]
    for copy in copies:
        copy.start()
    return copies


def back_rows(proj, wkv_ref, wq_ref):
    cols = wq_ref.shape[1]
    return dot_on(proj[:, :cols], wq_ref[...], 1, 1) + dot_on(proj[:, cols:], wkv_ref[...], 1, 1)


def dx_kernel(dims, at, half_ref, dq_ref, dkv_ref, next_ref, last_ref, mid_ref, wall_ref,
              keep_ref, send_ref, proj_ref, wkv_ref, wq_ref, sems):
    seqs, block_len, _, ext, _, globs, _ = dims
    head_cols = dq_ref.shape[1]
    copies = start_weights(wall_ref, at, head_cols, wkv_ref, wq_ref, sems)
    proj_ref[:, :head_cols] = dq_ref[: seqs * block_len]
    for seq in range(seqs):
        base, row = seq * (ext + globs) + RIM, seq * block_len
        middle = block_len - 2 * RIM
        own = dkv_ref[base : base + block_len].astype(F32)
        sums = [
            own[:RIM] + last_ref[seq * RIM : (seq + 1) * RIM].astype(F32),
            own[RIM : RIM + middle],
            own[RIM + middle :] + next_ref[seq * RIM : (seq + 1) * RIM].astype(F32),
        ]
        proj_ref[row : row + block_len, head_cols:] = jnp.concatenate(sums, axis=0).astype(BF)
    for copy in copies:
        copy.wait()
    per = block_len // 2
    for out_ref, half in ((keep_ref, half_ref[0]), (send_ref, 1 - half_ref[0])):
        for seq in range(seqs):
            rows = pl.ds(pl.multiple_of(seq * block_len + half * per, per), per)
            total = back_rows(proj_ref[rows, :], wkv_ref, wq_ref)
            if out_ref is keep_ref:
                total = total + mid_ref[rows, :]
            out_ref[seq] = total.astype(out_ref.dtype)


def dx_glob_kernel(dims, at, half_ref, dq_ref, kept_ref, got_ref, mid_ref, wall_ref,
                   keep_ref, send_ref, cells_ref, wkv_ref, wq_ref, sems):
    seqs, block_len, glob_block = dims[:3]
    head_cols = dq_ref.shape[1]
    base = seqs * block_len
    used, cols = seqs * glob_block, 2 * head_cols // LANES
    copies = start_weights(wall_ref, at, head_cols, wkv_ref, wq_ref, sems)
    first = kept_ref.shape[0] - used * cols
    cells_ref[...] = kept_ref[first:].astype(F32) + got_ref[first:].astype(F32)
    wide = [cells_ref[pl.ds(c, used, stride=cols), :] for c in range(cols)]
    dkv = jnp.concatenate(wide, axis=1)
    dkv = jnp.concatenate([dkv, jnp.zeros((dq_ref.shape[0] - base - used, 2 * head_cols), F32)], axis=0)
    proj = jnp.concatenate([dq_ref[base:], dkv.astype(BF)], axis=1)
    for copy in copies:
        copy.wait()
    total = back_rows(proj, wkv_ref, wq_ref)
    few = glob_block // 2
    here = half_ref[0] == 0
    for seq in range(seqs):
        start = seq * glob_block
        halves = [total[start : start + few], total[start + few : start + glob_block]]
        mids = [
            mid_ref[base + start : base + start + few, :],
            mid_ref[base + start + few : base + start + glob_block, :],
        ]
        keep_ref[seq] = jnp.where(here, halves[0] + mids[0], halves[1] + mids[1])
        send_ref[seq] = jnp.where(here, halves[1], halves[0]).astype(BF)


def swap_cores(values):
    count = lax.axis_size("ffn")
    return lax.ppermute(values, "ffn", [(i, i ^ 1) for i in range(count)])


def on_device(
    x_long,
    x_glob,
    sentence,
    dy_long,
    dy_glob,
    owner_list,
    w_master,
    m_old,
    v_old,
    left_basis,
    right_basis,
    left_stats,
    right_stats,
    rel_table,
    rel_m,
    rel_v,
    norm_params,
    norm_m,
    norm_v,
):
    ffn_count = lax.axis_size("ffn")
    seq_count = lax.axis_size("seq")
    seqs, tok_half, model_dim = x_long.shape
    glob_half = x_glob.shape[1]
    block_len = tok_half * ffn_count
    glob_block = glob_half * ffn_count
    globs = glob_block * seq_count
    head_cols = model_dim // ffn_count
    hidden = FF // ffn_count
    scale = (model_dim // HEADS) ** (-0.5)
    slots, side = w_master.shape[:2]
    attn_tiles = model_dim * head_cols // (side * side)
    ffn_tiles = model_dim * hidden // (side * side)
    tile_count = 4 * attn_tiles + 2 * ffn_tiles
    slot_count = owner_list.shape[0]
    labels = rel_table.shape[0]
    half_index = lax.axis_index("ffn")
    first_half = half_index == 0
    parts = slot_parts(slots, seq_count)

    glob_cells = seqs * glob_block * model_dim // LANES
    rows_per = part_rows(parts, side, glob_cells)
    places, place_rows = slot_places(owner_list, slots, rows_per, side)
    held = jnp.sum(
        jnp.where(
            places[None, :] == jnp.arange(slot_count, dtype=jnp.int32)[:, None],
            jnp.arange(slot_count, dtype=jnp.int32)[None, :],
            0,
        ),
        axis=1,
    )
    per_row = model_dim // side
    up_rows = hidden // model_dim * model_dim
    kv_at = up_rows + hidden
    q_at = kv_at + model_dim
    out_at = q_at + model_dim
    head_tiles = head_cols // side
    up_tiles = hidden // side

    def tile_row_col(tile):
        kind_qkv = tile // attn_tiles
        inner = tile % attn_tiles
        qkv_row = jnp.where(kind_qkv == 0, q_at, kv_at) + inner // head_tiles * side
        qkv_col = jnp.where(kind_qkv == 2, head_cols, 0) + inner % head_tiles * side
        out_row = out_at + inner // per_row * side
        up = tile - 4 * attn_tiles
        up_col = up % up_tiles * side
        up_row = up_col // model_dim * model_dim + up // up_tiles * side
        down = up - ffn_tiles
        down_row = up_rows + down // per_row * side
        row = jnp.where(
            tile < 3 * attn_tiles,
            qkv_row,
            jnp.where(
                tile < 4 * attn_tiles,
                out_row,
                jnp.where(up < ffn_tiles, up_row, down_row),
            ),
        )
        col = jnp.where(
            tile < 3 * attn_tiles,
            qkv_col,
            jnp.where(
                tile < 4 * attn_tiles,
                inner % per_row * side,
                jnp.where(up < ffn_tiles, up_col % model_dim, down % per_row * side),
            ),
        )
        return row, col

    wall_row, wall_col = tile_row_col(held)
    wall_kind = jnp.where(held < 4 * attn_tiles, 0, jnp.where(held < tile_count, 1, 2))

    weights_low = w_master.astype(BF).reshape(-1, LANES)
    glob_other = swap_cores(x_glob)
    glob_own = jnp.concatenate(
        [jnp.where(first_half, x_glob, glob_other), jnp.where(first_half, glob_other, x_glob)], axis=1
    )
    orders = [order for _, _, order in parts]
    gathered = gather_rows(
        weights_low, glob_own.reshape(-1, LANES), rows_per, orders
    )
    gathered = [
        [piece.reshape(-1, many, LANES) for piece in pieces] for pieces, many in zip(gathered, rows_per)
    ]
    tiles_per = tuple(last - first for (first, last, _), pieces in zip(parts, gathered) for _ in pieces)
    gathered = [piece for pieces in gathered for piece in pieces]

    rim = jnp.where(first_half, x_long[:, :RIM], x_long[:, tok_half - RIM :])
    mine = jnp.concatenate([x_long, dy_long, x_glob, dy_glob], axis=1)
    spare = -mine.shape[1] % 8
    mine = jnp.concatenate([mine, jnp.zeros((seqs, spare, model_dim), BF)], axis=1)
    first, second = mine.reshape(-1, model_dim), rim.reshape(-1, model_dim)
    first, second, _ = move_rows(
        [[(first.shape[0], (first, 0))], [(second.shape[0], (second, 0))], [(16, (weights_low, 0))]]
    )
    mine, rim = first.reshape(mine.shape), second
    other = swap_cores(mine)
    lower = jnp.where(first_half, mine, other)
    upper = jnp.where(first_half, other, mine)

    def block_rows(at, count):
        return jnp.concatenate([lower[:, at : at + count], upper[:, at : at + count]], axis=1)

    long_rows = block_rows(0, tok_half)
    dy_rows = block_rows(tok_half, tok_half)
    glob_rows = block_rows(2 * tok_half, glob_half)
    dy_globs = block_rows(2 * tok_half + glob_half, glob_half)
    used = seqs * (block_len + glob_block)
    row_count = seqs * block_len + up_to(seqs * glob_block, 16)
    pad_rows = jnp.zeros((row_count - used, model_dim), BF)

    def in_rows(long_part, glob_part):
        return jnp.concatenate(
            [long_part.reshape(-1, model_dim), glob_part.reshape(-1, model_dim), pad_rows]
        )

    x_rows = in_rows(long_rows, glob_rows)
    dy_all = in_rows(dy_rows, dy_globs)
    to_next = [(i * ffn_count + 1, (i + 1) * ffn_count + 1) for i in range(seq_count - 1)]
    to_last = [((i + 1) * ffn_count, i * ffn_count) for i in range(seq_count - 1)]
    rim = lax.ppermute(rim, ("seq", "ffn"), to_next + to_last)
    rim_other = swap_cores(rim)
    rim_left = jnp.where(first_half, rim_other, rim)
    rim_right = jnp.where(first_half, rim, rim_other)

    reach = 2 * RADIUS
    width = up_to(LANES + 2 * RIM, LANES) if globs % LANES == 0 else up_to(LANES + 2 * RIM + globs, LANES) - globs
    ext = block_len - LANES + width
    span = ext + globs
    rel_low = jnp.pad(
        rel_table.astype(BF), ((RIM - RADIUS, LABEL_PAD - labels - RIM + RADIUS), (0, 0))
    )

    glob_bias_rows = row_count - seqs * block_len
    row_at = jnp.arange(glob_bias_rows, dtype=jnp.int32)[None, :, None]
    seq_at = jnp.arange(seqs, dtype=jnp.int32)[:, None, None]
    spread = jnp.pad(sentence[:, 0], ((0, 0), (RIM, span - RIM - block_len)), constant_values=-1)
    span_at = jnp.arange(span, dtype=jnp.int32)[None, None, :]
    own = (spread[:, None, :] == row_at - seq_at * glob_block) & (spread[:, None, :] >= 0)
    glob_bias = jnp.where(own | (span_at >= ext), 0.0, NEG_FILL).astype(F32)

    spec_up = block_at((up_rows, model_dim), 0, 0)
    spec_down = block_at((hidden, model_dim), 1, 0)
    spec_out = block_at((head_cols, model_dim), out_at // head_cols, 0)

    def rows_of(cols, dtype=BF, rows=row_count):
        return jax.ShapeDtypeStruct((rows, cols), dtype)

    def specs(arrays):
        return [whole(a.shape) for a in arrays]

    dims = (seqs, block_len, glob_block, ext, width, globs, scale)
    fwd_shapes = (
        rows_of(head_cols),
        rows_of(head_cols, rows=seqs * span),
        rows_of(head_cols, rows=seqs * span),
        rows_of(head_cols),
        rows_of(model_dim),
        rows_of(model_dim, rows=seqs * span),
    )
    wall_at = (
        2 * ffn_tiles // per_row * side,
        4 * attn_tiles // per_row * side,
        kv_at,
        q_at,
        out_at,
        tiles_per,
    )
    wall_shape = jax.ShapeDtypeStruct((out_at + head_cols, model_dim), BF)
    block_now = lax.axis_index("seq").astype(jnp.int32).reshape(1)
    ins = [x_rows, rel_low, glob_bias]
    query, keys, values, heads_out, attn_part, x_ext, wall = kernel_call(
        functools.partial(attend_kernel, dims, wall_at, seq_count),
        "attend",
        28,
        fwd_shapes + (wall_shape,),
        [scalars()] * 4 + specs(ins) + [any_space()] * (2 + len(gathered)),
        tuple(specs(fwd_shapes)) + (any_space(),),
        [
            pltpu.VMEM(wall_shape.shape, BF),
            pltpu.VMEM((seq_count * glob_cells, LANES), BF),
            pltpu.VMEM((seq_count * glob_cells, LANES), F32),
            pltpu.SemaphoreType.DMA((5,)),
        ],
        flops=4 * 10**9,
        bytes_moved=10**7,
    )(wall_row, wall_col, wall_kind, block_now, *ins, rim_left, rim_right, *gathered)
    attn_got = swap_cores(attn_part)
    feed_shapes = (
        rows_of(model_dim, F32),
        rows_of(model_dim),
        rows_of(hidden, F32),
        rows_of(hidden),
        rows_of(model_dim),
    )
    norm_one, norm_low, up_pre, act_low, down_part = kernel_call(
        feed_kernel,
        "feed",
        24,
        feed_shapes,
        specs([x_rows, attn_part, attn_got, norm_params]) + [spec_up, spec_down],
        tuple(specs(feed_shapes)),
        flops=3 * 10**9,
        bytes_moved=10**7,
    )(x_rows, attn_part, attn_got, norm_params, wall, wall)
    down_got = swap_cores(down_part)
    norm_shape = jax.ShapeDtypeStruct((8, model_dim), F32)
    half_now = half_index.astype(jnp.int32).reshape(1)
    back_shapes = (
        jax.ShapeDtypeStruct(x_long.shape, BF),
        jax.ShapeDtypeStruct(x_glob.shape, BF),
        rows_of(model_dim, F32),
        rows_of(model_dim),
        rows_of(hidden),
        rows_of(model_dim),
        norm_shape,
    )
    y_long, y_glob, d_pre, d_pre_low, d_up, d_norm_part, norm_two_grad = kernel_call(
        functools.partial(feed_back_kernel, dims),
        "feed_back",
        30,
        back_shapes,
        [scalars()]
        + specs([norm_one, down_part, down_got, up_pre, dy_all, norm_params])
        + [spec_up, spec_down],
        tuple(specs(back_shapes)),
        [pltpu.VMEM((row_count, model_dim), F32)],
        flops=3 * 10**9,
        bytes_moved=10**7,
    )(half_now, norm_one, down_part, down_got, up_pre, dy_all, norm_params, wall, wall)
    d_norm_got = swap_cores(d_norm_part)
    grads_shape = jax.ShapeDtypeStruct((seq_count * sum(rows_per), LANES), BF)
    slot_grads = kernel_call(
        functools.partial(feed_grads_kernel, (4 * attn_tiles, 4 * attn_tiles + ffn_tiles)),
        "feed_grads",
        16,
        grads_shape,
        [scalars()] + specs([act_low, d_pre_low, norm_low, d_up]),
        any_space(),
        [
            pltpu.VMEM((hidden, model_dim), BF),
            pltpu.VMEM((model_dim, hidden), BF),
            pltpu.SemaphoreType.DMA((2,)),
        ],
        flops=3 * 10**9,
        bytes_moved=10**7,
    )(place_rows, act_low, d_pre_low, norm_low, d_up)
    ins = [
        x_rows,
        attn_part,
        attn_got,
        d_norm_part,
        d_norm_got,
        d_pre,
        heads_out,
        query,
        keys,
        values,
        x_ext,
    ]
    last_shapes = (
        grads_shape,
        rows_of(head_cols),
        rows_of(2 * head_cols, rows=seqs * span),
        rows_of(model_dim, F32),
        rows_of(head_cols, rows=SMALL_ROWS),
    )
    slot_grads, d_query, dkv, d_mid, small = kernel_call(
        functools.partial(
            attend_back_kernel,
            dims,
            seq_count,
            attn_tiles,
            (tile_count, slot_count),
            (seq_count * sum(rows_per[:-1]), rows_per[-1], glob_cells, glob_block),
        ),
        "attend_back",
        32,
        last_shapes,
        [scalars(), scalars(), whole(norm_shape.shape)]
        + specs(ins)
        + [spec_out]
        + specs([rel_low, glob_bias, norm_params])
        + [any_space()],
        (any_space(),) + tuple(specs(last_shapes[1:])),
        [
            pltpu.VMEM((row_count, head_cols), BF),
            pltpu.VMEM((row_count, model_dim), BF),
            pltpu.VMEM((2 * head_cols // LANES, seqs * span, LANES), F32),
            pltpu.VMEM((head_cols, model_dim), BF),
            pltpu.VMEM((model_dim, head_cols), BF),
            pltpu.VMEM((model_dim, head_cols), BF),
            pltpu.VMEM((model_dim, head_cols), BF),
            pltpu.VMEM((side, side), BF),
            pltpu.VMEM((LABEL_PAD, head_cols), F32),
            pltpu.VMEM((8, head_cols), F32),
            pltpu.VMEM((8, model_dim), F32),
            pltpu.VMEM((seq_count * glob_cells, LANES), F32),
            pltpu.VMEM((seq_count * glob_cells, LANES), BF),
            pltpu.SemaphoreType.DMA((6,)),
        ],
        {3 + len(ins) + 4: 0},
        flops=8 * 10**9,
        bytes_moved=2 * 10**7,
    )(block_now, place_rows, norm_two_grad, *ins, wall, rel_low, glob_bias, norm_params, slot_grads)

    bits = seq_bits(seq_count)
    carried = [
        [(RIM, (dkv, seq * span + at)) for seq in range(seqs)] for at in (0, RIM + block_len)
    ]
    sums, small, (to_last, to_next) = scatter_rows(
        slot_grads, rows_per, orders, small, bits[3:] + bits[:3], carried
    )
    from_next = lax.ppermute(to_last, "seq", [(i + 1, i) for i in range(seq_count - 1)])
    from_last = lax.ppermute(to_next, "seq", [(i, i + 1) for i in range(seq_count - 1)])

    weights_at = (kv_at, q_at)
    weights_held = [
        pltpu.VMEM((model_dim, model_dim), BF),
        pltpu.VMEM((model_dim, head_cols), BF),
        pltpu.SemaphoreType.DMA((2,)),
    ]
    dx_shapes = (
        jax.ShapeDtypeStruct(x_long.shape, F32),
        jax.ShapeDtypeStruct(x_long.shape, BF),
    )
    ins = [d_query, dkv, from_next, from_last, d_mid]
    dx_kept, dx_sent = kernel_call(
        functools.partial(dx_kernel, dims, weights_at),
        "dx_long",
        20,
        dx_shapes,
        [scalars()] + specs(ins) + [any_space()],
        tuple(specs(dx_shapes)),
        [pltpu.VMEM((seqs * block_len, 3 * head_cols), BF)] + weights_held,
        flops=10**9,
        bytes_moved=10**7,
    )(half_now, *ins, wall)
    dx_long = dx_kept + swap_cores(dx_sent).astype(F32)
    glob_shapes = (
        jax.ShapeDtypeStruct(x_glob.shape, F32),
        jax.ShapeDtypeStruct(x_glob.shape, BF),
    )
    ins = [d_query, sums[0], sums[1], d_mid]
    dx_kept, dx_sent = kernel_call(
        functools.partial(dx_glob_kernel, dims, weights_at),
        "dx_glob",
        12,
        glob_shapes,
        [scalars()] + specs(ins) + [any_space()],
        tuple(specs(glob_shapes)),
        [pltpu.VMEM((glob_cells, LANES), F32)] + weights_held,
        flops=10**8,
        bytes_moved=10**6,
    )(half_now, *ins, wall)
    dx_glob = dx_kept + swap_cores(dx_sent).astype(F32)

    state = (w_master, m_old, v_old, left_basis, right_basis, left_stats, right_stats)
    others = (rel_table, rel_m, rel_v, norm_params, norm_m, norm_v)
    new_state = soap_update(sums, small, state, others)
    w_new, m_new, v_new, left_q, right_q, left_s, right_s = new_state[:7]
    rel_new, rel_m_new, rel_v_new, norm_new, norm_m_new, norm_v_new = new_state[7:]
    return (
        y_long,
        y_glob,
        dx_long,
        dx_glob,
        w_new,
        m_new,
        v_new,
        left_q,
        right_q,
        left_s,
        right_s,
        rel_new,
        rel_m_new,
        rel_v_new,
        norm_new,
        norm_m_new,
        norm_v_new,
    )


def solution(mesh):
    in_specs = (
        P(None, ("seq", "ffn"), None),
        P(None, ("seq", "ffn"), None),
        P(None, "seq", None),
        P(None, ("seq", "ffn"), None),
        P(None, ("seq", "ffn"), None),
        P(),
        P(("seq", "ffn"), None, None),
        P(("seq", "ffn"), None, None),
        P(("seq", "ffn"), None, None),
        P(("seq", "ffn"), None, None),
        P(("seq", "ffn"), None, None),
        P(("seq", "ffn"), None, None),
        P(("seq", "ffn"), None, None),
        P(None, "ffn"),
        P(None, "ffn"),
        P(None, "ffn"),
        P(),
        P(),
        P(),
    )
    out_specs = (
        P(None, ("seq", "ffn"), None),
        P(None, ("seq", "ffn"), None),
        P(None, ("seq", "ffn"), None),
        P(None, ("seq", "ffn"), None),
        P(("seq", "ffn"), None, None),
        P(("seq", "ffn"), None, None),
        P(("seq", "ffn"), None, None),
        P(("seq", "ffn"), None, None),
        P(("seq", "ffn"), None, None),
        P(("seq", "ffn"), None, None),
        P(("seq", "ffn"), None, None),
        P(None, "ffn"),
        P(None, "ffn"),
        P(None, "ffn"),
        P(),
        P(),
        P(),
    )
    return jax.shard_map(
        on_device, mesh=mesh, in_specs=in_specs, out_specs=out_specs, check_vma=False
    )
```

```python
import functools
import math

import jax
import jax.numpy as jnp
from jax import lax
from jax.experimental import pallas as pl
from jax.experimental.pallas import tpu as pltpu
from jax.sharding import PartitionSpec as P

HEADS = 12
FF = 3072
RADIUS = 84
STEP = 10

BETA_ONE = 0.9
BETA_TWO = 0.95
LEARN_RATE = 0.02
ADAM_RATE = 0.6
WEIGHT_DECAY = 0.01
ADAM_EPS = 1e-08
NORM_EPS = 1e-12
NEG_FILL = -1e30
BF = jnp.bfloat16
F32 = jnp.float32


def seq_bits(count):
    return [1 << at for at in range(count.bit_length() - 1)]


def swap_with(values, bit):
    count = lax.axis_size("seq")
    return lax.ppermute(values, "seq", [(i, i ^ bit) for i in range(count)])


def slot_parts(slots, count):
    bits = seq_bits(count)
    low, high = bits[:3], bits[3:]
    cuts = [slots * at // 14 for at in (0, 5, 10, 14)]
    orders = [low[at:] + low[:at] + high for at in range(3)]
    return [(a, b, order) for a, b, order in zip(cuts, cuts[1:], orders) if b > a]


def part_rows(parts, side, extra):
    rows = [(last - first) * side for first, last, _ in parts]
    return rows[:-1] + [rows[-1] + extra]


def slot_places(owners, slots, rows, side):
    count = lax.axis_size("seq")
    apart = (owners // slots) ^ lax.axis_index("seq")
    inner = owners % slots
    place, row, base = jnp.zeros_like(owners), jnp.zeros_like(owners), 0
    for (first, last, order), many in zip(slot_parts(slots, count), rows):
        index = jnp.zeros_like(owners)
        for at, bit in enumerate(order):
            index = index + jnp.where((apart & bit) != 0, count >> (at + 1), 0)
        here = (inner >= first) & (inner < last)
        place = jnp.where(here, first * count + index * (last - first) + inner - first, place)
        row = jnp.where(here, base + index * many + (inner - first) * side, row)
        base += many * count
    return place, row


FAR_SIZE = 3 * 2**20


def move_kernel(plan, arrays, *refs):
    ins, outs, held, sems = refs[:arrays], refs[arrays : arrays + len(plan)], refs[arrays + len(plan) : -1], refs[-1]
    copies, sums, sem = [], [], 0
    for out, runs in zip(outs, plan):
        base = 0
        for rows, *terms in runs:
            here = out.at[pl.ds(base, rows)]
            targets = [here] if len(terms) == 1 else [held[len(sums) * 2 + k] for k in range(2)]
            waits = []
            for (at, start), target in zip(terms, targets):
                waits.append(pltpu.make_async_copy(ins[at].at[pl.ds(start, rows)], target, sems.at[sem]))
                waits[-1].start()
                sem += 1
            if len(terms) == 1:
                copies += waits
            else:
                sums.append((waits, targets, out, base, rows))
            base += rows
    for waits, (one, two), out, base, rows in sums:
        for wait in waits:
            wait.wait()
        step = next(s for s in (128, 112, 64, 48, 32, 16) if rows % s == 0)

        def add(i, carry):
            at = pl.multiple_of(i * step, 16)
            total = one[pl.ds(at, step), :].astype(F32) + two[pl.ds(at, step), :].astype(F32)
            out[pl.ds(base + at, step), :] = total.astype(BF)
            return carry

        lax.fori_loop(0, rows // step, add, 0)
    for copy in copies:
        copy.wait()


def move_rows(outputs):
    arrays, plan, scratch, count = [], [], [], 0
    for runs in outputs:
        plan.append([])
        for rows, *terms in runs:
            places = []
            for array, start in terms:
                found = [i for i, other in enumerate(arrays) if other is array]
                if not found:
                    arrays.append(array)
                places.append((found[0] if found else len(arrays) - 1, start))
                count += 1
            plan[-1].append((rows, *places))
            if len(terms) == 2:
                scratch += [pltpu.VMEM((rows, terms[0][0].shape[1]), BF)] * 2
    shapes = [(sum(run[0] for run in runs), runs[0][1][0].shape[1]) for runs in outputs]
    return pl.pallas_call(
        functools.partial(move_kernel, plan, len(arrays)),
        grid=(1,),
        out_shape=tuple(jax.ShapeDtypeStruct(shape, BF) for shape in shapes),
        in_specs=[
            pl.BlockSpec(memory_space=pltpu.HBM if array.size > FAR_SIZE else pl.ANY) for array in arrays
        ],
        out_specs=tuple(whole(shape) for shape in shapes),
        scratch_shapes=scratch + [pltpu.SemaphoreType.DMA((count,))],
        cost_estimate=pl.CostEstimate(
            flops=0, bytes_accessed=sum(6 * math.prod(s) for s in shapes), transcendentals=0
        ),
        compiler_params=pltpu.CompilerParams(vmem_limit_bytes=16 * 2**20),
        name="add_rows" if scratch else "join_rows",
    )(*arrays)


def run_sum(rows, one, one_at, two, two_at):
    return (rows, (one, one_at), (two, two_at))


def gather_rows(cells, extra, rows, orders):
    own = sum(rows)
    shared = orders[0][3:][::-1]
    got = [swap_with(values, shared[0]) for values in (cells, extra)]
    devices = [[(cells, 0), (extra, -cells.shape[0])], [(got[0], 0), (got[1], -cells.shape[0])]]
    if len(shared) > 1:
        (cells,) = move_rows([[(array.shape[0], (array, 0)) for runs in devices for array, _ in runs]])
        for bit in shared[1:-1]:
            got = swap_with(cells, bit)
            (cells,) = move_rows([[(cells.shape[0], (cells, 0)), (cells.shape[0], (got, 0))]])
        got = swap_with(cells, shared[-1])
        devices = [[(run, i * own)] for run in (cells, got) for i in range(cells.shape[0] // own)]
    starts = [sum(rows[:at]) for at in range(len(rows))]

    def runs_of(start, many):
        runs = []
        for pieces in devices:
            left, at = many, start
            for array, shift in pieces:
                here = min(left, array.shape[0] - (at + shift))
                if here > 0:
                    runs.append((here, (array, at + shift)))
                    left, at = left - here, at + here
        return runs

    parts = move_rows([runs_of(start, many) for start, many in zip(starts, rows)])
    for step in (2, 1):
        got = [swap_with(part, order[step]) for part, order in zip(parts, orders)]
        parts = move_rows([[(p.shape[0], (p, 0)), (p.shape[0], (g, 0))] for p, g in zip(parts, got)])
    got = [swap_with(part, order[0]) for part, order in zip(parts, orders)]
    return list(zip(parts, got))


def scatter_rows(cells, rows, orders, everywhere, order_everywhere, carried):
    count = lax.axis_size("seq")
    spans = [count * many for many in rows]
    starts = [sum(spans[:at]) for at in range(len(spans))]
    sends = [cells[a + r // 2 : a + r] for a, r in zip(starts, spans)]
    kept = move_rows([[(r // 2, (cells, a))] for a, r in zip(starts, spans)])
    kept = [(keep, 0, keep.shape[0]) for keep in kept]

    def all_sum():
        return [run_sum(everywhere.shape[0], everywhere, 0, all_got, 0)]

    for step in range(3):
        got = [swap_with(send, order[step]) for send, order in zip(sends, orders)]
        all_got = swap_with(everywhere, order_everywhere[step])
        halves = [r // 2 for _, _, r in kept]
        if step < 2:
            *sends, everywhere = move_rows(
                [[run_sum(h, k, a + h, g, h)] for h, (k, a, _), g in zip(halves, kept, got)] + [all_sum()]
            )
            keeps = move_rows([[run_sum(h, k, a, g, 0)] for h, (k, a, _), g in zip(halves, kept, got)])
            kept = [(keep, 0, h) for keep, h in zip(keeps, halves)]
    devices = count // 8

    def merged(at, many):
        return [
            run_sum(r, k, i * r, g, i * r)
            for i in range(at, at + many)
            for r, (k, _, _), g in zip(rows, kept, got)
        ]

    half = devices // 2
    send, everywhere, *carried = move_rows([merged(half, half), all_sum()] + carried)
    (keep,) = move_rows([merged(0, half)])
    for step, bit in enumerate(orders[0][3:]):
        got_all = swap_with(send, bit)
        all_got = swap_with(everywhere, order_everywhere[3 + step])
        if bit == orders[0][-1]:
            return (keep, got_all), (everywhere, all_got), carried
        half = keep.shape[0] // 2
        send, everywhere = move_rows([[run_sum(half, keep, half, got_all, half)], all_sum()])
        (keep,) = move_rows([[run_sum(half, keep, 0, got_all, 0)]])
    return None


def split_two(x):
    hi = x.astype(BF)
    return hi, (x - hi.astype(F32)).astype(BF)


def split_three(x):
    hi = x.astype(BF)
    rest = x - hi.astype(F32)
    mid = rest.astype(BF)
    return hi, mid, (rest - mid.astype(F32)).astype(BF)


def left_six(parts, axis):
    h, m, l = parts
    return jnp.concatenate([h, h, m, m, h, l], axis=axis)


def right_six(parts, axis):
    h, m, l = parts
    return jnp.concatenate([h, m, h, m, l, h], axis=axis)


def left_three(parts, axis):
    h, l = parts
    return jnp.concatenate([h, h, l], axis=axis)


def right_three(parts, axis):
    h, l = parts
    return jnp.concatenate([h, l, h], axis=axis)


def dot_on(a, b, ca, cb):
    return lax.dot_general(a, b, (((ca,), (cb,)), ((), ())), preferred_element_type=F32)


def dot_six(a, b, ca, cb):
    return dot_on(left_six(split_three(a), ca), right_six(split_three(b), cb), ca, cb)


def dot_one(a, b, ca, cb):
    return dot_on(a.astype(BF), b.astype(BF), ca, cb)


def dot_three(a, b, ca, cb):
    return dot_on(left_three(split_two(a), ca), right_three(split_two(b), cb), ca, cb)


PANEL = 32


def panel_inverse(a_ref, t_ref, npad, side, at):
    groups = PANEL // 8
    iota = lax.broadcasted_iota(jnp.int32, (8, npad), 0)
    a = []
    for i in range(PANEL):
        rows = a_ref[pl.ds(at + i, npad, stride=side), :]
        cols = rows.T[at : at + PANEL]
        a.append([cols[8 * g : 8 * g + 8] for g in range(groups)])
    z = [[None] * groups for _ in range(PANEL)]
    for j in range(PANEL):
        gj, sj = divmod(j, 8)
        r = lax.rsqrt(a[j][gj][sj : sj + 1])
        u = [None if g < gj else a[j][g] * r for g in range(groups)]
        below = list(u)
        below[gj] = jnp.where(iota > sj, u[gj], 0.0)
        for k in range(j + 1, PANEL):
            gk, sk = divmod(k, 8)
            row = u[gk][sk : sk + 1]
            for g in range(gk, groups):
                a[k][g] = a[k][g] - u[g] * row
        for c in range(j):
            row = z[c][gj][sj : sj + 1] * r
            z[c][gj] = jnp.where(iota == sj, row, z[c][gj]) - below[gj] * row
            for g in range(gj + 1, groups):
                z[c][g] = z[c][g] - u[g] * row
        z[j] = [
            jnp.zeros((8, npad), F32)
            if g < gj
            else (jnp.where(iota == sj, r, 0.0) - below[g] * r if g == gj else -u[g] * r)
            for g in range(groups)
        ]
    fill = jnp.zeros((side - PANEL, npad), F32)
    for c in range(PANEL):
        t_ref[pl.ds(c, npad, stride=PANEL), :] = jnp.concatenate(z[c] + [fill], axis=0).T


def adam_step(grad, refs, outs, where, decay_rate):
    param, first_mom, second_mom = [ref[where] for ref in refs]
    first_mom = BETA_ONE * first_mom + (1.0 - BETA_ONE) * grad
    second_mom = BETA_TWO * second_mom + (1.0 - BETA_TWO) * grad * grad
    direction = (
        first_mom
        / (1.0 - BETA_ONE**STEP)
        / (jnp.sqrt(second_mom / (1.0 - BETA_TWO**STEP)) + ADAM_EPS)
    )
    outs[0][where] = param - ADAM_RATE * (direction + decay_rate * param)
    outs[1][where] = first_mom
    outs[2][where] = second_mom


def small_updates(small_refs, refs, outs):
    total = small_refs[0][...].astype(F32) + small_refs[1][...].astype(F32)
    labels, cols = refs[0].shape
    rel = pltpu.roll(total, total.shape[0] - (RIM - RADIUS), 0)[:labels]
    adam_step(rel, refs[:3], outs[:3], (slice(None), slice(None)), WEIGHT_DECAY)
    halves = refs[3].shape[1] // cols
    for row in range(refs[3].shape[0]):
        for half in range(halves):
            at = SMALL_ROWS - 8 + row * halves + half
            where = (slice(row, row + 1), slice(half * cols, (half + 1) * cols))
            adam_step(total[at : at + 1], refs[3:], outs[3:], where, 0.0)


def soap_kernel(npad, kept_ref, got_ref, small_ref, small_got_ref, *refs):
    state, done = refs[:7], refs[13:20]
    given, a_ref, y_ref, mat_ref, t_ref, out_sems = refs[26:]
    n, side = state[0].shape[:2]
    many = next(k for k in (14, 7, 2, 1) if n % k == 0)
    batch = next(b for b in (28, 14, 7, 4, 2) if 2 * n % b == 0)
    small_updates((small_ref, small_got_ref), refs[7:13], refs[20:26])
    eye = (
        lax.broadcasted_iota(jnp.int32, (side, side), 0)
        == lax.broadcasted_iota(jnp.int32, (side, side), 1)
    ).astype(F32)

    def first(at, carry):
        slots = [at * many + k for k in range(many)]

        def old(kind):
            return [state[kind][i] for i in slots]

        lefts, rights = old(3), old(4)
        tiles = [pl.ds(pl.multiple_of(i * side, side), side) for i in slots]
        grads = [kept_ref[rows, :].astype(F32) + got_ref[rows, :].astype(F32) for rows in tiles]
        halves = [split_two(x) for x in grads]
        new_l = [
            BETA_TWO * x + (1.0 - BETA_TWO) * dot_on(left_three(p, 1), right_three(p, 1), 1, 1)
            for x, p in zip(old(5), halves)
        ]
        new_r = [
            BETA_TWO * x + (1.0 - BETA_TWO) * dot_on(left_three(p, 0), right_three(p, 0), 0, 0)
            for x, p in zip(old(6), halves)
        ]
        mats = [dot_six(x, y, 1, 0) for x, y in zip(new_l + new_r, lefts + rights)]
        thirds = [split_three(x) for x in mats]
        grams = [dot_on(left_six(p, 0), right_six(p, 0), 0, 0) for p in thirds]
        for k, i in enumerate(slots):
            given[5, i] = new_l[k]
            given[6, i] = new_r[k]
            for kind in range(2):
                mat_ref[2 * i + kind] = mats[kind * many + k]
                rows = pl.ds(pl.multiple_of((2 * i + kind) * side, side), side)
                a_ref[rows, :] = grams[kind * many + k]
                y_ref[rows, :] = eye
        return carry

    def rotate(slots):
        def old(kind):
            return [state[kind][i] for i in slots]

        lefts, rights = old(3), old(4)
        tiles = [slice(i * side, (i + 1) * side) for i in slots]
        grads = [kept_ref[rows, :].astype(F32) + got_ref[rows, :].astype(F32) for rows in tiles]
        turned = [dot_one(x, y, 0, 0) for x, y in zip(lefts, grads)]
        rotated = [dot_one(x, y, 1, 0) for x, y in zip(turned, rights)]
        moms = [BETA_ONE * old_m + (1.0 - BETA_ONE) * x for old_m, x in zip(old(1), rotated)]
        secs = [BETA_TWO * old_v + (1.0 - BETA_TWO) * x * x for old_v, x in zip(old(2), rotated)]
        steps = [
            x / (1.0 - BETA_ONE**STEP) / (jnp.sqrt(y / (1.0 - BETA_TWO**STEP)) + ADAM_EPS)
            for x, y in zip(moms, secs)
        ]
        turned = [dot_one(x, y, 1, 0) for x, y in zip(lefts, steps)]
        backs = [dot_one(x, y, 1, 1) for x, y in zip(turned, rights)]
        for k, (i, weight) in enumerate(zip(slots, old(0))):
            given[0, i] = weight - LEARN_RATE * (backs[k] + WEIGHT_DECAY * weight)
            given[1, i] = moms[k]
            given[2, i] = secs[k]

    def send(kinds):
        copies = [pltpu.make_async_copy(given.at[k], done[k], out_sems.at[k]) for k in kinds]
        for copy in copies:
            copy.start()
        return copies

    lax.fori_loop(0, n // many, first, 0)
    copies = send((5, 6))
    if npad > 2 * n:
        a_ref[2 * n * side :, :] = jnp.concatenate([eye] * (npad - 2 * n), axis=0)
    for at in range(0, side, PANEL):
        beside = range(at * n // side, (at + PANEL) * n // side)
        rotate(list(beside))
        panel_inverse(a_ref, t_ref, npad, side, at)

        def update(i, carry):
            bases = [pl.multiple_of((i * batch + b) * side, side) for b in range(batch)]
            rows = [pl.ds(base + at, PANEL) for base in bases]
            both = [jnp.concatenate([a_ref[r, :], y_ref[r, :]], axis=1) for r in rows]
            turns = [
                t_ref[pl.ds(pl.multiple_of((i * batch + b) * PANEL, PANEL), PANEL), :][:, :PANEL]
                for b in range(batch)
            ]
            if at + PANEL < side:
                rest = [pl.ds(base + at + PANEL, side - at - PANEL) for base in bases]
                old = [(a_ref[r, :], y_ref[r, :]) for r in rest]
            fresh = [dot_six(t, x, 0, 0) for t, x in zip(turns, both)]
            if at + PANEL < side:
                changes = []
                for x in fresh:
                    parts = split_three(x)
                    cut = tuple(p[:, at + PANEL : side] for p in parts)
                    changes.append(dot_on(left_six(cut, 0), right_six(parts, 0), 0, 0))
                for r, (old_a, old_y), change in zip(rest, old, changes):
                    a_ref[r, :] = old_a - change[:, :side]
                    y_ref[r, :] = old_y - change[:, side:]
            for r, x in zip(rows, fresh):
                y_ref[r, :] = x[:, side:]
            return carry

        lax.fori_loop(0, 2 * n // batch, update, 0)

    copies += send((0, 1, 2))

    def last(at, carry):
        slots = [at * many + k for k in range(many)]
        both = [2 * i + k for i in slots for k in range(2)]
        mats = [mat_ref[j] for j in both]
        turns = [y_ref[pl.ds(pl.multiple_of(j * side, side), side), :] for j in both]
        bases = [dot_three(x, y, 1, 1) for x, y in zip(mats, turns)]
        for k, i in enumerate(slots):
            for kind in range(2):
                given[3 + kind, i] = bases[2 * k + kind]
                target = done[3 + kind].at[i]
                pltpu.make_async_copy(given.at[3 + kind, i], target, out_sems.at[3 + kind]).start()
        return carry

    lax.fori_loop(0, n // many, last, 0)
    for copy in copies:
        copy.wait()
    for kind in (3, 4):
        pltpu.make_async_copy(given.at[kind], done[kind], out_sems.at[kind]).wait()


def soap_update(grads, small, state, others):
    n, side = state[0].shape[:2]
    npad = -(-2 * n // 8) * 8
    ins = [*grads, *small, *state, *others]
    outs = [*state, *others]
    return pl.pallas_call(
        functools.partial(soap_kernel, npad),
        grid=(1,),
        out_shape=tuple(jax.ShapeDtypeStruct(s.shape, F32) for s in outs),
        in_specs=[whole(array.shape) for array in ins],
        out_specs=(far_space(),) * len(state) + tuple(whole(array.shape) for array in others),
        scratch_shapes=[
            pltpu.VMEM((7, n, side, side), F32),
            pltpu.VMEM((npad * side, side), F32),
            pltpu.VMEM((npad * side, side), F32),
            pltpu.VMEM((2 * n, side, side), F32),
            pltpu.VMEM((npad * PANEL, side), F32),
            pltpu.SemaphoreType.DMA((7,)),
        ],
        cost_estimate=pl.CostEstimate(
            flops=n * 40 * side**3, bytes_accessed=n * 60 * side * side, transcendentals=0
        ),
        compiler_params=pltpu.CompilerParams(vmem_limit_bytes=32 * 2**20),
        name="soap",
    )(*ins)


LANES = 128
LABEL_PAD = 256
RIM = 96
SMALL_ROWS = 192


def up_to(value, unit):
    return -(-value // unit) * unit


def block_at(shape, *index):
    return pl.BlockSpec(shape, lambda i: index, pipeline_mode=pl.Buffered(1))


def whole(shape):
    return block_at(shape, *[0] * len(shape))


def any_space():
    return pl.BlockSpec(memory_space=pl.ANY)


def far_space():
    return pl.BlockSpec(memory_space=pltpu.HBM)


def scalars():
    return pl.BlockSpec(memory_space=pltpu.SMEM)


def kernel_call(body, name, mib, out_shape, in_specs, out_specs, scratch=(), aliases=None, flops=0, bytes_moved=0):
    return pl.pallas_call(
        body,
        name=name,
        grid=(1,),
        out_shape=out_shape,
        in_specs=in_specs,
        out_specs=out_specs,
        scratch_shapes=list(scratch),
        input_output_aliases=aliases or {},
        cost_estimate=pl.CostEstimate(flops=flops, bytes_accessed=bytes_moved, transcendentals=0),
        compiler_params=pltpu.CompilerParams(vmem_limit_bytes=mib * 2**20),
    )


def start_tiles(row_ref, col_ref, kind_ref, sources, tiles, wall_ref, sems):
    base = 0
    for source, many in zip(sources, tiles):

        def start(i, carry):
            for k in range(many):
                place = base + i * many + k
                kind = kind_ref[place]

                @pl.when(kind < 2)
                def _():
                    row = pl.multiple_of(row_ref[place], LANES)
                    col = pl.multiple_of(col_ref[place], LANES)
                    pltpu.make_async_copy(
                        source.at[i, pl.ds(k * LANES, LANES)],
                        wall_ref.at[pl.ds(row, LANES), pl.ds(col, LANES)],
                        sems.at[kind],
                    ).start()

            return carry

        lax.fori_loop(0, source.shape[0], start, 0)
        base += source.shape[0] * many


def wait_rows(wall_ref, rows, sem):
    part = wall_ref.at[pl.ds(0, rows)]
    pltpu.make_async_copy(part, part, sem).wait()


def low_lanes(rows):
    return lax.broadcasted_iota(jnp.int32, (rows, LANES), 1) < LANES // 2


def stack_heads(pair):
    low = low_lanes(pair.shape[0])
    zero = jnp.zeros_like(pair)
    return jnp.concatenate([jnp.where(low, pair, zero), jnp.where(low, zero, pair)], axis=0)


def merge_stack(stacked):
    rows = stacked.shape[0] // 2
    return jnp.where(low_lanes(rows), stacked[:rows], stacked[rows:])


def skew(table, width):
    rows = table.shape[0] // 2
    padded = jnp.concatenate(
        [table, jnp.zeros((table.shape[0], width - table.shape[1]), F32)], axis=1
    )
    halves = [
        pltpu.roll(padded[at : at + rows], 0, 1, stride=1, stride_axis=0) for at in (0, rows)
    ]
    return jnp.concatenate(halves, axis=0)


def unskew(grid, width):
    rows = grid.shape[0] // 2
    lanes = grid.shape[1]
    parts = []
    for at in range(0, 2 * rows, 8):
        shift = (at % rows) % lanes
        part = grid[at : at + 8]
        parts.append(part if shift == 0 else pltpu.roll(part, lanes - shift, 1))
    moved = jnp.concatenate([part[:, :width] for part in parts], axis=0)
    lanes = width
    index = lax.broadcasted_iota(jnp.int32, moved.shape, 0)
    for bit in (1, 2, 4):
        moved = jnp.where((index & bit) != 0, pltpu.roll(moved, lanes - bit, 1), moved)
    return moved


def softmax_rows(scores):
    top = jnp.max(scores, axis=-1, keepdims=True)
    raised = jnp.exp(scores - top)
    return raised * (1.0 / jnp.sum(raised, axis=-1, keepdims=True))


def window_keys(ref, base, at, width, ext, globs, cols):
    return jnp.concatenate(
        [ref[pl.ds(base + at, width), cols], ref[pl.ds(base + ext, globs), cols]], axis=0
    )


def glob_row_mask(shape, seq, glob_block):
    row = lax.broadcasted_iota(jnp.int32, shape, 0) % (shape[0] // 2)
    return (row >= seq * glob_block) & (row < (seq + 1) * glob_block)


def window_bias(block, blocks, chunk, dims):
    _, block_len, _, _, width, globs, _ = dims
    shape = (2 * LANES, width + globs)
    key = lax.broadcasted_iota(jnp.int32, shape, 1)
    query = lax.broadcasted_iota(jnp.int32, shape, 0) % LANES
    offset = key - query - (RIM - RADIUS)
    token = block * block_len - RIM + chunk * LANES + key
    near = (offset >= 0) & (offset <= 2 * RADIUS) & (token >= 0) & (token < blocks * block_len)
    return jnp.where(near | (key >= width), 0.0, NEG_FILL)


def attend_kernel(dims, wall_at, blocks, row_ref, col_ref, kind_ref, block_ref, xr_ref, rel_ref, gbias_ref,
                  left_ref, right_ref, *refs):
    q_ref, k_ref, v_ref, o_ref, part_ref, xe_ref, wall_out, wall_ref, glob_low, glob_cells, sems = refs[-11:]
    sources = refs[:-11]
    seqs, block_len, glob_block, ext, width, globs, scale = dims
    feed_rows, attn_rows, kv_at, q_at, out_at, tiles = wall_at
    model_dim = xr_ref.shape[1]
    head_cols = q_ref.shape[1]
    start_tiles(row_ref, col_ref, kind_ref, sources, tiles, wall_ref, sems)
    span = ext + globs
    cells = glob_low.shape[0] // blocks
    copies, base = [], 0
    for source in sources[-2:]:
        rows = source.shape[1] - cells
        for i in range(source.shape[0]):
            copies.append((source.at[i, pl.ds(rows, cells)], glob_low.at[pl.ds(base, cells)]))
            base += cells
    for source, target in copies:
        pltpu.make_async_copy(source, target, sems.at[3]).start()
    for seq in range(seqs):
        at = seq * span
        rim = pl.ds(seq * RIM, RIM)
        pltpu.make_async_copy(left_ref.at[rim], xe_ref.at[pl.ds(at, RIM)], sems.at[4]).start()
        pltpu.make_async_copy(
            right_ref.at[rim], xe_ref.at[pl.ds(at + RIM + block_len, RIM)], sems.at[4]
        ).start()
        at += RIM
        xe_ref[at : at + block_len] = xr_ref[seq * block_len : (seq + 1) * block_len]
        at += block_len + RIM
        if ext > block_len + 2 * RIM:
            xe_ref[at : seq * span + ext] = jnp.zeros((ext - block_len - 2 * RIM, model_dim), BF)
    pltpu.make_async_copy(glob_low, glob_low, sems.at[3]).wait()
    glob_cells[...] = glob_low[...].astype(F32)
    cols = model_dim // LANES
    for seq in range(seqs):
        for r in range(glob_block):
            at = seq * span + ext + r * blocks
            for c in range(cols):
                source = pl.ds((seq * glob_block + r) * cols + c, blocks, stride=cells)
                xe_ref[at : at + blocks, c * LANES : (c + 1) * LANES] = glob_cells[source, :].astype(BF)
    rims = xe_ref.at[pl.ds(0, 2 * seqs * RIM)]
    pltpu.make_async_copy(rims, rims, sems.at[4]).wait()
    wait_rows(wall_ref, attn_rows, sems.at[0])
    wq_ref = wall_ref.at[pl.ds(q_at, model_dim), pl.ds(0, head_cols)]
    wkv_ref = wall_ref.at[pl.ds(kv_at, model_dim)]
    wo_ref = wall_ref.at[pl.ds(out_at, head_cols)]
    pairs = head_cols // LANES
    glob_at = seqs * block_len
    glob_rows = q_ref.shape[0] - glob_at
    span = ext + globs
    chunks = block_len // LANES
    q_ref[...] = dot_on(xr_ref[...], wq_ref[...], 1, 0).astype(BF)

    def project(i, carry):
        rows = pl.ds(pl.multiple_of(i * 256, 256), 256)
        both = dot_on(xe_ref[rows, :], wkv_ref[...], 1, 0).astype(BF)
        k_ref[rows, :] = both[:, :head_cols]
        v_ref[rows, :] = both[:, head_cols:]
        return carry

    lax.fori_loop(0, seqs * span // 256, project, 0)
    wait_rows(wall_ref, feed_rows, sems.at[1])
    keep = pltpu.make_async_copy(wall_ref, wall_out, sems.at[2])
    keep.start()

    def window(i, carry):
        seq, chunk = i // chunks, i % chunks
        rows = pl.ds(pl.multiple_of(i * LANES, LANES), LANES)
        base = pl.multiple_of(seq * span, LANES)
        at = pl.multiple_of(chunk * LANES, LANES)
        bias = window_bias(block_ref[0], blocks, chunk, dims)
        cols = [slice(pair * LANES, (pair + 1) * LANES) for pair in range(pairs)]
        query = [stack_heads(q_ref[rows, c] * scale) for c in cols]
        keys = [window_keys(k_ref, base, at, width, ext, globs, c) for c in cols]
        values = [window_keys(v_ref, base, at, width, ext, globs, c) for c in cols]
        near = [dot_on(q, rel_ref[:, c], 1, 1) for q, c in zip(query, cols)]
        scores = [dot_on(q, k, 1, 1) for q, k in zip(query, keys)]
        scores = [x + skew(y, width + globs) + bias for x, y in zip(scores, near)]
        weights = [softmax_rows(x).astype(BF) for x in scores]
        outs = [merge_stack(dot_on(w, v, 1, 0)).astype(BF) for w, v in zip(weights, values)]
        for c, out in zip(cols, outs):
            o_ref[rows, c] = out
        return carry

    lax.fori_loop(0, seqs * chunks, window, 0)
    rows = slice(glob_at, glob_at + glob_rows)
    both = [(pair, seq) for pair in range(pairs) for seq in range(seqs)]
    cols = [slice(pair * LANES, (pair + 1) * LANES) for pair in range(pairs)]
    spans = [slice(seq * span, (seq + 1) * span) for seq in range(seqs)]
    query = [stack_heads(q_ref[rows, c] * scale) for c in cols]
    bias = [jnp.concatenate([gbias_ref[seq]] * 2, axis=0) for seq in range(seqs)]
    scores = [dot_on(query[pair], k_ref[spans[seq], cols[pair]], 1, 1) + bias[seq] for pair, seq in both]
    weights = [softmax_rows(x).astype(BF) for x in scores]
    outs = [dot_on(w, v_ref[spans[seq], cols[pair]], 1, 0) for w, (pair, seq) in zip(weights, both)]
    for pair in range(pairs):
        total = outs[pair * seqs]
        for seq in range(1, seqs):
            total = jnp.where(glob_row_mask(total.shape, seq, glob_block), outs[pair * seqs + seq], total)
        used = lax.broadcasted_iota(jnp.int32, total.shape, 0) % glob_rows < seqs * glob_block
        o_ref[rows, cols[pair]] = merge_stack(jnp.where(used, total, 0.0)).astype(BF)
    part_ref[...] = dot_on(o_ref[...], wo_ref[...], 1, 0).astype(BF)
    keep.wait()


def norm_parts(values):
    center = values - jnp.mean(values, axis=-1, keepdims=True)
    spread = jnp.mean(center * center, axis=-1, keepdims=True)
    rate = lax.rsqrt(spread + NORM_EPS)
    return center * rate, rate


def norm_back(grad, normed, rate, gain):
    scaled = grad * gain
    return (
        scaled
        - jnp.mean(scaled, axis=-1, keepdims=True)
        - normed * jnp.mean(scaled * normed, axis=-1, keepdims=True)
    ) * rate


def row_loop(total, body):
    step = 176 if total % 176 == 0 else 16

    def run(i, carry):
        body(pl.ds(pl.multiple_of(i * step, 16), step))
        return carry

    lax.fori_loop(0, total // step, run, 0)


def col_loop(total, body, step=256):
    def run(i, carry):
        body(i)
        return carry

    lax.fori_loop(0, total // step, run, 0)


GELU_RATE = 0.7978845608028654
GELU_CUBE = 0.044715


def gelu_parts(u):
    square = u * u
    curve = jnp.tanh(GELU_RATE * u * (1.0 + GELU_CUBE * square))
    return square, curve


def feed_kernel(xr_ref, part_ref, got_ref, norm_ref, wu_ref, wd_ref, h_ref, hb_ref, u_ref, a_ref, down_ref, mid_out,
                mid_ref, sems):
    model_dim = xr_ref.shape[1]
    gain, offset = norm_ref[0:1], norm_ref[1:2]

    def norm(rows):
        mid = xr_ref[rows, :].astype(F32) + (part_ref[rows, :].astype(F32) + got_ref[rows, :].astype(F32))
        mid_ref[rows, :] = mid
        normed, _ = norm_parts(mid)
        out = normed * gain + offset
        h_ref[rows, :] = out
        hb_ref[rows, :] = out.astype(BF)

    row_loop(xr_ref.shape[0], norm)
    keep = pltpu.make_async_copy(mid_ref, mid_out, sems.at[0])
    keep.start()
    per_half = model_dim // 256

    def up(j):
        rows = pl.ds(pl.multiple_of((j // per_half) * model_dim, 256), model_dim)
        cols = pl.ds(pl.multiple_of((j % per_half) * 256, 256), 256)
        here = pl.ds(pl.multiple_of(j * 256, 256), 256)
        u = dot_on(hb_ref[...], wu_ref[rows, cols], 1, 0)
        u_ref[:, here] = u
        _, curve = gelu_parts(u)
        a_ref[:, here] = (0.5 * u * (1.0 + curve)).astype(BF)

    col_loop(u_ref.shape[1], up)

    def down(j):
        cols = pl.ds(pl.multiple_of(j * 256, 256), 256)
        down_ref[:, cols] = dot_on(a_ref[...], wd_ref[:, cols], 1, 0).astype(BF)

    col_loop(model_dim, down)
    keep.wait()


def own_rows(ref, half, seqs, block_len, glob_block):
    per = block_len // 2
    long_part = [
        ref[pl.ds(pl.multiple_of(seq * block_len + half * per, per), per), :] for seq in range(seqs)
    ]
    base, few = seqs * block_len, glob_block // 2
    globs = ref[base:, :]
    glob_part = [
        jnp.where(
            half == 0,
            globs[seq * glob_block : seq * glob_block + few],
            globs[seq * glob_block + few : (seq + 1) * glob_block],
        )
        for seq in range(seqs)
    ]
    return long_part, glob_part


def feed_back_kernel(dims, half_ref, h_ref, down_ref, got_ref, u_ref, dy_ref, norm_ref, wu_ref, wd_ref,
                     y_long_ref, y_glob_ref, dx_out, dxb_ref, du_ref, dh_ref, gn_ref, y_ref, dx_ref, sems):
    model_dim = h_ref.shape[1]
    gain, offset = norm_ref[2:3], norm_ref[3:4]
    gn_ref[...] = jnp.zeros_like(gn_ref)

    def norm(rows):
        out = h_ref[rows, :] + (down_ref[rows, :].astype(F32) + got_ref[rows, :].astype(F32))
        normed, rate = norm_parts(out)
        y_ref[rows, :] = normed * gain + offset
        grad = dy_ref[rows, :].astype(F32)
        gn_ref[0:1] += jnp.sum(grad * normed, axis=0, keepdims=True)
        gn_ref[1:2] += jnp.sum(grad, axis=0, keepdims=True)
        dx = norm_back(grad, normed, rate, gain)
        dx_ref[rows, :] = dx
        dxb_ref[rows, :] = dx.astype(BF)

    row_loop(h_ref.shape[0], norm)
    keep = pltpu.make_async_copy(dx_ref, dx_out, sems.at[0])
    keep.start()
    long_part, glob_part = own_rows(y_ref, half_ref[0], *dims[:3])
    for seq in range(dims[0]):
        y_long_ref[seq] = long_part[seq].astype(BF)
        y_glob_ref[seq] = glob_part[seq].astype(BF)

    def act(j):
        here = pl.ds(pl.multiple_of(j * 256, 256), 256)
        da = dot_on(dxb_ref[...], wd_ref[here, :], 1, 1)
        u = u_ref[:, here]
        square, curve = gelu_parts(u)
        slope = 0.5 * (1.0 + curve) + 0.5 * u * (1.0 - curve * curve) * (
            GELU_RATE * (1.0 + 3.0 * GELU_CUBE * square)
        )
        du_ref[:, here] = (da * slope).astype(BF)

    col_loop(u_ref.shape[1], act)
    halves = u_ref.shape[1] // model_dim

    def lower(j):
        cols = pl.ds(pl.multiple_of(j * 256, 256), 256)
        total = 0.0
        for half in range(halves):
            rows = pl.ds(pl.multiple_of(half * model_dim + j * 256, 256), 256)
            total = total + dot_on(
                du_ref[:, half * model_dim : (half + 1) * model_dim], wu_ref[rows, :], 1, 1
            )
        dh_ref[:, cols] = total.astype(BF)

    col_loop(model_dim, lower)
    keep.wait()


def send_tiles(stage_ref, row, rows, first, place_ref, out_ref, sem):
    cols = stage_ref.shape[1] // LANES
    for r in range(rows):
        for c in range(cols):
            pltpu.make_async_copy(
                stage_ref.at[pl.ds(row + r * LANES, LANES), pl.ds(c * LANES, LANES)],
                out_ref.at[pl.ds(pl.multiple_of(place_ref[first + r * cols + c], 16), LANES)],
                sem,
            ).start()


def feed_grads_kernel(tiles_at, place_ref, a_ref, dxb_ref, hb_ref, du_ref, out_ref, down_stage, up_stage, sems):
    up_at, down_at = tiles_at
    model_dim = dxb_ref.shape[1]

    def down(j):
        row = pl.multiple_of(j * 256, 256)
        rows = pl.ds(row, 256)
        down_stage[rows, :] = dot_on(a_ref[:, rows], dxb_ref[...], 0, 0).astype(BF)
        send_tiles(down_stage, row, 2, down_at + j * 2 * (model_dim // LANES), place_ref, out_ref, sems.at[0])

    col_loop(a_ref.shape[1], down)

    def up(j):
        row = pl.multiple_of(j * 256, 256)
        rows = pl.ds(row, 256)
        up_stage[rows, :] = dot_on(hb_ref[:, rows], du_ref[...], 0, 0).astype(BF)
        send_tiles(
            up_stage, row, 2, up_at + j * 2 * (du_ref.shape[1] // LANES), place_ref, out_ref, sems.at[1]
        )

    col_loop(model_dim, up)
    pltpu.make_async_copy(down_stage, down_stage, sems.at[0]).wait()
    pltpu.make_async_copy(up_stage, up_stage, sems.at[1]).wait()


def attend_back_kernel(dims, blocks, attn_tiles, tile_counts, glob_at_rows, block_ref, place_ref, norm_two_ref, xr_ref, x1_ref, dh_ref, dh_got_ref, dx_ref, o_ref,
                       q_ref, k_ref, v_ref, xe_ref, wo_ref, rel_ref, gbias_ref, norm_ref, grads_in,
                       grads_ref, dq_ref, dkv_ref, mid_ref, small_ref,
                       do_ref, midb_ref, dkv_acc, out_stage, q_stage, k_stage, v_stage, none_ref,
                       drel_ref, norms_ref, gn_ref, glob_stage, glob_low, sems):
    seqs, block_len, glob_block, ext, width, globs, scale = dims
    head_cols = q_ref.shape[1]
    pairs = head_cols // LANES
    glob_at = seqs * block_len
    glob_rows = q_ref.shape[0] - glob_at
    span = ext + globs
    chunks = block_len // LANES
    gain = norm_ref[0:1]
    gn_ref[...] = jnp.zeros_like(gn_ref)

    def norm(rows):
        normed, rate = norm_parts(x1_ref[rows, :])
        grad = dh_ref[rows, :].astype(F32) + dh_got_ref[rows, :].astype(F32) + dx_ref[rows, :]
        gn_ref[0:1] += jnp.sum(grad * normed, axis=0, keepdims=True)
        gn_ref[1:2] += jnp.sum(grad, axis=0, keepdims=True)
        out = norm_back(grad, normed, rate, gain)
        mid_ref[rows, :] = out
        midb_ref[rows, :] = out.astype(BF)

    row_loop(xr_ref.shape[0], norm)
    do_ref[...] = dot_on(midb_ref[...], wo_ref[...], 1, 1).astype(BF)
    out_stage[...] = dot_on(o_ref[...], midb_ref[...], 0, 0).astype(BF)
    send_tiles(out_stage, 0, out_stage.shape[0] // LANES, 3 * attn_tiles, place_ref, grads_ref, sems.at[0])
    none_ref[...] = jnp.zeros_like(none_ref)
    spare = []
    for tile in range(*tile_counts):
        target = grads_ref.at[pl.ds(pl.multiple_of(place_ref[tile], 16), LANES)]
        spare.append(pltpu.make_async_copy(none_ref, target, sems.at[4]))
        spare[-1].start()
    dkv_acc[...] = jnp.zeros_like(dkv_acc)
    drel_ref[...] = jnp.zeros_like(drel_ref)

    def grads_of(scores, grad_out, values):
        weights = softmax_rows(scores)
        dp = dot_on(grad_out, values, 1, 1)
        delta = jnp.sum(weights * dp, axis=-1, keepdims=True)
        return weights.astype(BF), weights * (dp - delta)

    def window(i, carry):
        seq, chunk = i // chunks, i % chunks
        rows = pl.ds(pl.multiple_of(i * LANES, LANES), LANES)
        base = pl.multiple_of(seq * span, LANES)
        at = pl.multiple_of(chunk * LANES, LANES)
        near_rows = pl.ds(base + at, width)
        far_rows = pl.ds(base + ext, globs)
        bias = window_bias(block_ref[0], blocks, chunk, dims)
        near = lax.broadcasted_iota(jnp.int32, bias.shape, 1) < width
        cols = [slice(pair * LANES, (pair + 1) * LANES) for pair in range(pairs)]
        query = [stack_heads(q_ref[rows, c] * scale) for c in cols]
        grad_out = [stack_heads(do_ref[rows, c]) for c in cols]
        keys = [window_keys(k_ref, base, at, width, ext, globs, c) for c in cols]
        values = [window_keys(v_ref, base, at, width, ext, globs, c) for c in cols]
        labels = [rel_ref[:, c] for c in cols]
        shifted = [dot_on(q, x, 1, 1) for q, x in zip(query, labels)]
        scores = [dot_on(q, k, 1, 1) for q, k in zip(query, keys)]
        scores = [x + skew(y, width + globs) + bias for x, y in zip(scores, shifted)]
        pairs_of = [grads_of(x, g, v) for x, g, v in zip(scores, grad_out, values)]
        dsb = [ds.astype(BF) for _, ds in pairs_of]
        by_label = [unskew(jnp.where(near, x.astype(F32), 0.0), LABEL_PAD).astype(BF) for x in dsb]
        dv = [dot_on(w, g, 0, 0) for (w, _), g in zip(pairs_of, grad_out)]
        dk = [dot_on(x, q, 0, 0) for x, q in zip(dsb, query)]
        dq = [
            dot_on(x, k, 1, 0) + dot_on(y, l, 1, 0) for x, k, y, l in zip(dsb, keys, by_label, labels)
        ]
        drel = [dot_on(y, q, 0, 0) for y, q in zip(by_label, query)]
        for pair, c in enumerate(cols):
            dq_ref[rows, c] = (merge_stack(dq[pair]) * scale).astype(BF)
            drel_ref[:, c] += drel[pair]
            for at_acc, grad in ((pair, dk[pair]), (pairs + pair, dv[pair])):
                dkv_acc[at_acc, near_rows] += grad[:width]
                dkv_acc[at_acc, far_rows] += grad[width:]
        return carry

    lax.fori_loop(0, seqs * chunks, window, 0)
    rows = slice(glob_at, glob_at + glob_rows)
    both = [(pair, seq) for pair in range(pairs) for seq in range(seqs)]
    cols = [slice(pair * LANES, (pair + 1) * LANES) for pair in range(pairs)]
    spans = [slice(seq * span, (seq + 1) * span) for seq in range(seqs)]
    query = [stack_heads(q_ref[rows, c] * scale) for c in cols]
    grad_out = [stack_heads(do_ref[rows, c]) for c in cols]
    bias = [jnp.concatenate([gbias_ref[seq]] * 2, axis=0) for seq in range(seqs)]
    keys = [k_ref[spans[seq], cols[pair]] for pair, seq in both]
    scores = [dot_on(query[pair], k, 1, 1) + bias[seq] for k, (pair, seq) in zip(keys, both)]
    grads = [
        grads_of(x, grad_out[pair], v_ref[spans[seq], cols[pair]]) for x, (pair, seq) in zip(scores, both)
    ]
    own = [glob_row_mask(scores[0].shape, seq, glob_block) for seq in range(seqs)]
    weights = [jnp.where(own[seq], w.astype(F32), 0.0).astype(BF) for (w, _), (_, seq) in zip(grads, both)]
    dsb = [jnp.where(own[seq], ds, 0.0).astype(BF) for (_, ds), (_, seq) in zip(grads, both)]
    dk = [dot_on(x, query[pair], 0, 0) for x, (pair, _) in zip(dsb, both)]
    dv = [dot_on(w, grad_out[pair], 0, 0) for w, (pair, _) in zip(weights, both)]
    dq = [dot_on(x, k, 1, 0) for x, k in zip(dsb, keys)]
    for pair in range(pairs):
        dq_ref[rows, cols[pair]] = (merge_stack(sum(dq[pair * seqs : (pair + 1) * seqs])) * scale).astype(BF)
        for seq in range(seqs):
            dkv_acc[pair, spans[seq]] += dk[pair * seqs + seq]
            dkv_acc[pairs + pair, spans[seq]] += dv[pair * seqs + seq]
    first_row, row_step, cells, per_block = glob_at_rows
    for seq in range(seqs):
        for r in range(per_block):
            source = pl.ds(seq * span + ext + r * blocks, blocks)
            for c in range(2 * pairs):
                rows = pl.ds((seq * per_block + r) * 2 * pairs + c, blocks, stride=cells)
                glob_stage[rows, :] = dkv_acc[c, source, :]
    glob_low[...] = glob_stage[...].astype(BF)
    for i in range(blocks):
        pltpu.make_async_copy(
            glob_low.at[pl.ds(i * cells, cells)],
            grads_ref.at[pl.ds(first_row + (i + 1) * row_step - cells, cells)],
            sems.at[5],
        ).start()
    norms_ref[...] = jnp.zeros_like(norms_ref)
    for row, source in enumerate((gn_ref, gn_ref, norm_two_ref, norm_two_ref)):
        for half in range(source.shape[1] // head_cols):
            at = row * (source.shape[1] // head_cols) + half
            norms_ref[at : at + 1] = source[row % 2 : row % 2 + 1, half * head_cols : (half + 1) * head_cols]
    small_ref[...] = jnp.concatenate([drel_ref[: SMALL_ROWS - 8], norms_ref[...]], axis=0).astype(BF)
    for c in range(2 * pairs):
        dkv_ref[:, c * LANES : (c + 1) * LANES] = dkv_acc[c].astype(BF)
    per = head_cols // LANES

    def cut(j):
        row = pl.multiple_of(j * 256, 256)
        rows = pl.ds(row, 256)
        first = 2 * per * j
        q_stage[rows, :] = dot_on(xr_ref[:, rows], dq_ref[...], 0, 0).astype(BF)
        send_tiles(q_stage, row, 2, first, place_ref, grads_ref, sems.at[1])
        both = dot_on(xe_ref[:, rows], dkv_ref[...], 0, 0).astype(BF)
        k_stage[rows, :] = both[:, :head_cols]
        v_stage[rows, :] = both[:, head_cols:]
        send_tiles(k_stage, row, 2, attn_tiles + first, place_ref, grads_ref, sems.at[2])
        send_tiles(v_stage, row, 2, 2 * attn_tiles + first, place_ref, grads_ref, sems.at[3])

    col_loop(q_stage.shape[0], cut)
    for at, stage in enumerate((out_stage, q_stage, k_stage, v_stage)):
        pltpu.make_async_copy(stage, stage, sems.at[at]).wait()
    for copy in spare:
        copy.wait()
    pltpu.make_async_copy(glob_low, glob_low, sems.at[5]).wait()


def start_weights(wall_ref, at, head_cols, wkv_ref, wq_ref, sems):
    model_dim = wkv_ref.shape[0]
    copies = [
        pltpu.make_async_copy(wall_ref.at[pl.ds(at[0], model_dim)], wkv_ref, sems.at[0]),
        pltpu.make_async_copy(
            wall_ref.at[pl.ds(at[1], model_dim), pl.ds(0, head_cols)], wq_ref, sems.at[1]
        ),
    ]
    for copy in copies:
        copy.start()
    return copies


def back_rows(proj, wkv_ref, wq_ref):
    cols = wq_ref.shape[1]
    return dot_on(proj[:, :cols], wq_ref[...], 1, 1) + dot_on(proj[:, cols:], wkv_ref[...], 1, 1)


def dx_kernel(dims, at, half_ref, dq_ref, dkv_ref, next_ref, last_ref, mid_ref, wall_ref,
              keep_ref, send_ref, proj_ref, wkv_ref, wq_ref, sems):
    seqs, block_len, _, ext, _, globs, _ = dims
    head_cols = dq_ref.shape[1]
    copies = start_weights(wall_ref, at, head_cols, wkv_ref, wq_ref, sems)
    proj_ref[:, :head_cols] = dq_ref[: seqs * block_len]
    for seq in range(seqs):
        base, row = seq * (ext + globs) + RIM, seq * block_len
        middle = block_len - 2 * RIM
        own = dkv_ref[base : base + block_len].astype(F32)
        sums = [
            own[:RIM] + last_ref[seq * RIM : (seq + 1) * RIM].astype(F32),
            own[RIM : RIM + middle],
            own[RIM + middle :] + next_ref[seq * RIM : (seq + 1) * RIM].astype(F32),
        ]
        proj_ref[row : row + block_len, head_cols:] = jnp.concatenate(sums, axis=0).astype(BF)
    for copy in copies:
        copy.wait()
    per = block_len // 2
    for out_ref, half in ((keep_ref, half_ref[0]), (send_ref, 1 - half_ref[0])):
        for seq in range(seqs):
            rows = pl.ds(pl.multiple_of(seq * block_len + half * per, per), per)
            total = back_rows(proj_ref[rows, :], wkv_ref, wq_ref)
            if out_ref is keep_ref:
                total = total + mid_ref[rows, :]
            out_ref[seq] = total.astype(out_ref.dtype)


def dx_glob_kernel(dims, at, half_ref, dq_ref, kept_ref, got_ref, mid_ref, wall_ref,
                   keep_ref, send_ref, cells_ref, wkv_ref, wq_ref, sems):
    seqs, block_len, glob_block = dims[:3]
    head_cols = dq_ref.shape[1]
    base = seqs * block_len
    used, cols = seqs * glob_block, 2 * head_cols // LANES
    copies = start_weights(wall_ref, at, head_cols, wkv_ref, wq_ref, sems)
    first = kept_ref.shape[0] - used * cols
    cells_ref[...] = kept_ref[first:].astype(F32) + got_ref[first:].astype(F32)
    wide = [cells_ref[pl.ds(c, used, stride=cols), :] for c in range(cols)]
    dkv = jnp.concatenate(wide, axis=1)
    dkv = jnp.concatenate([dkv, jnp.zeros((dq_ref.shape[0] - base - used, 2 * head_cols), F32)], axis=0)
    proj = jnp.concatenate([dq_ref[base:], dkv.astype(BF)], axis=1)
    for copy in copies:
        copy.wait()
    total = back_rows(proj, wkv_ref, wq_ref)
    few = glob_block // 2
    here = half_ref[0] == 0
    for seq in range(seqs):
        start = seq * glob_block
        halves = [total[start : start + few], total[start + few : start + glob_block]]
        mids = [
            mid_ref[base + start : base + start + few, :],
            mid_ref[base + start + few : base + start + glob_block, :],
        ]
        keep_ref[seq] = jnp.where(here, halves[0] + mids[0], halves[1] + mids[1])
        send_ref[seq] = jnp.where(here, halves[1], halves[0]).astype(BF)


def swap_cores(values):
    count = lax.axis_size("ffn")
    return lax.ppermute(values, "ffn", [(i, i ^ 1) for i in range(count)])


def on_device(
    x_long,
    x_glob,
    sentence,
    dy_long,
    dy_glob,
    owner_list,
    w_master,
    m_old,
    v_old,
    left_basis,
    right_basis,
    left_stats,
    right_stats,
    rel_table,
    rel_m,
    rel_v,
    norm_params,
    norm_m,
    norm_v,
):
    ffn_count = lax.axis_size("ffn")
    seq_count = lax.axis_size("seq")
    seqs, tok_half, model_dim = x_long.shape
    glob_half = x_glob.shape[1]
    block_len = tok_half * ffn_count
    glob_block = glob_half * ffn_count
    globs = glob_block * seq_count
    head_cols = model_dim // ffn_count
    hidden = FF // ffn_count
    scale = (model_dim // HEADS) ** (-0.5)
    slots, side = w_master.shape[:2]
    attn_tiles = model_dim * head_cols // (side * side)
    ffn_tiles = model_dim * hidden // (side * side)
    tile_count = 4 * attn_tiles + 2 * ffn_tiles
    slot_count = owner_list.shape[0]
    labels = rel_table.shape[0]
    half_index = lax.axis_index("ffn")
    first_half = half_index == 0
    parts = slot_parts(slots, seq_count)

    glob_cells = seqs * glob_block * model_dim // LANES
    rows_per = part_rows(parts, side, glob_cells)
    places, place_rows = slot_places(owner_list, slots, rows_per, side)
    held = jnp.sum(
        jnp.where(
            places[None, :] == jnp.arange(slot_count, dtype=jnp.int32)[:, None],
            jnp.arange(slot_count, dtype=jnp.int32)[None, :],
            0,
        ),
        axis=1,
    )
    per_row = model_dim // side
    up_rows = hidden // model_dim * model_dim
    kv_at = up_rows + hidden
    q_at = kv_at + model_dim
    out_at = q_at + model_dim
    head_tiles = head_cols // side
    up_tiles = hidden // side

    def tile_row_col(tile):
        kind_qkv = tile // attn_tiles
        inner = tile % attn_tiles
        qkv_row = jnp.where(kind_qkv == 0, q_at, kv_at) + inner // head_tiles * side
        qkv_col = jnp.where(kind_qkv == 2, head_cols, 0) + inner % head_tiles * side
        out_row = out_at + inner // per_row * side
        up = tile - 4 * attn_tiles
        up_col = up % up_tiles * side
        up_row = up_col // model_dim * model_dim + up // up_tiles * side
        down = up - ffn_tiles
        down_row = up_rows + down // per_row * side
        row = jnp.where(
            tile < 3 * attn_tiles,
            qkv_row,
            jnp.where(
                tile < 4 * attn_tiles,
                out_row,
                jnp.where(up < ffn_tiles, up_row, down_row),
            ),
        )
        col = jnp.where(
            tile < 3 * attn_tiles,
            qkv_col,
            jnp.where(
                tile < 4 * attn_tiles,
                inner % per_row * side,
                jnp.where(up < ffn_tiles, up_col % model_dim, down % per_row * side),
            ),
        )
        return row, col

    wall_row, wall_col = tile_row_col(held)
    wall_kind = jnp.where(held < 4 * attn_tiles, 0, jnp.where(held < tile_count, 1, 2))

    weights_low = w_master.astype(BF).reshape(-1, LANES)
    glob_other = swap_cores(x_glob)
    glob_own = jnp.concatenate(
        [jnp.where(first_half, x_glob, glob_other), jnp.where(first_half, glob_other, x_glob)], axis=1
    )
    orders = [order for _, _, order in parts]
    gathered = gather_rows(
        weights_low, glob_own.reshape(-1, LANES), rows_per, orders
    )
    gathered = [
        [piece.reshape(-1, many, LANES) for piece in pieces] for pieces, many in zip(gathered, rows_per)
    ]
    tiles_per = tuple(last - first for (first, last, _), pieces in zip(parts, gathered) for _ in pieces)
    gathered = [piece for pieces in gathered for piece in pieces]

    rim = jnp.where(first_half, x_long[:, :RIM], x_long[:, tok_half - RIM :])
    mine = jnp.concatenate([x_long, dy_long, x_glob, dy_glob], axis=1)
    spare = -mine.shape[1] % 8
    mine = jnp.concatenate([mine, jnp.zeros((seqs, spare, model_dim), BF)], axis=1)
    first, second = mine.reshape(-1, model_dim), rim.reshape(-1, model_dim)
    first, second, _ = move_rows(
        [[(first.shape[0], (first, 0))], [(second.shape[0], (second, 0))], [(16, (weights_low, 0))]]
    )
    mine, rim = first.reshape(mine.shape), second
    other = swap_cores(mine)
    lower = jnp.where(first_half, mine, other)
    upper = jnp.where(first_half, other, mine)

    def block_rows(at, count):
        return jnp.concatenate([lower[:, at : at + count], upper[:, at : at + count]], axis=1)

    long_rows = block_rows(0, tok_half)
    dy_rows = block_rows(tok_half, tok_half)
    glob_rows = block_rows(2 * tok_half, glob_half)
    dy_globs = block_rows(2 * tok_half + glob_half, glob_half)
    used = seqs * (block_len + glob_block)
    row_count = seqs * block_len + up_to(seqs * glob_block, 16)
    pad_rows = jnp.zeros((row_count - used, model_dim), BF)

    def in_rows(long_part, glob_part):
        return jnp.concatenate(
            [long_part.reshape(-1, model_dim), glob_part.reshape(-1, model_dim), pad_rows]
        )

    x_rows = in_rows(long_rows, glob_rows)
    dy_all = in_rows(dy_rows, dy_globs)
    to_next = [(i * ffn_count + 1, (i + 1) * ffn_count + 1) for i in range(seq_count - 1)]
    to_last = [((i + 1) * ffn_count, i * ffn_count) for i in range(seq_count - 1)]
    rim = lax.ppermute(rim, ("seq", "ffn"), to_next + to_last)
    rim_other = swap_cores(rim)
    rim_left = jnp.where(first_half, rim_other, rim)
    rim_right = jnp.where(first_half, rim, rim_other)

    reach = 2 * RADIUS
    width = up_to(LANES + 2 * RIM, LANES) if globs % LANES == 0 else up_to(LANES + 2 * RIM + globs, LANES) - globs
    ext = block_len - LANES + width
    span = ext + globs
    rel_low = jnp.pad(
        rel_table.astype(BF), ((RIM - RADIUS, LABEL_PAD - labels - RIM + RADIUS), (0, 0))
    )

    glob_bias_rows = row_count - seqs * block_len
    row_at = jnp.arange(glob_bias_rows, dtype=jnp.int32)[None, :, None]
    seq_at = jnp.arange(seqs, dtype=jnp.int32)[:, None, None]
    spread = jnp.pad(sentence[:, 0], ((0, 0), (RIM, span - RIM - block_len)), constant_values=-1)
    span_at = jnp.arange(span, dtype=jnp.int32)[None, None, :]
    own = (spread[:, None, :] == row_at - seq_at * glob_block) & (spread[:, None, :] >= 0)
    glob_bias = jnp.where(own | (span_at >= ext), 0.0, NEG_FILL).astype(F32)

    spec_up = block_at((up_rows, model_dim), 0, 0)
    spec_down = block_at((hidden, model_dim), 1, 0)
    spec_out = block_at((head_cols, model_dim), out_at // head_cols, 0)

    def rows_of(cols, dtype=BF, rows=row_count):
        return jax.ShapeDtypeStruct((rows, cols), dtype)

    def specs(arrays):
        return [whole(a.shape) for a in arrays]

    dims = (seqs, block_len, glob_block, ext, width, globs, scale)
    fwd_shapes = (
        rows_of(head_cols),
        rows_of(head_cols, rows=seqs * span),
        rows_of(head_cols, rows=seqs * span),
        rows_of(head_cols),
        rows_of(model_dim),
        rows_of(model_dim, rows=seqs * span),
    )
    wall_at = (
        2 * ffn_tiles // per_row * side,
        4 * attn_tiles // per_row * side,
        kv_at,
        q_at,
        out_at,
        tiles_per,
    )
    wall_shape = jax.ShapeDtypeStruct((out_at + head_cols, model_dim), BF)
    block_now = lax.axis_index("seq").astype(jnp.int32).reshape(1)
    ins = [x_rows, rel_low, glob_bias]
    query, keys, values, heads_out, attn_part, x_ext, wall = kernel_call(
        functools.partial(attend_kernel, dims, wall_at, seq_count),
        "attend",
        28,
        fwd_shapes + (wall_shape,),
        [scalars()] * 4 + specs(ins) + [any_space()] * (2 + len(gathered)),
        tuple(specs(fwd_shapes)) + (any_space(),),
        [
            pltpu.VMEM(wall_shape.shape, BF),
            pltpu.VMEM((seq_count * glob_cells, LANES), BF),
            pltpu.VMEM((seq_count * glob_cells, LANES), F32),
            pltpu.SemaphoreType.DMA((5,)),
        ],
        flops=4 * 10**9,
        bytes_moved=10**7,
    )(wall_row, wall_col, wall_kind, block_now, *ins, rim_left, rim_right, *gathered)
    attn_got = swap_cores(attn_part)
    feed_shapes = (
        rows_of(model_dim, F32),
        rows_of(model_dim),
        rows_of(hidden, F32),
        rows_of(hidden),
        rows_of(model_dim),
        rows_of(model_dim, F32),
    )
    norm_one, norm_low, up_pre, act_low, down_part, mid_rows = kernel_call(
        feed_kernel,
        "feed",
        24,
        feed_shapes,
        specs([x_rows, attn_part, attn_got, norm_params]) + [spec_up, spec_down],
        tuple(specs(feed_shapes[:-1])) + (far_space(),),
        [pltpu.VMEM((row_count, model_dim), F32), pltpu.SemaphoreType.DMA((1,))],
        flops=3 * 10**9,
        bytes_moved=10**7,
    )(x_rows, attn_part, attn_got, norm_params, wall, wall)
    down_got = swap_cores(down_part)
    norm_shape = jax.ShapeDtypeStruct((8, model_dim), F32)
    half_now = half_index.astype(jnp.int32).reshape(1)
    back_shapes = (
        jax.ShapeDtypeStruct(x_long.shape, BF),
        jax.ShapeDtypeStruct(x_glob.shape, BF),
        rows_of(model_dim, F32),
        rows_of(model_dim),
        rows_of(hidden),
        rows_of(model_dim),
        norm_shape,
    )
    y_long, y_glob, d_pre, d_pre_low, d_up, d_norm_part, norm_two_grad = kernel_call(
        functools.partial(feed_back_kernel, dims),
        "feed_back",
        30,
        back_shapes,
        [scalars()]
        + specs([norm_one, down_part, down_got, up_pre, dy_all, norm_params])
        + [spec_up, spec_down],
        tuple(specs(back_shapes[:2])) + (far_space(),) + tuple(specs(back_shapes[3:])),
        [pltpu.VMEM((row_count, model_dim), F32)] * 2 + [pltpu.SemaphoreType.DMA((1,))],
        flops=3 * 10**9,
        bytes_moved=10**7,
    )(half_now, norm_one, down_part, down_got, up_pre, dy_all, norm_params, wall, wall)
    d_norm_got = swap_cores(d_norm_part)
    grads_shape = jax.ShapeDtypeStruct((seq_count * sum(rows_per), LANES), BF)
    slot_grads = kernel_call(
        functools.partial(feed_grads_kernel, (4 * attn_tiles, 4 * attn_tiles + ffn_tiles)),
        "feed_grads",
        16,
        grads_shape,
        [scalars()] + specs([act_low, d_pre_low, norm_low, d_up]),
        any_space(),
        [
            pltpu.VMEM((hidden, model_dim), BF),
            pltpu.VMEM((model_dim, hidden), BF),
            pltpu.SemaphoreType.DMA((2,)),
        ],
        flops=3 * 10**9,
        bytes_moved=10**7,
    )(place_rows, act_low, d_pre_low, norm_low, d_up)
    ins = [
        x_rows,
        mid_rows,
        d_norm_part,
        d_norm_got,
        d_pre,
        heads_out,
        query,
        keys,
        values,
        x_ext,
    ]
    last_shapes = (
        grads_shape,
        rows_of(head_cols),
        rows_of(2 * head_cols, rows=seqs * span),
        rows_of(model_dim, F32),
        rows_of(head_cols, rows=SMALL_ROWS),
    )
    slot_grads, d_query, dkv, d_mid, small = kernel_call(
        functools.partial(
            attend_back_kernel,
            dims,
            seq_count,
            attn_tiles,
            (tile_count, slot_count),
            (seq_count * sum(rows_per[:-1]), rows_per[-1], glob_cells, glob_block),
        ),
        "attend_back",
        32,
        last_shapes,
        [scalars(), scalars(), whole(norm_shape.shape)]
        + specs(ins)
        + [spec_out]
        + specs([rel_low, glob_bias, norm_params])
        + [any_space()],
        (any_space(),) + tuple(specs(last_shapes[1:])),
        [
            pltpu.VMEM((row_count, head_cols), BF),
            pltpu.VMEM((row_count, model_dim), BF),
            pltpu.VMEM((2 * head_cols // LANES, seqs * span, LANES), F32),
            pltpu.VMEM((head_cols, model_dim), BF),
            pltpu.VMEM((model_dim, head_cols), BF),
            pltpu.VMEM((model_dim, head_cols), BF),
            pltpu.VMEM((model_dim, head_cols), BF),
            pltpu.VMEM((side, side), BF),
            pltpu.VMEM((LABEL_PAD, head_cols), F32),
            pltpu.VMEM((8, head_cols), F32),
            pltpu.VMEM((8, model_dim), F32),
            pltpu.VMEM((seq_count * glob_cells, LANES), F32),
            pltpu.VMEM((seq_count * glob_cells, LANES), BF),
            pltpu.SemaphoreType.DMA((6,)),
        ],
        {3 + len(ins) + 4: 0},
        flops=8 * 10**9,
        bytes_moved=2 * 10**7,
    )(block_now, place_rows, norm_two_grad, *ins, wall, rel_low, glob_bias, norm_params, slot_grads)

    bits = seq_bits(seq_count)
    carried = [
        [(RIM, (dkv, seq * span + at)) for seq in range(seqs)] for at in (0, RIM + block_len)
    ]
    sums, small, (to_last, to_next) = scatter_rows(
        slot_grads, rows_per, orders, small, bits[3:] + bits[:3], carried
    )
    from_next = lax.ppermute(to_last, "seq", [(i + 1, i) for i in range(seq_count - 1)])
    from_last = lax.ppermute(to_next, "seq", [(i, i + 1) for i in range(seq_count - 1)])

    weights_at = (kv_at, q_at)
    weights_held = [
        pltpu.VMEM((model_dim, model_dim), BF),
        pltpu.VMEM((model_dim, head_cols), BF),
        pltpu.SemaphoreType.DMA((2,)),
    ]
    dx_shapes = (
        jax.ShapeDtypeStruct(x_long.shape, F32),
        jax.ShapeDtypeStruct(x_long.shape, BF),
    )
    ins = [d_query, dkv, from_next, from_last, d_mid]
    dx_kept, dx_sent = kernel_call(
        functools.partial(dx_kernel, dims, weights_at),
        "dx_long",
        20,
        dx_shapes,
        [scalars()] + specs(ins) + [any_space()],
        tuple(specs(dx_shapes)),
        [pltpu.VMEM((seqs * block_len, 3 * head_cols), BF)] + weights_held,
        flops=10**9,
        bytes_moved=10**7,
    )(half_now, *ins, wall)
    dx_long = dx_kept + swap_cores(dx_sent).astype(F32)
    glob_shapes = (
        jax.ShapeDtypeStruct(x_glob.shape, F32),
        jax.ShapeDtypeStruct(x_glob.shape, BF),
    )
    ins = [d_query, sums[0], sums[1], d_mid]
    dx_kept, dx_sent = kernel_call(
        functools.partial(dx_glob_kernel, dims, weights_at),
        "dx_glob",
        12,
        glob_shapes,
        [scalars()] + specs(ins) + [any_space()],
        tuple(specs(glob_shapes)),
        [pltpu.VMEM((glob_cells, LANES), F32)] + weights_held,
        flops=10**8,
        bytes_moved=10**6,
    )(half_now, *ins, wall)
    dx_glob = dx_kept + swap_cores(dx_sent).astype(F32)

    state = (w_master, m_old, v_old, left_basis, right_basis, left_stats, right_stats)
    others = (rel_table, rel_m, rel_v, norm_params, norm_m, norm_v)
    new_state = soap_update(sums, small, state, others)
    w_new, m_new, v_new, left_q, right_q, left_s, right_s = new_state[:7]
    rel_new, rel_m_new, rel_v_new, norm_new, norm_m_new, norm_v_new = new_state[7:]
    return (
        y_long,
        y_glob,
        dx_long,
        dx_glob,
        w_new,
        m_new,
        v_new,
        left_q,
        right_q,
        left_s,
        right_s,
        rel_new,
        rel_m_new,
        rel_v_new,
        norm_new,
        norm_m_new,
        norm_v_new,
    )


def solution(mesh):
    in_specs = (
        P(None, ("seq", "ffn"), None),
        P(None, ("seq", "ffn"), None),
        P(None, "seq", None),
        P(None, ("seq", "ffn"), None),
        P(None, ("seq", "ffn"), None),
        P(),
        P(("seq", "ffn"), None, None),
        P(("seq", "ffn"), None, None),
        P(("seq", "ffn"), None, None),
        P(("seq", "ffn"), None, None),
        P(("seq", "ffn"), None, None),
        P(("seq", "ffn"), None, None),
        P(("seq", "ffn"), None, None),
        P(None, "ffn"),
        P(None, "ffn"),
        P(None, "ffn"),
        P(),
        P(),
        P(),
    )
    out_specs = (
        P(None, ("seq", "ffn"), None),
        P(None, ("seq", "ffn"), None),
        P(None, ("seq", "ffn"), None),
        P(None, ("seq", "ffn"), None),
        P(("seq", "ffn"), None, None),
        P(("seq", "ffn"), None, None),
        P(("seq", "ffn"), None, None),
        P(("seq", "ffn"), None, None),
        P(("seq", "ffn"), None, None),
        P(("seq", "ffn"), None, None),
        P(("seq", "ffn"), None, None),
        P(None, "ffn"),
        P(None, "ffn"),
        P(None, "ffn"),
        P(),
        P(),
        P(),
    )
    return jax.shard_map(
        on_device, mesh=mesh, in_specs=in_specs, out_specs=out_specs, check_vma=False
    )
```

```python
import functools
import math

import jax
import jax.numpy as jnp
from jax import lax
from jax.experimental import pallas as pl
from jax.experimental.pallas import tpu as pltpu
from jax.sharding import PartitionSpec as P

HEADS = 12
FF = 3072
RADIUS = 84
STEP = 10

BETA_ONE = 0.9
BETA_TWO = 0.95
LEARN_RATE = 0.02
ADAM_RATE = 0.6
WEIGHT_DECAY = 0.01
ADAM_EPS = 1e-08
NORM_EPS = 1e-12
NEG_FILL = -1e30
BF = jnp.bfloat16
F32 = jnp.float32


def seq_bits(count):
    return [1 << at for at in range(count.bit_length() - 1)]


def swap_with(values, bit):
    count = lax.axis_size("seq")
    return lax.ppermute(values, "seq", [(i, i ^ bit) for i in range(count)])


def slot_parts(slots, count):
    bits = seq_bits(count)
    low, high = bits[:3], bits[3:]
    cuts = [slots * at // 14 for at in (0, 5, 10, 14)]
    orders = [low[at:] + low[:at] + high for at in range(3)]
    return [(a, b, order) for a, b, order in zip(cuts, cuts[1:], orders) if b > a]


def part_rows(parts, side, extra):
    rows = [(last - first) * side for first, last, _ in parts]
    return rows[:-1] + [rows[-1] + extra]


def slot_places(owners, slots, rows, side):
    count = lax.axis_size("seq")
    apart = (owners // slots) ^ lax.axis_index("seq")
    inner = owners % slots
    place, row, base = jnp.zeros_like(owners), jnp.zeros_like(owners), 0
    for (first, last, order), many in zip(slot_parts(slots, count), rows):
        index = jnp.zeros_like(owners)
        for at, bit in enumerate(order):
            index = index + jnp.where((apart & bit) != 0, count >> (at + 1), 0)
        here = (inner >= first) & (inner < last)
        place = jnp.where(here, first * count + index * (last - first) + inner - first, place)
        row = jnp.where(here, base + index * many + (inner - first) * side, row)
        base += many * count
    return place, row


FAR_SIZE = 3 * 2**20


def move_kernel(plan, arrays, *refs):
    ins, outs, held, sems = refs[:arrays], refs[arrays : arrays + len(plan)], refs[arrays + len(plan) : -1], refs[-1]
    copies, sums, sem = [], [], 0
    for out, runs in zip(outs, plan):
        base = 0
        for rows, *terms in runs:
            here = out.at[pl.ds(base, rows)]
            targets = [here] if len(terms) == 1 else [held[len(sums) * 2 + k] for k in range(2)]
            waits = []
            for (at, start), target in zip(terms, targets):
                waits.append(pltpu.make_async_copy(ins[at].at[pl.ds(start, rows)], target, sems.at[sem]))
                waits[-1].start()
                sem += 1
            if len(terms) == 1:
                copies += waits
            else:
                sums.append((waits, targets, out, base, rows))
            base += rows
    for waits, (one, two), out, base, rows in sums:
        for wait in waits:
            wait.wait()
        step = next(s for s in (128, 112, 64, 48, 32, 16) if rows % s == 0)

        def add(i, carry):
            at = pl.multiple_of(i * step, 16)
            total = one[pl.ds(at, step), :].astype(F32) + two[pl.ds(at, step), :].astype(F32)
            out[pl.ds(base + at, step), :] = total.astype(BF)
            return carry

        lax.fori_loop(0, rows // step, add, 0)
    for copy in copies:
        copy.wait()


def move_rows(outputs):
    arrays, plan, scratch, count = [], [], [], 0
    for runs in outputs:
        plan.append([])
        for rows, *terms in runs:
            places = []
            for array, start in terms:
                found = [i for i, other in enumerate(arrays) if other is array]
                if not found:
                    arrays.append(array)
                places.append((found[0] if found else len(arrays) - 1, start))
                count += 1
            plan[-1].append((rows, *places))
            if len(terms) == 2:
                scratch += [pltpu.VMEM((rows, terms[0][0].shape[1]), BF)] * 2
    shapes = [(sum(run[0] for run in runs), runs[0][1][0].shape[1]) for runs in outputs]
    return pl.pallas_call(
        functools.partial(move_kernel, plan, len(arrays)),
        grid=(1,),
        out_shape=tuple(jax.ShapeDtypeStruct(shape, BF) for shape in shapes),
        in_specs=[
            pl.BlockSpec(memory_space=pltpu.HBM if array.size > FAR_SIZE else pl.ANY) for array in arrays
        ],
        out_specs=tuple(whole(shape) for shape in shapes),
        scratch_shapes=scratch + [pltpu.SemaphoreType.DMA((count,))],
        cost_estimate=pl.CostEstimate(
            flops=0, bytes_accessed=sum(6 * math.prod(s) for s in shapes), transcendentals=0
        ),
        compiler_params=pltpu.CompilerParams(vmem_limit_bytes=16 * 2**20),
        name="add_rows" if scratch else "join_rows",
    )(*arrays)


def run_sum(rows, one, one_at, two, two_at):
    return (rows, (one, one_at), (two, two_at))


def gather_rows(cells, extra, rows, orders):
    own = sum(rows)
    shared = orders[0][3:][::-1]
    got = [swap_with(values, shared[0]) for values in (cells, extra)]
    devices = [[(cells, 0), (extra, -cells.shape[0])], [(got[0], 0), (got[1], -cells.shape[0])]]
    if len(shared) > 1:
        (cells,) = move_rows([[(array.shape[0], (array, 0)) for runs in devices for array, _ in runs]])
        for bit in shared[1:-1]:
            got = swap_with(cells, bit)
            (cells,) = move_rows([[(cells.shape[0], (cells, 0)), (cells.shape[0], (got, 0))]])
        got = swap_with(cells, shared[-1])
        devices = [[(run, i * own)] for run in (cells, got) for i in range(cells.shape[0] // own)]
    starts = [sum(rows[:at]) for at in range(len(rows))]

    def runs_of(start, many):
        runs = []
        for pieces in devices:
            left, at = many, start
            for array, shift in pieces:
                here = min(left, array.shape[0] - (at + shift))
                if here > 0:
                    runs.append((here, (array, at + shift)))
                    left, at = left - here, at + here
        return runs

    parts = move_rows([runs_of(start, many) for start, many in zip(starts, rows)])
    for step in (2, 1):
        got = [swap_with(part, order[step]) for part, order in zip(parts, orders)]
        parts = move_rows([[(p.shape[0], (p, 0)), (p.shape[0], (g, 0))] for p, g in zip(parts, got)])
    got = [swap_with(part, order[0]) for part, order in zip(parts, orders)]
    return list(zip(parts, got))


def scatter_rows(cells, rows, orders, everywhere, order_everywhere, carried):
    count = lax.axis_size("seq")
    spans = [count * many for many in rows]
    starts = [sum(spans[:at]) for at in range(len(spans))]
    sends = [cells[a + r // 2 : a + r] for a, r in zip(starts, spans)]
    kept = move_rows([[(r // 2, (cells, a))] for a, r in zip(starts, spans)])
    kept = [(keep, 0, keep.shape[0]) for keep in kept]

    def all_sum():
        return [run_sum(everywhere.shape[0], everywhere, 0, all_got, 0)]

    for step in range(3):
        got = [swap_with(send, order[step]) for send, order in zip(sends, orders)]
        all_got = swap_with(everywhere, order_everywhere[step])
        halves = [r // 2 for _, _, r in kept]
        if step < 2:
            *sends, everywhere = move_rows(
                [[run_sum(h, k, a + h, g, h)] for h, (k, a, _), g in zip(halves, kept, got)] + [all_sum()]
            )
            keeps = move_rows([[run_sum(h, k, a, g, 0)] for h, (k, a, _), g in zip(halves, kept, got)])
            kept = [(keep, 0, h) for keep, h in zip(keeps, halves)]
    devices = count // 8

    def merged(at, many):
        return [
            run_sum(r, k, i * r, g, i * r)
            for i in range(at, at + many)
            for r, (k, _, _), g in zip(rows, kept, got)
        ]

    half = devices // 2
    send, everywhere, *carried = move_rows([merged(half, half), all_sum()] + carried)
    (keep,) = move_rows([merged(0, half)])
    for step, bit in enumerate(orders[0][3:]):
        got_all = swap_with(send, bit)
        all_got = swap_with(everywhere, order_everywhere[3 + step])
        if bit == orders[0][-1]:
            return (keep, got_all), (everywhere, all_got), carried
        half = keep.shape[0] // 2
        send, everywhere = move_rows([[run_sum(half, keep, half, got_all, half)], all_sum()])
        (keep,) = move_rows([[run_sum(half, keep, 0, got_all, 0)]])
    return None


def split_two(x):
    hi = x.astype(BF)
    return hi, (x - hi.astype(F32)).astype(BF)


def split_three(x):
    hi = x.astype(BF)
    rest = x - hi.astype(F32)
    mid = rest.astype(BF)
    return hi, mid, (rest - mid.astype(F32)).astype(BF)


def left_six(parts, axis):
    h, m, l = parts
    return jnp.concatenate([h, h, m, m, h, l], axis=axis)


def right_six(parts, axis):
    h, m, l = parts
    return jnp.concatenate([h, m, h, m, l, h], axis=axis)


def left_three(parts, axis):
    h, l = parts
    return jnp.concatenate([h, h, l], axis=axis)


def right_three(parts, axis):
    h, l = parts
    return jnp.concatenate([h, l, h], axis=axis)


def dot_on(a, b, ca, cb):
    return lax.dot_general(a, b, (((ca,), (cb,)), ((), ())), preferred_element_type=F32)


def dot_six(a, b, ca, cb):
    return dot_on(left_six(split_three(a), ca), right_six(split_three(b), cb), ca, cb)


def dot_one(a, b, ca, cb):
    return dot_on(a.astype(BF), b.astype(BF), ca, cb)


def dot_three(a, b, ca, cb):
    return dot_on(left_three(split_two(a), ca), right_three(split_two(b), cb), ca, cb)


PANEL = 32


def panel_inverse(a_ref, t_ref, npad, side, at):
    groups = PANEL // 8
    iota = lax.broadcasted_iota(jnp.int32, (8, npad), 0)
    a = []
    for i in range(PANEL):
        rows = a_ref[pl.ds(at + i, npad, stride=side), :]
        cols = rows.T[at : at + PANEL]
        a.append([cols[8 * g : 8 * g + 8] for g in range(groups)])
    z = [[None] * groups for _ in range(PANEL)]
    for j in range(PANEL):
        gj, sj = divmod(j, 8)
        r = lax.rsqrt(a[j][gj][sj : sj + 1])
        u = [None if g < gj else a[j][g] * r for g in range(groups)]
        below = list(u)
        below[gj] = jnp.where(iota > sj, u[gj], 0.0)
        for k in range(j + 1, PANEL):
            gk, sk = divmod(k, 8)
            row = u[gk][sk : sk + 1]
            for g in range(gk, groups):
                a[k][g] = a[k][g] - u[g] * row
        for c in range(j):
            row = z[c][gj][sj : sj + 1] * r
            z[c][gj] = jnp.where(iota == sj, row, z[c][gj]) - below[gj] * row
            for g in range(gj + 1, groups):
                z[c][g] = z[c][g] - u[g] * row
        z[j] = [
            jnp.zeros((8, npad), F32)
            if g < gj
            else (jnp.where(iota == sj, r, 0.0) - below[g] * r if g == gj else -u[g] * r)
            for g in range(groups)
        ]
    fill = jnp.zeros((side - PANEL, npad), F32)
    for c in range(PANEL):
        t_ref[pl.ds(c, npad, stride=PANEL), :] = jnp.concatenate(z[c] + [fill], axis=0).T


def adam_step(grad, refs, outs, where, decay_rate):
    param, first_mom, second_mom = [ref[where] for ref in refs]
    first_mom = BETA_ONE * first_mom + (1.0 - BETA_ONE) * grad
    second_mom = BETA_TWO * second_mom + (1.0 - BETA_TWO) * grad * grad
    direction = (
        first_mom
        / (1.0 - BETA_ONE**STEP)
        / (jnp.sqrt(second_mom / (1.0 - BETA_TWO**STEP)) + ADAM_EPS)
    )
    outs[0][where] = param - ADAM_RATE * (direction + decay_rate * param)
    outs[1][where] = first_mom
    outs[2][where] = second_mom


def small_updates(small_refs, refs, outs):
    total = small_refs[0][...].astype(F32) + small_refs[1][...].astype(F32)
    labels, cols = refs[0].shape
    rel = pltpu.roll(total, total.shape[0] - (RIM - RADIUS), 0)[:labels]
    adam_step(rel, refs[:3], outs[:3], (slice(None), slice(None)), WEIGHT_DECAY)
    halves = refs[3].shape[1] // cols
    for row in range(refs[3].shape[0]):
        for half in range(halves):
            at = SMALL_ROWS - 8 + row * halves + half
            where = (slice(row, row + 1), slice(half * cols, (half + 1) * cols))
            adam_step(total[at : at + 1], refs[3:], outs[3:], where, 0.0)


def soap_kernel(npad, kept_ref, got_ref, small_ref, small_got_ref, *refs):
    state, done = refs[:7], refs[13:20]
    given, a_ref, y_ref, mat_ref, t_ref, out_sems = refs[26:]
    n, side = state[0].shape[:2]
    many = next(k for k in (7, 2, 1) if n % k == 0)
    batch = next(b for b in (14, 7, 4, 2) if 2 * n % b == 0)
    small_updates((small_ref, small_got_ref), refs[7:13], refs[20:26])
    eye = (
        lax.broadcasted_iota(jnp.int32, (side, side), 0)
        == lax.broadcasted_iota(jnp.int32, (side, side), 1)
    ).astype(F32)

    def first(at, carry):
        slots = [at * many + k for k in range(many)]

        def old(kind):
            return [state[kind][i] for i in slots]

        lefts, rights = old(3), old(4)
        tiles = [pl.ds(pl.multiple_of(i * side, side), side) for i in slots]
        grads = [kept_ref[rows, :].astype(F32) + got_ref[rows, :].astype(F32) for rows in tiles]
        halves = [split_two(x) for x in grads]
        new_l = [
            BETA_TWO * x + (1.0 - BETA_TWO) * dot_on(left_three(p, 1), right_three(p, 1), 1, 1)
            for x, p in zip(old(5), halves)
        ]
        new_r = [
            BETA_TWO * x + (1.0 - BETA_TWO) * dot_on(left_three(p, 0), right_three(p, 0), 0, 0)
            for x, p in zip(old(6), halves)
        ]
        mats = [dot_six(x, y, 1, 0) for x, y in zip(new_l + new_r, lefts + rights)]
        thirds = [split_three(x) for x in mats]
        grams = [dot_on(left_six(p, 0), right_six(p, 0), 0, 0) for p in thirds]
        for k, i in enumerate(slots):
            given[5, i] = new_l[k]
            given[6, i] = new_r[k]
            for kind in range(2):
                mat_ref[2 * i + kind] = mats[kind * many + k]
                rows = pl.ds(pl.multiple_of((2 * i + kind) * side, side), side)
                a_ref[rows, :] = grams[kind * many + k]
                y_ref[rows, :] = eye
        return carry

    def rotate(slots):
        def old(kind):
            return [state[kind][i] for i in slots]

        lefts, rights = old(3), old(4)
        tiles = [slice(i * side, (i + 1) * side) for i in slots]
        grads = [kept_ref[rows, :].astype(F32) + got_ref[rows, :].astype(F32) for rows in tiles]
        turned = [dot_one(x, y, 0, 0) for x, y in zip(lefts, grads)]
        rotated = [dot_one(x, y, 1, 0) for x, y in zip(turned, rights)]
        moms = [BETA_ONE * old_m + (1.0 - BETA_ONE) * x for old_m, x in zip(old(1), rotated)]
        secs = [BETA_TWO * old_v + (1.0 - BETA_TWO) * x * x for old_v, x in zip(old(2), rotated)]
        steps = [
            x / (1.0 - BETA_ONE**STEP) / (jnp.sqrt(y / (1.0 - BETA_TWO**STEP)) + ADAM_EPS)
            for x, y in zip(moms, secs)
        ]
        turned = [dot_one(x, y, 1, 0) for x, y in zip(lefts, steps)]
        backs = [dot_one(x, y, 1, 1) for x, y in zip(turned, rights)]
        for k, (i, weight) in enumerate(zip(slots, old(0))):
            given[0, i] = weight - LEARN_RATE * (backs[k] + WEIGHT_DECAY * weight)
            given[1, i] = moms[k]
            given[2, i] = secs[k]

    def send(kinds):
        copies = [pltpu.make_async_copy(given.at[k], done[k], out_sems.at[k]) for k in kinds]
        for copy in copies:
            copy.start()
        return copies

    lax.fori_loop(0, n // many, first, 0)
    copies = send((5, 6))
    if npad > 2 * n:
        a_ref[2 * n * side :, :] = jnp.concatenate([eye] * (npad - 2 * n), axis=0)
    for at in range(0, side, PANEL):
        beside = range(at * n // side, (at + PANEL) * n // side)
        rotate(list(beside))
        panel_inverse(a_ref, t_ref, npad, side, at)

        def update(i, carry):
            bases = [pl.multiple_of((i * batch + b) * side, side) for b in range(batch)]
            rows = [pl.ds(base + at, PANEL) for base in bases]
            both = [jnp.concatenate([a_ref[r, :], y_ref[r, :]], axis=1) for r in rows]
            turns = [
                t_ref[pl.ds(pl.multiple_of((i * batch + b) * PANEL, PANEL), PANEL), :][:, :PANEL]
                for b in range(batch)
            ]
            if at + PANEL < side:
                rest = [pl.ds(base + at + PANEL, side - at - PANEL) for base in bases]
                old = [(a_ref[r, :], y_ref[r, :]) for r in rest]
            fresh = [dot_six(t, x, 0, 0) for t, x in zip(turns, both)]
            if at + PANEL < side:
                changes = []
                for x in fresh:
                    parts = split_three(x)
                    cut = tuple(p[:, at + PANEL : side] for p in parts)
                    changes.append(dot_on(left_six(cut, 0), right_six(parts, 0), 0, 0))
                for r, (old_a, old_y), change in zip(rest, old, changes):
                    a_ref[r, :] = old_a - change[:, :side]
                    y_ref[r, :] = old_y - change[:, side:]
            for r, x in zip(rows, fresh):
                y_ref[r, :] = x[:, side:]
            return carry

        lax.fori_loop(0, 2 * n // batch, update, 0)

    copies += send((0, 1, 2))

    def last(at, carry):
        slots = [at * many + k for k in range(many)]
        both = [2 * i + k for i in slots for k in range(2)]
        mats = [mat_ref[j] for j in both]
        turns = [y_ref[pl.ds(pl.multiple_of(j * side, side), side), :] for j in both]
        bases = [dot_three(x, y, 1, 1) for x, y in zip(mats, turns)]
        for k, i in enumerate(slots):
            for kind in range(2):
                given[3 + kind, i] = bases[2 * k + kind]
                target = done[3 + kind].at[i]
                pltpu.make_async_copy(given.at[3 + kind, i], target, out_sems.at[3 + kind]).start()
        return carry

    lax.fori_loop(0, n // many, last, 0)
    for copy in copies:
        copy.wait()
    for kind in (3, 4):
        pltpu.make_async_copy(given.at[kind], done[kind], out_sems.at[kind]).wait()


def soap_update(grads, small, state, others):
    n, side = state[0].shape[:2]
    npad = -(-2 * n // 8) * 8
    ins = [*grads, *small, *state, *others]
    outs = [*state, *others]
    return pl.pallas_call(
        functools.partial(soap_kernel, npad),
        grid=(1,),
        out_shape=tuple(jax.ShapeDtypeStruct(s.shape, F32) for s in outs),
        in_specs=[whole(array.shape) for array in ins],
        out_specs=(far_space(),) * len(state) + tuple(whole(array.shape) for array in others),
        scratch_shapes=[
            pltpu.VMEM((7, n, side, side), F32),
            pltpu.VMEM((npad * side, side), F32),
            pltpu.VMEM((npad * side, side), F32),
            pltpu.VMEM((2 * n, side, side), F32),
            pltpu.VMEM((npad * PANEL, side), F32),
            pltpu.SemaphoreType.DMA((7,)),
        ],
        cost_estimate=pl.CostEstimate(
            flops=n * 40 * side**3, bytes_accessed=n * 60 * side * side, transcendentals=0
        ),
        compiler_params=pltpu.CompilerParams(vmem_limit_bytes=32 * 2**20),
        name="soap",
    )(*ins)


LANES = 128
LABEL_PAD = 256
RIM = 96
SMALL_ROWS = 192


def up_to(value, unit):
    return -(-value // unit) * unit


def block_at(shape, *index):
    return pl.BlockSpec(shape, lambda i: index, pipeline_mode=pl.Buffered(1))


def whole(shape):
    return block_at(shape, *[0] * len(shape))


def any_space():
    return pl.BlockSpec(memory_space=pl.ANY)


def far_space():
    return pl.BlockSpec(memory_space=pltpu.HBM)


def scalars():
    return pl.BlockSpec(memory_space=pltpu.SMEM)


def kernel_call(body, name, mib, out_shape, in_specs, out_specs, scratch=(), aliases=None, flops=0, bytes_moved=0):
    return pl.pallas_call(
        body,
        name=name,
        grid=(1,),
        out_shape=out_shape,
        in_specs=in_specs,
        out_specs=out_specs,
        scratch_shapes=list(scratch),
        input_output_aliases=aliases or {},
        cost_estimate=pl.CostEstimate(flops=flops, bytes_accessed=bytes_moved, transcendentals=0),
        compiler_params=pltpu.CompilerParams(vmem_limit_bytes=mib * 2**20),
    )


def start_tiles(row_ref, col_ref, kind_ref, sources, tiles, wall_ref, sems):
    base = 0
    for source, many in zip(sources, tiles):

        def start(i, carry):
            for k in range(many):
                place = base + i * many + k
                kind = kind_ref[place]

                @pl.when(kind < 2)
                def _():
                    row = pl.multiple_of(row_ref[place], LANES)
                    col = pl.multiple_of(col_ref[place], LANES)
                    pltpu.make_async_copy(
                        source.at[i, pl.ds(k * LANES, LANES)],
                        wall_ref.at[pl.ds(row, LANES), pl.ds(col, LANES)],
                        sems.at[kind],
                    ).start()

            return carry

        lax.fori_loop(0, source.shape[0], start, 0)
        base += source.shape[0] * many


def wait_rows(wall_ref, rows, sem):
    part = wall_ref.at[pl.ds(0, rows)]
    pltpu.make_async_copy(part, part, sem).wait()


def low_lanes(rows):
    return lax.broadcasted_iota(jnp.int32, (rows, LANES), 1) < LANES // 2


def stack_heads(pair):
    low = low_lanes(pair.shape[0])
    zero = jnp.zeros_like(pair)
    return jnp.concatenate([jnp.where(low, pair, zero), jnp.where(low, zero, pair)], axis=0)


def merge_stack(stacked):
    rows = stacked.shape[0] // 2
    return jnp.where(low_lanes(rows), stacked[:rows], stacked[rows:])


def skew(table, width):
    rows = table.shape[0] // 2
    padded = jnp.concatenate(
        [table, jnp.zeros((table.shape[0], width - table.shape[1]), F32)], axis=1
    )
    halves = [
        pltpu.roll(padded[at : at + rows], 0, 1, stride=1, stride_axis=0) for at in (0, rows)
    ]
    return jnp.concatenate(halves, axis=0)


def unskew(grid, width):
    rows = grid.shape[0] // 2
    lanes = grid.shape[1]
    parts = []
    for at in range(0, 2 * rows, 8):
        shift = (at % rows) % lanes
        part = grid[at : at + 8]
        parts.append(part if shift == 0 else pltpu.roll(part, lanes - shift, 1))
    moved = jnp.concatenate([part[:, :width] for part in parts], axis=0)
    lanes = width
    index = lax.broadcasted_iota(jnp.int32, moved.shape, 0)
    for bit in (1, 2, 4):
        moved = jnp.where((index & bit) != 0, pltpu.roll(moved, lanes - bit, 1), moved)
    return moved


def softmax_rows(scores):
    top = jnp.max(scores, axis=-1, keepdims=True)
    raised = jnp.exp(scores - top)
    return raised * (1.0 / jnp.sum(raised, axis=-1, keepdims=True))


def window_keys(ref, base, at, width, ext, globs, cols):
    return jnp.concatenate(
        [ref[pl.ds(base + at, width), cols], ref[pl.ds(base + ext, globs), cols]], axis=0
    )


def glob_row_mask(shape, seq, glob_block):
    row = lax.broadcasted_iota(jnp.int32, shape, 0) % (shape[0] // 2)
    return (row >= seq * glob_block) & (row < (seq + 1) * glob_block)


def window_bias(block, blocks, chunk, dims):
    _, block_len, _, _, width, globs, _ = dims
    shape = (2 * LANES, width + globs)
    key = lax.broadcasted_iota(jnp.int32, shape, 1)
    query = lax.broadcasted_iota(jnp.int32, shape, 0) % LANES
    offset = key - query - (RIM - RADIUS)
    token = block * block_len - RIM + chunk * LANES + key
    near = (offset >= 0) & (offset <= 2 * RADIUS) & (token >= 0) & (token < blocks * block_len)
    return jnp.where(near | (key >= width), 0.0, NEG_FILL)


def attend_kernel(dims, wall_at, blocks, row_ref, col_ref, kind_ref, block_ref, xr_ref, rel_ref, gbias_ref,
                  left_ref, right_ref, *refs):
    q_ref, k_ref, v_ref, o_ref, part_ref, xe_ref, wall_out, wall_ref, glob_low, glob_cells, sems = refs[-11:]
    sources = refs[:-11]
    seqs, block_len, glob_block, ext, width, globs, scale = dims
    feed_rows, attn_rows, kv_at, q_at, out_at, tiles = wall_at
    model_dim = xr_ref.shape[1]
    head_cols = q_ref.shape[1]
    start_tiles(row_ref, col_ref, kind_ref, sources, tiles, wall_ref, sems)
    span = ext + globs
    cells = glob_low.shape[0] // blocks
    copies, base = [], 0
    for source in sources[-2:]:
        rows = source.shape[1] - cells
        for i in range(source.shape[0]):
            copies.append((source.at[i, pl.ds(rows, cells)], glob_low.at[pl.ds(base, cells)]))
            base += cells
    for source, target in copies:
        pltpu.make_async_copy(source, target, sems.at[3]).start()
    for seq in range(seqs):
        at = seq * span
        rim = pl.ds(seq * RIM, RIM)
        pltpu.make_async_copy(left_ref.at[rim], xe_ref.at[pl.ds(at, RIM)], sems.at[4]).start()
        pltpu.make_async_copy(
            right_ref.at[rim], xe_ref.at[pl.ds(at + RIM + block_len, RIM)], sems.at[4]
        ).start()
        at += RIM
        xe_ref[at : at + block_len] = xr_ref[seq * block_len : (seq + 1) * block_len]
        at += block_len + RIM
        if ext > block_len + 2 * RIM:
            xe_ref[at : seq * span + ext] = jnp.zeros((ext - block_len - 2 * RIM, model_dim), BF)
    pltpu.make_async_copy(glob_low, glob_low, sems.at[3]).wait()
    glob_cells[...] = glob_low[...].astype(F32)
    cols = model_dim // LANES
    for seq in range(seqs):
        for r in range(glob_block):
            at = seq * span + ext + r * blocks
            for c in range(cols):
                source = pl.ds((seq * glob_block + r) * cols + c, blocks, stride=cells)
                xe_ref[at : at + blocks, c * LANES : (c + 1) * LANES] = glob_cells[source, :].astype(BF)
    rims = xe_ref.at[pl.ds(0, 2 * seqs * RIM)]
    pltpu.make_async_copy(rims, rims, sems.at[4]).wait()
    wait_rows(wall_ref, attn_rows, sems.at[0])
    wq_ref = wall_ref.at[pl.ds(q_at, model_dim), pl.ds(0, head_cols)]
    wkv_ref = wall_ref.at[pl.ds(kv_at, model_dim)]
    wo_ref = wall_ref.at[pl.ds(out_at, head_cols)]
    pairs = head_cols // LANES
    glob_at = seqs * block_len
    glob_rows = q_ref.shape[0] - glob_at
    span = ext + globs
    chunks = block_len // LANES
    q_ref[...] = dot_on(xr_ref[...], wq_ref[...], 1, 0).astype(BF)

    def project(i, carry):
        rows = pl.ds(pl.multiple_of(i * 256, 256), 256)
        both = dot_on(xe_ref[rows, :], wkv_ref[...], 1, 0).astype(BF)
        k_ref[rows, :] = both[:, :head_cols]
        v_ref[rows, :] = both[:, head_cols:]
        return carry

    lax.fori_loop(0, seqs * span // 256, project, 0)
    wait_rows(wall_ref, feed_rows, sems.at[1])
    keep = pltpu.make_async_copy(wall_ref, wall_out, sems.at[2])
    keep.start()

    def window(i, carry):
        seq, chunk = i // chunks, i % chunks
        rows = pl.ds(pl.multiple_of(i * LANES, LANES), LANES)
        base = pl.multiple_of(seq * span, LANES)
        at = pl.multiple_of(chunk * LANES, LANES)
        bias = window_bias(block_ref[0], blocks, chunk, dims)
        cols = [slice(pair * LANES, (pair + 1) * LANES) for pair in range(pairs)]
        query = [stack_heads(q_ref[rows, c] * scale) for c in cols]
        keys = [window_keys(k_ref, base, at, width, ext, globs, c) for c in cols]
        values = [window_keys(v_ref, base, at, width, ext, globs, c) for c in cols]
        near = [dot_on(q, rel_ref[:, c], 1, 1) for q, c in zip(query, cols)]
        scores = [dot_on(q, k, 1, 1) for q, k in zip(query, keys)]
        scores = [x + skew(y, width + globs) + bias for x, y in zip(scores, near)]
        weights = [softmax_rows(x).astype(BF) for x in scores]
        outs = [merge_stack(dot_on(w, v, 1, 0)).astype(BF) for w, v in zip(weights, values)]
        for c, out in zip(cols, outs):
            o_ref[rows, c] = out
        return carry

    lax.fori_loop(0, seqs * chunks, window, 0)
    rows = slice(glob_at, glob_at + glob_rows)
    both = [(pair, seq) for pair in range(pairs) for seq in range(seqs)]
    cols = [slice(pair * LANES, (pair + 1) * LANES) for pair in range(pairs)]
    spans = [slice(seq * span, (seq + 1) * span) for seq in range(seqs)]
    query = [stack_heads(q_ref[rows, c] * scale) for c in cols]
    bias = [jnp.concatenate([gbias_ref[seq]] * 2, axis=0) for seq in range(seqs)]
    scores = [dot_on(query[pair], k_ref[spans[seq], cols[pair]], 1, 1) + bias[seq] for pair, seq in both]
    weights = [softmax_rows(x).astype(BF) for x in scores]
    outs = [dot_on(w, v_ref[spans[seq], cols[pair]], 1, 0) for w, (pair, seq) in zip(weights, both)]
    for pair in range(pairs):
        total = outs[pair * seqs]
        for seq in range(1, seqs):
            total = jnp.where(glob_row_mask(total.shape, seq, glob_block), outs[pair * seqs + seq], total)
        used = lax.broadcasted_iota(jnp.int32, total.shape, 0) % glob_rows < seqs * glob_block
        o_ref[rows, cols[pair]] = merge_stack(jnp.where(used, total, 0.0)).astype(BF)
    part_ref[...] = dot_on(o_ref[...], wo_ref[...], 1, 0).astype(BF)
    keep.wait()


def norm_parts(values):
    center = values - jnp.mean(values, axis=-1, keepdims=True)
    spread = jnp.mean(center * center, axis=-1, keepdims=True)
    rate = lax.rsqrt(spread + NORM_EPS)
    return center * rate, rate


def norm_back(grad, normed, rate, gain):
    scaled = grad * gain
    return (
        scaled
        - jnp.mean(scaled, axis=-1, keepdims=True)
        - normed * jnp.mean(scaled * normed, axis=-1, keepdims=True)
    ) * rate


def row_loop(total, body):
    step = 176 if total % 176 == 0 else 16

    def run(i, carry):
        body(pl.ds(pl.multiple_of(i * step, 16), step))
        return carry

    lax.fori_loop(0, total // step, run, 0)


def col_loop(total, body, step=256):
    def run(i, carry):
        body(i)
        return carry

    lax.fori_loop(0, total // step, run, 0)


GELU_RATE = 0.7978845608028654
GELU_CUBE = 0.044715


def gelu_parts(u):
    square = u * u
    curve = jnp.tanh(GELU_RATE * u * (1.0 + GELU_CUBE * square))
    return square, curve


def feed_kernel(xr_ref, part_ref, got_ref, norm_ref, wu_ref, wd_ref, h_ref, hb_ref, u_ref, a_ref, down_ref, mid_out,
                mid_ref, sems):
    model_dim = xr_ref.shape[1]
    gain, offset = norm_ref[0:1], norm_ref[1:2]

    def norm(rows):
        mid = xr_ref[rows, :].astype(F32) + (part_ref[rows, :].astype(F32) + got_ref[rows, :].astype(F32))
        mid_ref[rows, :] = mid
        normed, _ = norm_parts(mid)
        out = normed * gain + offset
        h_ref[rows, :] = out
        hb_ref[rows, :] = out.astype(BF)

    row_loop(xr_ref.shape[0], norm)
    keep = pltpu.make_async_copy(mid_ref, mid_out, sems.at[0])
    keep.start()
    per_half = model_dim // 256

    def up(j):
        rows = pl.ds(pl.multiple_of((j // per_half) * model_dim, 256), model_dim)
        cols = pl.ds(pl.multiple_of((j % per_half) * 256, 256), 256)
        here = pl.ds(pl.multiple_of(j * 256, 256), 256)
        u = dot_on(hb_ref[...], wu_ref[rows, cols], 1, 0)
        u_ref[:, here] = u
        _, curve = gelu_parts(u)
        a_ref[:, here] = (0.5 * u * (1.0 + curve)).astype(BF)

    col_loop(u_ref.shape[1], up)

    def down(j):
        cols = pl.ds(pl.multiple_of(j * 256, 256), 256)
        down_ref[:, cols] = dot_on(a_ref[...], wd_ref[:, cols], 1, 0).astype(BF)

    col_loop(model_dim, down)
    keep.wait()


def own_rows(ref, half, seqs, block_len, glob_block):
    per = block_len // 2
    long_part = [
        ref[pl.ds(pl.multiple_of(seq * block_len + half * per, per), per), :] for seq in range(seqs)
    ]
    base, few = seqs * block_len, glob_block // 2
    globs = ref[base:, :]
    glob_part = [
        jnp.where(
            half == 0,
            globs[seq * glob_block : seq * glob_block + few],
            globs[seq * glob_block + few : (seq + 1) * glob_block],
        )
        for seq in range(seqs)
    ]
    return long_part, glob_part


def feed_back_kernel(dims, half_ref, h_ref, down_ref, got_ref, u_ref, dy_ref, norm_ref, wu_ref, wd_ref,
                     y_long_ref, y_glob_ref, dx_out, dxb_ref, du_ref, dh_ref, gn_ref, y_ref, dx_ref, sems):
    model_dim = h_ref.shape[1]
    gain, offset = norm_ref[2:3], norm_ref[3:4]
    gn_ref[...] = jnp.zeros_like(gn_ref)

    def norm(rows):
        out = h_ref[rows, :] + (down_ref[rows, :].astype(F32) + got_ref[rows, :].astype(F32))
        normed, rate = norm_parts(out)
        y_ref[rows, :] = normed * gain + offset
        grad = dy_ref[rows, :].astype(F32)
        gn_ref[0:1] += jnp.sum(grad * normed, axis=0, keepdims=True)
        gn_ref[1:2] += jnp.sum(grad, axis=0, keepdims=True)
        dx = norm_back(grad, normed, rate, gain)
        dx_ref[rows, :] = dx
        dxb_ref[rows, :] = dx.astype(BF)

    row_loop(h_ref.shape[0], norm)
    keep = pltpu.make_async_copy(dx_ref, dx_out, sems.at[0])
    keep.start()
    long_part, glob_part = own_rows(y_ref, half_ref[0], *dims[:3])
    for seq in range(dims[0]):
        y_long_ref[seq] = long_part[seq].astype(BF)
        y_glob_ref[seq] = glob_part[seq].astype(BF)

    def act(j):
        here = pl.ds(pl.multiple_of(j * 256, 256), 256)
        da = dot_on(dxb_ref[...], wd_ref[here, :], 1, 1)
        u = u_ref[:, here]
        square, curve = gelu_parts(u)
        slope = 0.5 * (1.0 + curve) + 0.5 * u * (1.0 - curve * curve) * (
            GELU_RATE * (1.0 + 3.0 * GELU_CUBE * square)
        )
        du_ref[:, here] = (da * slope).astype(BF)

    col_loop(u_ref.shape[1], act)
    halves = u_ref.shape[1] // model_dim

    def lower(j):
        cols = pl.ds(pl.multiple_of(j * 256, 256), 256)
        total = 0.0
        for half in range(halves):
            rows = pl.ds(pl.multiple_of(half * model_dim + j * 256, 256), 256)
            total = total + dot_on(
                du_ref[:, half * model_dim : (half + 1) * model_dim], wu_ref[rows, :], 1, 1
            )
        dh_ref[:, cols] = total.astype(BF)

    col_loop(model_dim, lower)
    keep.wait()


def send_tiles(stage_ref, row, rows, first, place_ref, out_ref, sem):
    cols = stage_ref.shape[1] // LANES
    for r in range(rows):
        for c in range(cols):
            pltpu.make_async_copy(
                stage_ref.at[pl.ds(row + r * LANES, LANES), pl.ds(c * LANES, LANES)],
                out_ref.at[pl.ds(pl.multiple_of(place_ref[first + r * cols + c], 16), LANES)],
                sem,
            ).start()


def feed_grads_kernel(tiles_at, place_ref, a_ref, dxb_ref, hb_ref, du_ref, out_ref, down_stage, up_stage, sems):
    up_at, down_at = tiles_at
    model_dim = dxb_ref.shape[1]

    def down(j):
        row = pl.multiple_of(j * 256, 256)
        rows = pl.ds(row, 256)
        down_stage[rows, :] = dot_on(a_ref[:, rows], dxb_ref[...], 0, 0).astype(BF)
        send_tiles(down_stage, row, 2, down_at + j * 2 * (model_dim // LANES), place_ref, out_ref, sems.at[0])

    col_loop(a_ref.shape[1], down)

    def up(j):
        row = pl.multiple_of(j * 256, 256)
        rows = pl.ds(row, 256)
        up_stage[rows, :] = dot_on(hb_ref[:, rows], du_ref[...], 0, 0).astype(BF)
        send_tiles(
            up_stage, row, 2, up_at + j * 2 * (du_ref.shape[1] // LANES), place_ref, out_ref, sems.at[1]
        )

    col_loop(model_dim, up)
    pltpu.make_async_copy(down_stage, down_stage, sems.at[0]).wait()
    pltpu.make_async_copy(up_stage, up_stage, sems.at[1]).wait()


def attend_back_kernel(dims, blocks, attn_tiles, tile_counts, glob_at_rows, block_ref, place_ref, norm_two_ref, xr_ref, x1_ref, dh_ref, dh_got_ref, dx_ref, o_ref,
                       q_ref, k_ref, v_ref, xe_ref, wo_ref, rel_ref, gbias_ref, norm_ref, grads_in,
                       grads_ref, dq_ref, dkv_ref, mid_ref, small_ref,
                       do_ref, midb_ref, dkv_acc, out_stage, q_stage, k_stage, v_stage, none_ref,
                       drel_ref, norms_ref, gn_ref, glob_stage, glob_low, sems):
    seqs, block_len, glob_block, ext, width, globs, scale = dims
    head_cols = q_ref.shape[1]
    pairs = head_cols // LANES
    glob_at = seqs * block_len
    glob_rows = q_ref.shape[0] - glob_at
    span = ext + globs
    chunks = block_len // LANES
    gain = norm_ref[0:1]
    gn_ref[...] = jnp.zeros_like(gn_ref)

    def norm(rows):
        normed, rate = norm_parts(x1_ref[rows, :])
        grad = dh_ref[rows, :].astype(F32) + dh_got_ref[rows, :].astype(F32) + dx_ref[rows, :]
        gn_ref[0:1] += jnp.sum(grad * normed, axis=0, keepdims=True)
        gn_ref[1:2] += jnp.sum(grad, axis=0, keepdims=True)
        out = norm_back(grad, normed, rate, gain)
        mid_ref[rows, :] = out
        midb_ref[rows, :] = out.astype(BF)

    row_loop(xr_ref.shape[0], norm)
    do_ref[...] = dot_on(midb_ref[...], wo_ref[...], 1, 1).astype(BF)
    out_stage[...] = dot_on(o_ref[...], midb_ref[...], 0, 0).astype(BF)
    send_tiles(out_stage, 0, out_stage.shape[0] // LANES, 3 * attn_tiles, place_ref, grads_ref, sems.at[0])
    none_ref[...] = jnp.zeros_like(none_ref)
    spare = []
    for tile in range(*tile_counts):
        target = grads_ref.at[pl.ds(pl.multiple_of(place_ref[tile], 16), LANES)]
        spare.append(pltpu.make_async_copy(none_ref, target, sems.at[4]))
        spare[-1].start()
    dkv_acc[...] = jnp.zeros_like(dkv_acc)
    drel_ref[...] = jnp.zeros_like(drel_ref)

    def grads_of(scores, grad_out, values):
        weights = softmax_rows(scores)
        dp = dot_on(grad_out, values, 1, 1)
        delta = jnp.sum(weights * dp, axis=-1, keepdims=True)
        return weights.astype(BF), weights * (dp - delta)

    def window(i, carry):
        seq, chunk = i // chunks, i % chunks
        rows = pl.ds(pl.multiple_of(i * LANES, LANES), LANES)
        base = pl.multiple_of(seq * span, LANES)
        at = pl.multiple_of(chunk * LANES, LANES)
        near_rows = pl.ds(base + at, width)
        far_rows = pl.ds(base + ext, globs)
        bias = window_bias(block_ref[0], blocks, chunk, dims)
        near = lax.broadcasted_iota(jnp.int32, bias.shape, 1) < width
        cols = [slice(pair * LANES, (pair + 1) * LANES) for pair in range(pairs)]
        query = [stack_heads(q_ref[rows, c] * scale) for c in cols]
        grad_out = [stack_heads(do_ref[rows, c]) for c in cols]
        keys = [window_keys(k_ref, base, at, width, ext, globs, c) for c in cols]
        values = [window_keys(v_ref, base, at, width, ext, globs, c) for c in cols]
        labels = [rel_ref[:, c] for c in cols]
        shifted = [dot_on(q, x, 1, 1) for q, x in zip(query, labels)]
        scores = [dot_on(q, k, 1, 1) for q, k in zip(query, keys)]
        scores = [x + skew(y, width + globs) + bias for x, y in zip(scores, shifted)]
        pairs_of = [grads_of(x, g, v) for x, g, v in zip(scores, grad_out, values)]
        dsb = [ds.astype(BF) for _, ds in pairs_of]
        by_label = [unskew(jnp.where(near, x.astype(F32), 0.0), LABEL_PAD).astype(BF) for x in dsb]
        dv = [dot_on(w, g, 0, 0) for (w, _), g in zip(pairs_of, grad_out)]
        dk = [dot_on(x, q, 0, 0) for x, q in zip(dsb, query)]
        dq = [
            dot_on(x, k, 1, 0) + dot_on(y, l, 1, 0) for x, k, y, l in zip(dsb, keys, by_label, labels)
        ]
        drel = [dot_on(y, q, 0, 0) for y, q in zip(by_label, query)]
        for pair, c in enumerate(cols):
            dq_ref[rows, c] = (merge_stack(dq[pair]) * scale).astype(BF)
            drel_ref[:, c] += drel[pair]
            for at_acc, grad in ((pair, dk[pair]), (pairs + pair, dv[pair])):
                dkv_acc[at_acc, near_rows] += grad[:width]
                dkv_acc[at_acc, far_rows] += grad[width:]
        return carry

    lax.fori_loop(0, seqs * chunks, window, 0)
    rows = slice(glob_at, glob_at + glob_rows)
    both = [(pair, seq) for pair in range(pairs) for seq in range(seqs)]
    cols = [slice(pair * LANES, (pair + 1) * LANES) for pair in range(pairs)]
    spans = [slice(seq * span, (seq + 1) * span) for seq in range(seqs)]
    query = [stack_heads(q_ref[rows, c] * scale) for c in cols]
    grad_out = [stack_heads(do_ref[rows, c]) for c in cols]
    bias = [jnp.concatenate([gbias_ref[seq]] * 2, axis=0) for seq in range(seqs)]
    keys = [k_ref[spans[seq], cols[pair]] for pair, seq in both]
    scores = [dot_on(query[pair], k, 1, 1) + bias[seq] for k, (pair, seq) in zip(keys, both)]
    grads = [
        grads_of(x, grad_out[pair], v_ref[spans[seq], cols[pair]]) for x, (pair, seq) in zip(scores, both)
    ]
    own = [glob_row_mask(scores[0].shape, seq, glob_block) for seq in range(seqs)]
    weights = [jnp.where(own[seq], w.astype(F32), 0.0).astype(BF) for (w, _), (_, seq) in zip(grads, both)]
    dsb = [jnp.where(own[seq], ds, 0.0).astype(BF) for (_, ds), (_, seq) in zip(grads, both)]
    dk = [dot_on(x, query[pair], 0, 0) for x, (pair, _) in zip(dsb, both)]
    dv = [dot_on(w, grad_out[pair], 0, 0) for w, (pair, _) in zip(weights, both)]
    dq = [dot_on(x, k, 1, 0) for x, k in zip(dsb, keys)]
    for pair in range(pairs):
        dq_ref[rows, cols[pair]] = (merge_stack(sum(dq[pair * seqs : (pair + 1) * seqs])) * scale).astype(BF)
        for seq in range(seqs):
            dkv_acc[pair, spans[seq]] += dk[pair * seqs + seq]
            dkv_acc[pairs + pair, spans[seq]] += dv[pair * seqs + seq]
    first_row, row_step, cells, per_block = glob_at_rows
    for seq in range(seqs):
        for r in range(per_block):
            source = pl.ds(seq * span + ext + r * blocks, blocks)
            for c in range(2 * pairs):
                rows = pl.ds((seq * per_block + r) * 2 * pairs + c, blocks, stride=cells)
                glob_stage[rows, :] = dkv_acc[c, source, :]
    glob_low[...] = glob_stage[...].astype(BF)
    for i in range(blocks):
        pltpu.make_async_copy(
            glob_low.at[pl.ds(i * cells, cells)],
            grads_ref.at[pl.ds(first_row + (i + 1) * row_step - cells, cells)],
            sems.at[5],
        ).start()
    norms_ref[...] = jnp.zeros_like(norms_ref)
    for row, source in enumerate((gn_ref, gn_ref, norm_two_ref, norm_two_ref)):
        for half in range(source.shape[1] // head_cols):
            at = row * (source.shape[1] // head_cols) + half
            norms_ref[at : at + 1] = source[row % 2 : row % 2 + 1, half * head_cols : (half + 1) * head_cols]
    small_ref[...] = jnp.concatenate([drel_ref[: SMALL_ROWS - 8], norms_ref[...]], axis=0).astype(BF)
    for c in range(2 * pairs):
        dkv_ref[:, c * LANES : (c + 1) * LANES] = dkv_acc[c].astype(BF)
    per = head_cols // LANES

    def cut(j):
        row = pl.multiple_of(j * 256, 256)
        rows = pl.ds(row, 256)
        first = 2 * per * j
        q_stage[rows, :] = dot_on(xr_ref[:, rows], dq_ref[...], 0, 0).astype(BF)
        send_tiles(q_stage, row, 2, first, place_ref, grads_ref, sems.at[1])
        both = dot_on(xe_ref[:, rows], dkv_ref[...], 0, 0).astype(BF)
        k_stage[rows, :] = both[:, :head_cols]
        v_stage[rows, :] = both[:, head_cols:]
        send_tiles(k_stage, row, 2, attn_tiles + first, place_ref, grads_ref, sems.at[2])
        send_tiles(v_stage, row, 2, 2 * attn_tiles + first, place_ref, grads_ref, sems.at[3])

    col_loop(q_stage.shape[0], cut)
    for at, stage in enumerate((out_stage, q_stage, k_stage, v_stage)):
        pltpu.make_async_copy(stage, stage, sems.at[at]).wait()
    for copy in spare:
        copy.wait()
    pltpu.make_async_copy(glob_low, glob_low, sems.at[5]).wait()


def start_weights(wall_ref, at, head_cols, wkv_ref, wq_ref, sems):
    model_dim = wkv_ref.shape[0]
    copies = [
        pltpu.make_async_copy(wall_ref.at[pl.ds(at[0], model_dim)], wkv_ref, sems.at[0]),
        pltpu.make_async_copy(
            wall_ref.at[pl.ds(at[1], model_dim), pl.ds(0, head_cols)], wq_ref, sems.at[1]
        ),
    ]
    for copy in copies:
        copy.start()
    return copies


def back_rows(proj, wkv_ref, wq_ref):
    cols = wq_ref.shape[1]
    return dot_on(proj[:, :cols], wq_ref[...], 1, 1) + dot_on(proj[:, cols:], wkv_ref[...], 1, 1)


def dx_kernel(dims, at, half_ref, dq_ref, dkv_ref, next_ref, last_ref, mid_ref, wall_ref,
              keep_ref, send_ref, proj_ref, wkv_ref, wq_ref, sems):
    seqs, block_len, _, ext, _, globs, _ = dims
    head_cols = dq_ref.shape[1]
    copies = start_weights(wall_ref, at, head_cols, wkv_ref, wq_ref, sems)
    proj_ref[:, :head_cols] = dq_ref[: seqs * block_len]
    for seq in range(seqs):
        base, row = seq * (ext + globs) + RIM, seq * block_len
        middle = block_len - 2 * RIM
        own = dkv_ref[base : base + block_len].astype(F32)
        sums = [
            own[:RIM] + last_ref[seq * RIM : (seq + 1) * RIM].astype(F32),
            own[RIM : RIM + middle],
            own[RIM + middle :] + next_ref[seq * RIM : (seq + 1) * RIM].astype(F32),
        ]
        proj_ref[row : row + block_len, head_cols:] = jnp.concatenate(sums, axis=0).astype(BF)
    for copy in copies:
        copy.wait()
    per = block_len // 2
    for out_ref, half in ((keep_ref, half_ref[0]), (send_ref, 1 - half_ref[0])):
        for seq in range(seqs):
            rows = pl.ds(pl.multiple_of(seq * block_len + half * per, per), per)
            total = back_rows(proj_ref[rows, :], wkv_ref, wq_ref)
            if out_ref is keep_ref:
                total = total + mid_ref[rows, :]
            out_ref[seq] = total.astype(out_ref.dtype)


def dx_glob_kernel(dims, at, half_ref, dq_ref, kept_ref, got_ref, mid_ref, wall_ref,
                   keep_ref, send_ref, cells_ref, wkv_ref, wq_ref, sems):
    seqs, block_len, glob_block = dims[:3]
    head_cols = dq_ref.shape[1]
    base = seqs * block_len
    used, cols = seqs * glob_block, 2 * head_cols // LANES
    copies = start_weights(wall_ref, at, head_cols, wkv_ref, wq_ref, sems)
    first = kept_ref.shape[0] - used * cols
    cells_ref[...] = kept_ref[first:].astype(F32) + got_ref[first:].astype(F32)
    wide = [cells_ref[pl.ds(c, used, stride=cols), :] for c in range(cols)]
    dkv = jnp.concatenate(wide, axis=1)
    dkv = jnp.concatenate([dkv, jnp.zeros((dq_ref.shape[0] - base - used, 2 * head_cols), F32)], axis=0)
    proj = jnp.concatenate([dq_ref[base:], dkv.astype(BF)], axis=1)
    for copy in copies:
        copy.wait()
    total = back_rows(proj, wkv_ref, wq_ref)
    few = glob_block // 2
    here = half_ref[0] == 0
    for seq in range(seqs):
        start = seq * glob_block
        halves = [total[start : start + few], total[start + few : start + glob_block]]
        mids = [
            mid_ref[base + start : base + start + few, :],
            mid_ref[base + start + few : base + start + glob_block, :],
        ]
        keep_ref[seq] = jnp.where(here, halves[0] + mids[0], halves[1] + mids[1])
        send_ref[seq] = jnp.where(here, halves[1], halves[0]).astype(BF)


def swap_cores(values):
    count = lax.axis_size("ffn")
    return lax.ppermute(values, "ffn", [(i, i ^ 1) for i in range(count)])


def on_device(
    x_long,
    x_glob,
    sentence,
    dy_long,
    dy_glob,
    owner_list,
    w_master,
    m_old,
    v_old,
    left_basis,
    right_basis,
    left_stats,
    right_stats,
    rel_table,
    rel_m,
    rel_v,
    norm_params,
    norm_m,
    norm_v,
):
    ffn_count = lax.axis_size("ffn")
    seq_count = lax.axis_size("seq")
    seqs, tok_half, model_dim = x_long.shape
    glob_half = x_glob.shape[1]
    block_len = tok_half * ffn_count
    glob_block = glob_half * ffn_count
    globs = glob_block * seq_count
    head_cols = model_dim // ffn_count
    hidden = FF // ffn_count
    scale = (model_dim // HEADS) ** (-0.5)
    slots, side = w_master.shape[:2]
    attn_tiles = model_dim * head_cols // (side * side)
    ffn_tiles = model_dim * hidden // (side * side)
    tile_count = 4 * attn_tiles + 2 * ffn_tiles
    slot_count = owner_list.shape[0]
    labels = rel_table.shape[0]
    half_index = lax.axis_index("ffn")
    first_half = half_index == 0
    parts = slot_parts(slots, seq_count)

    glob_cells = seqs * glob_block * model_dim // LANES
    rows_per = part_rows(parts, side, glob_cells)
    places, place_rows = slot_places(owner_list, slots, rows_per, side)
    held = jnp.sum(
        jnp.where(
            places[None, :] == jnp.arange(slot_count, dtype=jnp.int32)[:, None],
            jnp.arange(slot_count, dtype=jnp.int32)[None, :],
            0,
        ),
        axis=1,
    )
    per_row = model_dim // side
    up_rows = hidden // model_dim * model_dim
    kv_at = up_rows + hidden
    q_at = kv_at + model_dim
    out_at = q_at + model_dim
    head_tiles = head_cols // side
    up_tiles = hidden // side

    def tile_row_col(tile):
        kind_qkv = tile // attn_tiles
        inner = tile % attn_tiles
        qkv_row = jnp.where(kind_qkv == 0, q_at, kv_at) + inner // head_tiles * side
        qkv_col = jnp.where(kind_qkv == 2, head_cols, 0) + inner % head_tiles * side
        out_row = out_at + inner // per_row * side
        up = tile - 4 * attn_tiles
        up_col = up % up_tiles * side
        up_row = up_col // model_dim * model_dim + up // up_tiles * side
        down = up - ffn_tiles
        down_row = up_rows + down // per_row * side
        row = jnp.where(
            tile < 3 * attn_tiles,
            qkv_row,
            jnp.where(
                tile < 4 * attn_tiles,
                out_row,
                jnp.where(up < ffn_tiles, up_row, down_row),
            ),
        )
        col = jnp.where(
            tile < 3 * attn_tiles,
            qkv_col,
            jnp.where(
                tile < 4 * attn_tiles,
                inner % per_row * side,
                jnp.where(up < ffn_tiles, up_col % model_dim, down % per_row * side),
            ),
        )
        return row, col

    wall_row, wall_col = tile_row_col(held)
    wall_kind = jnp.where(held < 4 * attn_tiles, 0, jnp.where(held < tile_count, 1, 2))

    weights_low = w_master.astype(BF).reshape(-1, LANES)
    glob_other = swap_cores(x_glob)
    glob_own = jnp.concatenate(
        [jnp.where(first_half, x_glob, glob_other), jnp.where(first_half, glob_other, x_glob)], axis=1
    )
    orders = [order for _, _, order in parts]
    gathered = gather_rows(
        weights_low, glob_own.reshape(-1, LANES), rows_per, orders
    )
    gathered = [
        [piece.reshape(-1, many, LANES) for piece in pieces] for pieces, many in zip(gathered, rows_per)
    ]
    tiles_per = tuple(last - first for (first, last, _), pieces in zip(parts, gathered) for _ in pieces)
    gathered = [piece for pieces in gathered for piece in pieces]

    rim = jnp.where(first_half, x_long[:, :RIM], x_long[:, tok_half - RIM :])
    mine = jnp.concatenate([x_long, dy_long, x_glob, dy_glob], axis=1)
    spare = -mine.shape[1] % 8
    mine = jnp.concatenate([mine, jnp.zeros((seqs, spare, model_dim), BF)], axis=1)
    first, second = mine.reshape(-1, model_dim), rim.reshape(-1, model_dim)
    first, second, _ = move_rows(
        [[(first.shape[0], (first, 0))], [(second.shape[0], (second, 0))], [(16, (weights_low, 0))]]
    )
    mine, rim = first.reshape(mine.shape), second
    other = swap_cores(mine)
    lower = jnp.where(first_half, mine, other)
    upper = jnp.where(first_half, other, mine)

    def block_rows(at, count):
        return jnp.concatenate([lower[:, at : at + count], upper[:, at : at + count]], axis=1)

    long_rows = block_rows(0, tok_half)
    dy_rows = block_rows(tok_half, tok_half)
    glob_rows = block_rows(2 * tok_half, glob_half)
    dy_globs = block_rows(2 * tok_half + glob_half, glob_half)
    used = seqs * (block_len + glob_block)
    row_count = seqs * block_len + up_to(seqs * glob_block, 16)
    pad_rows = jnp.zeros((row_count - used, model_dim), BF)

    def in_rows(long_part, glob_part):
        return jnp.concatenate(
            [long_part.reshape(-1, model_dim), glob_part.reshape(-1, model_dim), pad_rows]
        )

    x_rows = in_rows(long_rows, glob_rows)
    dy_all = in_rows(dy_rows, dy_globs)
    to_next = [(i * ffn_count + 1, (i + 1) * ffn_count + 1) for i in range(seq_count - 1)]
    to_last = [((i + 1) * ffn_count, i * ffn_count) for i in range(seq_count - 1)]
    rim = lax.ppermute(rim, ("seq", "ffn"), to_next + to_last)
    rim_other = swap_cores(rim)
    rim_left = jnp.where(first_half, rim_other, rim)
    rim_right = jnp.where(first_half, rim, rim_other)

    reach = 2 * RADIUS
    width = up_to(LANES + 2 * RIM, LANES) if globs % LANES == 0 else up_to(LANES + 2 * RIM + globs, LANES) - globs
    ext = block_len - LANES + width
    span = ext + globs
    rel_low = jnp.pad(
        rel_table.astype(BF), ((RIM - RADIUS, LABEL_PAD - labels - RIM + RADIUS), (0, 0))
    )

    glob_bias_rows = row_count - seqs * block_len
    row_at = jnp.arange(glob_bias_rows, dtype=jnp.int32)[None, :, None]
    seq_at = jnp.arange(seqs, dtype=jnp.int32)[:, None, None]
    spread = jnp.pad(sentence[:, 0], ((0, 0), (RIM, span - RIM - block_len)), constant_values=-1)
    span_at = jnp.arange(span, dtype=jnp.int32)[None, None, :]
    own = (spread[:, None, :] == row_at - seq_at * glob_block) & (spread[:, None, :] >= 0)
    glob_bias = jnp.where(own | (span_at >= ext), 0.0, NEG_FILL).astype(F32)

    spec_up = block_at((up_rows, model_dim), 0, 0)
    spec_down = block_at((hidden, model_dim), 1, 0)
    spec_out = block_at((head_cols, model_dim), out_at // head_cols, 0)

    def rows_of(cols, dtype=BF, rows=row_count):
        return jax.ShapeDtypeStruct((rows, cols), dtype)

    def specs(arrays):
        return [whole(a.shape) for a in arrays]

    dims = (seqs, block_len, glob_block, ext, width, globs, scale)
    fwd_shapes = (
        rows_of(head_cols),
        rows_of(head_cols, rows=seqs * span),
        rows_of(head_cols, rows=seqs * span),
        rows_of(head_cols),
        rows_of(model_dim),
        rows_of(model_dim, rows=seqs * span),
    )
    wall_at = (
        2 * ffn_tiles // per_row * side,
        4 * attn_tiles // per_row * side,
        kv_at,
        q_at,
        out_at,
        tiles_per,
    )
    wall_shape = jax.ShapeDtypeStruct((out_at + head_cols, model_dim), BF)
    block_now = lax.axis_index("seq").astype(jnp.int32).reshape(1)
    ins = [x_rows, rel_low, glob_bias]
    query, keys, values, heads_out, attn_part, x_ext, wall = kernel_call(
        functools.partial(attend_kernel, dims, wall_at, seq_count),
        "attend",
        28,
        fwd_shapes + (wall_shape,),
        [scalars()] * 4 + specs(ins) + [any_space()] * (2 + len(gathered)),
        tuple(specs(fwd_shapes)) + (any_space(),),
        [
            pltpu.VMEM(wall_shape.shape, BF),
            pltpu.VMEM((seq_count * glob_cells, LANES), BF),
            pltpu.VMEM((seq_count * glob_cells, LANES), F32),
            pltpu.SemaphoreType.DMA((5,)),
        ],
        flops=4 * 10**9,
        bytes_moved=10**7,
    )(wall_row, wall_col, wall_kind, block_now, *ins, rim_left, rim_right, *gathered)
    attn_got = swap_cores(attn_part)
    feed_shapes = (
        rows_of(model_dim, F32),
        rows_of(model_dim),
        rows_of(hidden, F32),
        rows_of(hidden),
        rows_of(model_dim),
        rows_of(model_dim, F32),
    )
    norm_one, norm_low, up_pre, act_low, down_part, mid_rows = kernel_call(
        feed_kernel,
        "feed",
        24,
        feed_shapes,
        specs([x_rows, attn_part, attn_got, norm_params]) + [spec_up, spec_down],
        tuple(specs(feed_shapes[:-1])) + (far_space(),),
        [pltpu.VMEM((row_count, model_dim), F32), pltpu.SemaphoreType.DMA((1,))],
        flops=3 * 10**9,
        bytes_moved=10**7,
    )(x_rows, attn_part, attn_got, norm_params, wall, wall)
    down_got = swap_cores(down_part)
    norm_shape = jax.ShapeDtypeStruct((8, model_dim), F32)
    half_now = half_index.astype(jnp.int32).reshape(1)
    back_shapes = (
        jax.ShapeDtypeStruct(x_long.shape, BF),
        jax.ShapeDtypeStruct(x_glob.shape, BF),
        rows_of(model_dim, F32),
        rows_of(model_dim),
        rows_of(hidden),
        rows_of(model_dim),
        norm_shape,
    )
    y_long, y_glob, d_pre, d_pre_low, d_up, d_norm_part, norm_two_grad = kernel_call(
        functools.partial(feed_back_kernel, dims),
        "feed_back",
        30,
        back_shapes,
        [scalars()]
        + specs([norm_one, down_part, down_got, up_pre, dy_all, norm_params])
        + [spec_up, spec_down],
        tuple(specs(back_shapes[:2])) + (far_space(),) + tuple(specs(back_shapes[3:])),
        [pltpu.VMEM((row_count, model_dim), F32)] * 2 + [pltpu.SemaphoreType.DMA((1,))],
        flops=3 * 10**9,
        bytes_moved=10**7,
    )(half_now, norm_one, down_part, down_got, up_pre, dy_all, norm_params, wall, wall)
    d_norm_got = swap_cores(d_norm_part)
    grads_shape = jax.ShapeDtypeStruct((seq_count * sum(rows_per), LANES), BF)
    slot_grads = kernel_call(
        functools.partial(feed_grads_kernel, (4 * attn_tiles, 4 * attn_tiles + ffn_tiles)),
        "feed_grads",
        16,
        grads_shape,
        [scalars()] + specs([act_low, d_pre_low, norm_low, d_up]),
        any_space(),
        [
            pltpu.VMEM((hidden, model_dim), BF),
            pltpu.VMEM((model_dim, hidden), BF),
            pltpu.SemaphoreType.DMA((2,)),
        ],
        flops=3 * 10**9,
        bytes_moved=10**7,
    )(place_rows, act_low, d_pre_low, norm_low, d_up)
    ins = [
        x_rows,
        mid_rows,
        d_norm_part,
        d_norm_got,
        d_pre,
        heads_out,
        query,
        keys,
        values,
        x_ext,
    ]
    last_shapes = (
        grads_shape,
        rows_of(head_cols),
        rows_of(2 * head_cols, rows=seqs * span),
        rows_of(model_dim, F32),
        rows_of(head_cols, rows=SMALL_ROWS),
    )
    slot_grads, d_query, dkv, d_mid, small = kernel_call(
        functools.partial(
            attend_back_kernel,
            dims,
            seq_count,
            attn_tiles,
            (tile_count, slot_count),
            (seq_count * sum(rows_per[:-1]), rows_per[-1], glob_cells, glob_block),
        ),
        "attend_back",
        32,
        last_shapes,
        [scalars(), scalars(), whole(norm_shape.shape)]
        + specs(ins)
        + [spec_out]
        + specs([rel_low, glob_bias, norm_params])
        + [any_space()],
        (any_space(),) + tuple(specs(last_shapes[1:])),
        [
            pltpu.VMEM((row_count, head_cols), BF),
            pltpu.VMEM((row_count, model_dim), BF),
            pltpu.VMEM((2 * head_cols // LANES, seqs * span, LANES), F32),
            pltpu.VMEM((head_cols, model_dim), BF),
            pltpu.VMEM((model_dim, head_cols), BF),
            pltpu.VMEM((model_dim, head_cols), BF),
            pltpu.VMEM((model_dim, head_cols), BF),
            pltpu.VMEM((side, side), BF),
            pltpu.VMEM((LABEL_PAD, head_cols), F32),
            pltpu.VMEM((8, head_cols), F32),
            pltpu.VMEM((8, model_dim), F32),
            pltpu.VMEM((seq_count * glob_cells, LANES), F32),
            pltpu.VMEM((seq_count * glob_cells, LANES), BF),
            pltpu.SemaphoreType.DMA((6,)),
        ],
        {3 + len(ins) + 4: 0},
        flops=8 * 10**9,
        bytes_moved=2 * 10**7,
    )(block_now, place_rows, norm_two_grad, *ins, wall, rel_low, glob_bias, norm_params, slot_grads)

    bits = seq_bits(seq_count)
    carried = [
        [(RIM, (dkv, seq * span + at)) for seq in range(seqs)] for at in (0, RIM + block_len)
    ]
    sums, small, (to_last, to_next) = scatter_rows(
        slot_grads, rows_per, orders, small, bits[3:] + bits[:3], carried
    )
    from_next = lax.ppermute(to_last, "seq", [(i + 1, i) for i in range(seq_count - 1)])
    from_last = lax.ppermute(to_next, "seq", [(i, i + 1) for i in range(seq_count - 1)])

    weights_at = (kv_at, q_at)
    weights_held = [
        pltpu.VMEM((model_dim, model_dim), BF),
        pltpu.VMEM((model_dim, head_cols), BF),
        pltpu.SemaphoreType.DMA((2,)),
    ]
    dx_shapes = (
        jax.ShapeDtypeStruct(x_long.shape, F32),
        jax.ShapeDtypeStruct(x_long.shape, BF),
    )
    ins = [d_query, dkv, from_next, from_last, d_mid]
    dx_kept, dx_sent = kernel_call(
        functools.partial(dx_kernel, dims, weights_at),
        "dx_long",
        20,
        dx_shapes,
        [scalars()] + specs(ins) + [any_space()],
        tuple(specs(dx_shapes)),
        [pltpu.VMEM((seqs * block_len, 3 * head_cols), BF)] + weights_held,
        flops=10**9,
        bytes_moved=10**7,
    )(half_now, *ins, wall)
    dx_long = dx_kept + swap_cores(dx_sent).astype(F32)
    glob_shapes = (
        jax.ShapeDtypeStruct(x_glob.shape, F32),
        jax.ShapeDtypeStruct(x_glob.shape, BF),
    )
    ins = [d_query, sums[0], sums[1], d_mid]
    dx_kept, dx_sent = kernel_call(
        functools.partial(dx_glob_kernel, dims, weights_at),
        "dx_glob",
        12,
        glob_shapes,
        [scalars()] + specs(ins) + [any_space()],
        tuple(specs(glob_shapes)),
        [pltpu.VMEM((glob_cells, LANES), F32)] + weights_held,
        flops=10**8,
        bytes_moved=10**6,
    )(half_now, *ins, wall)
    dx_glob = dx_kept + swap_cores(dx_sent).astype(F32)

    state = (w_master, m_old, v_old, left_basis, right_basis, left_stats, right_stats)
    others = (rel_table, rel_m, rel_v, norm_params, norm_m, norm_v)
    new_state = soap_update(sums, small, state, others)
    w_new, m_new, v_new, left_q, right_q, left_s, right_s = new_state[:7]
    rel_new, rel_m_new, rel_v_new, norm_new, norm_m_new, norm_v_new = new_state[7:]
    return (
        y_long,
        y_glob,
        dx_long,
        dx_glob,
        w_new,
        m_new,
        v_new,
        left_q,
        right_q,
        left_s,
        right_s,
        rel_new,
        rel_m_new,
        rel_v_new,
        norm_new,
        norm_m_new,
        norm_v_new,
    )


def solution(mesh):
    in_specs = (
        P(None, ("seq", "ffn"), None),
        P(None, ("seq", "ffn"), None),
        P(None, "seq", None),
        P(None, ("seq", "ffn"), None),
        P(None, ("seq", "ffn"), None),
        P(),
        P(("seq", "ffn"), None, None),
        P(("seq", "ffn"), None, None),
        P(("seq", "ffn"), None, None),
        P(("seq", "ffn"), None, None),
        P(("seq", "ffn"), None, None),
        P(("seq", "ffn"), None, None),
        P(("seq", "ffn"), None, None),
        P(None, "ffn"),
        P(None, "ffn"),
        P(None, "ffn"),
        P(),
        P(),
        P(),
    )
    out_specs = (
        P(None, ("seq", "ffn"), None),
        P(None, ("seq", "ffn"), None),
        P(None, ("seq", "ffn"), None),
        P(None, ("seq", "ffn"), None),
        P(("seq", "ffn"), None, None),
        P(("seq", "ffn"), None, None),
        P(("seq", "ffn"), None, None),
        P(("seq", "ffn"), None, None),
        P(("seq", "ffn"), None, None),
        P(("seq", "ffn"), None, None),
        P(("seq", "ffn"), None, None),
        P(None, "ffn"),
        P(None, "ffn"),
        P(None, "ffn"),
        P(),
        P(),
        P(),
    )
    return jax.shard_map(
        on_device, mesh=mesh, in_specs=in_specs, out_specs=out_specs, check_vma=False
    )
```
